32 devices in a mesh: seq: 16 (over z, y, core), head: 2 (over x).
Axes of the slice: x: 2, y: 2, z: 4, core: 2. Of those that a mesh axis runs over, the one named last changes fastest.
Arguments:
- queries: bfloat16 [6144, 768], P('seq', 'head'), as said below
- keys: bfloat16 [6144, 768], P('seq', 'head'), as said below
- values: bfloat16 [6144, 768], P('seq', 'head'), may hold values from -6 to 6
- image_tiles: int32 [5], replicated, may hold values from 1 to 21, 48 in all
Outputs:
- attended: bfloat16 [6144, 768], P(('seq', 'head'))
The draws below stay inside these ranges and needn't reach their ends.
Inputs may be any that keep to these rules, and one draw needn't show every extreme that they name: `image_tiles`: the 5 images fill all 48 tiles in order; the longest holds exactly 21 tiles. `queries`: entries lie within -6 and 6. `keys`: entries lie within -6 and 6.
All inputs are finite; a program needn't handle non-finite values.
Results may differ from the reference program's by a relative error of at most 0.007.
Values may be sent and summed in bfloat16 or wider, within the bound.
No kernel may reach another device: no remote copies, remote signals or barrier semaphores. Data moves between devices by JAX's collectives and lax.ppermute only.
A program may use at most 64 MiB of HBM per device.

```python
import math
import jax
import jax.numpy as jnp
import numpy as np
from jax import lax

HEAD_DIM = 128
TILE = 128
HEADS = 6
WIDTH = 768
TOKENS = 6144
NT = 48
MOST_TILES = 21
IMAGES = 5


def base_draw(key):
    return jnp.clip(jax.random.normal(key, (TOKENS, WIDTH), jnp.float32), -6.0, 6.0)


def draw_queries(key, part):
    drawn = base_draw(jax.random.fold_in(key, 21))
    return drawn.astype(jnp.bfloat16)


def draw_keys(key, part):
    drawn = base_draw(jax.random.fold_in(key, 22))
    return drawn.astype(jnp.bfloat16)


def block_scale(key, dims, pieces, low, high):
    loudness, own = 1.0, jax.random.fold_in(key, 6)
    for axis_at, shards_of in pieces:
        heights = jnp.exp(jax.random.uniform(jax.random.fold_in(own, axis_at), (shards_of,), jnp.float32, low / len(pieces), high / len(pieces)))
        loudness = loudness * jnp.repeat(heights, dims[axis_at] // shards_of).reshape([-1 if axis == axis_at else 1 for axis in range(len(dims))])
    return loudness


def length_profile(number_of, total, bound, lean):
    portions = [(1 << 20) // math.isqrt(grade ** lean) + 1 for grade in range(2, number_of + 1)]
    surplus, counts = total - bound - (number_of - 1), [1] * (number_of - 1)
    while surplus > 0:
        free = [i for i in range(number_of - 1) if counts[i] < bound]
        mass, remaining = sum([portions[i] for i in free]), surplus
        for i in free:
            more = min(bound - counts[i], max(1, remaining * portions[i] // mass), surplus)
            counts[i] = counts[i] + more
            surplus = surplus - more
    return np.array([bound] + counts)


def uneven_parts(own_key, amount, total, limit, lean):
    if amount == 2:
        one = jax.random.randint(own_key, (), max(1, total - limit), min(limit, total - 1) + 1)
        return jnp.stack([one, total - one])
    sizes = jnp.asarray(length_profile(amount, total, limit, lean), jnp.int32)
    couples = (amount - 1) // 2
    source_of, receiver = sizes[1:1 + 2 * couples:2], sizes[2:2 + 2 * couples:2]
    room = jnp.minimum(source_of - 1, limit - receiver)
    shifted = jax.random.randint(jax.random.fold_in(own_key, 1), (couples,), 0, 1 << 20) % (room + 1)
    sizes = sizes.at[1:1 + 2 * couples:2].set(source_of - shifted).at[2:2 + 2 * couples:2].set(receiver + shifted)
    return sizes[jax.random.permutation(jax.random.fold_in(own_key, 2), amount)]


def normal_values(stream_key, extent, width, most, split=(), kind=jnp.bfloat16):
    array = width * jax.random.normal(stream_key, extent, jnp.float32)
    if split:
        array = array * block_scale(stream_key, extent, split, -0.22, 0.18)
    return jnp.clip(array, -most, most).astype(kind)


def setup_inputs(seed: int = 0) -> dict:
    splits = jax.random.split(jax.random.key(seed), 5)
    queries = draw_queries(jax.random.fold_in(splits[4], 71), 0)
    keys = draw_keys(jax.random.fold_in(splits[4], 71), 0)
    values = normal_values(splits[2], (TOKENS, WIDTH), 1.0, 6.0, ((0, 16), (1, 2)))
    image_tiles = uneven_parts(splits[3], IMAGES, NT, MOST_TILES, 2).astype(jnp.int32)
    return dict(queries=queries, keys=keys, values=values, image_tiles=image_tiles)


def image_of(positions, image_tiles):
    image_ends = jnp.cumsum(image_tiles).astype(jnp.int32) * TILE
    return lax.optimization_barrier(jnp.sum((positions[:, None] >= image_ends[None, :]).astype(jnp.int32), axis=1)).astype(jnp.int32)

def reference(queries, keys, values, image_tiles):
    positions = jnp.arange(TOKENS, dtype=jnp.int32)
    token_image = image_of(positions, image_tiles)
    image_starts = (jnp.cumsum(image_tiles) - image_tiles).astype(jnp.int32) * TILE
    window = MOST_TILES * TILE
    padded_keys = jnp.pad(keys, ((0, window), (0, 0)))
    padded_values = jnp.pad(values, ((0, window), (0, 0)))
    padded_images = jnp.pad(token_image, (0, window), constant_values=-1)
    score_scale = 1.0 / math.sqrt(HEAD_DIM)

    def one_tile(tile_index):
        first_row = (tile_index * TILE).astype(jnp.int32)
        query_tile = lax.dynamic_slice_in_dim(queries, first_row, TILE, 0)
        image_index = token_image[first_row]
        key_start = image_starts[image_index].astype(jnp.int32)
        key_tile = lax.dynamic_slice_in_dim(padded_keys, key_start, window, 0)
        value_tile = lax.dynamic_slice_in_dim(padded_values, key_start, window, 0)
        key_images = lax.dynamic_slice_in_dim(padded_images, key_start, window, 0)
        query_heads = query_tile.reshape(TILE, HEADS, HEAD_DIM).astype(jnp.float32)
        key_heads = key_tile.reshape(window, HEADS, HEAD_DIM).astype(jnp.float32)
        value_heads = value_tile.reshape(window, HEADS, HEAD_DIM).astype(jnp.float32)
        scores = jnp.einsum('qhd,khd->hqk', query_heads, key_heads) * score_scale
        key_mask = (key_images == image_index)[None, None, :]
        scores = jnp.where(key_mask, scores, -jnp.inf)
        largest = lax.optimization_barrier(jnp.max(scores, axis=2, keepdims=True))
        weights = jnp.where(key_mask, jnp.exp(scores - largest), 0.0)
        weight_total = lax.optimization_barrier(jnp.sum(weights, axis=2))
        rounded = lax.optimization_barrier(weights.astype(jnp.bfloat16)).astype(jnp.float32)
        summed = jnp.einsum('hqk,khd->qhd', rounded, value_heads)
        attended = summed / jnp.transpose(weight_total)[:, :, None]
        return attended.reshape(TILE, WIDTH).astype(jnp.bfloat16)
    tiles = lax.map(one_tile, jnp.arange(TOKENS // TILE, dtype=jnp.int32))
    return tiles.reshape(TOKENS, WIDTH)
```

```python
import functools
import math

import jax
import jax.numpy as jnp
from jax import lax
from jax.experimental import pallas as pl
from jax.experimental.pallas import tpu as pltpu
from jax.sharding import PartitionSpec as P

HEAD_DIM = 128
TILE = 128
MOST_TILES = 21

LOWEST = -1e30
SCALE2 = math.log2(math.e) / math.sqrt(HEAD_DIM)

VMEM = pl.BlockSpec(memory_space=pltpu.VMEM)
SMEM = pl.BlockSpec(memory_space=pltpu.SMEM)


def params():
    return pltpu.CompilerParams(vmem_limit_bytes=32 * 1024 * 1024)


def pack_kernel(k_ref, v_ref, out_ref):
    rows, columns = k_ref.shape
    out_ref[:rows, :columns] = k_ref[...]
    out_ref[rows:, :rows] = v_ref[...].T


def pack(keys, values):
    rows, columns = keys.shape
    return pl.pallas_call(
        pack_kernel,
        out_shape=jax.ShapeDtypeStruct((rows + columns, max(rows, columns)), keys.dtype),
        in_specs=[VMEM, VMEM],
        out_specs=VMEM,
        compiler_params=params(),
        name="pack",
    )(keys, values)


def image_bounds(tiles_ref, tile):
    first = jnp.int32(0)
    start, end = jnp.int32(0), jnp.int32(0)
    for i in range(tiles_ref.shape[0]):
        after = first + tiles_ref[i]
        inside = (tile >= first) & (tile < after)
        start = jnp.where(inside, first, start)
        end = jnp.where(inside, after, end)
        first = after
    return start, end


def attend_kernel(halves, slots, fresh, rows, columns, tiles_ref, owners_ref, *refs):
    heads = columns // HEAD_DIM
    tiles = rows // TILE
    q_refs, refs = refs[:halves], refs[halves:]
    slot_refs, refs = refs[: len(slots)], refs[len(slots) :]
    if fresh:
        old_refs, new_refs = refs, refs
    else:
        old_refs, new_refs = refs[:halves], refs[halves:]

    for half in range(halves):
        q_ref, old_ref, new_ref = q_refs[half], old_refs[half], new_refs[half]
        if fresh:
            new_ref[:columns] = jnp.zeros((columns, rows), jnp.float32)
            new_ref[columns : columns + heads] = jnp.full((heads, rows), LOWEST, jnp.float32)
            new_ref[columns + heads :] = jnp.zeros((new_ref.shape[0] - columns - heads, rows), jnp.float32)
        else:
            new_ref[...] = old_ref[...]

        @pl.loop(0, tiles)
        def _(at):
            lanes = pl.ds(pl.multiple_of(at * TILE, TILE), TILE)
            start, end = image_bounds(tiles_ref, owners_ref[half] * tiles + at)
            for slot_ref, owner_at in zip(slot_refs, slots):
                first = owners_ref[owner_at] * tiles

                @pl.when((first < end) & (first + tiles > start))
                def _():
                    off = [
                        jnp.where((first + j >= start) & (first + j < end), 0.0, -LOWEST).astype(jnp.float32)
                        for j in range(tiles)
                    ]
                    for h in range(heads):
                        columns_h = slice(h * HEAD_DIM, (h + 1) * HEAD_DIM)
                        scores = lax.dot_general(
                            slot_ref[:rows, columns_h],
                            q_ref[lanes, columns_h],
                            (((1,), (1,)), ((), ())),
                            preferred_element_type=jnp.float32,
                        )
                        parts = [scores[j * TILE : (j + 1) * TILE] for j in range(tiles)]
                        old_max = new_ref[columns + h : columns + h + 1, lanes]
                        new_max = old_max
                        for j in range(tiles):
                            new_max = jnp.maximum(new_max, jnp.max(parts[j], axis=0, keepdims=True) - off[j])
                        scaled = new_max * SCALE2
                        weights = [jnp.exp2(parts[j] * SCALE2 - (scaled + off[j])) for j in range(tiles)]
                        factor = jnp.exp2((old_max - new_max) * SCALE2)
                        total = functools.reduce(jnp.add, weights)
                        total = jnp.sum(total, axis=0, keepdims=True)
                        rounded = jnp.concatenate([w.astype(jnp.bfloat16) for w in weights], axis=0)
                        update = jnp.dot(
                            slot_ref[rows + h * HEAD_DIM : rows + (h + 1) * HEAD_DIM, :rows],
                            rounded,
                            preferred_element_type=jnp.float32,
                        )
                        at_total = slice(columns + heads + h, columns + heads + h + 1)
                        new_ref[columns_h, lanes] = new_ref[columns_h, lanes] * factor + update
                        new_ref[columns + h : columns + h + 1, lanes] = new_max
                        new_ref[at_total, lanes] = new_ref[at_total, lanes] * factor + total


def attend(image_tiles, owners, queries, blocks, slots, states):
    halves = len(queries)
    rows, columns = queries[0].shape
    heads = columns // HEAD_DIM
    state_rows = columns + -(-2 * heads // 8) * 8
    shape = jax.ShapeDtypeStruct((state_rows, rows), jnp.float32)
    fresh = not states
    pairs = halves * (rows // TILE) ** 2 * heads * len(blocks)
    return pl.pallas_call(
        functools.partial(attend_kernel, halves, slots, fresh, rows, columns),
        out_shape=[shape] * halves,
        in_specs=[SMEM, SMEM] + [VMEM] * (halves + len(blocks) + len(states)),
        out_specs=[VMEM] * halves,
        compiler_params=params(),
        cost_estimate=pl.CostEstimate(
            flops=pairs * 4 * TILE * TILE * HEAD_DIM,
            bytes_accessed=len(blocks) * rows * columns * 4 + 4 * halves * state_rows * rows,
            transcendentals=pairs * TILE * TILE,
        ),
        name="attend",
    )(image_tiles, owners, *queries, *blocks, *states)


def finish_kernel(states, rows, columns, *refs):
    heads = columns // HEAD_DIM
    out_ref = refs[states]
    for h in range(heads):
        columns_h = slice(h * HEAD_DIM, (h + 1) * HEAD_DIM)
        maxima = [refs[i][columns + h : columns + h + 1] for i in range(states)]
        totals = [refs[i][columns + heads + h : columns + heads + h + 1] for i in range(states)]
        largest = functools.reduce(jnp.maximum, maxima)
        factors = [jnp.exp2((m - largest) * SCALE2) for m in maxima]
        total = functools.reduce(jnp.add, [f * t for f, t in zip(factors, totals)])
        summed = functools.reduce(jnp.add, [refs[i][columns_h] * (factors[i] / total) for i in range(states)])
        out_ref[:, columns_h] = summed.T.astype(out_ref.dtype)


def finish(states, rows, columns):
    return pl.pallas_call(
        functools.partial(finish_kernel, len(states), rows, columns),
        out_shape=jax.ShapeDtypeStruct((rows, columns), jnp.bfloat16),
        in_specs=[VMEM] * len(states),
        out_specs=VMEM,
        compiler_params=params(),
        name="finish",
    )(*states)


def chip_pairs(mesh):
    places = [tuple(getattr(d, "coords", ())) for d in mesh.devices[:, 0]]
    count = len(places)
    if count % 4 or not places[0]:
        return False
    cores = all(places[i] == places[i + 1] for i in range(0, count, 2))
    level = all(places[i][2] == places[i + 3][2] for i in range(0, count, 4))
    climb = all(places[i][2] != places[i + 4][2] for i in range(0, count - 4))
    return cores and level and climb


def paired_shards(owner_count, queries, keys, values, image_tiles):
    rows, columns = queries.shape
    tiles = rows // TILE
    every = range(owner_count)

    def sign(s):
        return 1 - 2 * ((s // 2) % 2)

    def moved(array, source):
        return lax.ppermute(array, "seq", [(source(s), s) for s in every if 0 <= source(s) < owner_count])

    along = lambda s: s + 4 * sign(s)
    against = lambda s: s - 4 * sign(s)
    across = lambda s: s + 2 * sign(s)
    corner = lambda s: s + 8 * (1 - 2 * (s % 2))
    sibling = lambda s: s + 1 - 2 * (s % 2)

    me = lax.axis_index("seq")
    owners = jnp.stack(
        [
            me,
            sibling(me),
            along(me),
            against(me),
            across(me),
            me - 2 * sign(me),
            me + 6 * sign(me),
            me - 6 * sign(me),
            corner(me),
        ]
    ).astype(jnp.int32)

    ends = jnp.cumsum(image_tiles)
    chip_tiles = 2 * tiles
    first_chip = (ends - image_tiles) // chip_tiles
    last_chip = (ends - 1) // chip_tiles
    odd_chip = first_chip + 1 - first_chip % 2
    far = jnp.where(last_chip - first_chip >= 4, 2, jnp.where(last_chip - odd_chip >= 3, 1, 0))
    far = jnp.max(far).astype(jnp.int32)

    block = pack(keys, values)
    a1 = moved(block, along)
    b1 = moved(block, against)
    y1 = moved(block, across)
    other = moved(queries, sibling)
    both = (queries, other)

    fold = functools.partial(attend, image_tiles, owners, both)
    states = fold([block], [0], [])
    ya = moved(a1, across)
    ay = moved(y1, along)
    states = fold([a1, b1, y1], [2, 3, 4], states)

    def near(block, ya, ay, states):
        return fold([ya, ay], [5, 6], states)

    def further(block, ya, ay, states):
        bya = moved(ya, against)
        states = fold([ya, ay], [5, 6], states)
        return fold([bya], [7], states)

    def furthest(block, ya, ay, states):
        bya = moved(ya, against)
        corner_block = moved(block, corner)
        states = fold([ya, ay], [5, 6], states)
        return fold([bya, corner_block], [7, 8], states)

    mine, theirs = lax.switch(far, [near, further, furthest], block, ya, ay, states)
    return finish([mine, moved(theirs, sibling)], rows, columns)


def ring_shards(owner_count, queries, keys, values, image_tiles):
    rows, columns = queries.shape
    reach = min(owner_count - 1, -(-(MOST_TILES - 1) // (rows // TILE)))
    me = lax.axis_index("seq")
    block = pack(keys, values)
    owners = jnp.stack([me] + [me - k for k in range(1, reach + 1)] + [me + k for k in range(1, reach + 1)])
    owners = owners.astype(jnp.int32)
    fold = functools.partial(attend, image_tiles, owners, (queries,))
    up = [(i, i + 1) for i in range(owner_count - 1)]
    down = [(i + 1, i) for i in range(owner_count - 1)]
    below = above = block
    states = []
    held, slots = [block], [0]
    for k in range(1, reach + 1):
        below = lax.ppermute(below, "seq", up)
        above = lax.ppermute(above, "seq", down)
        states = fold(held, slots, states)
        held, slots = [below, above], [k, reach + k]
    states = fold(held, slots, states)
    return finish(states, rows, columns)


def solution(mesh):
    owner_count = mesh.shape["seq"]
    plan = paired_shards if chip_pairs(mesh) else ring_shards

    def shards(queries, keys, values, image_tiles):
        attended = plan(owner_count, queries, keys, values, image_tiles)
        return lax.all_to_all(attended, "head", split_axis=0, concat_axis=1, tiled=True)

    placed = (P("seq", "head"), P("seq", "head"), P("seq", "head"), P())
    return jax.shard_map(
        shards, mesh=mesh, in_specs=placed, out_specs=P(("seq", "head"), None), check_vma=False
    )
```

```python
import functools
import math

import jax
import jax.numpy as jnp
from jax import lax
from jax.experimental import pallas as pl
from jax.experimental.pallas import tpu as pltpu
from jax.sharding import PartitionSpec as P

HEAD_DIM = 128
TILE = 128
MOST_TILES = 21

LOWEST = -1e30
SCALE2 = math.log2(math.e) / math.sqrt(HEAD_DIM)

VMEM = pl.BlockSpec(memory_space=pltpu.VMEM)
SMEM = pl.BlockSpec(memory_space=pltpu.SMEM)


def params():
    return pltpu.CompilerParams(vmem_limit_bytes=32 * 1024 * 1024)


def image_bounds(tiles_ref, tile):
    first = jnp.int32(0)
    start, end = jnp.int32(0), jnp.int32(0)
    for i in range(tiles_ref.shape[0]):
        after = first + tiles_ref[i]
        inside = (tile >= first) & (tile < after)
        start = jnp.where(inside, first, start)
        end = jnp.where(inside, after, end)
        first = after
    return start, end


def chip_spans(tiles_ref, chip_tiles):
    first = jnp.int32(0)
    even, odd, four = jnp.int32(0), jnp.int32(0), jnp.int32(0)
    for i in range(tiles_ref.shape[0]):
        after = first + tiles_ref[i]
        low, high = first // chip_tiles, (after - 1) // chip_tiles
        parity = low % 2
        even = jnp.where(high - (low + parity) >= 3, 1, even)
        odd = jnp.where(high - (low + 1 - parity) >= 3, 1, odd)
        four = jnp.where(high - low >= 4, 1, four)
        first = after
    return jnp.where(four > 0, 3, jnp.where(odd > 0, 1 + even, 0))


def pack_kernel(chunks, halves, tiles_ref, places_ref, k_ref, v_ref, *refs):
    rows = k_ref.shape[0]
    tiles = rows // TILE
    chunk_refs, (bounds_ref, spans_ref) = refs[: len(chunks)], refs[len(chunks) :]
    for half in range(halves):
        for at in range(tiles):
            start, end = image_bounds(tiles_ref, places_ref[half] * tiles + at)
            bounds_ref[2 * (half * tiles + at)] = start
            bounds_ref[2 * (half * tiles + at) + 1] = end
    spans_ref[0] = chip_spans(tiles_ref, 2 * tiles).astype(jnp.int32)
    for chunk, out_ref in zip(chunks, chunk_refs):
        for i, h in enumerate(chunk):
            source, target = slice(h * HEAD_DIM, (h + 1) * HEAD_DIM), slice(i * HEAD_DIM, (i + 1) * HEAD_DIM)
            out_ref[:rows, target] = k_ref[:, source]
            for j in range(tiles):
                out_ref[rows + j * TILE : rows + (j + 1) * TILE, target] = v_ref[j * TILE : (j + 1) * TILE, source].T


def pack(chunks, halves, image_tiles, places, keys, values):
    rows, _ = keys.shape
    shapes = [jax.ShapeDtypeStruct((2 * rows, len(c) * HEAD_DIM), keys.dtype) for c in chunks]
    *blocks, bounds, spans = pl.pallas_call(
        functools.partial(pack_kernel, chunks, halves),
        out_shape=shapes
        + [
            jax.ShapeDtypeStruct((2 * halves * (rows // TILE),), jnp.int32),
            jax.ShapeDtypeStruct((1,), jnp.int32),
        ],
        in_specs=[SMEM, SMEM, VMEM, VMEM],
        out_specs=[VMEM] * len(chunks) + [SMEM, SMEM],
        compiler_params=params(),
        name="pack",
    )(image_tiles, places, keys, values)
    return blocks, bounds, spans[0]


def corner_kernel(chunks, places_ref, *refs):
    out_ref = refs[-1]
    half = out_ref.shape[0] // 2
    skip = pl.multiple_of((places_ref[0] % 2) * TILE, TILE)
    base = 0
    for chunk, ref in zip(chunks, refs):
        rows, columns = ref.shape[0] // 2, len(chunk) * HEAD_DIM
        out_ref[:half, base : base + columns] = ref[pl.ds(skip, half), :]
        out_ref[half:, base : base + columns] = ref[pl.ds(rows + skip, half), :]
        base += columns


def corner_of(chunks, places, blocks):
    rows = blocks[0].shape[0] - 2 * TILE
    columns = sum(len(c) for c in chunks) * HEAD_DIM
    return pl.pallas_call(
        functools.partial(corner_kernel, chunks),
        out_shape=jax.ShapeDtypeStruct((rows, columns), blocks[0].dtype),
        in_specs=[SMEM] + [VMEM] * len(blocks),
        out_specs=VMEM,
        compiler_params=params(),
        name="corner",
    )(places, *blocks)


def attend_kernel(halves, chunk, slots, fresh, rows, bounds_ref, firsts_ref, *refs):
    heads = len(chunk)
    columns = heads * HEAD_DIM
    tiles = rows // TILE
    q_refs, refs = refs[:halves], refs[halves:]
    slot_refs, refs = refs[: len(slots)], refs[len(slots) :]
    old_refs, new_refs = (refs, refs) if fresh else (refs[:halves], refs[halves:])

    for half in range(halves):
        q_ref, old_ref, new_ref = q_refs[half], old_refs[half], new_refs[half]
        if fresh:
            new_ref[:columns] = jnp.zeros((columns, rows), jnp.float32)
            new_ref[columns : columns + heads] = jnp.full((heads, rows), LOWEST, jnp.float32)
            new_ref[columns + heads :] = jnp.zeros((new_ref.shape[0] - columns - heads, rows), jnp.float32)
        else:
            new_ref[...] = old_ref[...]

        at = 2 * half * tiles
        starts = [bounds_ref[at + 2 * t] for t in range(tiles)]
        ends = [bounds_ref[at + 2 * t + 1] for t in range(tiles)]

        def fold(slot_ref, first, base):
            count = slot_ref.shape[0] // 2 // TILE
            off = [
                [
                    jnp.where((first + j >= starts[t]) & (first + j < ends[t]), 0.0, -LOWEST).astype(jnp.float32)
                    for t in range(tiles)
                ]
                for j in range(count)
            ]
            for i, h in enumerate(chunk):
                own = slice(i * HEAD_DIM, (i + 1) * HEAD_DIM)
                there = slice((base + i) * HEAD_DIM, (base + i + 1) * HEAD_DIM)
                scores = lax.dot_general(
                    slot_ref[: count * TILE, there],
                    q_ref[:, h * HEAD_DIM : (h + 1) * HEAD_DIM],
                    (((1,), (1,)), ((), ())),
                    preferred_element_type=jnp.float32,
                )
                max_at = slice(columns + i, columns + i + 1)
                total_at = slice(columns + heads + i, columns + heads + i + 1)
                factors, rounded, totals, maxima = [], [], [], []
                for t in range(tiles):
                    lanes = slice(t * TILE, (t + 1) * TILE)
                    parts = [scores[j * TILE : (j + 1) * TILE, lanes] for j in range(count)]
                    old_max = new_ref[max_at, lanes]
                    new_max = old_max
                    for j in range(count):
                        new_max = jnp.maximum(new_max, jnp.max(parts[j], axis=0, keepdims=True) - off[j][t])
                    scaled = new_max * SCALE2
                    weights = [jnp.exp2(parts[j] * SCALE2 - (scaled + off[j][t])) for j in range(count)]
                    factors.append(jnp.exp2((old_max - new_max) * SCALE2))
                    totals.append(jnp.sum(functools.reduce(jnp.add, weights), axis=0, keepdims=True))
                    maxima.append(new_max)
                    rounded.append(jnp.concatenate([w.astype(jnp.bfloat16) for w in weights], axis=0))
                factor = jnp.concatenate(factors, axis=1)
                values = [
                    slot_ref[(count + j) * TILE : (count + j + 1) * TILE, there] for j in range(count)
                ]
                update = jnp.dot(
                    jnp.concatenate(values, axis=1),
                    jnp.concatenate(rounded, axis=1),
                    preferred_element_type=jnp.float32,
                )
                new_ref[own] = new_ref[own] * factor + update
                new_ref[max_at] = jnp.concatenate(maxima, axis=1)
                new_ref[total_at] = new_ref[total_at] * factor + jnp.concatenate(totals, axis=1)

        for slot_ref, (first_at, base) in zip(slot_refs, slots):
            first = firsts_ref[first_at]
            after = first + slot_ref.shape[0] // 2 // TILE
            pl.when((first < ends[-1]) & (after > starts[0]))(functools.partial(fold, slot_ref, first, base))


def attend(bounds, firsts, queries, chunk, blocks, slots, states):
    halves = len(queries)
    rows = queries[0].shape[0]
    heads = len(chunk)
    state_rows = heads * HEAD_DIM + -(-2 * heads // 8) * 8
    shape = jax.ShapeDtypeStruct((state_rows, rows), jnp.float32)
    pairs = halves * (rows // TILE) ** 2 * heads * len(blocks)
    return pl.pallas_call(
        functools.partial(attend_kernel, halves, chunk, slots, not states, rows),
        out_shape=[shape] * halves,
        in_specs=[SMEM, SMEM] + [VMEM] * (halves + len(blocks) + len(states)),
        out_specs=[VMEM] * halves,
        compiler_params=params(),
        cost_estimate=pl.CostEstimate(
            flops=pairs * 4 * TILE * TILE * HEAD_DIM,
            bytes_accessed=len(blocks) * rows * heads * HEAD_DIM * 4 + 4 * halves * state_rows * rows,
            transcendentals=pairs * TILE * TILE,
        ),
        name="attend",
    )(bounds, firsts, *queries, *blocks, *states)


def merged(chunk, states):
    heads = len(chunk)
    columns = heads * HEAD_DIM
    for i, h in enumerate(chunk):
        maxima = [ref[columns + i : columns + i + 1] for ref in states]
        totals = [ref[columns + heads + i : columns + heads + i + 1] for ref in states]
        largest = functools.reduce(jnp.maximum, maxima)
        factors = [jnp.exp2((m - largest) * SCALE2) for m in maxima]
        total = functools.reduce(jnp.add, [f * t for f, t in zip(factors, totals)])
        parts = [ref[i * HEAD_DIM : (i + 1) * HEAD_DIM] * (f / total) for ref, f in zip(states, factors)]
        yield h, functools.reduce(jnp.add, parts).T


def finish_kernel(chunks, each, *refs):
    out_ref = refs[-1]
    for c, chunk in enumerate(chunks):
        for h, done in merged(chunk, refs[c * each : (c + 1) * each]):
            out_ref[:, h * HEAD_DIM : (h + 1) * HEAD_DIM] = done.astype(out_ref.dtype)


def finish(chunks, states, rows):
    columns = sum(len(c) for c in chunks) * HEAD_DIM
    return pl.pallas_call(
        functools.partial(finish_kernel, chunks, len(states[0])),
        out_shape=jax.ShapeDtypeStruct((rows, columns), jnp.bfloat16),
        in_specs=[VMEM] * sum(len(s) for s in states),
        out_specs=VMEM,
        compiler_params=params(),
        name="finish",
    )(*[state for group in states for state in group])


def part_kernel(chunks, each, places_ref, *refs):
    keep_ref, send_ref, held = refs[-3:]
    for c, chunk in enumerate(chunks):
        for h, done in merged(chunk, refs[c * each : (c + 1) * each]):
            held[:, h * HEAD_DIM : (h + 1) * HEAD_DIM] = done.astype(held.dtype)
    rows = keep_ref.shape[0]
    mine = places_ref[2]
    keep_ref[...] = held[pl.ds(pl.multiple_of(mine * rows, 16), rows), :]
    send_ref[...] = held[pl.ds(pl.multiple_of((1 - mine) * rows, 16), rows), :]


def join_kernel(places_ref, keep_ref, got_ref, out_ref):
    columns = keep_ref.shape[1]
    mine = places_ref[2]
    out_ref[:, pl.ds(pl.multiple_of(mine * columns, TILE), columns)] = keep_ref[...]
    out_ref[:, pl.ds(pl.multiple_of((1 - mine) * columns, TILE), columns)] = got_ref[...]


def finish_in_two(chunks, places, states, rows):
    columns = sum(len(c) for c in chunks) * HEAD_DIM
    part = jax.ShapeDtypeStruct((rows // 2, columns), jnp.bfloat16)
    keep, send = pl.pallas_call(
        functools.partial(part_kernel, chunks, len(states[0])),
        out_shape=[part, part],
        in_specs=[SMEM] + [VMEM] * sum(len(s) for s in states),
        out_specs=[VMEM, VMEM],
        scratch_shapes=[pltpu.VMEM((rows, columns), jnp.bfloat16)],
        compiler_params=params(),
        name="part",
    )(places, *[state for group in states for state in group])
    got = lax.ppermute(send, "head", [(0, 1), (1, 0)])
    return pl.pallas_call(
        join_kernel,
        out_shape=jax.ShapeDtypeStruct((rows // 2, 2 * columns), jnp.bfloat16),
        in_specs=[SMEM, VMEM, VMEM],
        out_specs=VMEM,
        compiler_params=params(),
        name="join",
    )(places, keep, got)


def chip_pairs(mesh):
    places = [tuple(getattr(d, "coords", ())) for d in mesh.devices[:, 0]]
    count = len(places)
    if count % 4 or not places[0] or mesh.shape["head"] != 2:
        return False
    cores = all(places[i] == places[i + 1] for i in range(0, count, 2))
    level = all(places[i][2] == places[i + 3][2] for i in range(0, count, 4))
    climb = all(places[i][2] != places[i + 4][2] for i in range(0, count - 4))
    return cores and level and climb


def paired_shards(owner_count, queries, keys, values, image_tiles):
    rows, columns = queries.shape
    tiles = rows // TILE
    heads = columns // HEAD_DIM
    most = heads - heads // 3
    chunks = [list(range(most)), list(range(most, heads))]
    every = range(owner_count)

    def sign(s):
        return 1 - 2 * ((s // 2) % 2)

    def moved(array, source):
        return lax.ppermute(array, "seq", [(source(s), s) for s in every if 0 <= source(s) < owner_count])

    along = lambda s: s + 4 * sign(s)
    against = lambda s: s - 4 * sign(s)
    across = lambda s: s + 2 * sign(s)
    corner = lambda s: s + 8 * (1 - 2 * (s % 2))
    sibling = lambda s: s + 1 - 2 * (s % 2)

    me = lax.axis_index("seq")
    places = jnp.stack([me, sibling(me), lax.axis_index("head")]).astype(jnp.int32)
    owners = [me, along(me), against(me), across(me), me - 2 * sign(me), me + 6 * sign(me), me - 6 * sign(me)]
    firsts = jnp.stack([o * tiles for o in owners] + [corner(me) * tiles + me % 2]).astype(jnp.int32)
    OWN, A1, B1, Y1, YA, AY, BYA, CORNER = range(8)

    (block_a, block_b), bounds, spans = pack(chunks, 2, image_tiles, places, keys, values)

    def exchange(kind, block_a, block_b, queries, bounds, firsts, places):
        other = moved(queries, sibling)
        y1a, a1a, b1a = moved(block_a, across), moved(block_a, along), moved(block_a, against)
        a1b, b1b, y1b = moved(block_b, along), moved(block_b, against), moved(block_b, across)

        def fold(chunk, items, states):
            blocks = [block for block, _, _ in items]
            slots = [(first_at, base) for _, first_at, base in items]
            return attend(bounds, firsts, (queries, other), chunks[chunk], blocks, slots, states)

        near_a, near_b, last_a, last_b = [], [], [], []
        if kind == 0:
            near_a = [(moved(y1a, along), AY, 0), (moved(y1a, against), YA, 0)]
            near_b = [(moved(a1b, across), YA, 0), (moved(b1b, across), AY, 0)]
        else:
            yaa, yab = moved(a1a, across), moved(y1b, against)
            near_a, near_b = [(yaa, YA, 0)], [(yab, YA, 0)]
            if kind >= 2:
                near_a.append((moved(y1a, along), AY, 0))
                near_b.append((moved(y1b, along), AY, 0))
            last_b = [(moved(yab, against), BYA, 0)]
            last_a = [(moved(yaa, against), BYA, 0)]
            if kind == 3:
                far = moved(corner_of(chunks, places, [block_a, block_b]), corner)
                last_a.append((far, CORNER, 0))
                last_b.append((far, CORNER, most))
        state_a = fold(0, [(block_a, OWN, 0)], [])
        state_b = fold(1, [(block_b, OWN, 0)], [])
        state_a = fold(0, [(a1a, A1, 0), (b1a, B1, 0), (y1a, Y1, 0)], state_a)
        state_b = fold(1, [(a1b, A1, 0), (b1b, B1, 0), (y1b, Y1, 0)], state_b)
        state_b = fold(1, near_b, state_b)
        state_a = fold(0, near_a, state_a)
        if kind:
            state_b = fold(1, last_b, state_b)
            state_a = fold(0, last_a, state_a)
        return [[state_a[0], moved(state_a[1], sibling)], [state_b[0], moved(state_b[1], sibling)]]

    branches = [functools.partial(exchange, kind) for kind in range(4)]
    states = lax.switch(spans, branches, block_a, block_b, queries, bounds, firsts, places)
    return finish_in_two(chunks, places, states, rows)


def ring_shards(owner_count, queries, keys, values, image_tiles):
    rows, columns = queries.shape
    tiles = rows // TILE
    chunks = [list(range(columns // HEAD_DIM))]
    reach = min(owner_count - 1, -(-(MOST_TILES - 1) // tiles))
    me = lax.axis_index("seq")
    places = jnp.stack([me, me, lax.axis_index("head")]).astype(jnp.int32)
    (block,), bounds, _ = pack(chunks, 1, image_tiles, places, keys, values)
    firsts = jnp.stack([me + k for k in range(-reach, reach + 1)]).astype(jnp.int32) * tiles
    fold = functools.partial(attend, bounds, firsts, (queries,), chunks[0])
    up = [(i, i + 1) for i in range(owner_count - 1)]
    down = [(i + 1, i) for i in range(owner_count - 1)]
    below = above = block
    states = []
    held, slots = [block], [(reach, 0)]
    for k in range(1, reach + 1):
        below = lax.ppermute(below, "seq", up)
        above = lax.ppermute(above, "seq", down)
        states = fold(held, slots, states)
        held, slots = [below, above], [(reach - k, 0), (reach + k, 0)]
    states = fold(held, slots, states)
    attended = finish(chunks, [states], rows)
    return lax.all_to_all(attended, "head", split_axis=0, concat_axis=1, tiled=True)


def solution(mesh):
    owner_count = mesh.shape["seq"]
    plan = paired_shards if chip_pairs(mesh) else ring_shards
    placed = (P("seq", "head"), P("seq", "head"), P("seq", "head"), P())
    return jax.shard_map(
        functools.partial(plan, owner_count),
        mesh=mesh,
        in_specs=placed,
        out_specs=P(("seq", "head"), None),
        check_vma=False,
    )
```

```python
import functools
import math

import jax
import jax.numpy as jnp
from jax import lax
from jax.experimental import pallas as pl
from jax.experimental.pallas import tpu as pltpu
from jax.sharding import PartitionSpec as P

HEAD_DIM = 128
TILE = 128
MOST_TILES = 21

LOWEST = -1e30
SCALE2 = math.log2(math.e) / math.sqrt(HEAD_DIM)
COST = 6

VMEM = pl.BlockSpec(memory_space=pltpu.VMEM)
SMEM = pl.BlockSpec(memory_space=pltpu.SMEM)
HBM = pl.BlockSpec(memory_space=pl.ANY)


def params():
    return pltpu.CompilerParams(vmem_limit_bytes=32 * 1024 * 1024)


def head_columns(h):
    return slice(h * HEAD_DIM, (h + 1) * HEAD_DIM)


def image_bounds(tiles_ref, tile):
    first = jnp.int32(0)
    start, end = jnp.int32(0), jnp.int32(0)
    for i in range(tiles_ref.shape[0]):
        after = first + tiles_ref[i]
        inside = (tile >= first) & (tile < after)
        start = jnp.where(inside, first, start)
        end = jnp.where(inside, after, end)
        first = after
    return start, end


def chip_spans(tiles_ref, chip_tiles):
    first = jnp.int32(0)
    spans = jnp.int32(0)
    for i in range(tiles_ref.shape[0]):
        after = first + tiles_ref[i]
        low, high = first // chip_tiles, (after - 1) // chip_tiles
        odd = low + 1 - low % 2
        far = jnp.where(high - low >= 4, 2, jnp.where(high - odd >= 3, 1, 0))
        spans = jnp.maximum(spans, far)
        first = after
    return spans


def pack_kernel(halves, tiles_ref, places_ref, k_ref, v_ref, out_ref, bounds_ref, spans_ref, sems):
    rows = k_ref.shape[0]
    tiles = rows // TILE
    copies = [
        pltpu.make_async_copy(k_ref, out_ref.at[:rows], sems.at[0]),
        pltpu.make_async_copy(v_ref, out_ref.at[rows:], sems.at[1]),
    ]
    for copy in copies:
        copy.start()
    for half in range(halves):
        for at in range(tiles):
            start, end = image_bounds(tiles_ref, places_ref[half] * tiles + at)
            bounds_ref[2 * (half * tiles + at)] = start
            bounds_ref[2 * (half * tiles + at) + 1] = end
    spans_ref[0] = chip_spans(tiles_ref, 2 * tiles)
    for copy in copies:
        copy.wait()


def pack(halves, image_tiles, places, keys, values):
    rows, columns = keys.shape
    block, bounds, spans = pl.pallas_call(
        functools.partial(pack_kernel, halves),
        out_shape=[
            jax.ShapeDtypeStruct((2 * rows, columns), keys.dtype),
            jax.ShapeDtypeStruct((2 * halves * (rows // TILE),), jnp.int32),
            jax.ShapeDtypeStruct((1,), jnp.int32),
        ],
        in_specs=[SMEM, SMEM, HBM, HBM],
        out_specs=[VMEM, SMEM, SMEM],
        scratch_shapes=[pltpu.SemaphoreType.DMA((2,))],
        name="pack",
    )(image_tiles, places, keys, values)
    return block, bounds, spans[0]


def corner_kernel(places_ref, block_ref, out_ref):
    half = out_ref.shape[0] // 2
    skip = pl.multiple_of((places_ref[0] % 2) * TILE, TILE)
    out_ref[:half] = block_ref[pl.ds(skip, half)]
    out_ref[half:] = block_ref[pl.ds(block_ref.shape[0] // 2 + skip, half)]


def corner_of(places, block):
    return pl.pallas_call(
        corner_kernel,
        out_shape=jax.ShapeDtypeStruct((block.shape[0] - 2 * TILE, block.shape[1]), block.dtype),
        in_specs=[SMEM, VMEM],
        out_specs=VMEM,
        compiler_params=params(),
        name="corner",
    )(places, block)


def attend_kernel(halves, slots, fresh, bounds_ref, firsts_ref, *refs):
    q_refs, refs = refs[:halves], refs[halves:]
    slot_refs, refs = refs[: len(slots)], refs[len(slots) :]
    old_refs, refs = (None, refs) if fresh else (refs[:halves], refs[halves:])
    new_refs, (held_q, held, state) = refs[:halves], refs[halves:]
    rows, columns = q_refs[0].shape
    tiles = rows // TILE
    count = held.shape[1] // 2 // TILE
    heads = columns // HEAD_DIM

    for half in range(halves):
        held_q[half] = q_refs[half][...]
        if fresh:
            state[half, :, :columns] = jnp.zeros((rows, columns), jnp.float32)
            lane = lax.broadcasted_iota(jnp.int32, (rows, TILE), 1)
            state[half, :, columns:] = jnp.where(lane < heads, LOWEST, 0.0)
        else:
            state[half] = old_refs[half][...]
    for slot, ref in enumerate(slot_refs):
        held[slot] = ref[...]

    def fold(half, slot, first, starts, ends):
        for h in range(heads):
            own = head_columns(h)
            scores = lax.dot_general(
                held_q[half, :, own],
                held[slot, : count * TILE, own],
                (((1,), (1,)), ((), ())),
                preferred_element_type=jnp.float32,
            )
            max_at = slice(columns + h, columns + h + 1)
            total_at = slice(columns + heads + h, columns + heads + h + 1)
            rounded, factors = [], []
            for t in range(tiles):
                at = slice(t * TILE, (t + 1) * TILE)
                parts = []
                for j in range(count):
                    inside = (first + j >= starts[t]) & (first + j < ends[t])
                    off = jnp.where(inside, 0.0, 2 * LOWEST).astype(jnp.float32)
                    parts.append(scores[at, j * TILE : (j + 1) * TILE] * SCALE2 + off)
                old_max = state[half, at, max_at]
                new_max = jnp.maximum(old_max, jnp.max(functools.reduce(jnp.maximum, parts), axis=1, keepdims=True))
                weights = [jnp.exp2(part - new_max) for part in parts]
                factor = jnp.exp2(old_max - new_max)
                total = jnp.sum(functools.reduce(jnp.add, weights), axis=1, keepdims=True)
                state[half, at, max_at] = new_max
                state[half, at, total_at] = state[half, at, total_at] * factor + total
                factors.append(factor)
                rounded.append(jnp.concatenate([w.astype(jnp.bfloat16) for w in weights], axis=1))
            update = jnp.dot(
                jnp.concatenate(rounded, axis=0),
                held[slot, count * TILE :, own],
                preferred_element_type=jnp.float32,
            )
            for t in range(tiles):
                at = slice(t * TILE, (t + 1) * TILE)
                state[half, at, own] = state[half, at, own] * factors[t] + update[at]

    firsts = [firsts_ref[at] for at in slots]

    @pl.loop(0, halves * len(slots))
    def _(unit):
        half, slot = unit // len(slots), unit % len(slots)
        first = firsts[0]
        for i in range(1, len(slots)):
            first = jnp.where(slot == i, firsts[i], first)
        starts = [bounds_ref[2 * (half * tiles + t)] for t in range(tiles)]
        ends = [bounds_ref[2 * (half * tiles + t) + 1] for t in range(tiles)]

        @pl.when((first < ends[-1]) & (first + count > starts[0]))
        def _():
            fold(half, slot, first, starts, ends)

    for half in range(halves):
        new_refs[half][...] = state[half]


def attend(bounds, firsts, queries, blocks, slots, states):
    halves = len(queries)
    rows, columns = queries[0].shape
    heads = columns // HEAD_DIM
    shape = jax.ShapeDtypeStruct((rows, columns + TILE), jnp.float32)
    pairs = halves * (rows // TILE) * heads * sum(b.shape[0] // 2 // TILE for b in blocks)
    return pl.pallas_call(
        functools.partial(attend_kernel, halves, slots, not states),
        out_shape=[shape] * halves,
        in_specs=[SMEM, SMEM] + [VMEM] * (halves + len(blocks) + len(states)),
        out_specs=[VMEM] * halves,
        scratch_shapes=[
            pltpu.VMEM((halves, rows, columns), queries[0].dtype),
            pltpu.VMEM((len(blocks),) + blocks[0].shape, blocks[0].dtype),
            pltpu.VMEM((halves, rows, columns + TILE), jnp.float32),
        ],
        compiler_params=params(),
        cost_estimate=pl.CostEstimate(
            flops=COST * pairs * 4 * TILE * TILE * HEAD_DIM,
            bytes_accessed=len(blocks) * rows * columns * 4 + 4 * halves * rows * (columns + TILE),
            transcendentals=pairs * TILE * TILE,
        ),
        name="attend",
    )(bounds, firsts, *queries, *blocks, *states)


def merged(states, rows, columns):
    heads = columns // HEAD_DIM
    for h in range(heads):
        maxima = [ref[rows, columns + h : columns + h + 1] for ref in states]
        totals = [ref[rows, columns + heads + h : columns + heads + h + 1] for ref in states]
        largest = functools.reduce(jnp.maximum, maxima)
        factors = [jnp.exp2(m - largest) for m in maxima]
        total = functools.reduce(jnp.add, [f * t for f, t in zip(factors, totals)])
        parts = [ref[rows, head_columns(h)] * (f / total) for ref, f in zip(states, factors)]
        yield head_columns(h), functools.reduce(jnp.add, parts)


def finish_kernel(*refs):
    out_ref = refs[-1]
    for own, done in merged(refs[:-1], slice(None), out_ref.shape[1]):
        out_ref[:, own] = done.astype(out_ref.dtype)


def finish(states, columns):
    return pl.pallas_call(
        finish_kernel,
        out_shape=jax.ShapeDtypeStruct((states[0].shape[0], columns), jnp.bfloat16),
        in_specs=[VMEM] * len(states),
        out_specs=VMEM,
        compiler_params=params(),
        name="finish",
    )(*states)


def part_kernel(places_ref, *refs):
    keep_ref, send_ref = refs[-2:]
    rows, columns = keep_ref.shape
    mine = places_ref[2]
    for out_ref, which in ((send_ref, 1 - mine), (keep_ref, mine)):
        there = pl.ds(pl.multiple_of(which * rows, 16), rows)
        for own, done in merged(refs[:-2], there, columns):
            out_ref[:, own] = done.astype(out_ref.dtype)


def join_kernel(places_ref, keep_ref, got_ref, out_ref):
    columns = keep_ref.shape[1]
    mine = places_ref[2]
    out_ref[:, pl.ds(pl.multiple_of(mine * columns, TILE), columns)] = keep_ref[...]
    out_ref[:, pl.ds(pl.multiple_of((1 - mine) * columns, TILE), columns)] = got_ref[...]


def finish_in_two(places, states, columns):
    rows = states[0].shape[0]
    part = jax.ShapeDtypeStruct((rows // 2, columns), jnp.bfloat16)
    keep, send = pl.pallas_call(
        part_kernel,
        out_shape=[part, part],
        in_specs=[SMEM] + [VMEM] * len(states),
        out_specs=[VMEM, VMEM],
        compiler_params=params(),
        name="part",
    )(places, *states)
    got = lax.ppermute(send, "head", [(0, 1), (1, 0)])
    return pl.pallas_call(
        join_kernel,
        out_shape=jax.ShapeDtypeStruct((rows // 2, 2 * columns), jnp.bfloat16),
        in_specs=[SMEM, VMEM, VMEM],
        out_specs=VMEM,
        compiler_params=params(),
        name="join",
    )(places, keep, got)


def chip_pairs(mesh):
    places = [tuple(getattr(d, "coords", ())) for d in mesh.devices[:, 0]]
    count = len(places)
    if count % 4 or not places[0] or mesh.shape["head"] != 2:
        return False
    cores = all(places[i] == places[i + 1] for i in range(0, count, 2))
    level = all(places[i][2] == places[i + 3][2] for i in range(0, count, 4))
    climb = all(places[i][2] != places[i + 4][2] for i in range(0, count - 4))
    return cores and level and climb


def paired_shards(owner_count, queries, keys, values, image_tiles):
    rows, columns = queries.shape
    tiles = rows // TILE
    every = range(owner_count)

    def sign(s):
        return 1 - 2 * ((s // 2) % 2)

    def moved(array, source):
        return lax.ppermute(array, "seq", [(source(s), s) for s in every if 0 <= source(s) < owner_count])

    along = lambda s: s + 4 * sign(s)
    against = lambda s: s - 4 * sign(s)
    across = lambda s: s + 2 * sign(s)
    corner = lambda s: s + 8 * (1 - 2 * (s % 2))
    sibling = lambda s: s + 1 - 2 * (s % 2)

    me = lax.axis_index("seq")
    places = jnp.stack([me, sibling(me), lax.axis_index("head")]).astype(jnp.int32)
    owners = [me, along(me), against(me), across(me), me - 2 * sign(me), me + 6 * sign(me), me - 6 * sign(me)]
    firsts = jnp.stack([o * tiles for o in owners] + [corner(me) * tiles + me % 2]).astype(jnp.int32)
    OWN, A1, B1, Y1, YA, AY, BYA, CORNER = range(8)

    block, bounds, spans = pack(2, image_tiles, places, keys, values)
    y1, a1, b1 = moved(block, across), moved(block, along), moved(block, against)
    both = (queries, moved(queries, sibling))
    fold = functools.partial(attend, bounds, firsts, both)
    states = fold([block], [OWN], [])
    ya, ay = moved(a1, across), moved(y1, along)
    states = fold([a1, b1, y1], [A1, B1, Y1], states)

    def near(block, ya, ay, states):
        return fold([ya, ay], [YA, AY], states)

    def further(block, ya, ay, states):
        bya = moved(ya, against)
        states = fold([ya, ay], [YA, AY], states)
        return fold([bya], [BYA], states)

    def furthest(block, ya, ay, states):
        bya = moved(ya, against)
        far = moved(corner_of(places, block), corner)
        states = fold([ya, ay], [YA, AY], states)
        states = fold([bya], [BYA], states)
        return fold([far], [CORNER], states)

    mine, theirs = lax.switch(spans, [near, further, furthest], block, ya, ay, states)
    return finish_in_two(places, [mine, moved(theirs, sibling)], columns)


def ring_shards(owner_count, queries, keys, values, image_tiles):
    rows, columns = queries.shape
    tiles = rows // TILE
    reach = min(owner_count - 1, -(-(MOST_TILES - 1) // tiles))
    me = lax.axis_index("seq")
    places = jnp.stack([me, me, lax.axis_index("head")]).astype(jnp.int32)
    block, bounds, _ = pack(1, image_tiles, places, keys, values)
    firsts = jnp.stack([me + k for k in range(-reach, reach + 1)]).astype(jnp.int32) * tiles
    fold = functools.partial(attend, bounds, firsts, (queries,))
    up = [(i, i + 1) for i in range(owner_count - 1)]
    down = [(i + 1, i) for i in range(owner_count - 1)]
    below = above = block
    states = []
    held, slots = [block], [reach]
    for k in range(1, reach + 1):
        below = lax.ppermute(below, "seq", up)
        above = lax.ppermute(above, "seq", down)
        states = fold(held, slots, states)
        held, slots = [below, above], [reach - k, reach + k]
    attended = finish(fold(held, slots, states), columns)
    return lax.all_to_all(attended, "head", split_axis=0, concat_axis=1, tiled=True)


def solution(mesh):
    owner_count = mesh.shape["seq"]
    plan = paired_shards if chip_pairs(mesh) else ring_shards
    placed = (P("seq", "head"), P("seq", "head"), P("seq", "head"), P())
    return jax.shard_map(
        functools.partial(plan, owner_count),
        mesh=mesh,
        in_specs=placed,
        out_specs=P(("seq", "head"), None),
        check_vma=False,
    )
```

```python
import functools
import math

import jax
import jax.numpy as jnp
from jax import lax
from jax.experimental import pallas as pl
from jax.experimental.pallas import tpu as pltpu
from jax.sharding import PartitionSpec as P

HEAD_DIM = 128
TILE = 128
MOST_TILES = 21

LOWEST = -1e30
SCALE2 = math.log2(math.e) / math.sqrt(HEAD_DIM)
COST = 6

VMEM = pl.BlockSpec(memory_space=pltpu.VMEM)
SMEM = pl.BlockSpec(memory_space=pltpu.SMEM)
HBM = pl.BlockSpec(memory_space=pl.ANY)


def params():
    return pltpu.CompilerParams(vmem_limit_bytes=32 * 1024 * 1024)


def head_columns(h):
    return slice(h * HEAD_DIM, (h + 1) * HEAD_DIM)


def tile_rows(t):
    return slice(t * TILE, (t + 1) * TILE)


def image_bounds(tiles_ref, tile):
    first = jnp.int32(0)
    start, end = jnp.int32(0), jnp.int32(0)
    for i in range(tiles_ref.shape[0]):
        after = first + tiles_ref[i]
        inside = (tile >= first) & (tile < after)
        start = jnp.where(inside, first, start)
        end = jnp.where(inside, after, end)
        first = after
    return start, end


def chip_spans(tiles_ref, chip_tiles):
    first = jnp.int32(0)
    spans = jnp.int32(0)
    for i in range(tiles_ref.shape[0]):
        after = first + tiles_ref[i]
        low, high = first // chip_tiles, (after - 1) // chip_tiles
        odd = low + 1 - low % 2
        far = jnp.where(high - low >= 4, 2, jnp.where(high - odd >= 3, 1, 0))
        spans = jnp.maximum(spans, far)
        first = after
    return spans


def meta_kernel(halves, tiles_ref, bounds_ref, spans_ref):
    tiles = bounds_ref.shape[1] // TILE
    me = lax.axis_index("seq")
    bounds_ref[...] = jnp.zeros(bounds_ref.shape, jnp.int32)
    for half, owner in enumerate(halves(me)):
        for t in range(tiles):
            start, end = image_bounds(tiles_ref, owner * tiles + t)
            bounds_ref[2 * half : 2 * half + 1, tile_rows(t)] = jnp.full((1, TILE), start, jnp.int32)
            bounds_ref[2 * half + 1 : 2 * half + 2, tile_rows(t)] = jnp.full((1, TILE), end, jnp.int32)
    spans_ref[0] = chip_spans(tiles_ref, 2 * tiles)


def meta(halves, image_tiles, rows):
    bounds, spans = pl.pallas_call(
        functools.partial(meta_kernel, halves),
        out_shape=[jax.ShapeDtypeStruct((8, rows), jnp.int32), jax.ShapeDtypeStruct((1,), jnp.int32)],
        in_specs=[SMEM],
        out_specs=[VMEM, SMEM],
        compiler_params=params(),
        name="meta",
    )(image_tiles)
    return bounds, spans[0]


def pack_kernel(k_ref, v_ref, out_ref, held, sems):
    rows, columns = k_ref.shape
    tiles = rows // TILE
    copies = []
    for t in range(tiles):
        copies.append(pltpu.make_async_copy(v_ref.at[tile_rows(t)], held.at[tile_rows(t)], sems.at[t]))
    for t in range(tiles):
        copies.append(pltpu.make_async_copy(k_ref.at[tile_rows(t)], out_ref.at[tile_rows(t)], sems.at[tiles + t]))
    for copy in copies:
        copy.start()
    for t in range(tiles):
        copies[t].wait()
        for h in range(columns // HEAD_DIM):
            out_ref[tile_rows(tiles + t), head_columns(h)] = held[tile_rows(t), head_columns(h)].T
    for copy in copies[tiles:]:
        copy.wait()


def pack(keys, values):
    rows, columns = keys.shape
    return pl.pallas_call(
        pack_kernel,
        out_shape=jax.ShapeDtypeStruct((2 * rows, columns), keys.dtype),
        in_specs=[HBM, HBM],
        out_specs=VMEM,
        scratch_shapes=[pltpu.VMEM(values.shape, values.dtype), pltpu.SemaphoreType.DMA((2 * rows // TILE,))],
        name="pack",
    )(keys, values)


def corner_kernel(block_ref, out_ref):
    half = out_ref.shape[0] // 2
    skip = pl.multiple_of((lax.axis_index("seq") % 2) * TILE, TILE)
    out_ref[:half] = block_ref[pl.ds(skip, half)]
    out_ref[half:] = block_ref[pl.ds(block_ref.shape[0] // 2 + skip, half)]


def corner_of(block):
    return pl.pallas_call(
        corner_kernel,
        out_shape=jax.ShapeDtypeStruct((block.shape[0] - 2 * TILE, block.shape[1]), block.dtype),
        in_specs=[VMEM],
        out_specs=VMEM,
        compiler_params=params(),
        name="corner",
    )(block)


def attend_kernel(halves, slots, fresh, bounds_ref, *refs):
    q_refs, refs = refs[:halves], refs[halves:]
    slot_refs, refs = refs[: len(slots)], refs[len(slots) :]
    old_refs, refs = (None, refs) if fresh else (refs[:halves], refs[halves:])
    new_refs, (held_q, held, state) = refs[:halves], refs[halves:]
    rows, columns = q_refs[0].shape
    tiles = rows // TILE
    count = held.shape[1] // 2 // TILE
    heads = columns // HEAD_DIM
    me = lax.axis_index("seq")

    for half in range(halves):
        held_q[half] = q_refs[half][...]
        if fresh:
            state[half, :columns] = jnp.zeros((columns, rows), jnp.float32)
            state[half, columns : columns + heads] = jnp.full((heads, rows), LOWEST, jnp.float32)
            state[half, columns + heads :] = jnp.zeros((state.shape[1] - columns - heads, rows), jnp.float32)
        else:
            state[half] = old_refs[half][...]
    for slot, ref in enumerate(slot_refs):
        held[slot] = ref[...]
    begins = [bounds_ref[2 * half, 0] for half in range(halves)]
    stops = [bounds_ref[2 * half + 1, rows - 1] for half in range(halves)]

    def chosen(at, options):
        return functools.reduce(lambda x, i: jnp.where(at == i, options[i], x), range(1, len(options)), options[0])

    def fold(half, slot, first):
        low = bounds_ref[pl.ds(2 * half, 1), :]
        high = bounds_ref[pl.ds(2 * half + 1, 1), :]
        off = [
            jnp.where((first + j >= low) & (first + j < high), 0.0, -LOWEST).astype(jnp.float32)
            for j in range(count)
        ]
        for h in range(heads):
            own = head_columns(h)
            scores = lax.dot_general(
                held[slot, : count * TILE, own],
                held_q[half, :, own],
                (((1,), (1,)), ((), ())),
                preferred_element_type=jnp.float32,
            )
            max_at, total_at = pl.ds(columns + h, 1), pl.ds(columns + heads + h, 1)
            factors, rounded, totals, maxima = [], [], [], []
            for t in range(tiles):
                lanes = tile_rows(t)
                parts = [scores[tile_rows(j), lanes] for j in range(count)]
                old_max = state[half, max_at, lanes]
                new_max = old_max
                for j in range(count):
                    new_max = jnp.maximum(new_max, jnp.max(parts[j], axis=0, keepdims=True) - off[j][:, lanes])
                scaled = new_max * SCALE2
                weights = [jnp.exp2(parts[j] * SCALE2 - (scaled + off[j][:, lanes])) for j in range(count)]
                factors.append(jnp.exp2((old_max - new_max) * SCALE2))
                totals.append(jnp.sum(functools.reduce(jnp.add, weights), axis=0, keepdims=True))
                maxima.append(new_max)
                rounded.append(jnp.concatenate([w.astype(jnp.bfloat16) for w in weights], axis=0))
            factor = jnp.concatenate(factors, axis=1)
            update = jnp.dot(
                jnp.concatenate([held[slot, tile_rows(count + j), own] for j in range(count)], axis=1),
                jnp.concatenate(rounded, axis=1),
                preferred_element_type=jnp.float32,
            )
            state[half, own] = state[half, own] * factor + update
            state[half, max_at] = jnp.concatenate(maxima, axis=1)
            state[half, total_at] = state[half, total_at] * factor + jnp.concatenate(totals, axis=1)

    @pl.loop(0, halves * len(slots))
    def _(unit):
        half, slot = unit // len(slots), unit % len(slots)
        first = chosen(slot, [place(me) for place in slots])

        @pl.when((first < chosen(half, stops)) & (first + count > chosen(half, begins)))
        def _():
            fold(half, slot, first)

    for half in range(halves):
        new_refs[half][...] = state[half]


def attend(bounds, queries, blocks, slots, states):
    halves = len(queries)
    rows, columns = queries[0].shape
    heads = columns // HEAD_DIM
    shape = jax.ShapeDtypeStruct((columns + -(-2 * heads // 8) * 8, rows), jnp.float32)
    pairs = halves * (rows // TILE) * heads * sum(b.shape[0] // 2 // TILE for b in blocks)
    return pl.pallas_call(
        functools.partial(attend_kernel, halves, slots, not states),
        out_shape=[shape] * halves,
        in_specs=[VMEM] * (1 + halves + len(blocks) + len(states)),
        out_specs=[VMEM] * halves,
        scratch_shapes=[
            pltpu.VMEM((halves, rows, columns), queries[0].dtype),
            pltpu.VMEM((len(blocks),) + blocks[0].shape, blocks[0].dtype),
            pltpu.VMEM((halves,) + shape.shape, jnp.float32),
        ],
        compiler_params=params(),
        cost_estimate=pl.CostEstimate(
            flops=COST * pairs * 4 * TILE * TILE * HEAD_DIM,
            bytes_accessed=len(blocks) * rows * columns * 4 + 4 * halves * rows * columns,
            transcendentals=pairs * TILE * TILE,
        ),
        name="attend",
    )(bounds, *queries, *blocks, *states)


def merged(states, columns):
    heads = columns // HEAD_DIM
    for h in range(heads):
        maxima = [ref[columns + h : columns + h + 1] for ref in states]
        totals = [ref[columns + heads + h : columns + heads + h + 1] for ref in states]
        largest = functools.reduce(jnp.maximum, maxima)
        factors = [jnp.exp2((m - largest) * SCALE2) for m in maxima]
        total = functools.reduce(jnp.add, [f * t for f, t in zip(factors, totals)])
        parts = [ref[head_columns(h)] * (f / total) for ref, f in zip(states, factors)]
        yield head_columns(h), functools.reduce(jnp.add, parts).T


def finish_kernel(*refs):
    out_ref = refs[-1]
    for own, done in merged(refs[:-1], out_ref.shape[1]):
        out_ref[:, own] = done.astype(out_ref.dtype)


def finish(states, rows, columns):
    return pl.pallas_call(
        finish_kernel,
        out_shape=jax.ShapeDtypeStruct((rows, columns), jnp.bfloat16),
        in_specs=[VMEM] * len(states),
        out_specs=VMEM,
        compiler_params=params(),
        name="finish",
    )(*states)


def part_kernel(*refs):
    keep_ref, send_ref, held = refs[-3:]
    rows, columns = keep_ref.shape
    mine = lax.axis_index("head")
    for own, done in merged(refs[:-3], columns):
        held[:, own] = done.astype(held.dtype)
    send_ref[...] = held[pl.ds(pl.multiple_of((1 - mine) * rows, 16), rows), :]
    keep_ref[...] = held[pl.ds(pl.multiple_of(mine * rows, 16), rows), :]


def join_kernel(keep_ref, got_ref, out_ref):
    columns = keep_ref.shape[1]
    mine = lax.axis_index("head")
    out_ref[:, pl.ds(pl.multiple_of(mine * columns, TILE), columns)] = keep_ref[...]
    out_ref[:, pl.ds(pl.multiple_of((1 - mine) * columns, TILE), columns)] = got_ref[...]


def finish_in_two(states, rows, columns):
    part = jax.ShapeDtypeStruct((rows // 2, columns), jnp.bfloat16)
    keep, send = pl.pallas_call(
        part_kernel,
        out_shape=[part, part],
        in_specs=[VMEM] * len(states),
        out_specs=[VMEM, VMEM],
        scratch_shapes=[pltpu.VMEM((rows, columns), jnp.bfloat16)],
        compiler_params=params(),
        name="part",
    )(*states)
    got = lax.ppermute(send, "head", [(0, 1), (1, 0)])
    return pl.pallas_call(
        join_kernel,
        out_shape=jax.ShapeDtypeStruct((rows // 2, 2 * columns), jnp.bfloat16),
        in_specs=[VMEM, VMEM],
        out_specs=VMEM,
        compiler_params=params(),
        name="join",
    )(keep, got)


def chip_pairs(mesh):
    places = [tuple(getattr(d, "coords", ())) for d in mesh.devices[:, 0]]
    count = len(places)
    if count % 4 or not places[0] or mesh.shape["head"] != 2:
        return False
    cores = all(places[i] == places[i + 1] for i in range(0, count, 2))
    level = all(places[i][2] == places[i + 3][2] for i in range(0, count, 4))
    climb = all(places[i][2] != places[i + 4][2] for i in range(0, count - 4))
    return cores and level and climb


def paired_shards(owner_count, queries, keys, values, image_tiles):
    rows, columns = queries.shape
    tiles = rows // TILE
    every = range(owner_count)

    def sign(s):
        return 1 - 2 * ((s // 2) % 2)

    def moved(array, source):
        return lax.ppermute(array, "seq", [(source(s), s) for s in every if 0 <= source(s) < owner_count])

    along = lambda s: s + 4 * sign(s)
    against = lambda s: s - 4 * sign(s)
    across = lambda s: s + 2 * sign(s)
    corner = lambda s: s + 8 * (1 - 2 * (s % 2))
    sibling = lambda s: s + 1 - 2 * (s % 2)

    OWN = lambda s: s * tiles
    A1 = lambda s: along(s) * tiles
    B1 = lambda s: against(s) * tiles
    Y1 = lambda s: across(s) * tiles
    YA = lambda s: (s - 2 * sign(s)) * tiles
    AY = lambda s: (s + 6 * sign(s)) * tiles
    BYA = lambda s: (s - 6 * sign(s)) * tiles
    CORNER = lambda s: corner(s) * tiles + s % 2

    block = pack(keys, values)
    y1, a1, b1 = moved(block, across), moved(block, along), moved(block, against)
    bounds, spans = meta(lambda s: [s, sibling(s)], image_tiles, rows)
    both = (queries, moved(queries, sibling))
    fold = functools.partial(attend, bounds, both)
    states = fold([block], [OWN], [])
    ya, ay = moved(a1, across), moved(y1, along)
    states = fold([a1, b1, y1], [A1, B1, Y1], states)

    def near(block, ya, ay, states):
        return fold([ya, ay], [YA, AY], states)

    def further(block, ya, ay, states):
        bya = moved(ya, against)
        states = fold([ya, ay], [YA, AY], states)
        return fold([bya], [BYA], states)

    def furthest(block, ya, ay, states):
        bya = moved(ya, against)
        far = moved(corner_of(block), corner)
        states = fold([ya, ay], [YA, AY], states)
        states = fold([bya], [BYA], states)
        return fold([far], [CORNER], states)

    mine, theirs = lax.switch(spans, [near, further, furthest], block, ya, ay, states)
    return finish_in_two([mine, moved(theirs, sibling)], rows, columns)


def ring_shards(owner_count, queries, keys, values, image_tiles):
    rows, columns = queries.shape
    tiles = rows // TILE
    reach = min(owner_count - 1, -(-(MOST_TILES - 1) // tiles))
    block = pack(keys, values)
    bounds, _ = meta(lambda s: [s], image_tiles, rows)
    fold = functools.partial(attend, bounds, (queries,))
    up = [(i, i + 1) for i in range(owner_count - 1)]
    down = [(i + 1, i) for i in range(owner_count - 1)]
    below = above = block
    states = []
    held, slots = [block], [lambda s: s * tiles]
    for k in range(1, reach + 1):
        below = lax.ppermute(below, "seq", up)
        above = lax.ppermute(above, "seq", down)
        states = fold(held, slots, states)
        held, slots = [below, above], [lambda s, k=k: (s - k) * tiles, lambda s, k=k: (s + k) * tiles]
    attended = finish(fold(held, slots, states), rows, columns)
    return lax.all_to_all(attended, "head", split_axis=0, concat_axis=1, tiled=True)


def solution(mesh):
    owner_count = mesh.shape["seq"]
    plan = paired_shards if chip_pairs(mesh) else ring_shards
    placed = (P("seq", "head"), P("seq", "head"), P("seq", "head"), P())
    return jax.shard_map(
        functools.partial(plan, owner_count),
        mesh=mesh,
        in_specs=placed,
        out_specs=P(("seq", "head"), None),
        check_vma=False,
    )
```

```python
import functools
import math

import jax
import jax.numpy as jnp
from jax import lax
from jax.experimental import pallas as pl
from jax.experimental.pallas import tpu as pltpu
from jax.sharding import PartitionSpec as P

HEAD_DIM = 128
TILE = 128
MOST_TILES = 21

LOWEST = -1e30
SCALE2 = math.log2(math.e) / math.sqrt(HEAD_DIM)
COST = 6

VMEM = pl.BlockSpec(memory_space=pltpu.VMEM)
SMEM = pl.BlockSpec(memory_space=pltpu.SMEM)
HBM = pl.BlockSpec(memory_space=pl.ANY)


def params():
    return pltpu.CompilerParams(vmem_limit_bytes=32 * 1024 * 1024)


def head_columns(h):
    return slice(h * HEAD_DIM, (h + 1) * HEAD_DIM)


def tile_rows(t):
    return slice(t * TILE, (t + 1) * TILE)


def image_bounds(tiles_ref, tile):
    first = jnp.int32(0)
    start, end = jnp.int32(0), jnp.int32(0)
    for i in range(tiles_ref.shape[0]):
        after = first + tiles_ref[i]
        inside = (tile >= first) & (tile < after)
        start = jnp.where(inside, first, start)
        end = jnp.where(inside, after, end)
        first = after
    return start, end


def chip_spans(tiles_ref, chip_tiles):
    first = jnp.int32(0)
    spans = jnp.int32(0)
    for i in range(tiles_ref.shape[0]):
        after = first + tiles_ref[i]
        low, high = first // chip_tiles, (after - 1) // chip_tiles
        odd = low + 1 - low % 2
        far = jnp.where(high - low >= 4, 2, jnp.where(high - odd >= 3, 1, 0))
        spans = jnp.maximum(spans, far)
        first = after
    return spans


def meta_kernel(halves, tiles_ref, bounds_ref, spans_ref):
    tiles = bounds_ref.shape[1] // TILE
    me = lax.axis_index("seq")
    bounds_ref[...] = jnp.zeros(bounds_ref.shape, jnp.int32)
    for half, owner in enumerate(halves(me)):
        for t in range(tiles):
            start, end = image_bounds(tiles_ref, owner * tiles + t)
            bounds_ref[2 * half : 2 * half + 1, tile_rows(t)] = jnp.full((1, TILE), start, jnp.int32)
            bounds_ref[2 * half + 1 : 2 * half + 2, tile_rows(t)] = jnp.full((1, TILE), end, jnp.int32)
    spans_ref[0] = chip_spans(tiles_ref, 2 * tiles)


def meta(halves, image_tiles, rows):
    bounds, spans = pl.pallas_call(
        functools.partial(meta_kernel, halves),
        out_shape=[jax.ShapeDtypeStruct((8, rows), jnp.int32), jax.ShapeDtypeStruct((1,), jnp.int32)],
        in_specs=[SMEM],
        out_specs=[VMEM, SMEM],
        compiler_params=params(),
        name="meta",
    )(image_tiles)
    return bounds, spans[0]


def pack_kernel(cuts, k_ref, v_ref, *refs):
    (block_ref, *chunk_refs), (held, sems) = refs[:-2], refs[-2:]
    rows, columns = k_ref.shape
    tiles = rows // TILE
    copies = []
    for t in range(tiles):
        copies.append(pltpu.make_async_copy(v_ref.at[tile_rows(t)], held.at[1, tile_rows(t)], sems.at[2 * t]))
        copies.append(pltpu.make_async_copy(k_ref.at[tile_rows(t)], held.at[0, tile_rows(t)], sems.at[2 * t + 1]))
    for copy in copies:
        copy.start()
    for t in range(tiles):
        copies[2 * t].wait()
        copies[2 * t + 1].wait()
        targets = [(block_ref, t)] + [(ref, t - low) for ref, (low, high) in zip(chunk_refs, cuts) if low <= t < high]
        for h in range(columns // HEAD_DIM):
            own = head_columns(h)
            turned = held[1, tile_rows(t), own].T
            for ref, at in targets:
                ref[tile_rows(2 * at), own] = held[0, tile_rows(t), own]
                ref[tile_rows(2 * at + 1), own] = turned


def pack(keys, values, cuts):
    rows, columns = keys.shape
    depths = [2 * rows] + [2 * TILE * (high - low) for low, high in cuts]
    return pl.pallas_call(
        functools.partial(pack_kernel, cuts),
        out_shape=[jax.ShapeDtypeStruct((depth, columns), keys.dtype) for depth in depths],
        in_specs=[HBM, HBM],
        out_specs=[VMEM] * len(depths),
        scratch_shapes=[
            pltpu.VMEM((2,) + values.shape, values.dtype),
            pltpu.SemaphoreType.DMA((2 * rows // TILE,)),
        ],
        name="pack",
    )(keys, values)


def corner_kernel(block_ref, out_ref):
    skip = pl.multiple_of((lax.axis_index("seq") % 2) * 2 * TILE, 2 * TILE)
    out_ref[...] = block_ref[pl.ds(skip, out_ref.shape[0])]


def corner_of(block):
    return pl.pallas_call(
        corner_kernel,
        out_shape=jax.ShapeDtypeStruct((block.shape[0] - 2 * TILE, block.shape[1]), block.dtype),
        in_specs=[VMEM],
        out_specs=VMEM,
        compiler_params=params(),
        name="corner",
    )(block)


def attend_kernel(halves, places, pieces, fresh, bounds_ref, *refs):
    q_refs, refs = refs[:halves], refs[halves:]
    arrays = 1 + max(array for array, _, _, _, _ in pieces)
    array_refs, refs = refs[:arrays], refs[arrays:]
    old_refs, refs = (None, refs) if fresh else (refs[:halves], refs[halves:])
    new_refs, (held_q, held, state) = refs[:halves], refs[halves:]
    rows, columns = q_refs[0].shape
    tiles = rows // TILE
    count = held.shape[1] // 2 // TILE
    heads = columns // HEAD_DIM
    me = lax.axis_index("seq")

    for half in range(halves):
        held_q[half] = q_refs[half][...]
        if fresh:
            state[half, :columns] = jnp.zeros((columns, rows), jnp.float32)
            state[half, columns : columns + heads] = jnp.full((heads, rows), LOWEST, jnp.float32)
            state[half, columns + heads :] = jnp.zeros((state.shape[1] - columns - heads, rows), jnp.float32)
        else:
            state[half] = old_refs[half][...]
    for array, source, slot, target, size in pieces:
        held[slot, target : target + size] = array_refs[array][source : source + size]
    begins = [bounds_ref[2 * half, 0] for half in range(halves)]
    stops = [bounds_ref[2 * half + 1, rows - 1] for half in range(halves)]

    def chosen(at, options):
        return functools.reduce(lambda x, i: jnp.where(at == i, options[i], x), range(1, len(options)), options[0])

    def fold(half, slot, first):
        low = bounds_ref[pl.ds(2 * half, 1), :]
        high = bounds_ref[pl.ds(2 * half + 1, 1), :]
        off = [
            jnp.where((first + j >= low) & (first + j < high), 0.0, -LOWEST).astype(jnp.float32)
            for j in range(count)
        ]
        for h in range(heads):
            own = head_columns(h)
            scores = lax.dot_general(
                jnp.concatenate([held[slot, tile_rows(2 * j), own] for j in range(count)], axis=0),
                held_q[half, :, own],
                (((1,), (1,)), ((), ())),
                preferred_element_type=jnp.float32,
            )
            max_at, total_at = pl.ds(columns + h, 1), pl.ds(columns + heads + h, 1)
            factors, rounded, totals, maxima = [], [], [], []
            for t in range(tiles):
                lanes = tile_rows(t)
                parts = [scores[tile_rows(j), lanes] for j in range(count)]
                old_max = state[half, max_at, lanes]
                new_max = old_max
                for j in range(count):
                    new_max = jnp.maximum(new_max, jnp.max(parts[j], axis=0, keepdims=True) - off[j][:, lanes])
                scaled = new_max * SCALE2
                weights = [jnp.exp2(parts[j] * SCALE2 - (scaled + off[j][:, lanes])) for j in range(count)]
                factors.append(jnp.exp2((old_max - new_max) * SCALE2))
                totals.append(jnp.sum(functools.reduce(jnp.add, weights), axis=0, keepdims=True))
                maxima.append(new_max)
                rounded.append(jnp.concatenate([w.astype(jnp.bfloat16) for w in weights], axis=0))
            factor = jnp.concatenate(factors, axis=1)
            update = jnp.dot(
                jnp.concatenate([held[slot, tile_rows(2 * j + 1), own] for j in range(count)], axis=1),
                jnp.concatenate(rounded, axis=1),
                preferred_element_type=jnp.float32,
            )
            state[half, own] = state[half, own] * factor + update
            state[half, max_at] = jnp.concatenate(maxima, axis=1)
            state[half, total_at] = state[half, total_at] * factor + jnp.concatenate(totals, axis=1)

    @pl.loop(0, halves * len(places))
    def _(unit):
        half, slot = unit // len(places), unit % len(places)
        first = chosen(slot, [place(me) for place in places])

        @pl.when((first < chosen(half, stops)) & (first + count > chosen(half, begins)))
        def _():
            fold(half, slot, first)

    for half in range(halves):
        new_refs[half][...] = state[half]


def attend(bounds, queries, blocks, places, states):
    halves = len(queries)
    rows, columns = queries[0].shape
    heads = columns // HEAD_DIM
    shape = jax.ShapeDtypeStruct((columns + -(-2 * heads // 8) * 8, rows), jnp.float32)
    arrays, pieces = [], []
    for slot, block in enumerate(blocks):
        depth = 0
        for array, source, size in block:
            known = [i for i, other in enumerate(arrays) if other is array]
            if not known:
                arrays.append(array)
            pieces.append((known[0] if known else len(arrays) - 1, source, slot, depth, size))
            depth += size
    pairs = halves * (rows // TILE) * heads * len(blocks) * (depth // 2 // TILE)
    return pl.pallas_call(
        functools.partial(attend_kernel, halves, places, pieces, not states),
        out_shape=[shape] * halves,
        in_specs=[VMEM] * (1 + halves + len(arrays) + len(states)),
        out_specs=[VMEM] * halves,
        scratch_shapes=[
            pltpu.VMEM((halves, rows, columns), queries[0].dtype),
            pltpu.VMEM((len(blocks), depth, columns), arrays[0].dtype),
            pltpu.VMEM((halves,) + shape.shape, jnp.float32),
        ],
        compiler_params=params(),
        cost_estimate=pl.CostEstimate(
            flops=COST * pairs * 4 * TILE * TILE * HEAD_DIM,
            bytes_accessed=2 * len(blocks) * depth * columns + 4 * halves * rows * columns,
            transcendentals=pairs * TILE * TILE,
        ),
        name="attend",
    )(bounds, *queries, *arrays, *states)


def merged(states, columns):
    heads = columns // HEAD_DIM
    for h in range(heads):
        maxima = [ref[columns + h : columns + h + 1] for ref in states]
        totals = [ref[columns + heads + h : columns + heads + h + 1] for ref in states]
        largest = functools.reduce(jnp.maximum, maxima)
        factors = [jnp.exp2((m - largest) * SCALE2) for m in maxima]
        total = functools.reduce(jnp.add, [f * t for f, t in zip(factors, totals)])
        parts = [ref[head_columns(h)] * (f / total) for ref, f in zip(states, factors)]
        yield head_columns(h), functools.reduce(jnp.add, parts).T


def finish_kernel(*refs):
    out_ref = refs[-1]
    for own, done in merged(refs[:-1], out_ref.shape[1]):
        out_ref[:, own] = done.astype(out_ref.dtype)


def finish(states, rows, columns):
    return pl.pallas_call(
        finish_kernel,
        out_shape=jax.ShapeDtypeStruct((rows, columns), jnp.bfloat16),
        in_specs=[VMEM] * len(states),
        out_specs=VMEM,
        compiler_params=params(),
        name="finish",
    )(*states)


def part_kernel(*refs):
    keep_ref, send_ref, held = refs[-3:]
    rows, columns = keep_ref.shape
    mine = lax.axis_index("head")
    for own, done in merged(refs[:-3], columns):
        held[:, own] = done.astype(held.dtype)
    send_ref[...] = held[pl.ds(pl.multiple_of((1 - mine) * rows, 16), rows), :]
    keep_ref[...] = held[pl.ds(pl.multiple_of(mine * rows, 16), rows), :]


def join_kernel(keep_ref, got_ref, out_ref):
    columns = keep_ref.shape[1]
    mine = lax.axis_index("head")
    out_ref[:, pl.ds(pl.multiple_of(mine * columns, TILE), columns)] = keep_ref[...]
    out_ref[:, pl.ds(pl.multiple_of((1 - mine) * columns, TILE), columns)] = got_ref[...]


def finish_in_two(states, rows, columns):
    part = jax.ShapeDtypeStruct((rows // 2, columns), jnp.bfloat16)
    keep, send = pl.pallas_call(
        part_kernel,
        out_shape=[part, part],
        in_specs=[VMEM] * len(states),
        out_specs=[VMEM, VMEM],
        scratch_shapes=[pltpu.VMEM((rows, columns), jnp.bfloat16)],
        compiler_params=params(),
        name="part",
    )(*states)
    got = lax.ppermute(send, "head", [(0, 1), (1, 0)])
    return pl.pallas_call(
        join_kernel,
        out_shape=jax.ShapeDtypeStruct((rows // 2, 2 * columns), jnp.bfloat16),
        in_specs=[VMEM, VMEM],
        out_specs=VMEM,
        compiler_params=params(),
        name="join",
    )(keep, got)


def chip_pairs(mesh):
    places = [tuple(getattr(d, "coords", ())) for d in mesh.devices[:, 0]]
    count = len(places)
    if count % 4 or not places[0] or mesh.shape["head"] != 2:
        return False
    cores = all(places[i] == places[i + 1] for i in range(0, count, 2))
    level = all(places[i][2] == places[i + 3][2] for i in range(0, count, 4))
    climb = all(places[i][2] != places[i + 4][2] for i in range(0, count - 4))
    return cores and level and climb


def paired_shards(owner_count, queries, keys, values, image_tiles):
    rows, columns = queries.shape
    tiles = rows // TILE
    every = range(owner_count)

    def sign(s):
        return 1 - 2 * ((s // 2) % 2)

    def moved(array, source):
        return lax.ppermute(array, "seq", [(source(s), s) for s in every if 0 <= source(s) < owner_count])

    along = lambda s: s + 4 * sign(s)
    against = lambda s: s - 4 * sign(s)
    across = lambda s: s + 2 * sign(s)
    corner = lambda s: s + 8 * (1 - 2 * (s % 2))
    sibling = lambda s: s + 1 - 2 * (s % 2)

    OWN = lambda s: s * tiles
    A1 = lambda s: along(s) * tiles
    B1 = lambda s: against(s) * tiles
    Y1 = lambda s: across(s) * tiles
    YA = lambda s: (s - 2 * sign(s)) * tiles
    AY = lambda s: (s + 6 * sign(s)) * tiles
    BYA = lambda s: (s - 6 * sign(s)) * tiles
    CORNER = lambda s: corner(s) * tiles + s % 2

    block, big, small = pack(keys, values, [(0, tiles - 1), (tiles - 1, tiles)])
    depth, cut = block.shape[0], big.shape[0]
    y1_big, a1, b1, y1_small = moved(big, across), moved(block, along), moved(block, against), moved(small, across)
    bounds, spans = meta(lambda s: [s, sibling(s)], image_tiles, rows)
    both = (queries, moved(queries, sibling))
    fold = functools.partial(attend, bounds, both)
    states = fold([[(block, 0, depth)]], [OWN], [])
    ay_big, ya_big = moved(y1_big, along), moved(y1_big, against)
    smalls = moved(jnp.concatenate([a1[cut:], b1[cut:]], axis=0), across)
    y1 = [(y1_big, 0, cut), (y1_small, 0, depth - cut)]
    states = fold([[(a1, 0, depth)], [(b1, 0, depth)], y1], [A1, B1, Y1], states)

    def near(block, ya_big, ay_big, smalls, states):
        ya = [(ya_big, 0, cut), (smalls, 0, depth - cut)]
        ay = [(ay_big, 0, cut), (smalls, depth - cut, depth - cut)]
        return fold([ya, ay], [YA, AY], states)

    def further(block, ya_big, ay_big, smalls, states):
        bya_big, bya_small = moved(ya_big, against), moved(smalls[: depth - cut], against)
        states = near(block, ya_big, ay_big, smalls, states)
        return fold([[(bya_big, 0, cut), (bya_small, 0, depth - cut)]], [BYA], states)

    def furthest(block, ya_big, ay_big, smalls, states):
        far = moved(corner_of(block), corner)
        states = further(block, ya_big, ay_big, smalls, states)
        return fold([[(far, 0, far.shape[0])]], [CORNER], states)

    mine, theirs = lax.switch(spans, [near, further, furthest], block, ya_big, ay_big, smalls, states)
    return finish_in_two([mine, moved(theirs, sibling)], rows, columns)


def ring_shards(owner_count, queries, keys, values, image_tiles):
    rows, columns = queries.shape
    tiles = rows // TILE
    reach = min(owner_count - 1, -(-(MOST_TILES - 1) // tiles))
    (block,) = pack(keys, values, [])
    bounds, _ = meta(lambda s: [s], image_tiles, rows)
    fold = functools.partial(attend, bounds, (queries,))
    up = [(i, i + 1) for i in range(owner_count - 1)]
    down = [(i + 1, i) for i in range(owner_count - 1)]
    below = above = block
    states = []
    held, places = [block], [lambda s: s * tiles]
    for k in range(1, reach + 1):
        below = lax.ppermute(below, "seq", up)
        above = lax.ppermute(above, "seq", down)
        states = fold([[(b, 0, 2 * rows)] for b in held], places, states)
        held, places = [below, above], [lambda s, k=k: (s - k) * tiles, lambda s, k=k: (s + k) * tiles]
    states = fold([[(b, 0, 2 * rows)] for b in held], places, states)
    attended = finish(states, rows, columns)
    return lax.all_to_all(attended, "head", split_axis=0, concat_axis=1, tiled=True)


def solution(mesh):
    owner_count = mesh.shape["seq"]
    plan = paired_shards if chip_pairs(mesh) else ring_shards
    placed = (P("seq", "head"), P("seq", "head"), P("seq", "head"), P())
    return jax.shard_map(
        functools.partial(plan, owner_count),
        mesh=mesh,
        in_specs=placed,
        out_specs=P(("seq", "head"), None),
        check_vma=False,
    )
```

```python
import functools
import math

import jax
import jax.numpy as jnp
from jax import lax
from jax.experimental import pallas as pl
from jax.experimental.pallas import tpu as pltpu
from jax.sharding import PartitionSpec as P

HEAD_DIM = 128
TILE = 128
MOST_TILES = 21

LOWEST = -1e30
SCALE2 = math.log2(math.e) / math.sqrt(HEAD_DIM)
COST = 6

VMEM = pl.BlockSpec(memory_space=pltpu.VMEM)
SMEM = pl.BlockSpec(memory_space=pltpu.SMEM)
HBM = pl.BlockSpec(memory_space=pl.ANY)


def params():
    return pltpu.CompilerParams(vmem_limit_bytes=32 * 1024 * 1024)


def head_columns(h):
    return slice(h * HEAD_DIM, (h + 1) * HEAD_DIM)


def tile_rows(t):
    return slice(t * TILE, (t + 1) * TILE)


def image_bounds(tiles_ref, tile):
    first = jnp.int32(0)
    start, end = jnp.int32(0), jnp.int32(0)
    for i in range(tiles_ref.shape[0]):
        after = first + tiles_ref[i]
        inside = (tile >= first) & (tile < after)
        start = jnp.where(inside, first, start)
        end = jnp.where(inside, after, end)
        first = after
    return start, end


def chip_spans(tiles_ref, chip_tiles):
    first = jnp.int32(0)
    even, odd, four = jnp.int32(0), jnp.int32(0), jnp.int32(0)
    for i in range(tiles_ref.shape[0]):
        after = first + tiles_ref[i]
        low, high = first // chip_tiles, (after - 1) // chip_tiles
        parity = low % 2
        even = jnp.where(high - (low + parity) >= 3, 1, even)
        odd = jnp.where(high - (low + 1 - parity) >= 3, 1, odd)
        four = jnp.where(high - low >= 4, 1, four)
        first = after
    return jnp.where(odd + four == 0, 0, jnp.where(even + four == 0, 1, 2)).astype(jnp.int32)


def meta_kernel(halves, tiles_ref, bounds_ref, spans_ref):
    tiles = bounds_ref.shape[1] // TILE
    me = lax.axis_index("seq")
    bounds_ref[...] = jnp.zeros(bounds_ref.shape, jnp.int32)
    for half, owner in enumerate(halves(me)):
        for t in range(tiles):
            start, end = image_bounds(tiles_ref, owner * tiles + t)
            bounds_ref[2 * half : 2 * half + 1, tile_rows(t)] = jnp.full((1, TILE), start, jnp.int32)
            bounds_ref[2 * half + 1 : 2 * half + 2, tile_rows(t)] = jnp.full((1, TILE), end, jnp.int32)
    spans_ref[0] = chip_spans(tiles_ref, 2 * tiles)


def meta(halves, image_tiles, rows):
    bounds, spans = pl.pallas_call(
        functools.partial(meta_kernel, halves),
        out_shape=[jax.ShapeDtypeStruct((8, rows), jnp.int32), jax.ShapeDtypeStruct((1,), jnp.int32)],
        in_specs=[SMEM],
        out_specs=[VMEM, SMEM],
        compiler_params=params(),
        name="meta",
    )(image_tiles)
    return bounds, spans[0]


def pack_kernel(k_ref, v_ref, out_ref, held, sems):
    rows, columns = k_ref.shape
    tiles = rows // TILE
    copies = []
    for t in range(tiles):
        copies.append(pltpu.make_async_copy(v_ref.at[tile_rows(t)], held.at[tile_rows(t)], sems.at[2 * t]))
        copies.append(pltpu.make_async_copy(k_ref.at[tile_rows(t)], out_ref.at[tile_rows(2 * t)], sems.at[2 * t + 1]))
    for copy in copies:
        copy.start()
    for t in range(tiles):
        copies[2 * t].wait()
        for h in range(columns // HEAD_DIM):
            out_ref[tile_rows(2 * t + 1), head_columns(h)] = held[tile_rows(t), head_columns(h)].T
    for copy in copies[1::2]:
        copy.wait()


def pack(keys, values):
    rows, columns = keys.shape
    return pl.pallas_call(
        pack_kernel,
        out_shape=jax.ShapeDtypeStruct((2 * rows, columns), keys.dtype),
        in_specs=[HBM, HBM],
        out_specs=VMEM,
        scratch_shapes=[pltpu.VMEM(values.shape, values.dtype), pltpu.SemaphoreType.DMA((2 * rows // TILE,))],
        name="pack",
    )(keys, values)


def corner_kernel(block_ref, out_ref):
    skip = pl.multiple_of((lax.axis_index("seq") % 2) * 2 * TILE, 2 * TILE)
    out_ref[...] = block_ref[pl.ds(skip, out_ref.shape[0])]


def corner_of(block):
    return pl.pallas_call(
        corner_kernel,
        out_shape=jax.ShapeDtypeStruct((block.shape[0] - 2 * TILE, block.shape[1]), block.dtype),
        in_specs=[VMEM],
        out_specs=VMEM,
        compiler_params=params(),
        name="corner",
    )(block)


def attend_kernel(halves, places, pieces, fresh, bounds_ref, *refs):
    q_refs, refs = refs[:halves], refs[halves:]
    arrays = 1 + max(array for array, _, _, _, _ in pieces)
    array_refs, refs = refs[:arrays], refs[arrays:]
    old_refs, refs = (None, refs) if fresh else (refs[:halves], refs[halves:])
    new_refs, (held_q, held, state) = refs[:halves], refs[halves:]
    rows, columns = q_refs[0].shape
    tiles = rows // TILE
    count = held.shape[1] // 2 // TILE
    heads = columns // HEAD_DIM
    me = lax.axis_index("seq")

    for half in range(halves):
        held_q[half] = q_refs[half][...]
        if fresh:
            state[half, :columns] = jnp.zeros((columns, rows), jnp.float32)
            state[half, columns : columns + heads] = jnp.full((heads, rows), LOWEST, jnp.float32)
            state[half, columns + heads :] = jnp.zeros((state.shape[1] - columns - heads, rows), jnp.float32)
        else:
            state[half] = old_refs[half][...]
    for array, source, slot, target, size in pieces:
        held[slot, target : target + size] = array_refs[array][source : source + size]
    begins = [bounds_ref[2 * half, 0] for half in range(halves)]
    stops = [bounds_ref[2 * half + 1, rows - 1] for half in range(halves)]

    def chosen(at, options):
        return functools.reduce(lambda x, i: jnp.where(at == i, options[i], x), range(1, len(options)), options[0])

    def fold(half, slot, first):
        low = bounds_ref[pl.ds(2 * half, 1), :]
        high = bounds_ref[pl.ds(2 * half + 1, 1), :]
        off = [
            jnp.where((first + j >= low) & (first + j < high), 0.0, -LOWEST).astype(jnp.float32)
            for j in range(count)
        ]
        for h in range(heads):
            own = head_columns(h)
            scores = lax.dot_general(
                jnp.concatenate([held[slot, tile_rows(2 * j), own] for j in range(count)], axis=0),
                held_q[half, :, own],
                (((1,), (1,)), ((), ())),
                preferred_element_type=jnp.float32,
            )
            max_at, total_at = pl.ds(columns + h, 1), pl.ds(columns + heads + h, 1)
            factors, rounded, totals, maxima = [], [], [], []
            for t in range(tiles):
                lanes = tile_rows(t)
                parts = [scores[tile_rows(j), lanes] for j in range(count)]
                old_max = state[half, max_at, lanes]
                new_max = old_max
                for j in range(count):
                    new_max = jnp.maximum(new_max, jnp.max(parts[j], axis=0, keepdims=True) - off[j][:, lanes])
                scaled = new_max * SCALE2
                weights = [jnp.exp2(parts[j] * SCALE2 - (scaled + off[j][:, lanes])) for j in range(count)]
                factors.append(jnp.exp2((old_max - new_max) * SCALE2))
                totals.append(jnp.sum(functools.reduce(jnp.add, weights), axis=0, keepdims=True))
                maxima.append(new_max)
                rounded.append(jnp.concatenate([w.astype(jnp.bfloat16) for w in weights], axis=0))
            factor = jnp.concatenate(factors, axis=1)
            update = jnp.dot(
                jnp.concatenate([held[slot, tile_rows(2 * j + 1), own] for j in range(count)], axis=1),
                jnp.concatenate(rounded, axis=1),
                preferred_element_type=jnp.float32,
            )
            state[half, own] = state[half, own] * factor + update
            state[half, max_at] = jnp.concatenate(maxima, axis=1)
            state[half, total_at] = state[half, total_at] * factor + jnp.concatenate(totals, axis=1)

    @pl.loop(0, halves * len(places))
    def _(unit):
        half, slot = unit // len(places), unit % len(places)
        first = chosen(slot, [place(me) for place in places])

        @pl.when((first < chosen(half, stops)) & (first + count > chosen(half, begins)))
        def _():
            fold(half, slot, first)

    for half in range(halves):
        new_refs[half][...] = state[half]


def attend(bounds, queries, blocks, places, states):
    halves = len(queries)
    rows, columns = queries[0].shape
    heads = columns // HEAD_DIM
    shape = jax.ShapeDtypeStruct((columns + -(-2 * heads // 8) * 8, rows), jnp.float32)
    arrays, pieces = [], []
    for slot, block in enumerate(blocks):
        depth = 0
        for array, source, size in block:
            known = [i for i, other in enumerate(arrays) if other is array]
            if not known:
                arrays.append(array)
            pieces.append((known[0] if known else len(arrays) - 1, source, slot, depth, size))
            depth += size
    pairs = halves * (rows // TILE) * heads * len(blocks) * (depth // 2 // TILE)
    return pl.pallas_call(
        functools.partial(attend_kernel, halves, places, pieces, not states),
        out_shape=[shape] * halves,
        in_specs=[VMEM] * (1 + halves + len(arrays) + len(states)),
        out_specs=[VMEM] * halves,
        scratch_shapes=[
            pltpu.VMEM((halves, rows, columns), queries[0].dtype),
            pltpu.VMEM((len(blocks), depth, columns), arrays[0].dtype),
            pltpu.VMEM((halves,) + shape.shape, jnp.float32),
        ],
        compiler_params=params(),
        cost_estimate=pl.CostEstimate(
            flops=COST * pairs * 4 * TILE * TILE * HEAD_DIM,
            bytes_accessed=2 * len(blocks) * depth * columns + 4 * halves * rows * columns,
            transcendentals=pairs * TILE * TILE,
        ),
        name="attend",
    )(bounds, *queries, *arrays, *states)


def merged(states, columns):
    heads = columns // HEAD_DIM
    for h in range(heads):
        maxima = [ref[columns + h : columns + h + 1] for ref in states]
        totals = [ref[columns + heads + h : columns + heads + h + 1] for ref in states]
        largest = functools.reduce(jnp.maximum, maxima)
        factors = [jnp.exp2((m - largest) * SCALE2) for m in maxima]
        total = functools.reduce(jnp.add, [f * t for f, t in zip(factors, totals)])
        parts = [ref[head_columns(h)] * (f / total) for ref, f in zip(states, factors)]
        yield head_columns(h), functools.reduce(jnp.add, parts).T


def finish_kernel(*refs):
    out_ref = refs[-1]
    for own, done in merged(refs[:-1], out_ref.shape[1]):
        out_ref[:, own] = done.astype(out_ref.dtype)


def finish(states, rows, columns):
    return pl.pallas_call(
        finish_kernel,
        out_shape=jax.ShapeDtypeStruct((rows, columns), jnp.bfloat16),
        in_specs=[VMEM] * len(states),
        out_specs=VMEM,
        compiler_params=params(),
        name="finish",
    )(*states)


def part_kernel(*refs):
    keep_ref, send_ref, held = refs[-3:]
    rows, columns = keep_ref.shape
    mine = lax.axis_index("head")
    for own, done in merged(refs[:-3], columns):
        held[:, own] = done.astype(held.dtype)
    send_ref[...] = held[pl.ds(pl.multiple_of((1 - mine) * rows, 16), rows), :]
    keep_ref[...] = held[pl.ds(pl.multiple_of(mine * rows, 16), rows), :]


def join_kernel(keep_ref, got_ref, out_ref):
    columns = keep_ref.shape[1]
    mine = lax.axis_index("head")
    out_ref[:, pl.ds(pl.multiple_of(mine * columns, TILE), columns)] = keep_ref[...]
    out_ref[:, pl.ds(pl.multiple_of((1 - mine) * columns, TILE), columns)] = got_ref[...]


def finish_in_two(states, rows, columns):
    part = jax.ShapeDtypeStruct((rows // 2, columns), jnp.bfloat16)
    keep, send = pl.pallas_call(
        part_kernel,
        out_shape=[part, part],
        in_specs=[VMEM] * len(states),
        out_specs=[VMEM, VMEM],
        scratch_shapes=[pltpu.VMEM((rows, columns), jnp.bfloat16)],
        compiler_params=params(),
        name="part",
    )(*states)
    got = lax.ppermute(send, "head", [(0, 1), (1, 0)])
    return pl.pallas_call(
        join_kernel,
        out_shape=jax.ShapeDtypeStruct((rows // 2, 2 * columns), jnp.bfloat16),
        in_specs=[VMEM, VMEM],
        out_specs=VMEM,
        compiler_params=params(),
        name="join",
    )(keep, got)


def chip_pairs(mesh):
    places = [tuple(getattr(d, "coords", ())) for d in mesh.devices[:, 0]]
    count = len(places)
    if count % 4 or not places[0] or mesh.shape["head"] != 2:
        return False
    cores = all(places[i] == places[i + 1] for i in range(0, count, 2))
    level = all(places[i][2] == places[i + 3][2] for i in range(0, count, 4))
    climb = all(places[i][2] != places[i + 4][2] for i in range(0, count - 4))
    return cores and level and climb


def paired_shards(owner_count, queries, keys, values, image_tiles):
    rows, columns = queries.shape
    tiles = rows // TILE
    every = range(owner_count)

    def sign(s):
        return 1 - 2 * ((s // 2) % 2)

    def moved(array, source):
        return lax.ppermute(array, "seq", [(source(s), s) for s in every if 0 <= source(s) < owner_count])

    along = lambda s: s + 4 * sign(s)
    against = lambda s: s - 4 * sign(s)
    across = lambda s: s + 2 * sign(s)
    corner = lambda s: s + 8 * (1 - 2 * (s % 2))
    sibling = lambda s: s + 1 - 2 * (s % 2)

    OWN = lambda s: s * tiles
    A1 = lambda s: along(s) * tiles
    B1 = lambda s: against(s) * tiles
    Y1 = lambda s: across(s) * tiles
    YA = lambda s: (s - 2 * sign(s)) * tiles
    AY = lambda s: (s + 6 * sign(s)) * tiles
    BYA = lambda s: (s - 6 * sign(s)) * tiles
    CORNER = lambda s: corner(s) * tiles + s % 2

    block = pack(keys, values)
    depth = block.shape[0]
    half, most = depth // 2, depth - 2 * TILE
    y1, a1, b1 = moved(block, across), moved(block, along), moved(block, against)
    bounds, spans = meta(lambda s: [s, sibling(s)], image_tiles, rows)
    both = (queries, moved(queries, sibling))
    fold = functools.partial(attend, bounds, both)
    states = fold([[(block, 0, depth)]], [OWN], [])

    def first_hop(a1, b1, y1, states):
        return fold([[(a1, 0, depth)], [(b1, 0, depth)], [(y1, 0, depth)]], [A1, B1, Y1], states)

    def near(block, a1, b1, y1, states):
        ay, ya = moved(y1[:most], along), moved(y1[:most], against)
        rest = moved(jnp.concatenate([a1[most:], b1[most:]], axis=0), across)
        states = first_hop(a1, b1, y1, states)
        ya, ay = [(ya, 0, most), (rest, 0, depth - most)], [(ay, 0, most), (rest, depth - most, depth - most)]
        return fold([ya, ay], [YA, AY], states)

    def odd(block, a1, b1, y1, states):
        ya = moved(y1[:half], against), moved(a1[half:], across)
        aa = moved(a1[half:], along)
        states = first_hop(a1, b1, y1, states)
        bya = moved(ya[0], against), moved(aa, across)
        states = fold([[(part, 0, half) for part in ya]], [YA], states)
        return fold([[(part, 0, half) for part in bya]], [BYA], states)

    def every_way(block, a1, b1, y1, states):
        ya = moved(y1[:half], against), moved(a1[half:], across)
        aa = moved(a1[half:], along)
        states = first_hop(a1, b1, y1, states)
        bya = moved(ya[0], against), moved(aa, across)
        ay = moved(y1, along)
        far = moved(corner_of(block), corner)
        states = fold([[(part, 0, half) for part in ya]], [YA], states)
        states = fold([[(part, 0, half) for part in bya], [(ay, 0, depth)]], [BYA, AY], states)
        return fold([[(far, 0, far.shape[0])]], [CORNER], states)

    mine, theirs = lax.switch(spans, [near, odd, every_way], block, a1, b1, y1, states)
    return finish_in_two([mine, moved(theirs, sibling)], rows, columns)


def ring_shards(owner_count, queries, keys, values, image_tiles):
    rows, columns = queries.shape
    tiles = rows // TILE
    reach = min(owner_count - 1, -(-(MOST_TILES - 1) // tiles))
    block = pack(keys, values)
    bounds, _ = meta(lambda s: [s], image_tiles, rows)
    fold = functools.partial(attend, bounds, (queries,))
    up = [(i, i + 1) for i in range(owner_count - 1)]
    down = [(i + 1, i) for i in range(owner_count - 1)]
    below = above = block
    states = []
    held, places = [block], [lambda s: s * tiles]
    for k in range(1, reach + 1):
        below = lax.ppermute(below, "seq", up)
        above = lax.ppermute(above, "seq", down)
        states = fold([[(b, 0, 2 * rows)] for b in held], places, states)
        held, places = [below, above], [lambda s, k=k: (s - k) * tiles, lambda s, k=k: (s + k) * tiles]
    states = fold([[(b, 0, 2 * rows)] for b in held], places, states)
    attended = finish(states, rows, columns)
    return lax.all_to_all(attended, "head", split_axis=0, concat_axis=1, tiled=True)


def solution(mesh):
    owner_count = mesh.shape["seq"]
    plan = paired_shards if chip_pairs(mesh) else ring_shards
    placed = (P("seq", "head"), P("seq", "head"), P("seq", "head"), P())
    return jax.shard_map(
        functools.partial(plan, owner_count),
        mesh=mesh,
        in_specs=placed,
        out_specs=P(("seq", "head"), None),
        check_vma=False,
    )
```

```python
import functools
import math

import jax
import jax.numpy as jnp
from jax import lax
from jax.experimental import pallas as pl
from jax.experimental.pallas import tpu as pltpu
from jax.sharding import PartitionSpec as P

HEAD_DIM = 128
TILE = 128
MOST_TILES = 21

LOWEST = -1e30
SCALE2 = math.log2(math.e) / math.sqrt(HEAD_DIM)
COST = 6

VMEM = pl.BlockSpec(memory_space=pltpu.VMEM)
SMEM = pl.BlockSpec(memory_space=pltpu.SMEM)
HBM = pl.BlockSpec(memory_space=pl.ANY)


def params():
    return pltpu.CompilerParams(vmem_limit_bytes=32 * 1024 * 1024)


def head_columns(h):
    return slice(h * HEAD_DIM, (h + 1) * HEAD_DIM)


def tile_rows(t):
    return slice(t * TILE, (t + 1) * TILE)


def image_bounds(tiles_ref, tile):
    first = jnp.int32(0)
    start, end = jnp.int32(0), jnp.int32(0)
    for i in range(tiles_ref.shape[0]):
        after = first + tiles_ref[i]
        inside = (tile >= first) & (tile < after)
        start = jnp.where(inside, first, start)
        end = jnp.where(inside, after, end)
        first = after
    return start, end


def chip_spans(tiles_ref, chip_tiles):
    first = jnp.int32(0)
    even, odd, four = jnp.int32(0), jnp.int32(0), jnp.int32(0)
    for i in range(tiles_ref.shape[0]):
        after = first + tiles_ref[i]
        low, high = first // chip_tiles, (after - 1) // chip_tiles
        parity = low % 2
        even = jnp.where(high - (low + parity) >= 3, 1, even)
        odd = jnp.where(high - (low + 1 - parity) >= 3, 1, odd)
        four = jnp.where(high - low >= 4, 1, four)
        first = after
    return jnp.where(odd + four == 0, 0, jnp.where(even + four == 0, 1, 2)).astype(jnp.int32)


def meta_kernel(halves, tiles_ref, bounds_ref, spans_ref):
    tiles = bounds_ref.shape[1] // TILE
    me = lax.axis_index("seq")
    bounds_ref[...] = jnp.zeros(bounds_ref.shape, jnp.int32)
    for half, owner in enumerate(halves(me)):
        for t in range(tiles):
            start, end = image_bounds(tiles_ref, owner * tiles + t)
            bounds_ref[2 * half : 2 * half + 1, tile_rows(t)] = jnp.full((1, TILE), start, jnp.int32)
            bounds_ref[2 * half + 1 : 2 * half + 2, tile_rows(t)] = jnp.full((1, TILE), end, jnp.int32)
    spans_ref[0] = chip_spans(tiles_ref, 2 * tiles)


def meta(halves, image_tiles, rows):
    bounds, spans = pl.pallas_call(
        functools.partial(meta_kernel, halves),
        out_shape=[jax.ShapeDtypeStruct((8, rows), jnp.int32), jax.ShapeDtypeStruct((1,), jnp.int32)],
        in_specs=[SMEM],
        out_specs=[VMEM, SMEM],
        compiler_params=params(),
        cost_estimate=pl.CostEstimate(flops=COST * 2**31, bytes_accessed=0, transcendentals=0),
        name="meta",
    )(image_tiles)
    return bounds, spans[0]


def pack_kernel(k_ref, v_ref, out_ref, held, sems):
    rows, columns = k_ref.shape
    tiles = rows // TILE
    copies = []
    for t in range(tiles):
        copies.append(pltpu.make_async_copy(v_ref.at[tile_rows(t)], held.at[tile_rows(t)], sems.at[2 * t]))
        copies.append(pltpu.make_async_copy(k_ref.at[tile_rows(t)], out_ref.at[tile_rows(2 * t)], sems.at[2 * t + 1]))
    for copy in copies:
        copy.start()
    for t in range(tiles):
        copies[2 * t].wait()
        for h in range(columns // HEAD_DIM):
            out_ref[tile_rows(2 * t + 1), head_columns(h)] = held[tile_rows(t), head_columns(h)].T
    for copy in copies[1::2]:
        copy.wait()


def pack(keys, values):
    rows, columns = keys.shape
    return pl.pallas_call(
        pack_kernel,
        out_shape=jax.ShapeDtypeStruct((2 * rows, columns), keys.dtype),
        in_specs=[HBM, HBM],
        out_specs=VMEM,
        scratch_shapes=[pltpu.VMEM(values.shape, values.dtype), pltpu.SemaphoreType.DMA((2 * rows // TILE,))],
        name="pack",
    )(keys, values)


def corner_kernel(block_ref, out_ref):
    skip = pl.multiple_of((lax.axis_index("seq") % 2) * 2 * TILE, 2 * TILE)
    out_ref[...] = block_ref[pl.ds(skip, out_ref.shape[0])]


def corner_of(block):
    return pl.pallas_call(
        corner_kernel,
        out_shape=jax.ShapeDtypeStruct((block.shape[0] - 2 * TILE, block.shape[1]), block.dtype),
        in_specs=[VMEM],
        out_specs=VMEM,
        compiler_params=params(),
        name="corner",
    )(block)


def attend_kernel(which, places, pieces, fresh, bounds_ref, *refs):
    halves = len(which)
    q_refs, refs = refs[:halves], refs[halves:]
    arrays = 1 + max(array for array, _, _, _, _ in pieces)
    array_refs, refs = refs[:arrays], refs[arrays:]
    old_refs, refs = (None, refs) if fresh else (refs[:halves], refs[halves:])
    new_refs, (held_q, held, state) = refs[:halves], refs[halves:]
    rows, columns = q_refs[0].shape
    tiles = rows // TILE
    count = held.shape[1] // 2 // TILE
    heads = columns // HEAD_DIM
    me = lax.axis_index("seq")

    for half in range(halves):
        held_q[half] = q_refs[half][...]
        if fresh:
            state[half, :columns] = jnp.zeros((columns, rows), jnp.float32)
            state[half, columns : columns + heads] = jnp.full((heads, rows), LOWEST, jnp.float32)
            state[half, columns + heads :] = jnp.zeros((state.shape[1] - columns - heads, rows), jnp.float32)
        else:
            state[half] = old_refs[half][...]
    for array, source, slot, target, size in pieces:
        held[slot, target : target + size] = array_refs[array][source : source + size]
    begins = [bounds_ref[2 * w, 0] for w in which]
    stops = [bounds_ref[2 * w + 1, rows - 1] for w in which]

    def chosen(at, options):
        return functools.reduce(lambda x, i: jnp.where(at == i, options[i], x), range(1, len(options)), options[0])

    def fold(half, slot, first):
        low = bounds_ref[pl.ds(2 * (half + which[0]), 1), :]
        high = bounds_ref[pl.ds(2 * (half + which[0]) + 1, 1), :]
        off = [
            jnp.where((first + j >= low) & (first + j < high), 0.0, -LOWEST).astype(jnp.float32)
            for j in range(count)
        ]
        for h in range(heads):
            own = head_columns(h)
            scores = lax.dot_general(
                jnp.concatenate([held[slot, tile_rows(2 * j), own] for j in range(count)], axis=0),
                held_q[half, :, own],
                (((1,), (1,)), ((), ())),
                preferred_element_type=jnp.float32,
            )
            max_at, total_at = pl.ds(columns + h, 1), pl.ds(columns + heads + h, 1)
            factors, rounded, totals, maxima = [], [], [], []
            for t in range(tiles):
                lanes = tile_rows(t)
                parts = [scores[tile_rows(j), lanes] for j in range(count)]
                old_max = state[half, max_at, lanes]
                new_max = old_max
                for j in range(count):
                    new_max = jnp.maximum(new_max, jnp.max(parts[j], axis=0, keepdims=True) - off[j][:, lanes])
                scaled = new_max * SCALE2
                weights = [jnp.exp2(parts[j] * SCALE2 - (scaled + off[j][:, lanes])) for j in range(count)]
                factors.append(jnp.exp2((old_max - new_max) * SCALE2))
                totals.append(jnp.sum(functools.reduce(jnp.add, weights), axis=0, keepdims=True))
                maxima.append(new_max)
                rounded.append(jnp.concatenate([w.astype(jnp.bfloat16) for w in weights], axis=0))
            factor = jnp.concatenate(factors, axis=1)
            update = jnp.dot(
                jnp.concatenate([held[slot, tile_rows(2 * j + 1), own] for j in range(count)], axis=1),
                jnp.concatenate(rounded, axis=1),
                preferred_element_type=jnp.float32,
            )
            state[half, own] = state[half, own] * factor + update
            state[half, max_at] = jnp.concatenate(maxima, axis=1)
            state[half, total_at] = state[half, total_at] * factor + jnp.concatenate(totals, axis=1)

    @pl.loop(0, halves * len(places))
    def _(unit):
        half, slot = unit // len(places), unit % len(places)
        first = chosen(slot, [place(me) for place in places])

        @pl.when((first < chosen(half, stops)) & (first + count > chosen(half, begins)))
        def _():
            fold(half, slot, first)

    for half in range(halves):
        new_refs[half][...] = state[half]


def attend(bounds, queries, blocks, places, states, which=None):
    which = list(range(len(queries))) if which is None else which
    queries, states = [queries[w] for w in which], [states[w] for w in which] if states else []
    halves = len(which)
    rows, columns = queries[0].shape
    heads = columns // HEAD_DIM
    shape = jax.ShapeDtypeStruct((columns + -(-2 * heads // 8) * 8, rows), jnp.float32)
    arrays, pieces = [], []
    for slot, block in enumerate(blocks):
        depth = 0
        for array, source, size in block:
            known = [i for i, other in enumerate(arrays) if other is array]
            if not known:
                arrays.append(array)
            pieces.append((known[0] if known else len(arrays) - 1, source, slot, depth, size))
            depth += size
    pairs = halves * (rows // TILE) * heads * len(blocks) * (depth // 2 // TILE)
    return pl.pallas_call(
        functools.partial(attend_kernel, which, places, pieces, not states),
        out_shape=[shape] * halves,
        in_specs=[VMEM] * (1 + halves + len(arrays) + len(states)),
        out_specs=[VMEM] * halves,
        scratch_shapes=[
            pltpu.VMEM((halves, rows, columns), queries[0].dtype),
            pltpu.VMEM((len(blocks), depth, columns), arrays[0].dtype),
            pltpu.VMEM((halves,) + shape.shape, jnp.float32),
        ],
        compiler_params=params(),
        cost_estimate=pl.CostEstimate(
            flops=COST * pairs * 4 * TILE * TILE * HEAD_DIM,
            bytes_accessed=2 * len(blocks) * depth * columns + 4 * halves * rows * columns,
            transcendentals=pairs * TILE * TILE,
        ),
        name="attend",
    )(bounds, *queries, *arrays, *states)


def merged(states, columns):
    heads = columns // HEAD_DIM
    for h in range(heads):
        maxima = [ref[columns + h : columns + h + 1] for ref in states]
        totals = [ref[columns + heads + h : columns + heads + h + 1] for ref in states]
        largest = functools.reduce(jnp.maximum, maxima)
        factors = [jnp.exp2((m - largest) * SCALE2) for m in maxima]
        total = functools.reduce(jnp.add, [f * t for f, t in zip(factors, totals)])
        parts = [ref[head_columns(h)] * (f / total) for ref, f in zip(states, factors)]
        yield head_columns(h), functools.reduce(jnp.add, parts).T


def finish_kernel(*refs):
    out_ref = refs[-1]
    for own, done in merged(refs[:-1], out_ref.shape[1]):
        out_ref[:, own] = done.astype(out_ref.dtype)


def finish(states, rows, columns):
    return pl.pallas_call(
        finish_kernel,
        out_shape=jax.ShapeDtypeStruct((rows, columns), jnp.bfloat16),
        in_specs=[VMEM] * len(states),
        out_specs=VMEM,
        compiler_params=params(),
        name="finish",
    )(*states)


def part_kernel(*refs):
    keep_ref, send_ref, held = refs[-3:]
    rows, columns = keep_ref.shape
    mine = lax.axis_index("head")
    for own, done in merged(refs[:-3], columns):
        held[:, own] = done.astype(held.dtype)
    send_ref[...] = held[pl.ds(pl.multiple_of((1 - mine) * rows, 16), rows), :]
    keep_ref[...] = held[pl.ds(pl.multiple_of(mine * rows, 16), rows), :]


def join_kernel(keep_ref, got_ref, out_ref):
    columns = keep_ref.shape[1]
    mine = lax.axis_index("head")
    out_ref[:, pl.ds(pl.multiple_of(mine * columns, TILE), columns)] = keep_ref[...]
    out_ref[:, pl.ds(pl.multiple_of((1 - mine) * columns, TILE), columns)] = got_ref[...]


def finish_in_two(states, rows, columns):
    part = jax.ShapeDtypeStruct((rows // 2, columns), jnp.bfloat16)
    keep, send = pl.pallas_call(
        part_kernel,
        out_shape=[part, part],
        in_specs=[VMEM] * len(states),
        out_specs=[VMEM, VMEM],
        scratch_shapes=[pltpu.VMEM((rows, columns), jnp.bfloat16)],
        compiler_params=params(),
        name="part",
    )(*states)
    got = lax.ppermute(send, "head", [(0, 1), (1, 0)])
    return pl.pallas_call(
        join_kernel,
        out_shape=jax.ShapeDtypeStruct((rows // 2, 2 * columns), jnp.bfloat16),
        in_specs=[VMEM, VMEM],
        out_specs=VMEM,
        compiler_params=params(),
        name="join",
    )(keep, got)


def chip_pairs(mesh):
    places = [tuple(getattr(d, "coords", ())) for d in mesh.devices[:, 0]]
    count = len(places)
    if count % 4 or not places[0] or mesh.shape["head"] != 2:
        return False
    cores = all(places[i] == places[i + 1] for i in range(0, count, 2))
    level = all(places[i][2] == places[i + 3][2] for i in range(0, count, 4))
    climb = all(places[i][2] != places[i + 4][2] for i in range(0, count - 4))
    return cores and level and climb


def paired_shards(owner_count, queries, keys, values, image_tiles):
    rows, columns = queries.shape
    tiles = rows // TILE
    every = range(owner_count)

    def sign(s):
        return 1 - 2 * ((s // 2) % 2)

    def moved(array, source):
        return lax.ppermute(array, "seq", [(source(s), s) for s in every if 0 <= source(s) < owner_count])

    along = lambda s: s + 4 * sign(s)
    against = lambda s: s - 4 * sign(s)
    across = lambda s: s + 2 * sign(s)
    corner = lambda s: s + 8 * (1 - 2 * (s % 2))
    sibling = lambda s: s + 1 - 2 * (s % 2)

    OWN = lambda s: s * tiles
    A1 = lambda s: along(s) * tiles
    B1 = lambda s: against(s) * tiles
    Y1 = lambda s: across(s) * tiles
    YA = lambda s: (s - 2 * sign(s)) * tiles
    AY = lambda s: (s + 6 * sign(s)) * tiles
    BYA = lambda s: (s - 6 * sign(s)) * tiles
    CORNER = lambda s: corner(s) * tiles + s % 2

    block = pack(keys, values)
    depth = block.shape[0]
    half, most = depth // 2, depth - 2 * TILE
    less = depth - most
    y1, a1, b1 = moved(block, across), moved(block, along), moved(block, against)
    bounds, spans = meta(lambda s: [s, sibling(s)], image_tiles, rows)
    both = (queries, moved(queries, sibling))
    fold = functools.partial(attend, bounds, both)
    states = fold([[(block, 0, depth)]], [OWN], [])
    ya_big = moved(y1[:most], against)
    either = moved(jnp.where(spans == 0, y1[:most], a1[less:]), along)
    ya_small, ay_small = moved(a1[most:], across), moved(b1[most:], across)
    states = fold([[(y1, 0, depth)], [(a1, 0, depth)], [(b1, 0, depth)]], [Y1, A1, B1], states)

    def last(blocks, places, states):
        (theirs,) = fold(blocks, places, states, which=[1])
        got = moved(theirs, sibling)
        (mine,) = fold(blocks, places, states, which=[0])
        return mine, got

    def near(block, y1, ya_big, ya_small, either, ay_small, states):
        ya, ay = [(ya_big, 0, most), (ya_small, 0, less)], [(either, 0, most), (ay_small, 0, less)]
        return last([ya, ay], [YA, AY], states)

    def odd(block, y1, ya_big, ya_small, either, ay_small, states):
        bya = moved(ya_big[:half], against), moved(either[half - less :], across)
        states = fold([[(ya_big, 0, most), (ya_small, 0, less)]], [YA], states)
        return last([[(part, 0, half) for part in bya]], [BYA], states)

    def every_way(block, y1, ya_big, ya_small, either, ay_small, states):
        bya = moved(ya_big[:half], against), moved(either[half - less :], across)
        ay_big = moved(y1[:most], along)
        far = moved(corner_of(block), corner)
        states = fold([[(ya_big, 0, most), (ya_small, 0, less)]], [YA], states)
        bya, ay = [(part, 0, half) for part in bya], [(ay_big, 0, most), (ay_small, 0, less)]
        states = fold([bya, ay], [BYA, AY], states)
        return last([[(far, 0, far.shape[0])]], [CORNER], states)

    branches = [near, odd, every_way]
    mine, got = lax.switch(spans, branches, block, y1, ya_big, ya_small, either, ay_small, states)
    return finish_in_two([mine, got], rows, columns)


def ring_shards(owner_count, queries, keys, values, image_tiles):
    rows, columns = queries.shape
    tiles = rows // TILE
    reach = min(owner_count - 1, -(-(MOST_TILES - 1) // tiles))
    block = pack(keys, values)
    bounds, _ = meta(lambda s: [s], image_tiles, rows)
    fold = functools.partial(attend, bounds, (queries,))
    up = [(i, i + 1) for i in range(owner_count - 1)]
    down = [(i + 1, i) for i in range(owner_count - 1)]
    below = above = block
    states = []
    held, places = [block], [lambda s: s * tiles]
    for k in range(1, reach + 1):
        below = lax.ppermute(below, "seq", up)
        above = lax.ppermute(above, "seq", down)
        states = fold([[(b, 0, 2 * rows)] for b in held], places, states)
        held, places = [below, above], [lambda s, k=k: (s - k) * tiles, lambda s, k=k: (s + k) * tiles]
    states = fold([[(b, 0, 2 * rows)] for b in held], places, states)
    attended = finish(states, rows, columns)
    return lax.all_to_all(attended, "head", split_axis=0, concat_axis=1, tiled=True)


def solution(mesh):
    owner_count = mesh.shape["seq"]
    plan = paired_shards if chip_pairs(mesh) else ring_shards
    placed = (P("seq", "head"), P("seq", "head"), P("seq", "head"), P())
    return jax.shard_map(
        functools.partial(plan, owner_count),
        mesh=mesh,
        in_specs=placed,
        out_specs=P(("seq", "head"), None),
        check_vma=False,
    )
```

```python
import functools
import math

import jax
import jax.numpy as jnp
from jax import lax
from jax.experimental import pallas as pl
from jax.experimental.pallas import tpu as pltpu
from jax.sharding import PartitionSpec as P

HEAD_DIM = 128
TILE = 128
MOST_TILES = 21

LOWEST = -1e30
SCALE2 = math.log2(math.e) / math.sqrt(HEAD_DIM)
COST = 6

VMEM = pl.BlockSpec(memory_space=pltpu.VMEM)
SMEM = pl.BlockSpec(memory_space=pltpu.SMEM)
HBM = pl.BlockSpec(memory_space=pl.ANY)


def params():
    return pltpu.CompilerParams(vmem_limit_bytes=32 * 1024 * 1024)


def head_columns(h):
    return slice(h * HEAD_DIM, (h + 1) * HEAD_DIM)


def tile_rows(t):
    return slice(t * TILE, (t + 1) * TILE)


def image_bounds(tiles_ref, tile):
    first = jnp.int32(0)
    start, end = jnp.int32(0), jnp.int32(0)
    for i in range(tiles_ref.shape[0]):
        after = first + tiles_ref[i]
        inside = (tile >= first) & (tile < after)
        start = jnp.where(inside, first, start)
        end = jnp.where(inside, after, end)
        first = after
    return start, end


def chip_spans(tiles_ref, chip_tiles):
    first = jnp.int32(0)
    even, odd, four = jnp.int32(0), jnp.int32(0), jnp.int32(0)
    for i in range(tiles_ref.shape[0]):
        after = first + tiles_ref[i]
        low, high = first // chip_tiles, (after - 1) // chip_tiles
        parity = low % 2
        even = jnp.where(high - (low + parity) >= 3, 1, even)
        odd = jnp.where(high - (low + 1 - parity) >= 3, 1, odd)
        four = jnp.where(high - low >= 4, 1, four)
        first = after
    return jnp.where(odd + four == 0, 0, jnp.where(even + four == 0, 1, 2)).astype(jnp.int32)


def meta_kernel(halves, tiles_ref, bounds_ref, spans_ref):
    tiles = bounds_ref.shape[1] // TILE
    me = lax.axis_index("seq")
    bounds_ref[...] = jnp.zeros(bounds_ref.shape, jnp.int32)
    for half, owner in enumerate(halves(me)):
        for t in range(tiles):
            start, end = image_bounds(tiles_ref, owner * tiles + t)
            bounds_ref[2 * half : 2 * half + 1, tile_rows(t)] = jnp.full((1, TILE), start, jnp.int32)
            bounds_ref[2 * half + 1 : 2 * half + 2, tile_rows(t)] = jnp.full((1, TILE), end, jnp.int32)
    spans_ref[0] = chip_spans(tiles_ref, 2 * tiles)


def meta(halves, image_tiles, rows):
    bounds, spans = pl.pallas_call(
        functools.partial(meta_kernel, halves),
        out_shape=[jax.ShapeDtypeStruct((8, rows), jnp.int32), jax.ShapeDtypeStruct((1,), jnp.int32)],
        in_specs=[SMEM],
        out_specs=[VMEM, SMEM],
        compiler_params=params(),
        cost_estimate=pl.CostEstimate(flops=COST * 2**29, bytes_accessed=0, transcendentals=0),
        name="meta",
    )(image_tiles)
    return bounds, spans[0]


def pack_kernel(k_ref, v_ref, out_ref, held, sems):
    rows, columns = k_ref.shape
    tiles = rows // TILE
    copies = []
    for t in range(tiles):
        copies.append(pltpu.make_async_copy(v_ref.at[tile_rows(t)], held.at[tile_rows(t)], sems.at[2 * t]))
        copies.append(pltpu.make_async_copy(k_ref.at[tile_rows(t)], out_ref.at[tile_rows(2 * t)], sems.at[2 * t + 1]))
    for copy in copies:
        copy.start()
    for t in range(tiles):
        copies[2 * t].wait()
        for h in range(columns // HEAD_DIM):
            out_ref[tile_rows(2 * t + 1), head_columns(h)] = held[tile_rows(t), head_columns(h)].T
    for copy in copies[1::2]:
        copy.wait()


def pack(keys, values):
    rows, columns = keys.shape
    return pl.pallas_call(
        pack_kernel,
        out_shape=jax.ShapeDtypeStruct((2 * rows, columns), keys.dtype),
        in_specs=[HBM, HBM],
        out_specs=VMEM,
        scratch_shapes=[pltpu.VMEM(values.shape, values.dtype), pltpu.SemaphoreType.DMA((2 * rows // TILE,))],
        name="pack",
    )(keys, values)


def corner_kernel(a1_ref, b1_ref, out_ref):
    me = lax.axis_index("seq")
    rows = pl.ds(pl.multiple_of((me % 2) * 2 * TILE, 2 * TILE), out_ref.shape[0])

    @pl.when((me // 2) % 2 == 0)
    def _():
        out_ref[...] = a1_ref[rows]

    @pl.when((me // 2) % 2 == 1)
    def _():
        out_ref[...] = b1_ref[rows]


def corner_of(a1, b1):
    return pl.pallas_call(
        corner_kernel,
        out_shape=jax.ShapeDtypeStruct((a1.shape[0] - 2 * TILE, a1.shape[1]), a1.dtype),
        in_specs=[VMEM, VMEM],
        out_specs=VMEM,
        compiler_params=params(),
        name="corner",
    )(a1, b1)


def attend_kernel(which, places, arrays, fresh, bounds_ref, *refs):
    halves = len(which)
    q_refs, refs = refs[:halves], refs[halves:]
    array_refs, refs = refs[: len(arrays)], refs[len(arrays) :]
    old_refs, refs = (None, refs) if fresh else (refs[:halves], refs[halves:])
    new_refs, (held_q, held, state) = refs[:halves], refs[halves:]
    rows, columns = q_refs[0].shape
    tiles = rows // TILE
    count = held.shape[1] // 2 // TILE
    heads = columns // HEAD_DIM
    me = lax.axis_index("seq")

    for half in range(halves):
        held_q[half] = q_refs[half][...]
        if fresh:
            state[half, :columns] = jnp.zeros((columns, rows), jnp.float32)
            state[half, columns : columns + heads] = jnp.full((heads, rows), LOWEST, jnp.float32)
            state[half, columns + heads :] = jnp.zeros((state.shape[1] - columns - heads, rows), jnp.float32)
        else:
            state[half] = old_refs[half][...]
    for slot, (array, shift) in enumerate(arrays):
        size = array_refs[array].shape[0]
        if size < held.shape[1]:
            held[slot] = jnp.zeros(held.shape[1:], held.dtype)
        at = 0 if shift is None else pl.multiple_of(shift(me), 2 * TILE)
        held[slot, pl.ds(at, size)] = array_refs[array][...]
    begins = [bounds_ref[2 * w, 0] for w in which]
    stops = [bounds_ref[2 * w + 1, rows - 1] for w in which]

    def chosen(at, options):
        return functools.reduce(lambda x, i: jnp.where(at == i, options[i], x), range(1, len(options)), options[0])

    def fold(half, slot, first):
        low = bounds_ref[pl.ds(2 * (half + which[0]), 1), :]
        high = bounds_ref[pl.ds(2 * (half + which[0]) + 1, 1), :]
        off = [
            jnp.where((first + j >= low) & (first + j < high), 0.0, -LOWEST).astype(jnp.float32)
            for j in range(count)
        ]
        for h in range(heads):
            own = head_columns(h)
            scores = lax.dot_general(
                jnp.concatenate([held[slot, tile_rows(2 * j), own] for j in range(count)], axis=0),
                held_q[half, :, own],
                (((1,), (1,)), ((), ())),
                preferred_element_type=jnp.float32,
            )
            max_at, total_at = pl.ds(columns + h, 1), pl.ds(columns + heads + h, 1)
            factors, rounded, totals, maxima = [], [], [], []
            for t in range(tiles):
                lanes = tile_rows(t)
                parts = [scores[tile_rows(j), lanes] for j in range(count)]
                old_max = state[half, max_at, lanes]
                new_max = old_max
                for j in range(count):
                    new_max = jnp.maximum(new_max, jnp.max(parts[j], axis=0, keepdims=True) - off[j][:, lanes])
                scaled = new_max * SCALE2
                weights = [jnp.exp2(parts[j] * SCALE2 - (scaled + off[j][:, lanes])) for j in range(count)]
                factors.append(jnp.exp2((old_max - new_max) * SCALE2))
                totals.append(jnp.sum(functools.reduce(jnp.add, weights), axis=0, keepdims=True))
                maxima.append(new_max)
                rounded.append(jnp.concatenate([w.astype(jnp.bfloat16) for w in weights], axis=0))
            factor = jnp.concatenate(factors, axis=1)
            update = jnp.dot(
                jnp.concatenate([held[slot, tile_rows(2 * j + 1), own] for j in range(count)], axis=1),
                jnp.concatenate(rounded, axis=1),
                preferred_element_type=jnp.float32,
            )
            state[half, own] = state[half, own] * factor + update
            state[half, max_at] = jnp.concatenate(maxima, axis=1)
            state[half, total_at] = state[half, total_at] * factor + jnp.concatenate(totals, axis=1)

    @pl.loop(0, halves * len(places))
    def _(unit):
        half, slot = unit // len(places), unit % len(places)
        first = chosen(slot, [place(me) for place in places])

        @pl.when((first < chosen(half, stops)) & (first + count > chosen(half, begins)))
        def _():
            fold(half, slot, first)

    for half in range(halves):
        new_refs[half][...] = state[half]


def attend(bounds, queries, blocks, places, states, which=None, shifts=None):
    which = list(range(len(queries))) if which is None else which
    queries, states = [queries[w] for w in which], [states[w] for w in which] if states else []
    halves = len(which)
    rows, columns = queries[0].shape
    depth = blocks[0].shape[0]
    heads = columns // HEAD_DIM
    shape = jax.ShapeDtypeStruct((columns + -(-2 * heads // 8) * 8, rows), jnp.float32)
    arrays = list(enumerate(shifts or [None] * len(blocks)))
    pairs = halves * (rows // TILE) * heads * len(blocks) * (depth // 2 // TILE)
    return pl.pallas_call(
        functools.partial(attend_kernel, which, places, arrays, not states),
        out_shape=[shape] * halves,
        in_specs=[VMEM] * (1 + halves + len(blocks) + len(states)),
        out_specs=[VMEM] * halves,
        scratch_shapes=[
            pltpu.VMEM((halves, rows, columns), queries[0].dtype),
            pltpu.VMEM((len(blocks), depth, columns), blocks[0].dtype),
            pltpu.VMEM((halves,) + shape.shape, jnp.float32),
        ],
        compiler_params=params(),
        cost_estimate=pl.CostEstimate(
            flops=COST * pairs * 4 * TILE * TILE * HEAD_DIM,
            bytes_accessed=2 * len(blocks) * depth * columns + 4 * halves * rows * columns,
            transcendentals=pairs * TILE * TILE,
        ),
        name="attend",
    )(bounds, *queries, *blocks, *states)


def merged(states, columns):
    heads = columns // HEAD_DIM
    for h in range(heads):
        maxima = [ref[columns + h : columns + h + 1] for ref in states]
        totals = [ref[columns + heads + h : columns + heads + h + 1] for ref in states]
        largest = functools.reduce(jnp.maximum, maxima)
        factors = [jnp.exp2((m - largest) * SCALE2) for m in maxima]
        total = functools.reduce(jnp.add, [f * t for f, t in zip(factors, totals)])
        parts = [ref[head_columns(h)] * (f / total) for ref, f in zip(states, factors)]
        yield head_columns(h), functools.reduce(jnp.add, parts).T


def finish_kernel(*refs):
    out_ref = refs[-1]
    for own, done in merged(refs[:-1], out_ref.shape[1]):
        out_ref[:, own] = done.astype(out_ref.dtype)


def finish(states, rows, columns):
    return pl.pallas_call(
        finish_kernel,
        out_shape=jax.ShapeDtypeStruct((rows, columns), jnp.bfloat16),
        in_specs=[VMEM] * len(states),
        out_specs=VMEM,
        compiler_params=params(),
        name="finish",
    )(*states)


def part_kernel(*refs):
    keep_ref, send_ref, held = refs[-3:]
    rows, columns = keep_ref.shape
    mine = lax.axis_index("head")
    for own, done in merged(refs[:-3], columns):
        held[:, own] = done.astype(held.dtype)
    send_ref[...] = held[pl.ds(pl.multiple_of((1 - mine) * rows, 16), rows), :]
    keep_ref[...] = held[pl.ds(pl.multiple_of(mine * rows, 16), rows), :]


def join_kernel(keep_ref, got_ref, out_ref):
    columns = keep_ref.shape[1]
    mine = lax.axis_index("head")
    out_ref[:, pl.ds(pl.multiple_of(mine * columns, TILE), columns)] = keep_ref[...]
    out_ref[:, pl.ds(pl.multiple_of((1 - mine) * columns, TILE), columns)] = got_ref[...]


def finish_in_two(states, rows, columns):
    part = jax.ShapeDtypeStruct((rows // 2, columns), jnp.bfloat16)
    keep, send = pl.pallas_call(
        part_kernel,
        out_shape=[part, part],
        in_specs=[VMEM] * len(states),
        out_specs=[VMEM, VMEM],
        scratch_shapes=[pltpu.VMEM((rows, columns), jnp.bfloat16)],
        compiler_params=params(),
        name="part",
    )(*states)
    got = lax.ppermute(send, "head", [(0, 1), (1, 0)])
    return pl.pallas_call(
        join_kernel,
        out_shape=jax.ShapeDtypeStruct((rows // 2, 2 * columns), jnp.bfloat16),
        in_specs=[VMEM, VMEM],
        out_specs=VMEM,
        compiler_params=params(),
        name="join",
    )(keep, got)


def chip_pairs(mesh):
    places = [tuple(getattr(d, "coords", ())) for d in mesh.devices[:, 0]]
    count = len(places)
    if count % 4 or not places[0] or mesh.shape["head"] != 2:
        return False
    cores = all(places[i] == places[i + 1] for i in range(0, count, 2))
    level = all(places[i][2] == places[i + 3][2] for i in range(0, count, 4))
    climb = all(places[i][2] != places[i + 4][2] for i in range(0, count - 4))
    return cores and level and climb


def paired_shards(owner_count, queries, keys, values, image_tiles):
    rows, columns = queries.shape
    tiles = rows // TILE

    def flip(s):
        return 1 - 2 * ((s // 2) % 2)

    def core(s):
        return s % 2

    def turn(s):
        return flip(s) * (1 - 2 * core(s))

    def moved(array, source, takes=lambda s: True):
        pairs = [(source(s), s) for s in range(owner_count) if takes(s) and 0 <= source(s) < owner_count]
        return lax.ppermute(array, "seq", pairs)

    across = lambda s: s + 2 * flip(s)
    along = lambda s: s + 4 * turn(s)
    against = lambda s: s - 4 * turn(s)
    sibling = lambda s: s + 1 - 2 * core(s)

    nobody = -owner_count
    OWN = lambda s: s * tiles
    Y1 = lambda s: across(s) * tiles
    A1 = lambda s: along(s) * tiles
    B1 = lambda s: against(s) * tiles
    YA = lambda s: (s + 2 * flip(s) - 4 * turn(s)) * tiles
    AY = lambda s: (s + 2 * flip(s) + 4 * turn(s)) * tiles
    AY_OR_AA = lambda s: jnp.where(core(s) == 0, s + 8 * turn(s), s + 2 * flip(s) + 4 * turn(s)) * tiles
    THIRD = lambda s: (s - 6 * flip(s)) * tiles
    AY_LEFT = lambda s: jnp.where(core(s) == 0, s + 6 * flip(s), nobody) * tiles
    has_corner = lambda s: (core(s) == 1) | ((s // 2) % 2 == 1)
    CORNER = lambda s: jnp.where(has_corner(s), s + 8 * (1 - 2 * core(s)), nobody) * tiles

    block = pack(keys, values)
    y1, a1, b1 = moved(block, across), moved(block, along), moved(block, against)
    bounds, spans = meta(lambda s: [s, sibling(s)], image_tiles, rows)
    both = (queries, moved(queries, sibling))
    fold = functools.partial(attend, bounds, both)
    states = fold([block], [OWN], [])
    ay = moved(jnp.where((spans == 0) | (core(lax.axis_index("seq")) == 1), y1, a1), along)
    ya = moved(a1, across)
    states = fold([y1, a1, b1], [Y1, A1, B1], states)

    def last(blocks, places, states, shifts=None):
        (theirs,) = fold(blocks, places, states, which=[1], shifts=shifts)
        got = moved(theirs, sibling)
        (mine,) = fold(blocks, places, states, which=[0], shifts=shifts)
        return finish_in_two([mine, got], rows, columns)

    def near(y1, a1, b1, ya, ay, states):
        return last([ya, ay], [YA, AY], states)

    def third_of(ay):
        return moved(ay, lambda s: along(s) if core(s) else across(s))

    def odd(y1, a1, b1, ya, ay, states):
        third = third_of(ay)
        states = fold([ya, ay], [YA, AY_OR_AA], states)
        return last([third], [THIRD], states)

    def every_way(y1, a1, b1, ya, ay, states):
        third = third_of(ay)
        left = moved(y1, along, lambda s: core(s) == 0)
        corner = moved(corner_of(a1, b1), lambda s: s + 4 * (1 - 2 * core(s)), has_corner)
        states = fold([ya, ay], [YA, AY_OR_AA], states)
        shifts = [None, None, lambda s: 2 * TILE * core(s)]
        return last([third, left, corner], [THIRD, AY_LEFT, CORNER], states, shifts)

    return lax.switch(spans, [near, odd, every_way], y1, a1, b1, ya, ay, states)


def ring_shards(owner_count, queries, keys, values, image_tiles):
    rows, columns = queries.shape
    tiles = rows // TILE
    reach = min(owner_count - 1, -(-(MOST_TILES - 1) // tiles))
    block = pack(keys, values)
    bounds, _ = meta(lambda s: [s], image_tiles, rows)
    fold = functools.partial(attend, bounds, (queries,))
    up = [(i, i + 1) for i in range(owner_count - 1)]
    down = [(i + 1, i) for i in range(owner_count - 1)]
    below = above = block
    states = []
    held, places = [block], [lambda s: s * tiles]
    for k in range(1, reach + 1):
        below = lax.ppermute(below, "seq", up)
        above = lax.ppermute(above, "seq", down)
        states = fold(held, places, states)
        held, places = [below, above], [lambda s, k=k: (s - k) * tiles, lambda s, k=k: (s + k) * tiles]
    attended = finish(fold(held, places, states), rows, columns)
    return lax.all_to_all(attended, "head", split_axis=0, concat_axis=1, tiled=True)


def solution(mesh):
    owner_count = mesh.shape["seq"]
    plan = paired_shards if chip_pairs(mesh) else ring_shards
    placed = (P("seq", "head"), P("seq", "head"), P("seq", "head"), P())
    return jax.shard_map(
        functools.partial(plan, owner_count),
        mesh=mesh,
        in_specs=placed,
        out_specs=P(("seq", "head"), None),
        check_vma=False,
    )
```

```python
import functools
import math

import jax
import jax.numpy as jnp
from jax import lax
from jax.experimental import pallas as pl
from jax.experimental.pallas import tpu as pltpu
from jax.sharding import PartitionSpec as P

HEAD_DIM = 128
TILE = 128
MOST_TILES = 21

LOWEST = -1e30
SCALE2 = math.log2(math.e) / math.sqrt(HEAD_DIM)
COST = 6

VMEM = pl.BlockSpec(memory_space=pltpu.VMEM)
SMEM = pl.BlockSpec(memory_space=pltpu.SMEM)
HBM = pl.BlockSpec(memory_space=pl.ANY)


def params():
    return pltpu.CompilerParams(vmem_limit_bytes=16 * 1024 * 1024)


def head_columns(h):
    return slice(h * HEAD_DIM, (h + 1) * HEAD_DIM)


def tile_rows(t):
    return slice(t * TILE, (t + 1) * TILE)


def image_bounds(tiles_ref, tile):
    first = jnp.int32(0)
    start, end = jnp.int32(0), jnp.int32(0)
    for i in range(tiles_ref.shape[0]):
        after = first + tiles_ref[i]
        inside = (tile >= first) & (tile < after)
        start = jnp.where(inside, first, start)
        end = jnp.where(inside, after, end)
        first = after
    return start, end


def chip_spans(tiles_ref, chip_tiles):
    first = jnp.int32(0)
    even, odd, four = jnp.int32(0), jnp.int32(0), jnp.int32(0)
    for i in range(tiles_ref.shape[0]):
        after = first + tiles_ref[i]
        low, high = first // chip_tiles, (after - 1) // chip_tiles
        parity = low % 2
        even = jnp.where(high - (low + parity) >= 3, 1, even)
        odd = jnp.where(high - (low + 1 - parity) >= 3, 1, odd)
        four = jnp.where(high - low >= 4, 1, four)
        first = after
    return jnp.where(odd + four == 0, 0, jnp.where(even + four == 0, 1, 2)).astype(jnp.int32)


def meta_kernel(halves, tiles_ref, bounds_ref, spans_ref):
    tiles = bounds_ref.shape[1] // TILE
    me = lax.axis_index("seq")
    bounds_ref[...] = jnp.zeros(bounds_ref.shape, jnp.int32)
    for half, owner in enumerate(halves(me)):
        for t in range(tiles):
            start, end = image_bounds(tiles_ref, owner * tiles + t)
            bounds_ref[2 * half : 2 * half + 1, tile_rows(t)] = jnp.full((1, TILE), start, jnp.int32)
            bounds_ref[2 * half + 1 : 2 * half + 2, tile_rows(t)] = jnp.full((1, TILE), end, jnp.int32)
    spans_ref[0] = chip_spans(tiles_ref, 2 * tiles)


def meta(halves, image_tiles, rows):
    bounds, spans = pl.pallas_call(
        functools.partial(meta_kernel, halves),
        out_shape=[jax.ShapeDtypeStruct((8, rows), jnp.int32), jax.ShapeDtypeStruct((1,), jnp.int32)],
        in_specs=[SMEM],
        out_specs=[VMEM, SMEM],
        compiler_params=params(),
        cost_estimate=pl.CostEstimate(flops=COST * 2**29, bytes_accessed=0, transcendentals=0),
        name="meta",
    )(image_tiles)
    return bounds, spans[0]


def pack_kernel(k_ref, v_ref, out_ref, held, sems):
    rows, columns = k_ref.shape
    tiles = rows // TILE
    copies = []
    for t in range(tiles):
        copies.append(pltpu.make_async_copy(v_ref.at[tile_rows(t)], held.at[tile_rows(t)], sems.at[2 * t]))
        copies.append(pltpu.make_async_copy(k_ref.at[tile_rows(t)], out_ref.at[tile_rows(2 * t)], sems.at[2 * t + 1]))
    for copy in copies:
        copy.start()
    for t in range(tiles):
        copies[2 * t].wait()
        for h in range(columns // HEAD_DIM):
            out_ref[tile_rows(2 * t + 1), head_columns(h)] = held[tile_rows(t), head_columns(h)].T
    for copy in copies[1::2]:
        copy.wait()


def pack(keys, values):
    rows, columns = keys.shape
    return pl.pallas_call(
        pack_kernel,
        out_shape=jax.ShapeDtypeStruct((2 * rows, columns), keys.dtype),
        in_specs=[HBM, HBM],
        out_specs=VMEM,
        scratch_shapes=[pltpu.VMEM(values.shape, values.dtype), pltpu.SemaphoreType.DMA((2 * rows // TILE,))],
        name="pack",
    )(keys, values)


def corner_kernel(a1_ref, b1_ref, out_ref):
    me = lax.axis_index("seq")
    rows = pl.ds(pl.multiple_of((me % 2) * 2 * TILE, 2 * TILE), out_ref.shape[0])

    @pl.when((me // 2) % 2 == 0)
    def _():
        out_ref[...] = a1_ref[rows]

    @pl.when((me // 2) % 2 == 1)
    def _():
        out_ref[...] = b1_ref[rows]


def corner_of(a1, b1):
    return pl.pallas_call(
        corner_kernel,
        out_shape=jax.ShapeDtypeStruct((a1.shape[0] - 2 * TILE, a1.shape[1]), a1.dtype),
        in_specs=[VMEM, VMEM],
        out_specs=VMEM,
        compiler_params=params(),
        name="corner",
    )(a1, b1)


def attend_kernel(which, places, arrays, fresh, bounds_ref, *refs):
    halves = len(which)
    q_refs, refs = refs[:halves], refs[halves:]
    array_refs, refs = refs[: len(arrays)], refs[len(arrays) :]
    old_refs, refs = (None, refs) if fresh else (refs[:halves], refs[halves:])
    new_refs, (held_q, held, state) = refs[:halves], refs[halves:]
    rows, columns = q_refs[0].shape
    tiles = rows // TILE
    count = held.shape[1] // 2 // TILE
    heads = columns // HEAD_DIM
    me = lax.axis_index("seq")

    for half in range(halves):
        held_q[half] = q_refs[half][...]
        if fresh:
            state[half, :columns] = jnp.zeros((columns, rows), jnp.float32)
            state[half, columns : columns + heads] = jnp.full((heads, rows), LOWEST, jnp.float32)
            state[half, columns + heads :] = jnp.zeros((state.shape[1] - columns - heads, rows), jnp.float32)
        else:
            state[half] = old_refs[half][...]
    for slot, (array, shift) in enumerate(arrays):
        size = array_refs[array].shape[0]
        if size < held.shape[1]:
            held[slot] = jnp.zeros(held.shape[1:], held.dtype)
        at = 0 if shift is None else pl.multiple_of(shift(me), 2 * TILE)
        held[slot, pl.ds(at, size)] = array_refs[array][...]
    begins = [bounds_ref[2 * w, 0] for w in which]
    stops = [bounds_ref[2 * w + 1, rows - 1] for w in which]

    def chosen(at, options):
        return functools.reduce(lambda x, i: jnp.where(at == i, options[i], x), range(1, len(options)), options[0])

    def fold(half, slot, first):
        low = bounds_ref[pl.ds(2 * (half + which[0]), 1), :]
        high = bounds_ref[pl.ds(2 * (half + which[0]) + 1, 1), :]
        off = [
            jnp.where((first + j >= low) & (first + j < high), 0.0, -LOWEST).astype(jnp.float32)
            for j in range(count)
        ]
        for h in range(heads):
            own = head_columns(h)
            scores = lax.dot_general(
                jnp.concatenate([held[slot, tile_rows(2 * j), own] for j in range(count)], axis=0),
                held_q[half, :, own],
                (((1,), (1,)), ((), ())),
                preferred_element_type=jnp.float32,
            )
            max_at, total_at = pl.ds(columns + h, 1), pl.ds(columns + heads + h, 1)
            factors, rounded, totals, maxima = [], [], [], []
            for t in range(tiles):
                lanes = tile_rows(t)
                parts = [scores[tile_rows(j), lanes] for j in range(count)]
                old_max = state[half, max_at, lanes]
                new_max = old_max
                for j in range(count):
                    new_max = jnp.maximum(new_max, jnp.max(parts[j], axis=0, keepdims=True) - off[j][:, lanes])
                scaled = new_max * SCALE2
                weights = [jnp.exp2(parts[j] * SCALE2 - (scaled + off[j][:, lanes])) for j in range(count)]
                factors.append(jnp.exp2((old_max - new_max) * SCALE2))
                totals.append(jnp.sum(functools.reduce(jnp.add, weights), axis=0, keepdims=True))
                maxima.append(new_max)
                rounded.append(jnp.concatenate([w.astype(jnp.bfloat16) for w in weights], axis=0))
            factor = jnp.concatenate(factors, axis=1)
            update = jnp.dot(
                jnp.concatenate([held[slot, tile_rows(2 * j + 1), own] for j in range(count)], axis=1),
                jnp.concatenate(rounded, axis=1),
                preferred_element_type=jnp.float32,
            )
            state[half, own] = state[half, own] * factor + update
            state[half, max_at] = jnp.concatenate(maxima, axis=1)
            state[half, total_at] = state[half, total_at] * factor + jnp.concatenate(totals, axis=1)

    @pl.loop(0, halves * len(places))
    def _(unit):
        half, slot = unit // len(places), unit % len(places)
        first = chosen(slot, [place(me) for place in places])

        @pl.when((first < chosen(half, stops)) & (first + count > chosen(half, begins)))
        def _():
            fold(half, slot, first)

    for half in range(halves):
        new_refs[half][...] = state[half]


def attend(bounds, queries, blocks, places, states, which=None, shifts=None):
    which = list(range(len(queries))) if which is None else which
    queries, states = [queries[w] for w in which], [states[w] for w in which] if states else []
    halves = len(which)
    rows, columns = queries[0].shape
    depth = blocks[0].shape[0]
    heads = columns // HEAD_DIM
    shape = jax.ShapeDtypeStruct((columns + -(-2 * heads // 8) * 8, rows), jnp.float32)
    arrays = list(enumerate(shifts or [None] * len(blocks)))
    pairs = halves * (rows // TILE) * heads * len(blocks) * (depth // 2 // TILE)
    return pl.pallas_call(
        functools.partial(attend_kernel, which, places, arrays, not states),
        out_shape=[shape] * halves,
        in_specs=[VMEM] * (1 + halves + len(blocks) + len(states)),
        out_specs=[VMEM] * halves,
        scratch_shapes=[
            pltpu.VMEM((halves, rows, columns), queries[0].dtype),
            pltpu.VMEM((len(blocks), depth, columns), blocks[0].dtype),
            pltpu.VMEM((halves,) + shape.shape, jnp.float32),
        ],
        compiler_params=params(),
        cost_estimate=pl.CostEstimate(
            flops=COST * pairs * 4 * TILE * TILE * HEAD_DIM,
            bytes_accessed=2 * len(blocks) * depth * columns + 4 * halves * rows * columns,
            transcendentals=pairs * TILE * TILE,
        ),
        name="attend",
    )(bounds, *queries, *blocks, *states)


def merged(states, columns):
    heads = columns // HEAD_DIM
    for h in range(heads):
        maxima = [ref[columns + h : columns + h + 1] for ref in states]
        totals = [ref[columns + heads + h : columns + heads + h + 1] for ref in states]
        largest = functools.reduce(jnp.maximum, maxima)
        factors = [jnp.exp2((m - largest) * SCALE2) for m in maxima]
        total = functools.reduce(jnp.add, [f * t for f, t in zip(factors, totals)])
        parts = [ref[head_columns(h)] * (f / total) for ref, f in zip(states, factors)]
        yield head_columns(h), functools.reduce(jnp.add, parts).T


def finish_kernel(*refs):
    out_ref = refs[-1]
    for own, done in merged(refs[:-1], out_ref.shape[1]):
        out_ref[:, own] = done.astype(out_ref.dtype)


def finish(states, rows, columns):
    return pl.pallas_call(
        finish_kernel,
        out_shape=jax.ShapeDtypeStruct((rows, columns), jnp.bfloat16),
        in_specs=[VMEM] * len(states),
        out_specs=VMEM,
        compiler_params=params(),
        name="finish",
    )(*states)


def part_kernel(*refs):
    keep_ref, send_ref, held = refs[-3:]
    rows, columns = keep_ref.shape
    mine = lax.axis_index("head")
    for own, done in merged(refs[:-3], columns):
        held[:, own] = done.astype(held.dtype)
    send_ref[...] = held[pl.ds(pl.multiple_of((1 - mine) * rows, 16), rows), :]
    keep_ref[...] = held[pl.ds(pl.multiple_of(mine * rows, 16), rows), :]


def join_kernel(keep_ref, got_ref, out_ref):
    columns = keep_ref.shape[1]
    mine = lax.axis_index("head")
    out_ref[:, pl.ds(pl.multiple_of(mine * columns, TILE), columns)] = keep_ref[...]
    out_ref[:, pl.ds(pl.multiple_of((1 - mine) * columns, TILE), columns)] = got_ref[...]


def finish_in_two(states, rows, columns):
    part = jax.ShapeDtypeStruct((rows // 2, columns), jnp.bfloat16)
    keep, send = pl.pallas_call(
        part_kernel,
        out_shape=[part, part],
        in_specs=[VMEM] * len(states),
        out_specs=[VMEM, VMEM],
        scratch_shapes=[pltpu.VMEM((rows, columns), jnp.bfloat16)],
        compiler_params=params(),
        name="part",
    )(*states)
    got = lax.ppermute(send, "head", [(0, 1), (1, 0)])
    return pl.pallas_call(
        join_kernel,
        out_shape=jax.ShapeDtypeStruct((rows // 2, 2 * columns), jnp.bfloat16),
        in_specs=[VMEM, VMEM],
        out_specs=VMEM,
        compiler_params=params(),
        name="join",
    )(keep, got)


def chip_pairs(mesh):
    places = [tuple(getattr(d, "coords", ())) for d in mesh.devices[:, 0]]
    count = len(places)
    if count % 4 or not places[0] or mesh.shape["head"] != 2:
        return False
    cores = all(places[i] == places[i + 1] for i in range(0, count, 2))
    level = all(places[i][2] == places[i + 3][2] for i in range(0, count, 4))
    climb = all(places[i][2] != places[i + 4][2] for i in range(0, count - 4))
    return cores and level and climb


def paired_shards(owner_count, queries, keys, values, image_tiles):
    rows, columns = queries.shape
    tiles = rows // TILE

    def flip(s):
        return 1 - 2 * ((s // 2) % 2)

    def core(s):
        return s % 2

    def turn(s):
        return flip(s) * (1 - 2 * core(s))

    def moved(array, source, takes=lambda s: True):
        pairs = [(source(s), s) for s in range(owner_count) if takes(s) and 0 <= source(s) < owner_count]
        return lax.ppermute(array, "seq", pairs)

    across = lambda s: s + 2 * flip(s)
    along = lambda s: s + 4 * turn(s)
    against = lambda s: s - 4 * turn(s)
    sibling = lambda s: s + 1 - 2 * core(s)

    nobody = -owner_count
    OWN = lambda s: s * tiles
    Y1 = lambda s: across(s) * tiles
    A1 = lambda s: along(s) * tiles
    B1 = lambda s: against(s) * tiles
    YA = lambda s: (s + 2 * flip(s) - 4 * turn(s)) * tiles
    AY = lambda s: (s + 2 * flip(s) + 4 * turn(s)) * tiles
    AY_OR_AA = lambda s: jnp.where(core(s) == 0, s + 8 * turn(s), s + 2 * flip(s) + 4 * turn(s)) * tiles
    THIRD = lambda s: (s - 6 * flip(s)) * tiles
    AY_LEFT = lambda s: jnp.where(core(s) == 0, s + 6 * flip(s), nobody) * tiles
    has_corner = lambda s: (core(s) == 1) | ((s // 2) % 2 == 1)
    CORNER = lambda s: jnp.where(has_corner(s), s + 8 * (1 - 2 * core(s)), nobody) * tiles

    def over_y(array):
        both = lax.all_gather(array, "seq", axis_index_groups=pairs)
        return lax.dynamic_index_in_dim(both, 1 - (lax.axis_index("seq") // 2) % 2, 0, keepdims=False)

    pairs = [[s, s + 2] for s in range(owner_count) if (s // 2) % 2 == 0]
    block = pack(keys, values)
    y1, a1, b1 = over_y(block), moved(block, along), moved(block, against)
    bounds, spans = meta(lambda s: [s, sibling(s)], image_tiles, rows)
    both = (queries, moved(queries, sibling))
    fold = functools.partial(attend, bounds, both)
    states = fold([block], [OWN], [])
    ya = over_y(a1)
    ay = moved(jnp.where((spans == 0) | (core(lax.axis_index("seq")) == 1), y1, a1), along)
    states = fold([y1, a1, b1], [Y1, A1, B1], states)

    def last(blocks, places, states, shifts=None):
        (theirs,) = fold(blocks, places, states, which=[1], shifts=shifts)
        got = moved(theirs, sibling)
        (mine,) = fold(blocks, places, states, which=[0], shifts=shifts)
        return finish_in_two([mine, got], rows, columns)

    def near(y1, a1, b1, ya, ay, states):
        return last([ya, ay], [YA, AY], states)

    def third_of(ay):
        return moved(ay, lambda s: along(s) if core(s) else across(s))

    def odd(y1, a1, b1, ya, ay, states):
        third = third_of(ay)
        states = fold([ya, ay], [YA, AY_OR_AA], states)
        return last([third], [THIRD], states)

    def every_way(y1, a1, b1, ya, ay, states):
        third = third_of(ay)
        left = moved(y1, along, lambda s: core(s) == 0)
        corner = moved(corner_of(a1, b1), lambda s: s + 4 * (1 - 2 * core(s)), has_corner)
        states = fold([ya, ay], [YA, AY_OR_AA], states)
        shifts = [None, None, lambda s: 2 * TILE * core(s)]
        return last([third, left, corner], [THIRD, AY_LEFT, CORNER], states, shifts)

    return lax.switch(spans, [near, odd, every_way], y1, a1, b1, ya, ay, states)


def ring_shards(owner_count, queries, keys, values, image_tiles):
    rows, columns = queries.shape
    tiles = rows // TILE
    reach = min(owner_count - 1, -(-(MOST_TILES - 1) // tiles))
    block = pack(keys, values)
    bounds, _ = meta(lambda s: [s], image_tiles, rows)
    fold = functools.partial(attend, bounds, (queries,))
    up = [(i, i + 1) for i in range(owner_count - 1)]
    down = [(i + 1, i) for i in range(owner_count - 1)]
    below = above = block
    states = []
    held, places = [block], [lambda s: s * tiles]
    for k in range(1, reach + 1):
        below = lax.ppermute(below, "seq", up)
        above = lax.ppermute(above, "seq", down)
        states = fold(held, places, states)
        held, places = [below, above], [lambda s, k=k: (s - k) * tiles, lambda s, k=k: (s + k) * tiles]
    attended = finish(fold(held, places, states), rows, columns)
    return lax.all_to_all(attended, "head", split_axis=0, concat_axis=1, tiled=True)


def solution(mesh):
    owner_count = mesh.shape["seq"]
    plan = paired_shards if chip_pairs(mesh) else ring_shards
    placed = (P("seq", "head"), P("seq", "head"), P("seq", "head"), P())
    return jax.shard_map(
        functools.partial(plan, owner_count),
        mesh=mesh,
        in_specs=placed,
        out_specs=P(("seq", "head"), None),
        check_vma=False,
    )
```

```python
import functools
import math

import jax
import jax.numpy as jnp
from jax import lax
from jax.experimental import pallas as pl
from jax.experimental.pallas import tpu as pltpu
from jax.sharding import PartitionSpec as P

HEAD_DIM = 128
TILE = 128
MOST_TILES = 21

LOWEST = -1e30
SCALE2 = math.log2(math.e) / math.sqrt(HEAD_DIM)
COST = 2

VMEM = pl.BlockSpec(memory_space=pltpu.VMEM)
SMEM = pl.BlockSpec(memory_space=pltpu.SMEM)
HBM = pl.BlockSpec(memory_space=pl.ANY)


def params():
    return pltpu.CompilerParams(vmem_limit_bytes=24 * 1024 * 1024)


def head_columns(h):
    return slice(h * HEAD_DIM, (h + 1) * HEAD_DIM)


def tile_rows(t):
    return slice(t * TILE, (t + 1) * TILE)


def image_bounds(tiles_ref, tile):
    first = jnp.int32(0)
    start, end = jnp.int32(0), jnp.int32(0)
    for i in range(tiles_ref.shape[0]):
        after = first + tiles_ref[i]
        inside = (tile >= first) & (tile < after)
        start = jnp.where(inside, first, start)
        end = jnp.where(inside, after, end)
        first = after
    return start, end


def meta_kernel(halves, tiles_ref, bounds_ref):
    tiles = bounds_ref.shape[1] // TILE
    me = lax.axis_index("seq")
    bounds_ref[...] = jnp.zeros(bounds_ref.shape, jnp.int32)
    for half, owner in enumerate(halves(me)):
        for t in range(tiles):
            start, end = image_bounds(tiles_ref, owner * tiles + t)
            bounds_ref[2 * half : 2 * half + 1, tile_rows(t)] = jnp.full((1, TILE), start, jnp.int32)
            bounds_ref[2 * half + 1 : 2 * half + 2, tile_rows(t)] = jnp.full((1, TILE), end, jnp.int32)


def meta(halves, image_tiles, rows):
    return pl.pallas_call(
        functools.partial(meta_kernel, halves),
        out_shape=jax.ShapeDtypeStruct((8, rows), jnp.int32),
        in_specs=[SMEM],
        out_specs=VMEM,
        compiler_params=params(),
        cost_estimate=pl.CostEstimate(flops=COST * 2**28, bytes_accessed=0, transcendentals=0),
        name="meta",
    )(image_tiles)


def pack_kernel(k_ref, v_ref, out_ref, held, sems):
    rows, columns = k_ref.shape
    tiles = rows // TILE
    copies = []
    for t in range(tiles):
        copies.append(pltpu.make_async_copy(v_ref.at[tile_rows(t)], held.at[tile_rows(t)], sems.at[2 * t]))
        copies.append(pltpu.make_async_copy(k_ref.at[tile_rows(t)], out_ref.at[tile_rows(2 * t)], sems.at[2 * t + 1]))
    for copy in copies:
        copy.start()
    for t in range(tiles):
        copies[2 * t].wait()
        for h in range(columns // HEAD_DIM):
            out_ref[tile_rows(2 * t + 1), head_columns(h)] = held[tile_rows(t), head_columns(h)].T
    for copy in copies[1::2]:
        copy.wait()


def pack(keys, values):
    rows, columns = keys.shape
    return pl.pallas_call(
        pack_kernel,
        out_shape=jax.ShapeDtypeStruct((2 * rows, columns), keys.dtype),
        in_specs=[HBM, HBM],
        out_specs=VMEM,
        scratch_shapes=[pltpu.VMEM(values.shape, values.dtype), pltpu.SemaphoreType.DMA((2 * rows // TILE,))],
        name="pack",
    )(keys, values)


def corner_kernel(block_ref, after_ref, out_ref):
    skip = pl.multiple_of((lax.axis_index("seq") % 2) * 2 * TILE, 2 * TILE)
    out_ref[...] = block_ref[pl.ds(skip, out_ref.shape[0])]


def corner_of(block, after):
    return pl.pallas_call(
        corner_kernel,
        out_shape=jax.ShapeDtypeStruct((block.shape[0] - 2 * TILE, block.shape[1]), block.dtype),
        in_specs=[VMEM, HBM],
        out_specs=VMEM,
        compiler_params=params(),
        name="corner",
    )(block, after)


def attend_kernel(which, places, arrays, fresh, bounds_ref, *refs):
    halves = len(which)
    q_refs, refs = refs[:halves], refs[halves:]
    array_refs, refs = refs[: len(arrays)], refs[len(arrays) :]
    old_refs, refs = (None, refs) if fresh else (refs[:halves], refs[halves:])
    new_refs, (held_q, held, state) = refs[:halves], refs[halves:]
    rows, columns = q_refs[0].shape
    tiles = rows // TILE
    count = held.shape[1] // 2 // TILE
    heads = columns // HEAD_DIM
    me = lax.axis_index("seq")

    for half in range(halves):
        held_q[half] = q_refs[half][...]
        if fresh:
            state[half, :columns] = jnp.zeros((columns, rows), jnp.float32)
            state[half, columns : columns + heads] = jnp.full((heads, rows), LOWEST, jnp.float32)
            state[half, columns + heads :] = jnp.zeros((state.shape[1] - columns - heads, rows), jnp.float32)
        else:
            state[half] = old_refs[half][...]
    for slot, (array, shift) in enumerate(arrays):
        size = array_refs[array].shape[0]
        if size < held.shape[1]:
            held[slot] = jnp.zeros(held.shape[1:], held.dtype)
        at = 0 if shift is None else pl.multiple_of(shift(me), 2 * TILE)
        held[slot, pl.ds(at, size)] = array_refs[array][...]
    begins = [bounds_ref[2 * w, 0] for w in which]
    stops = [bounds_ref[2 * w + 1, rows - 1] for w in which]

    def chosen(at, options):
        return functools.reduce(lambda x, i: jnp.where(at == i, options[i], x), range(1, len(options)), options[0])

    def fold(half, slot, first):
        row = 2 * (which[0] + half * (which[-1] - which[0]) // max(len(which) - 1, 1))
        low = bounds_ref[pl.ds(row, 1), :]
        high = bounds_ref[pl.ds(row + 1, 1), :]
        off = [
            jnp.where((first + j >= low) & (first + j < high), 0.0, -LOWEST).astype(jnp.float32)
            for j in range(count)
        ]
        for h in range(heads):
            own = head_columns(h)
            scores = lax.dot_general(
                jnp.concatenate([held[slot, tile_rows(2 * j), own] for j in range(count)], axis=0),
                held_q[half, :, own],
                (((1,), (1,)), ((), ())),
                preferred_element_type=jnp.float32,
            )
            max_at, total_at = pl.ds(columns + h, 1), pl.ds(columns + heads + h, 1)
            factors, rounded, totals, maxima = [], [], [], []
            for t in range(tiles):
                lanes = tile_rows(t)
                parts = [scores[tile_rows(j), lanes] for j in range(count)]
                old_max = state[half, max_at, lanes]
                new_max = old_max
                for j in range(count):
                    new_max = jnp.maximum(new_max, jnp.max(parts[j], axis=0, keepdims=True) - off[j][:, lanes])
                scaled = new_max * SCALE2
                weights = [jnp.exp2(parts[j] * SCALE2 - (scaled + off[j][:, lanes])) for j in range(count)]
                factors.append(jnp.exp2((old_max - new_max) * SCALE2))
                totals.append(jnp.sum(functools.reduce(jnp.add, weights), axis=0, keepdims=True))
                maxima.append(new_max)
                rounded.append(jnp.concatenate([w.astype(jnp.bfloat16) for w in weights], axis=0))
            factor = jnp.concatenate(factors, axis=1)
            update = jnp.dot(
                jnp.concatenate([held[slot, tile_rows(2 * j + 1), own] for j in range(count)], axis=1),
                jnp.concatenate(rounded, axis=1),
                preferred_element_type=jnp.float32,
            )
            state[half, own] = state[half, own] * factor + update
            state[half, max_at] = jnp.concatenate(maxima, axis=1)
            state[half, total_at] = state[half, total_at] * factor + jnp.concatenate(totals, axis=1)

    @pl.loop(0, halves * len(places))
    def _(unit):
        half, slot = unit // len(places), unit % len(places)
        first = chosen(slot, [place(me) for place in places])

        @pl.when((first < chosen(half, stops)) & (first + count > chosen(half, begins)))
        def _():
            fold(half, slot, first)

    for half in range(halves):
        new_refs[half][...] = state[half]


def attend(bounds, queries, blocks, places, states, which=None, shifts=None):
    which = list(range(len(queries))) if which is None else which
    queries, states = [queries[w] for w in which], [states[w] for w in which] if states else []
    halves = len(which)
    rows, columns = queries[0].shape
    depth = blocks[0].shape[0]
    heads = columns // HEAD_DIM
    shape = jax.ShapeDtypeStruct((columns + -(-2 * heads // 8) * 8, rows), jnp.float32)
    arrays = list(enumerate(shifts or [None] * len(blocks)))
    pairs = halves * (rows // TILE) * heads * len(blocks) * (depth // 2 // TILE)
    return pl.pallas_call(
        functools.partial(attend_kernel, which, places, arrays, not states),
        out_shape=[shape] * halves,
        in_specs=[VMEM] * (1 + halves + len(blocks) + len(states)),
        out_specs=[VMEM] * halves,
        scratch_shapes=[
            pltpu.VMEM((halves, rows, columns), queries[0].dtype),
            pltpu.VMEM((len(blocks), depth, columns), blocks[0].dtype),
            pltpu.VMEM((halves,) + shape.shape, jnp.float32),
        ],
        compiler_params=params(),
        cost_estimate=pl.CostEstimate(
            flops=COST * pairs * 4 * TILE * TILE * HEAD_DIM,
            bytes_accessed=2 * len(blocks) * depth * columns + 4 * halves * rows * columns,
            transcendentals=pairs * TILE * TILE,
        ),
        name="attend",
    )(bounds, *queries, *blocks, *states)


def merged(states, columns):
    heads = columns // HEAD_DIM
    for h in range(heads):
        maxima = [ref[columns + h : columns + h + 1] for ref in states]
        totals = [ref[columns + heads + h : columns + heads + h + 1] for ref in states]
        largest = functools.reduce(jnp.maximum, maxima)
        factors = [jnp.exp2((m - largest) * SCALE2) for m in maxima]
        total = functools.reduce(jnp.add, [f * t for f, t in zip(factors, totals)])
        parts = [ref[head_columns(h)] * (f / total) for ref, f in zip(states, factors)]
        yield head_columns(h), functools.reduce(jnp.add, parts).T


def finish_kernel(*refs):
    out_ref = refs[-1]
    for own, done in merged(refs[:-1], out_ref.shape[1]):
        out_ref[:, own] = done.astype(out_ref.dtype)


def finish(states, rows, columns):
    return pl.pallas_call(
        finish_kernel,
        out_shape=jax.ShapeDtypeStruct((rows, columns), jnp.bfloat16),
        in_specs=[VMEM] * len(states),
        out_specs=VMEM,
        compiler_params=params(),
        name="finish",
    )(*states)


def message_kernel(*refs):
    states, outs, held = refs[:4], refs[4:8], refs[8]
    rows = outs[0].shape[0] - 2 * 8
    columns = outs[0].shape[1]
    heads = columns // HEAD_DIM
    mine = lax.axis_index("head")
    for part in range(2):
        pair, (keep_ref, send_ref) = states[2 * part : 2 * part + 2], outs[2 * part : 2 * part + 2]
        logs = []
        for h in range(heads):
            maxima = [ref[columns + h : columns + h + 1] for ref in pair]
            totals = [ref[columns + heads + h : columns + heads + h + 1] for ref in pair]
            largest = jnp.maximum(*maxima)
            factors = [jnp.exp2((m - largest) * SCALE2) for m in maxima]
            total = factors[0] * totals[0] + factors[1] * totals[1]
            some = jnp.where(total > 0, total, 1.0)
            scale = [f / some for f in factors]
            own = head_columns(h)
            held[:, own] = (pair[0][own] * scale[0] + pair[1][own] * scale[1]).T.astype(held.dtype)
            left = jnp.where(total > 0, largest * SCALE2 + jnp.log2(some), LOWEST)
            for _ in range(3):
                summand = left.astype(held.dtype).astype(jnp.float32)
                logs.append(summand)
                left = left - summand
        logs = jnp.concatenate(logs + [jnp.zeros((2 * 8 - len(logs), held.shape[0]), jnp.float32)], axis=0)
        later = pltpu.roll(logs, rows, 1)
        for ref, which in ((send_ref, 1 - mine), (keep_ref, mine)):
            ref[:rows] = held[pl.ds(pl.multiple_of(which * rows, 2 * 8), rows), :]
            ref[rows:] = jnp.where(which == 0, logs, later).astype(ref.dtype)


def messages(mine, peers):
    rows, columns = mine[0].shape[1], mine[0].shape[0] // HEAD_DIM * HEAD_DIM
    shape = jax.ShapeDtypeStruct((rows // 2 + 2 * 8, columns), jnp.bfloat16)
    return pl.pallas_call(
        message_kernel,
        out_shape=[shape] * 4,
        in_specs=[VMEM] * 4,
        out_specs=[VMEM] * 4,
        scratch_shapes=[pltpu.VMEM((rows, columns), jnp.bfloat16)],
        compiler_params=params(),
        name="message",
    )(*mine, *peers)


def settle_kernel(*refs):
    parts, out_ref, logs = refs[:4], refs[4], refs[5]
    rows, columns = out_ref.shape[0], parts[0].shape[1]
    heads = columns // HEAD_DIM
    mine = lax.axis_index("head")
    logs[...] = jnp.zeros(logs.shape, jnp.float32)
    for i, ref in enumerate(parts):
        summands = ref[rows:].astype(jnp.float32)
        for h in range(heads):
            at = i * heads + h
            logs[at : at + 1] = functools.reduce(jnp.add, [summands[3 * h + n : 3 * h + n + 1] for n in range(3)])
    turned = logs[...].T[:rows]
    for side, base in ((0, mine), (1, 1 - mine)):
        for h in range(heads):
            both = [turned[:, at : at + 1] for at in (2 * side * heads + h, (2 * side + 1) * heads + h)]
            largest = jnp.maximum(*both)
            weights = [jnp.exp2(x - largest) for x in both]
            sums = [ref[:rows, head_columns(h)].astype(jnp.float32) for ref in parts[2 * side : 2 * side + 2]]
            total = weights[0] + weights[1]
            done = sums[0] * (weights[0] / total) + sums[1] * (weights[1] / total)
            at = pl.multiple_of(base * columns + h * HEAD_DIM, HEAD_DIM)
            out_ref[:, pl.ds(at, HEAD_DIM)] = done.astype(out_ref.dtype)


def settle(own, across, beside, diagonal):
    rows, columns = own.shape[0] - 2 * 8, own.shape[1]
    return pl.pallas_call(
        settle_kernel,
        out_shape=jax.ShapeDtypeStruct((rows, 2 * columns), own.dtype),
        in_specs=[VMEM] * 4,
        out_specs=VMEM,
        scratch_shapes=[pltpu.VMEM((TILE, columns), jnp.float32)],
        compiler_params=params(),
        name="settle",
    )(own, across, beside, diagonal)


def chip_pairs(mesh):
    places = [tuple(getattr(d, "coords", ())) for d in mesh.devices[:, 0]]
    count = len(places)
    if count % 4 or not places[0] or mesh.shape["head"] != 2:
        return False
    cores = all(places[i] == places[i + 1] for i in range(0, count, 2))
    level = all(places[i][2] == places[i + 3][2] for i in range(0, count, 4))
    climb = all(places[i][2] != places[i + 4][2] for i in range(0, count - 4))
    return cores and level and climb


def paired_shards(owner_count, queries, keys, values, image_tiles):
    rows, columns = queries.shape
    tiles = rows // TILE
    owners = range(owner_count)

    def flip(s):
        return 1 - 2 * ((s // 2) % 2)

    def core(s):
        return s % 2

    def moved(array, source, takes=lambda s: True):
        pairs = [(source(s), s) for s in owners if takes(s) and 0 <= source(s) < owner_count]
        return lax.ppermute(array, "seq", pairs)

    across = lambda s: s + 2 * flip(s)
    along = lambda s: s + 4 * flip(s)
    against = lambda s: s - 4 * flip(s)
    sibling = lambda s: s + 1 - 2 * core(s)
    inner = lambda s: core(s) == (1 - (s // 2) % 2)

    OWN = lambda s: s * tiles
    A1 = lambda s: along(s) * tiles
    B1 = lambda s: against(s) * tiles
    A2 = lambda s: (s + 8 * flip(s)) * tiles
    B2 = lambda s: jnp.where(inner(s), s - 8 * flip(s), -owner_count) * tiles

    block = pack(keys, values)
    a1, b1 = moved(block, along), moved(block, against)
    peers = moved(queries, across)
    level = (queries, moved(queries, sibling), peers, moved(peers, sibling))
    bounds = meta(lambda s: [s, sibling(s), across(s), sibling(across(s))], image_tiles, rows)
    fold = functools.partial(attend, bounds, level)
    states = fold([block], [OWN], [], which=[0, 1])
    a2 = moved(a1, along)
    states = states + fold([block], [OWN], [], which=[2, 3])
    states = fold([a1], [A1], states)
    b2 = moved(corner_of(b1, states[0]), against, inner)
    states = fold([b1], [B1], states)

    shifts = [None, lambda s: 2 * TILE * core(s)]
    beside, diagonal = fold([a2, b2], [A2, B2], states, which=[1, 3], shifts=shifts)
    beside, diagonal = moved(beside, sibling), moved(diagonal, sibling)
    mine, peer = fold([a2, b2], [A2, B2], states, which=[0, 2], shifts=shifts)
    keep, over_x, over_y, over_both = messages([mine, beside], [peer, diagonal])
    over_y = moved(over_y, across)
    over_x = lax.ppermute(over_x, "head", [(0, 1), (1, 0)])
    pairs = [(2 * across(s) + 1 - x, 2 * s + x) for s in owners for x in range(2)]
    over_both = lax.ppermute(over_both, ("seq", "head"), pairs)
    return settle(keep, over_y, over_x, over_both)


def ring_shards(owner_count, queries, keys, values, image_tiles):
    rows, columns = queries.shape
    tiles = rows // TILE
    reach = min(owner_count - 1, -(-(MOST_TILES - 1) // tiles))
    block = pack(keys, values)
    bounds = meta(lambda s: [s], image_tiles, rows)
    fold = functools.partial(attend, bounds, (queries,))
    up = [(i, i + 1) for i in range(owner_count - 1)]
    down = [(i + 1, i) for i in range(owner_count - 1)]
    below = above = block
    states = []
    held, places = [block], [lambda s: s * tiles]
    for k in range(1, reach + 1):
        below = lax.ppermute(below, "seq", up)
        above = lax.ppermute(above, "seq", down)
        states = fold(held, places, states)
        held, places = [below, above], [lambda s, k=k: (s - k) * tiles, lambda s, k=k: (s + k) * tiles]
    attended = finish(fold(held, places, states), rows, columns)
    return lax.all_to_all(attended, "head", split_axis=0, concat_axis=1, tiled=True)


def solution(mesh):
    owner_count = mesh.shape["seq"]
    plan = paired_shards if chip_pairs(mesh) else ring_shards
    placed = (P("seq", "head"), P("seq", "head"), P("seq", "head"), P())
    return jax.shard_map(
        functools.partial(plan, owner_count),
        mesh=mesh,
        in_specs=placed,
        out_specs=P(("seq", "head"), None),
        check_vma=False,
    )
```

```python
import functools
import math

import jax
import jax.numpy as jnp
from jax import lax
from jax.experimental import pallas as pl
from jax.experimental.pallas import tpu as pltpu
from jax.sharding import PartitionSpec as P

HEAD_DIM = 128
TILE = 128
MOST_TILES = 21

LOWEST = -1e30
SCALE2 = math.log2(math.e) / math.sqrt(HEAD_DIM)
COST = 2

VMEM = pl.BlockSpec(memory_space=pltpu.VMEM)
SMEM = pl.BlockSpec(memory_space=pltpu.SMEM)
HBM = pl.BlockSpec(memory_space=pl.ANY)


def params():
    return pltpu.CompilerParams(vmem_limit_bytes=24 * 1024 * 1024)


def head_columns(h):
    return slice(h * HEAD_DIM, (h + 1) * HEAD_DIM)


def tile_rows(t):
    return slice(t * TILE, (t + 1) * TILE)


def image_bounds(tiles_ref, tile):
    first = jnp.int32(0)
    start, end = jnp.int32(0), jnp.int32(0)
    for i in range(tiles_ref.shape[0]):
        after = first + tiles_ref[i]
        inside = (tile >= first) & (tile < after)
        start = jnp.where(inside, first, start)
        end = jnp.where(inside, after, end)
        first = after
    return start, end


def meta_kernel(halves, tiles_ref, bounds_ref, far_ref):
    tiles = bounds_ref.shape[1] // TILE
    me = lax.axis_index("seq")
    bounds_ref[...] = jnp.zeros(bounds_ref.shape, jnp.int32)
    for half, owner in enumerate(halves(me)):
        for t in range(tiles):
            start, end = image_bounds(tiles_ref, owner * tiles + t)
            bounds_ref[2 * half : 2 * half + 1, tile_rows(t)] = jnp.full((1, TILE), start, jnp.int32)
            bounds_ref[2 * half + 1 : 2 * half + 2, tile_rows(t)] = jnp.full((1, TILE), end, jnp.int32)
    first = jnp.int32(0)
    far = jnp.int32(0)
    for i in range(tiles_ref.shape[0]):
        after = first + tiles_ref[i]
        levels = (after - 1) // (4 * tiles) - first // (4 * tiles)
        far = jnp.where(levels >= 2, 1, far)
        first = after
    far_ref[0] = far


def meta(halves, image_tiles, rows):
    bounds, far = pl.pallas_call(
        functools.partial(meta_kernel, halves),
        out_shape=[jax.ShapeDtypeStruct((8, rows), jnp.int32), jax.ShapeDtypeStruct((1,), jnp.int32)],
        in_specs=[SMEM],
        out_specs=[VMEM, SMEM],
        compiler_params=params(),
        cost_estimate=pl.CostEstimate(flops=COST * 2**28, bytes_accessed=0, transcendentals=0),
        name="meta",
    )(image_tiles)
    return bounds, far[0]


def pack_kernel(k_ref, v_ref, out_ref, held, sems):
    rows, columns = k_ref.shape
    tiles = rows // TILE
    copies = []
    for t in range(tiles):
        copies.append(pltpu.make_async_copy(v_ref.at[tile_rows(t)], held.at[tile_rows(t)], sems.at[2 * t]))
        copies.append(pltpu.make_async_copy(k_ref.at[tile_rows(t)], out_ref.at[tile_rows(2 * t)], sems.at[2 * t + 1]))
    for copy in copies:
        copy.start()
    for t in range(tiles):
        copies[2 * t].wait()
        for h in range(columns // HEAD_DIM):
            out_ref[tile_rows(2 * t + 1), head_columns(h)] = held[tile_rows(t), head_columns(h)].T
    for copy in copies[1::2]:
        copy.wait()


def pack(keys, values):
    rows, columns = keys.shape
    return pl.pallas_call(
        pack_kernel,
        out_shape=jax.ShapeDtypeStruct((2 * rows, columns), keys.dtype),
        in_specs=[HBM, HBM],
        out_specs=VMEM,
        scratch_shapes=[pltpu.VMEM(values.shape, values.dtype), pltpu.SemaphoreType.DMA((2 * rows // TILE,))],
        name="pack",
    )(keys, values)


def corner_kernel(block_ref, out_ref):
    skip = pl.multiple_of((lax.axis_index("seq") % 2) * 2 * TILE, 2 * TILE)
    out_ref[...] = block_ref[pl.ds(skip, out_ref.shape[0])]


def corner_of(block):
    return pl.pallas_call(
        corner_kernel,
        out_shape=jax.ShapeDtypeStruct((block.shape[0] - 2 * TILE, block.shape[1]), block.dtype),
        in_specs=[VMEM],
        out_specs=VMEM,
        compiler_params=params(),
        name="corner",
    )(block)


def attend_kernel(which, places, arrays, fresh, bounds_ref, *refs):
    halves = len(which)
    q_refs, refs = refs[:halves], refs[halves:]
    array_refs, refs = refs[: len(arrays)], refs[len(arrays) :]
    old_refs, refs = (None, refs) if fresh else (refs[:halves], refs[halves:])
    new_refs, (held_q, held, state) = refs[:halves], refs[halves:]
    rows, columns = q_refs[0].shape
    tiles = rows // TILE
    count = held.shape[1] // 2 // TILE
    heads = columns // HEAD_DIM
    me = lax.axis_index("seq")

    for half in range(halves):
        held_q[half] = q_refs[half][...]
        if fresh:
            state[half, :columns] = jnp.zeros((columns, rows), jnp.float32)
            state[half, columns : columns + heads] = jnp.full((heads, rows), LOWEST, jnp.float32)
            state[half, columns + heads :] = jnp.zeros((state.shape[1] - columns - heads, rows), jnp.float32)
        else:
            state[half] = old_refs[half][...]
    for slot, (array, shift) in enumerate(arrays):
        size = array_refs[array].shape[0]
        if size < held.shape[1]:
            held[slot] = jnp.zeros(held.shape[1:], held.dtype)
        at = 0 if shift is None else pl.multiple_of(shift(me), 2 * TILE)
        held[slot, pl.ds(at, size)] = array_refs[array][...]
    begins = [bounds_ref[2 * w, 0] for w in which]
    stops = [bounds_ref[2 * w + 1, rows - 1] for w in which]

    def chosen(at, options):
        return functools.reduce(lambda x, i: jnp.where(at == i, options[i], x), range(1, len(options)), options[0])

    def fold(half, slot, first):
        row = 2 * (which[0] + half * (which[-1] - which[0]) // max(len(which) - 1, 1))
        low = bounds_ref[pl.ds(row, 1), :]
        high = bounds_ref[pl.ds(row + 1, 1), :]
        off = [
            jnp.where((first + j >= low) & (first + j < high), 0.0, -LOWEST).astype(jnp.float32)
            for j in range(count)
        ]
        for h in range(heads):
            own = head_columns(h)
            scores = lax.dot_general(
                jnp.concatenate([held[slot, tile_rows(2 * j), own] for j in range(count)], axis=0),
                held_q[half, :, own],
                (((1,), (1,)), ((), ())),
                preferred_element_type=jnp.float32,
            )
            max_at, total_at = pl.ds(columns + h, 1), pl.ds(columns + heads + h, 1)
            factors, rounded, totals, maxima = [], [], [], []
            for t in range(tiles):
                lanes = tile_rows(t)
                parts = [scores[tile_rows(j), lanes] for j in range(count)]
                old_max = state[half, max_at, lanes]
                new_max = old_max
                for j in range(count):
                    new_max = jnp.maximum(new_max, jnp.max(parts[j], axis=0, keepdims=True) - off[j][:, lanes])
                scaled = new_max * SCALE2
                weights = [jnp.exp2(parts[j] * SCALE2 - (scaled + off[j][:, lanes])) for j in range(count)]
                factors.append(jnp.exp2((old_max - new_max) * SCALE2))
                totals.append(jnp.sum(functools.reduce(jnp.add, weights), axis=0, keepdims=True))
                maxima.append(new_max)
                rounded.append(jnp.concatenate([w.astype(jnp.bfloat16) for w in weights], axis=0))
            factor = jnp.concatenate(factors, axis=1)
            update = jnp.dot(
                jnp.concatenate([held[slot, tile_rows(2 * j + 1), own] for j in range(count)], axis=1),
                jnp.concatenate(rounded, axis=1),
                preferred_element_type=jnp.float32,
            )
            state[half, own] = state[half, own] * factor + update
            state[half, max_at] = jnp.concatenate(maxima, axis=1)
            state[half, total_at] = state[half, total_at] * factor + jnp.concatenate(totals, axis=1)

    @pl.loop(0, halves * len(places))
    def _(unit):
        half, slot = unit // len(places), unit % len(places)
        first = chosen(slot, [place(me) for place in places])

        @pl.when((first < chosen(half, stops)) & (first + count > chosen(half, begins)))
        def _():
            fold(half, slot, first)

    for half in range(halves):
        new_refs[half][...] = state[half]


def attend(bounds, queries, blocks, places, states, which=None, shifts=None):
    which = list(range(len(queries))) if which is None else which
    queries, states = [queries[w] for w in which], [states[w] for w in which] if states else []
    halves = len(which)
    rows, columns = queries[0].shape
    depth = blocks[0].shape[0]
    heads = columns // HEAD_DIM
    shape = jax.ShapeDtypeStruct((columns + -(-2 * heads // 8) * 8, rows), jnp.float32)
    arrays = list(enumerate(shifts or [None] * len(blocks)))
    pairs = halves * (rows // TILE) * heads * len(blocks) * (depth // 2 // TILE)
    return pl.pallas_call(
        functools.partial(attend_kernel, which, places, arrays, not states),
        out_shape=[shape] * halves,
        in_specs=[VMEM] * (1 + halves + len(blocks) + len(states)),
        out_specs=[VMEM] * halves,
        scratch_shapes=[
            pltpu.VMEM((halves, rows, columns), queries[0].dtype),
            pltpu.VMEM((len(blocks), depth, columns), blocks[0].dtype),
            pltpu.VMEM((halves,) + shape.shape, jnp.float32),
        ],
        compiler_params=params(),
        cost_estimate=pl.CostEstimate(
            flops=COST * pairs * 4 * TILE * TILE * HEAD_DIM,
            bytes_accessed=2 * len(blocks) * depth * columns + 4 * halves * rows * columns,
            transcendentals=pairs * TILE * TILE,
        ),
        name="attend",
    )(bounds, *queries, *blocks, *states)


def merged(states, columns):
    heads = columns // HEAD_DIM
    for h in range(heads):
        maxima = [ref[columns + h : columns + h + 1] for ref in states]
        totals = [ref[columns + heads + h : columns + heads + h + 1] for ref in states]
        largest = functools.reduce(jnp.maximum, maxima)
        factors = [jnp.exp2((m - largest) * SCALE2) for m in maxima]
        total = functools.reduce(jnp.add, [f * t for f, t in zip(factors, totals)])
        parts = [ref[head_columns(h)] * (f / total) for ref, f in zip(states, factors)]
        yield head_columns(h), functools.reduce(jnp.add, parts).T


def finish_kernel(*refs):
    out_ref = refs[-1]
    for own, done in merged(refs[:-1], out_ref.shape[1]):
        out_ref[:, own] = done.astype(out_ref.dtype)


def finish(states, rows, columns):
    return pl.pallas_call(
        finish_kernel,
        out_shape=jax.ShapeDtypeStruct((rows, columns), jnp.bfloat16),
        in_specs=[VMEM] * len(states),
        out_specs=VMEM,
        compiler_params=params(),
        name="finish",
    )(*states)


def message_kernel(*refs):
    states, outs, held = refs[:4], refs[4:8], refs[8]
    rows = outs[0].shape[0] - 2 * 8
    columns = outs[0].shape[1]
    heads = columns // HEAD_DIM
    mine = lax.axis_index("head")
    for part in range(2):
        pair, (keep_ref, send_ref) = states[2 * part : 2 * part + 2], outs[2 * part : 2 * part + 2]
        logs = []
        for h in range(heads):
            maxima = [ref[columns + h : columns + h + 1] for ref in pair]
            totals = [ref[columns + heads + h : columns + heads + h + 1] for ref in pair]
            largest = jnp.maximum(*maxima)
            factors = [jnp.exp2((m - largest) * SCALE2) for m in maxima]
            total = factors[0] * totals[0] + factors[1] * totals[1]
            some = jnp.where(total > 0, total, 1.0)
            scale = [f / some for f in factors]
            own = head_columns(h)
            held[:, own] = (pair[0][own] * scale[0] + pair[1][own] * scale[1]).T.astype(held.dtype)
            left = jnp.where(total > 0, largest * SCALE2 + jnp.log2(some), LOWEST)
            for _ in range(3):
                summand = left.astype(held.dtype).astype(jnp.float32)
                logs.append(summand)
                left = left - summand
        logs = jnp.concatenate(logs + [jnp.zeros((2 * 8 - len(logs), held.shape[0]), jnp.float32)], axis=0)
        later = pltpu.roll(logs, rows, 1)
        for ref, which in ((send_ref, 1 - mine), (keep_ref, mine)):
            ref[:rows] = held[pl.ds(pl.multiple_of(which * rows, 2 * 8), rows), :]
            ref[rows:] = jnp.where(which == 0, logs, later).astype(ref.dtype)


def messages(mine, peers):
    rows, columns = mine[0].shape[1], mine[0].shape[0] // HEAD_DIM * HEAD_DIM
    shape = jax.ShapeDtypeStruct((rows // 2 + 2 * 8, columns), jnp.bfloat16)
    return pl.pallas_call(
        message_kernel,
        out_shape=[shape] * 4,
        in_specs=[VMEM] * 4,
        out_specs=[VMEM] * 4,
        scratch_shapes=[pltpu.VMEM((rows, columns), jnp.bfloat16)],
        compiler_params=params(),
        name="message",
    )(*mine, *peers)


def settle_kernel(*refs):
    parts, out_ref, logs = refs[:4], refs[4], refs[5]
    rows, columns = out_ref.shape[0], parts[0].shape[1]
    heads = columns // HEAD_DIM
    mine = lax.axis_index("head")
    logs[...] = jnp.zeros(logs.shape, jnp.float32)
    for i, ref in enumerate(parts):
        summands = ref[rows:].astype(jnp.float32)
        for h in range(heads):
            at = i * heads + h
            logs[at : at + 1] = functools.reduce(jnp.add, [summands[3 * h + n : 3 * h + n + 1] for n in range(3)])
    turned = logs[...].T[:rows]
    for side, base in ((0, mine), (1, 1 - mine)):
        for h in range(heads):
            both = [turned[:, at : at + 1] for at in (2 * side * heads + h, (2 * side + 1) * heads + h)]
            largest = jnp.maximum(*both)
            weights = [jnp.exp2(x - largest) for x in both]
            sums = [ref[:rows, head_columns(h)].astype(jnp.float32) for ref in parts[2 * side : 2 * side + 2]]
            total = weights[0] + weights[1]
            done = sums[0] * (weights[0] / total) + sums[1] * (weights[1] / total)
            at = pl.multiple_of(base * columns + h * HEAD_DIM, HEAD_DIM)
            out_ref[:, pl.ds(at, HEAD_DIM)] = done.astype(out_ref.dtype)


def settle(own, across, beside, diagonal):
    rows, columns = own.shape[0] - 2 * 8, own.shape[1]
    return pl.pallas_call(
        settle_kernel,
        out_shape=jax.ShapeDtypeStruct((rows, 2 * columns), own.dtype),
        in_specs=[VMEM] * 4,
        out_specs=VMEM,
        scratch_shapes=[pltpu.VMEM((TILE, columns), jnp.float32)],
        compiler_params=params(),
        name="settle",
    )(own, across, beside, diagonal)


def chip_pairs(mesh):
    places = [tuple(getattr(d, "coords", ())) for d in mesh.devices[:, 0]]
    count = len(places)
    if count % 4 or not places[0] or mesh.shape["head"] != 2:
        return False
    cores = all(places[i] == places[i + 1] for i in range(0, count, 2))
    level = all(places[i][2] == places[i + 3][2] for i in range(0, count, 4))
    climb = all(places[i][2] != places[i + 4][2] for i in range(0, count - 4))
    return cores and level and climb


def paired_shards(owner_count, queries, keys, values, image_tiles):
    rows, columns = queries.shape
    tiles = rows // TILE
    owners = range(owner_count)

    def flip(s):
        return 1 - 2 * ((s // 2) % 2)

    def core(s):
        return s % 2

    def moved(array, source, takes=lambda s: True):
        pairs = [(source(s), s) for s in owners if takes(s) and 0 <= source(s) < owner_count]
        return lax.ppermute(array, "seq", pairs)

    across = lambda s: s + 2 * flip(s)
    along = lambda s: s + 4 * flip(s)
    against = lambda s: s - 4 * flip(s)
    sibling = lambda s: s + 1 - 2 * core(s)
    inner = lambda s: core(s) == (1 - (s // 2) % 2)

    OWN = lambda s: s * tiles
    A1 = lambda s: along(s) * tiles
    B1 = lambda s: against(s) * tiles
    A2 = lambda s: (s + 8 * flip(s)) * tiles
    B2 = lambda s: jnp.where(inner(s), s - 8 * flip(s), -owner_count) * tiles

    peers = moved(queries, across)
    block = pack(keys, values)
    a1, b1 = moved(block, along), moved(block, against)
    level = (queries, moved(queries, sibling), peers, moved(peers, sibling))
    bounds, far = meta(lambda s: [s, sibling(s), across(s), sibling(across(s))], image_tiles, rows)
    fold = functools.partial(attend, bounds, level)
    states = fold([block], [OWN], [], which=[0, 1]) + fold([block], [OWN], [], which=[2, 3])

    def merge(blocks, places, states, shifts=None):
        beside, diagonal = fold(blocks, places, states, which=[1, 3], shifts=shifts)
        beside, diagonal = moved(beside, sibling), moved(diagonal, sibling)
        mine, peer = fold(blocks, places, states, which=[0, 2], shifts=shifts)
        keep, over_x, over_y, over_both = messages([mine, beside], [peer, diagonal])
        pairs = [(2 * across(s) + 1 - x, 2 * s + x) for s in owners for x in range(2)]
        over_both = lax.ppermute(over_both, ("seq", "head"), pairs)
        over_y = moved(over_y, across)
        over_x = lax.ppermute(over_x, "head", [(0, 1), (1, 0)])
        return settle(keep, over_y, over_x, over_both)

    def near_only(a1, b1, states):
        return merge([a1, b1], [A1, B1], states)

    def both_ways(a1, b1, states):
        a2, b2 = moved(a1, along), moved(corner_of(b1), against, inner)
        states = fold([a1, b1], [A1, B1], states)
        return merge([a2, b2], [A2, B2], states, [None, lambda s: 2 * TILE * core(s)])

    return lax.cond(far > 0, both_ways, near_only, a1, b1, states)


def ring_shards(owner_count, queries, keys, values, image_tiles):
    rows, columns = queries.shape
    tiles = rows // TILE
    reach = min(owner_count - 1, -(-(MOST_TILES - 1) // tiles))
    block = pack(keys, values)
    bounds, _ = meta(lambda s: [s], image_tiles, rows)
    fold = functools.partial(attend, bounds, (queries,))
    up = [(i, i + 1) for i in range(owner_count - 1)]
    down = [(i + 1, i) for i in range(owner_count - 1)]
    below = above = block
    states = []
    held, places = [block], [lambda s: s * tiles]
    for k in range(1, reach + 1):
        below = lax.ppermute(below, "seq", up)
        above = lax.ppermute(above, "seq", down)
        states = fold(held, places, states)
        held, places = [below, above], [lambda s, k=k: (s - k) * tiles, lambda s, k=k: (s + k) * tiles]
    attended = finish(fold(held, places, states), rows, columns)
    return lax.all_to_all(attended, "head", split_axis=0, concat_axis=1, tiled=True)


def solution(mesh):
    owner_count = mesh.shape["seq"]
    plan = paired_shards if chip_pairs(mesh) else ring_shards
    placed = (P("seq", "head"), P("seq", "head"), P("seq", "head"), P())
    return jax.shard_map(
        functools.partial(plan, owner_count),
        mesh=mesh,
        in_specs=placed,
        out_specs=P(("seq", "head"), None),
        check_vma=False,
    )
```

```python
import functools
import math

import jax
import jax.numpy as jnp
from jax import lax
from jax.experimental import pallas as pl
from jax.experimental.pallas import tpu as pltpu
from jax.sharding import PartitionSpec as P

HEAD_DIM = 128
TILE = 128
MOST_TILES = 21

LOWEST = -1e30
SCALE2 = math.log2(math.e) / math.sqrt(HEAD_DIM)
COST = 2

VMEM = pl.BlockSpec(memory_space=pltpu.VMEM)
SMEM = pl.BlockSpec(memory_space=pltpu.SMEM)
HBM = pl.BlockSpec(memory_space=pl.ANY)


def params():
    return pltpu.CompilerParams(vmem_limit_bytes=24 * 1024 * 1024)


def head_columns(h):
    return slice(h * HEAD_DIM, (h + 1) * HEAD_DIM)


def tile_rows(t):
    return slice(t * TILE, (t + 1) * TILE)


def image_bounds(tiles_ref, tile):
    first = jnp.int32(0)
    start, end = jnp.int32(0), jnp.int32(0)
    for i in range(tiles_ref.shape[0]):
        after = first + tiles_ref[i]
        inside = (tile >= first) & (tile < after)
        start = jnp.where(inside, first, start)
        end = jnp.where(inside, after, end)
        first = after
    return start, end


def meta_kernel(halves, tiles_ref, bounds_ref, far_ref):
    tiles = bounds_ref.shape[1] // TILE
    me = lax.axis_index("seq")
    bounds_ref[...] = jnp.zeros(bounds_ref.shape, jnp.int32)
    for half, owner in enumerate(halves(me)):
        for t in range(tiles):
            start, end = image_bounds(tiles_ref, owner * tiles + t)
            bounds_ref[2 * half : 2 * half + 1, tile_rows(t)] = jnp.full((1, TILE), start, jnp.int32)
            bounds_ref[2 * half + 1 : 2 * half + 2, tile_rows(t)] = jnp.full((1, TILE), end, jnp.int32)
    first = jnp.int32(0)
    far = jnp.int32(0)
    for i in range(tiles_ref.shape[0]):
        after = first + tiles_ref[i]
        levels = (after - 1) // (4 * tiles) - first // (4 * tiles)
        far = jnp.where(levels >= 2, 1, far)
        first = after
    far_ref[0] = far


def meta(halves, image_tiles, rows):
    bounds, far = pl.pallas_call(
        functools.partial(meta_kernel, halves),
        out_shape=[jax.ShapeDtypeStruct((8, rows), jnp.int32), jax.ShapeDtypeStruct((1,), jnp.int32)],
        in_specs=[SMEM],
        out_specs=[VMEM, SMEM],
        compiler_params=params(),
        cost_estimate=pl.CostEstimate(flops=COST * 2**28, bytes_accessed=0, transcendentals=0),
        name="meta",
    )(image_tiles)
    return bounds, far[0]


def pack_kernel(k_ref, v_ref, out_ref, held, sems):
    rows, columns = k_ref.shape
    tiles = rows // TILE
    copies = []
    for t in range(tiles):
        copies.append(pltpu.make_async_copy(v_ref.at[tile_rows(t)], held.at[tile_rows(t)], sems.at[2 * t]))
        copies.append(pltpu.make_async_copy(k_ref.at[tile_rows(t)], out_ref.at[tile_rows(2 * t)], sems.at[2 * t + 1]))
    for copy in copies:
        copy.start()
    for t in range(tiles):
        copies[2 * t].wait()
        for h in range(columns // HEAD_DIM):
            out_ref[tile_rows(2 * t + 1), head_columns(h)] = held[tile_rows(t), head_columns(h)].T
    for copy in copies[1::2]:
        copy.wait()


def pack(keys, values):
    rows, columns = keys.shape
    return pl.pallas_call(
        pack_kernel,
        out_shape=jax.ShapeDtypeStruct((2 * rows, columns), keys.dtype),
        in_specs=[HBM, HBM],
        out_specs=VMEM,
        scratch_shapes=[pltpu.VMEM(values.shape, values.dtype), pltpu.SemaphoreType.DMA((2 * rows // TILE,))],
        name="pack",
    )(keys, values)


def corner_kernel(block_ref, own_ref, out_ref):
    skip = pl.multiple_of((lax.axis_index("seq") % 2) * 2 * TILE, 2 * TILE)
    out_ref[...] = block_ref[pl.ds(skip, out_ref.shape[0])]


def corner_of(block, own):
    return pl.pallas_call(
        corner_kernel,
        out_shape=jax.ShapeDtypeStruct((block.shape[0] - 2 * TILE, block.shape[1]), block.dtype),
        in_specs=[VMEM, HBM],
        out_specs=VMEM,
        compiler_params=params(),
        name="corner",
    )(block, own)


def attend_kernel(which, places, arrays, fresh, bounds_ref, *refs):
    halves = len(which)
    q_refs, refs = refs[:halves], refs[halves:]
    array_refs, refs = refs[: len(arrays)], refs[len(arrays) :]
    old_refs, refs = (None, refs) if fresh else (refs[:halves], refs[halves:])
    new_refs, (held_q, held, state) = refs[:halves], refs[halves:]
    rows, columns = q_refs[0].shape
    tiles = rows // TILE
    count = held.shape[1] // 2 // TILE
    heads = columns // HEAD_DIM
    me = lax.axis_index("seq")

    for half in range(halves):
        held_q[half] = q_refs[half][...]
        if fresh:
            state[half, :columns] = jnp.zeros((columns, rows), jnp.float32)
            state[half, columns : columns + heads] = jnp.full((heads, rows), LOWEST, jnp.float32)
            state[half, columns + heads :] = jnp.zeros((state.shape[1] - columns - heads, rows), jnp.float32)
        else:
            state[half] = old_refs[half][...]
    for slot, (array, shift) in enumerate(arrays):
        size = array_refs[array].shape[0]
        if size < held.shape[1]:
            held[slot] = jnp.zeros(held.shape[1:], held.dtype)
        at = 0 if shift is None else pl.multiple_of(shift(me), 2 * TILE)
        held[slot, pl.ds(at, size)] = array_refs[array][...]
    begins = [bounds_ref[2 * w, 0] for w in which]
    stops = [bounds_ref[2 * w + 1, rows - 1] for w in which]

    def chosen(at, options):
        return functools.reduce(lambda x, i: jnp.where(at == i, options[i], x), range(1, len(options)), options[0])

    def fold(half, slot, first):
        row = 2 * (which[0] + half * (which[-1] - which[0]) // max(len(which) - 1, 1))
        low = bounds_ref[pl.ds(row, 1), :]
        high = bounds_ref[pl.ds(row + 1, 1), :]
        off = [
            jnp.where((first + j >= low) & (first + j < high), 0.0, -LOWEST).astype(jnp.float32)
            for j in range(count)
        ]
        for h in range(heads):
            own = head_columns(h)
            scores = lax.dot_general(
                jnp.concatenate([held[slot, tile_rows(2 * j), own] for j in range(count)], axis=0),
                held_q[half, :, own],
                (((1,), (1,)), ((), ())),
                preferred_element_type=jnp.float32,
            )
            max_at, total_at = pl.ds(columns + h, 1), pl.ds(columns + heads + h, 1)
            factors, rounded, totals, maxima = [], [], [], []
            for t in range(tiles):
                lanes = tile_rows(t)
                parts = [scores[tile_rows(j), lanes] for j in range(count)]
                old_max = state[half, max_at, lanes]
                new_max = old_max
                for j in range(count):
                    new_max = jnp.maximum(new_max, jnp.max(parts[j], axis=0, keepdims=True) - off[j][:, lanes])
                scaled = new_max * SCALE2
                weights = [jnp.exp2(parts[j] * SCALE2 - (scaled + off[j][:, lanes])) for j in range(count)]
                factors.append(jnp.exp2((old_max - new_max) * SCALE2))
                totals.append(jnp.sum(functools.reduce(jnp.add, weights), axis=0, keepdims=True))
                maxima.append(new_max)
                rounded.append(jnp.concatenate([w.astype(jnp.bfloat16) for w in weights], axis=0))
            factor = jnp.concatenate(factors, axis=1)
            update = jnp.dot(
                jnp.concatenate([held[slot, tile_rows(2 * j + 1), own] for j in range(count)], axis=1),
                jnp.concatenate(rounded, axis=1),
                preferred_element_type=jnp.float32,
            )
            state[half, own] = state[half, own] * factor + update
            state[half, max_at] = jnp.concatenate(maxima, axis=1)
            state[half, total_at] = state[half, total_at] * factor + jnp.concatenate(totals, axis=1)

    @pl.loop(0, halves * len(places))
    def _(unit):
        half, slot = unit // len(places), unit % len(places)
        first = chosen(slot, [place(me) for place in places])

        @pl.when((first < chosen(half, stops)) & (first + count > chosen(half, begins)))
        def _():
            fold(half, slot, first)

    for half in range(halves):
        new_refs[half][...] = state[half]


def attend(bounds, queries, blocks, places, states, which=None, shifts=None):
    which = list(range(len(queries))) if which is None else which
    queries, states = [queries[w] for w in which], [states[w] for w in which] if states else []
    halves = len(which)
    rows, columns = queries[0].shape
    depth = blocks[0].shape[0]
    heads = columns // HEAD_DIM
    shape = jax.ShapeDtypeStruct((columns + -(-2 * heads // 8) * 8, rows), jnp.float32)
    arrays = list(enumerate(shifts or [None] * len(blocks)))
    pairs = halves * (rows // TILE) * heads * len(blocks) * (depth // 2 // TILE)
    return pl.pallas_call(
        functools.partial(attend_kernel, which, places, arrays, not states),
        out_shape=[shape] * halves,
        in_specs=[VMEM] * (1 + halves + len(blocks) + len(states)),
        out_specs=[VMEM] * halves,
        scratch_shapes=[
            pltpu.VMEM((halves, rows, columns), queries[0].dtype),
            pltpu.VMEM((len(blocks), depth, columns), blocks[0].dtype),
            pltpu.VMEM((halves,) + shape.shape, jnp.float32),
        ],
        compiler_params=params(),
        cost_estimate=pl.CostEstimate(
            flops=COST * pairs * 4 * TILE * TILE * HEAD_DIM,
            bytes_accessed=2 * len(blocks) * depth * columns + 4 * halves * rows * columns,
            transcendentals=pairs * TILE * TILE,
        ),
        name="attend",
    )(bounds, *queries, *blocks, *states)


def merged(states, columns):
    heads = columns // HEAD_DIM
    for h in range(heads):
        maxima = [ref[columns + h : columns + h + 1] for ref in states]
        totals = [ref[columns + heads + h : columns + heads + h + 1] for ref in states]
        largest = functools.reduce(jnp.maximum, maxima)
        factors = [jnp.exp2((m - largest) * SCALE2) for m in maxima]
        total = functools.reduce(jnp.add, [f * t for f, t in zip(factors, totals)])
        parts = [ref[head_columns(h)] * (f / total) for ref, f in zip(states, factors)]
        yield head_columns(h), functools.reduce(jnp.add, parts).T


def finish_kernel(*refs):
    out_ref = refs[-1]
    for own, done in merged(refs[:-1], out_ref.shape[1]):
        out_ref[:, own] = done.astype(out_ref.dtype)


def finish(states, rows, columns):
    return pl.pallas_call(
        finish_kernel,
        out_shape=jax.ShapeDtypeStruct((rows, columns), jnp.bfloat16),
        in_specs=[VMEM] * len(states),
        out_specs=VMEM,
        compiler_params=params(),
        name="finish",
    )(*states)


def message_kernel(*refs):
    states, outs, held = refs[:4], refs[4:8], refs[8]
    rows = outs[0].shape[0] - 2 * 8
    columns = outs[0].shape[1]
    heads = columns // HEAD_DIM
    mine = lax.axis_index("head")
    for part in range(2):
        pair, (keep_ref, send_ref) = states[2 * part : 2 * part + 2], outs[2 * part : 2 * part + 2]
        logs = []
        for h in range(heads):
            maxima = [ref[columns + h : columns + h + 1] for ref in pair]
            totals = [ref[columns + heads + h : columns + heads + h + 1] for ref in pair]
            largest = jnp.maximum(*maxima)
            factors = [jnp.exp2((m - largest) * SCALE2) for m in maxima]
            total = factors[0] * totals[0] + factors[1] * totals[1]
            some = jnp.where(total > 0, total, 1.0)
            scale = [f / some for f in factors]
            own = head_columns(h)
            held[:, own] = (pair[0][own] * scale[0] + pair[1][own] * scale[1]).T.astype(held.dtype)
            left = jnp.where(total > 0, largest * SCALE2 + jnp.log2(some), LOWEST)
            for _ in range(3):
                summand = left.astype(held.dtype).astype(jnp.float32)
                logs.append(summand)
                left = left - summand
        logs = jnp.concatenate(logs + [jnp.zeros((2 * 8 - len(logs), held.shape[0]), jnp.float32)], axis=0)
        later = pltpu.roll(logs, rows, 1)
        for ref, which in ((send_ref, 1 - mine), (keep_ref, mine)):
            ref[:rows] = held[pl.ds(pl.multiple_of(which * rows, 2 * 8), rows), :]
            ref[rows:] = jnp.where(which == 0, logs, later).astype(ref.dtype)


def messages(mine, peers):
    rows, columns = mine[0].shape[1], mine[0].shape[0] // HEAD_DIM * HEAD_DIM
    shape = jax.ShapeDtypeStruct((rows // 2 + 2 * 8, columns), jnp.bfloat16)
    return pl.pallas_call(
        message_kernel,
        out_shape=[shape] * 4,
        in_specs=[VMEM] * 4,
        out_specs=[VMEM] * 4,
        scratch_shapes=[pltpu.VMEM((rows, columns), jnp.bfloat16)],
        compiler_params=params(),
        name="message",
    )(*mine, *peers)


def settle_kernel(*refs):
    parts, out_ref, logs = refs[:4], refs[4], refs[5]
    rows, columns = out_ref.shape[0], parts[0].shape[1]
    heads = columns // HEAD_DIM
    mine = lax.axis_index("head")
    logs[...] = jnp.zeros(logs.shape, jnp.float32)
    for i, ref in enumerate(parts):
        summands = ref[rows:].astype(jnp.float32)
        for h in range(heads):
            at = i * heads + h
            logs[at : at + 1] = functools.reduce(jnp.add, [summands[3 * h + n : 3 * h + n + 1] for n in range(3)])
    turned = logs[...].T[:rows]
    for side, base in ((0, 1 - mine), (1, mine)):
        for h in range(heads):
            both = [turned[:, at : at + 1] for at in (2 * side * heads + h, (2 * side + 1) * heads + h)]
            largest = jnp.maximum(*both)
            weights = [jnp.exp2(x - largest) for x in both]
            sums = [ref[:rows, head_columns(h)].astype(jnp.float32) for ref in parts[2 * side : 2 * side + 2]]
            total = weights[0] + weights[1]
            done = sums[0] * (weights[0] / total) + sums[1] * (weights[1] / total)
            at = pl.multiple_of(base * columns + h * HEAD_DIM, HEAD_DIM)
            out_ref[:, pl.ds(at, HEAD_DIM)] = done.astype(out_ref.dtype)


def settle(diagonal, beside, across, own):
    rows, columns = own.shape[0] - 2 * 8, own.shape[1]
    return pl.pallas_call(
        settle_kernel,
        out_shape=jax.ShapeDtypeStruct((rows, 2 * columns), own.dtype),
        in_specs=[VMEM] * 4,
        out_specs=VMEM,
        scratch_shapes=[pltpu.VMEM((TILE, columns), jnp.float32)],
        compiler_params=params(),
        name="settle",
    )(diagonal, beside, across, own)


def chip_pairs(mesh):
    places = [tuple(getattr(d, "coords", ())) for d in mesh.devices[:, 0]]
    count = len(places)
    if count % 4 or not places[0] or mesh.shape["head"] != 2:
        return False
    cores = all(places[i] == places[i + 1] for i in range(0, count, 2))
    level = all(places[i][2] == places[i + 3][2] for i in range(0, count, 4))
    climb = all(places[i][2] != places[i + 4][2] for i in range(0, count - 4))
    return cores and level and climb


def paired_shards(owner_count, queries, keys, values, image_tiles):
    rows, columns = queries.shape
    tiles = rows // TILE
    owners = range(owner_count)

    def flip(s):
        return 1 - 2 * ((s // 2) % 2)

    def core(s):
        return s % 2

    def moved(array, source, takes=lambda s: True):
        pairs = [(source(s), s) for s in owners if takes(s) and 0 <= source(s) < owner_count]
        return lax.ppermute(array, "seq", pairs)

    across = lambda s: s + 2 * flip(s)
    along = lambda s: s + 4 * flip(s)
    against = lambda s: s - 4 * flip(s)
    sibling = lambda s: s + 1 - 2 * core(s)
    inner = lambda s: core(s) == (1 - (s // 2) % 2)

    OWN = lambda s: s * tiles
    A1 = lambda s: along(s) * tiles
    B1 = lambda s: against(s) * tiles
    A2 = lambda s: (s + 8 * flip(s)) * tiles
    B2 = lambda s: jnp.where(inner(s), s - 8 * flip(s), -owner_count) * tiles

    peers = moved(queries, across)
    block = pack(keys, values)
    a1, b1 = moved(block, along), moved(block, against)
    level = (queries, moved(queries, sibling), peers, moved(peers, sibling))
    bounds, far = meta(lambda s: [s, sibling(s), across(s), sibling(across(s))], image_tiles, rows)
    fold = functools.partial(attend, bounds, level)
    states = fold([block], [OWN], [], which=[0, 1]) + fold([block], [OWN], [], which=[2, 3])
    states = fold([b1], [B1], states)

    def merge(blocks, places, states, shifts=None):
        beside, diagonal = fold(blocks, places, states, which=[1, 3], shifts=shifts)
        beside, diagonal = moved(beside, sibling), moved(diagonal, sibling)
        mine, peer = fold(blocks, places, states, which=[0, 2], shifts=shifts)
        keep, over_x, over_y, over_both = messages([mine, beside], [peer, diagonal])
        pairs = [(2 * across(s) + 1 - x, 2 * s + x) for s in owners for x in range(2)]
        over_both = lax.ppermute(over_both, ("seq", "head"), pairs)
        over_y = moved(over_y, across)
        over_x = lax.ppermute(over_x, "head", [(0, 1), (1, 0)])
        return settle(over_both, over_x, over_y, keep)

    def near_only(block, a1, b1, states):
        return merge([a1], [A1], states)

    def both_ways(block, a1, b1, states):
        a2, b2 = moved(a1, along), moved(corner_of(b1, block), against, inner)
        states = fold([a1], [A1], states)
        return merge([a2, b2], [A2, B2], states, [None, lambda s: 2 * TILE * core(s)])

    return lax.cond(far > 0, both_ways, near_only, block, a1, b1, states)


def ring_shards(owner_count, queries, keys, values, image_tiles):
    rows, columns = queries.shape
    tiles = rows // TILE
    reach = min(owner_count - 1, -(-(MOST_TILES - 1) // tiles))
    block = pack(keys, values)
    bounds, _ = meta(lambda s: [s], image_tiles, rows)
    fold = functools.partial(attend, bounds, (queries,))
    up = [(i, i + 1) for i in range(owner_count - 1)]
    down = [(i + 1, i) for i in range(owner_count - 1)]
    below = above = block
    states = []
    held, places = [block], [lambda s: s * tiles]
    for k in range(1, reach + 1):
        below = lax.ppermute(below, "seq", up)
        above = lax.ppermute(above, "seq", down)
        states = fold(held, places, states)
        held, places = [below, above], [lambda s, k=k: (s - k) * tiles, lambda s, k=k: (s + k) * tiles]
    attended = finish(fold(held, places, states), rows, columns)
    return lax.all_to_all(attended, "head", split_axis=0, concat_axis=1, tiled=True)


def solution(mesh):
    owner_count = mesh.shape["seq"]
    plan = paired_shards if chip_pairs(mesh) else ring_shards
    placed = (P("seq", "head"), P("seq", "head"), P("seq", "head"), P())
    return jax.shard_map(
        functools.partial(plan, owner_count),
        mesh=mesh,
        in_specs=placed,
        out_specs=P(("seq", "head"), None),
        check_vma=False,
    )
```

```python
import functools
import math

import jax
import jax.numpy as jnp
from jax import lax
from jax.experimental import pallas as pl
from jax.experimental.pallas import tpu as pltpu
from jax.sharding import PartitionSpec as P

HEAD_DIM = 128
TILE = 128
MOST_TILES = 21

LOWEST = -1e30
SCALE2 = math.log2(math.e) / math.sqrt(HEAD_DIM)
COST = 2

VMEM = pl.BlockSpec(memory_space=pltpu.VMEM)
SMEM = pl.BlockSpec(memory_space=pltpu.SMEM)
HBM = pl.BlockSpec(memory_space=pl.ANY)


def params():
    return pltpu.CompilerParams(vmem_limit_bytes=24 * 1024 * 1024)


def head_columns(h):
    return slice(h * HEAD_DIM, (h + 1) * HEAD_DIM)


def tile_rows(t):
    return slice(t * TILE, (t + 1) * TILE)


def image_bounds(tiles_ref, tile):
    first = jnp.int32(0)
    start, end = jnp.int32(0), jnp.int32(0)
    for i in range(tiles_ref.shape[0]):
        after = first + tiles_ref[i]
        inside = (tile >= first) & (tile < after)
        start = jnp.where(inside, first, start)
        end = jnp.where(inside, after, end)
        first = after
    return start, end


def meta_kernel(halves, tiles_ref, bounds_ref, far_ref):
    tiles = bounds_ref.shape[1] // TILE
    me = lax.axis_index("seq")
    bounds_ref[...] = jnp.zeros(bounds_ref.shape, jnp.int32)
    for half, owner in enumerate(halves(me)):
        for t in range(tiles):
            start, end = image_bounds(tiles_ref, owner * tiles + t)
            bounds_ref[2 * half : 2 * half + 1, tile_rows(t)] = jnp.full((1, TILE), start, jnp.int32)
            bounds_ref[2 * half + 1 : 2 * half + 2, tile_rows(t)] = jnp.full((1, TILE), end, jnp.int32)
    first = jnp.int32(0)
    far = jnp.int32(0)
    for i in range(tiles_ref.shape[0]):
        after = first + tiles_ref[i]
        levels = (after - 1) // (4 * tiles) - first // (4 * tiles)
        far = jnp.where(levels >= 2, 1, far)
        first = after
    far_ref[0] = far


def meta(halves, image_tiles, rows):
    bounds, far = pl.pallas_call(
        functools.partial(meta_kernel, halves),
        out_shape=[jax.ShapeDtypeStruct((8, rows), jnp.int32), jax.ShapeDtypeStruct((1,), jnp.int32)],
        in_specs=[SMEM],
        out_specs=[VMEM, SMEM],
        compiler_params=params(),
        cost_estimate=pl.CostEstimate(flops=COST * 2**28, bytes_accessed=0, transcendentals=0),
        name="meta",
    )(image_tiles)
    return bounds, far[0]


def pack_kernel(k_ref, v_ref, out_ref, held, sems):
    rows, columns = k_ref.shape
    tiles = rows // TILE
    copies = []
    for t in range(tiles):
        copies.append(pltpu.make_async_copy(v_ref.at[tile_rows(t)], held.at[tile_rows(t)], sems.at[2 * t]))
        copies.append(pltpu.make_async_copy(k_ref.at[tile_rows(t)], out_ref.at[tile_rows(2 * t)], sems.at[2 * t + 1]))
    for copy in copies:
        copy.start()
    for t in range(tiles):
        copies[2 * t].wait()
        for h in range(columns // HEAD_DIM):
            out_ref[tile_rows(2 * t + 1), head_columns(h)] = held[tile_rows(t), head_columns(h)].T
    for copy in copies[1::2]:
        copy.wait()


def pack(keys, values):
    rows, columns = keys.shape
    return pl.pallas_call(
        pack_kernel,
        out_shape=jax.ShapeDtypeStruct((2 * rows, columns), keys.dtype),
        in_specs=[HBM, HBM],
        out_specs=VMEM,
        scratch_shapes=[pltpu.VMEM(values.shape, values.dtype), pltpu.SemaphoreType.DMA((2 * rows // TILE,))],
        name="pack",
    )(keys, values)


def corner_kernel(block_ref, own_ref, out_ref):
    skip = pl.multiple_of((lax.axis_index("seq") % 2) * 2 * TILE, 2 * TILE)
    out_ref[...] = block_ref[pl.ds(skip, out_ref.shape[0])]


def corner_of(block, own):
    return pl.pallas_call(
        corner_kernel,
        out_shape=jax.ShapeDtypeStruct((block.shape[0] - 2 * TILE, block.shape[1]), block.dtype),
        in_specs=[VMEM, HBM],
        out_specs=VMEM,
        compiler_params=params(),
        name="corner",
    )(block, own)


def attend_kernel(which, places, arrays, fresh, bounds_ref, *refs):
    halves = len(which)
    q_refs, refs = refs[:halves], refs[halves:]
    array_refs, refs = refs[: len(arrays)], refs[len(arrays) :]
    old_refs, refs = (None, refs) if fresh else (refs[:halves], refs[halves:])
    new_refs, (held_q, held, state) = refs[:halves], refs[halves:]
    rows, columns = q_refs[0].shape
    tiles = rows // TILE
    count = held.shape[1] // 2 // TILE
    heads = columns // HEAD_DIM
    me = lax.axis_index("seq")

    for half in range(halves):
        held_q[half] = q_refs[half][...]
        if fresh:
            state[half, :columns] = jnp.zeros((columns, rows), jnp.float32)
            state[half, columns : columns + heads] = jnp.full((heads, rows), LOWEST, jnp.float32)
            state[half, columns + heads :] = jnp.zeros((state.shape[1] - columns - heads, rows), jnp.float32)
        else:
            state[half] = old_refs[half][...]
    for slot, (array, shift) in enumerate(arrays):
        size = array_refs[array].shape[0]
        if size < held.shape[1]:
            held[slot] = jnp.zeros(held.shape[1:], held.dtype)
        at = 0 if shift is None else pl.multiple_of(shift(me), 2 * TILE)
        held[slot, pl.ds(at, size)] = array_refs[array][...]
    begins = [bounds_ref[2 * w, 0] for w in which]
    stops = [bounds_ref[2 * w + 1, rows - 1] for w in which]

    def chosen(at, options):
        return functools.reduce(lambda x, i: jnp.where(at == i, options[i], x), range(1, len(options)), options[0])

    def fold(half, slot, first):
        row = 2 * (which[0] + half * (which[-1] - which[0]) // max(len(which) - 1, 1))
        low = bounds_ref[pl.ds(row, 1), :]
        high = bounds_ref[pl.ds(row + 1, 1), :]
        off = [
            jnp.where((first + j >= low) & (first + j < high), 0.0, -LOWEST).astype(jnp.float32)
            for j in range(count)
        ]
        maxima = [[state[half, pl.ds(columns + h, 1), tile_rows(t)] for t in range(tiles)] for h in range(heads)]
        totals = [state[half, pl.ds(columns + heads + h, 1), :] for h in range(heads)]
        scores = [
            lax.dot_general(
                jnp.concatenate([held[slot, tile_rows(2 * j), head_columns(h)] for j in range(count)], axis=0),
                held_q[half, :, head_columns(h)],
                (((1,), (1,)), ((), ())),
                preferred_element_type=jnp.float32,
            )
            for h in range(heads)
        ]
        factors, sums, updates, largest = [], [], [], []
        for h in range(heads):
            factor, rounded, total, new = [], [], [], []
            for t in range(tiles):
                lanes = tile_rows(t)
                parts = [scores[h][tile_rows(j), lanes] for j in range(count)]
                new_max = maxima[h][t]
                for j in range(count):
                    new_max = jnp.maximum(new_max, jnp.max(parts[j], axis=0, keepdims=True) - off[j][:, lanes])
                scaled = new_max * SCALE2
                weights = [jnp.exp2(parts[j] * SCALE2 - (scaled + off[j][:, lanes])) for j in range(count)]
                factor.append(jnp.exp2((maxima[h][t] - new_max) * SCALE2))
                total.append(jnp.sum(functools.reduce(jnp.add, weights), axis=0, keepdims=True))
                new.append(new_max)
                rounded.append(jnp.concatenate([w.astype(jnp.bfloat16) for w in weights], axis=0))
            updates.append(
                jnp.dot(
                    jnp.concatenate([held[slot, tile_rows(2 * j + 1), head_columns(h)] for j in range(count)], axis=1),
                    jnp.concatenate(rounded, axis=1),
                    preferred_element_type=jnp.float32,
                )
            )
            factors.append(jnp.concatenate(factor, axis=1))
            sums.append(jnp.concatenate(total, axis=1))
            largest.append(jnp.concatenate(new, axis=1))
        for h in range(heads):
            own = head_columns(h)
            state[half, own] = state[half, own] * factors[h] + updates[h]
            state[half, pl.ds(columns + h, 1), :] = largest[h]
            state[half, pl.ds(columns + heads + h, 1), :] = totals[h] * factors[h] + sums[h]

    @pl.loop(0, halves * len(places))
    def _(unit):
        half, slot = unit // len(places), unit % len(places)
        first = chosen(slot, [place(me) for place in places])

        @pl.when((first < chosen(half, stops)) & (first + count > chosen(half, begins)))
        def _():
            fold(half, slot, first)

    for half in range(halves):
        new_refs[half][...] = state[half]


def attend(bounds, queries, blocks, places, states, which=None, shifts=None):
    which = list(range(len(queries))) if which is None else which
    queries, states = [queries[w] for w in which], [states[w] for w in which] if states else []
    halves = len(which)
    rows, columns = queries[0].shape
    depth = blocks[0].shape[0]
    heads = columns // HEAD_DIM
    shape = jax.ShapeDtypeStruct((columns + -(-2 * heads // 8) * 8, rows), jnp.float32)
    arrays = list(enumerate(shifts or [None] * len(blocks)))
    pairs = halves * (rows // TILE) * heads * len(blocks) * (depth // 2 // TILE)
    return pl.pallas_call(
        functools.partial(attend_kernel, which, places, arrays, not states),
        out_shape=[shape] * halves,
        in_specs=[VMEM] * (1 + halves + len(blocks) + len(states)),
        out_specs=[VMEM] * halves,
        scratch_shapes=[
            pltpu.VMEM((halves, rows, columns), queries[0].dtype),
            pltpu.VMEM((len(blocks), depth, columns), blocks[0].dtype),
            pltpu.VMEM((halves,) + shape.shape, jnp.float32),
        ],
        compiler_params=params(),
        cost_estimate=pl.CostEstimate(
            flops=COST * pairs * 4 * TILE * TILE * HEAD_DIM,
            bytes_accessed=2 * len(blocks) * depth * columns + 4 * halves * rows * columns,
            transcendentals=pairs * TILE * TILE,
        ),
        name="attend",
    )(bounds, *queries, *blocks, *states)


def merged(states, columns):
    heads = columns // HEAD_DIM
    for h in range(heads):
        maxima = [ref[columns + h : columns + h + 1] for ref in states]
        totals = [ref[columns + heads + h : columns + heads + h + 1] for ref in states]
        largest = functools.reduce(jnp.maximum, maxima)
        factors = [jnp.exp2((m - largest) * SCALE2) for m in maxima]
        total = functools.reduce(jnp.add, [f * t for f, t in zip(factors, totals)])
        parts = [ref[head_columns(h)] * (f / total) for ref, f in zip(states, factors)]
        yield head_columns(h), functools.reduce(jnp.add, parts).T


def finish_kernel(*refs):
    out_ref = refs[-1]
    for own, done in merged(refs[:-1], out_ref.shape[1]):
        out_ref[:, own] = done.astype(out_ref.dtype)


def finish(states, rows, columns):
    return pl.pallas_call(
        finish_kernel,
        out_shape=jax.ShapeDtypeStruct((rows, columns), jnp.bfloat16),
        in_specs=[VMEM] * len(states),
        out_specs=VMEM,
        compiler_params=params(),
        name="finish",
    )(*states)


def message_kernel(*refs):
    states, outs, held = refs[:4], refs[4:8], refs[8]
    rows = outs[0].shape[0] - 2 * 8
    columns = outs[0].shape[1]
    heads = columns // HEAD_DIM
    mine = lax.axis_index("head")
    for part in range(2):
        pair, (keep_ref, send_ref) = states[2 * part : 2 * part + 2], outs[2 * part : 2 * part + 2]
        logs = []
        for h in range(heads):
            maxima = [ref[columns + h : columns + h + 1] for ref in pair]
            totals = [ref[columns + heads + h : columns + heads + h + 1] for ref in pair]
            largest = jnp.maximum(*maxima)
            factors = [jnp.exp2((m - largest) * SCALE2) for m in maxima]
            total = factors[0] * totals[0] + factors[1] * totals[1]
            some = jnp.where(total > 0, total, 1.0)
            scale = [f / some for f in factors]
            own = head_columns(h)
            held[:, own] = (pair[0][own] * scale[0] + pair[1][own] * scale[1]).T.astype(held.dtype)
            left = jnp.where(total > 0, largest * SCALE2 + jnp.log2(some), LOWEST)
            for _ in range(3):
                summand = left.astype(held.dtype).astype(jnp.float32)
                logs.append(summand)
                left = left - summand
        logs = jnp.concatenate(logs + [jnp.zeros((2 * 8 - len(logs), held.shape[0]), jnp.float32)], axis=0)
        later = pltpu.roll(logs, rows, 1)
        for ref, which in ((send_ref, 1 - mine), (keep_ref, mine)):
            ref[:rows] = held[pl.ds(pl.multiple_of(which * rows, 2 * 8), rows), :]
            ref[rows:] = jnp.where(which == 0, logs, later).astype(ref.dtype)


def messages(mine, peers):
    rows, columns = mine[0].shape[1], mine[0].shape[0] // HEAD_DIM * HEAD_DIM
    shape = jax.ShapeDtypeStruct((rows // 2 + 2 * 8, columns), jnp.bfloat16)
    return pl.pallas_call(
        message_kernel,
        out_shape=[shape] * 4,
        in_specs=[VMEM] * 4,
        out_specs=[VMEM] * 4,
        scratch_shapes=[pltpu.VMEM((rows, columns), jnp.bfloat16)],
        compiler_params=params(),
        name="message",
    )(*mine, *peers)


def settle_kernel(*refs):
    parts, out_ref, logs = refs[:4], refs[4], refs[5]
    rows, columns = out_ref.shape[0], parts[0].shape[1]
    heads = columns // HEAD_DIM
    mine = lax.axis_index("head")
    logs[...] = jnp.zeros(logs.shape, jnp.float32)
    for i, ref in enumerate(parts):
        summands = ref[rows:].astype(jnp.float32)
        for h in range(heads):
            at = i * heads + h
            logs[at : at + 1] = functools.reduce(jnp.add, [summands[3 * h + n : 3 * h + n + 1] for n in range(3)])
    turned = logs[...].T[:rows]
    for side, base in ((0, 1 - mine), (1, mine)):
        for h in range(heads):
            both = [turned[:, at : at + 1] for at in (2 * side * heads + h, (2 * side + 1) * heads + h)]
            largest = jnp.maximum(*both)
            weights = [jnp.exp2(x - largest) for x in both]
            sums = [ref[:rows, head_columns(h)].astype(jnp.float32) for ref in parts[2 * side : 2 * side + 2]]
            total = weights[0] + weights[1]
            done = sums[0] * (weights[0] / total) + sums[1] * (weights[1] / total)
            at = pl.multiple_of(base * columns + h * HEAD_DIM, HEAD_DIM)
            out_ref[:, pl.ds(at, HEAD_DIM)] = done.astype(out_ref.dtype)


def settle(diagonal, beside, across, own):
    rows, columns = own.shape[0] - 2 * 8, own.shape[1]
    return pl.pallas_call(
        settle_kernel,
        out_shape=jax.ShapeDtypeStruct((rows, 2 * columns), own.dtype),
        in_specs=[VMEM] * 4,
        out_specs=VMEM,
        scratch_shapes=[pltpu.VMEM((TILE, columns), jnp.float32)],
        compiler_params=params(),
        name="settle",
    )(diagonal, beside, across, own)


def chip_pairs(mesh):
    places = [tuple(getattr(d, "coords", ())) for d in mesh.devices[:, 0]]
    count = len(places)
    if count % 4 or not places[0] or mesh.shape["head"] != 2:
        return False
    cores = all(places[i] == places[i + 1] for i in range(0, count, 2))
    level = all(places[i][2] == places[i + 3][2] for i in range(0, count, 4))
    climb = all(places[i][2] != places[i + 4][2] for i in range(0, count - 4))
    return cores and level and climb


def paired_shards(owner_count, queries, keys, values, image_tiles):
    rows, columns = queries.shape
    tiles = rows // TILE
    owners = range(owner_count)

    def flip(s):
        return 1 - 2 * ((s // 2) % 2)

    def core(s):
        return s % 2

    def moved(array, source, takes=lambda s: True):
        pairs = [(source(s), s) for s in owners if takes(s) and 0 <= source(s) < owner_count]
        return lax.ppermute(array, "seq", pairs)

    across = lambda s: s + 2 * flip(s)
    near_side = lambda s: s + 4 * flip(s)
    far_side = lambda s: s - 4 * flip(s)
    along = lambda s: s + 4 * flip(s) * (1 - 2 * core(s))
    against = lambda s: s - 4 * flip(s) * (1 - 2 * core(s))
    sibling = lambda s: s + 1 - 2 * core(s)
    inner = lambda s: core(s) == (1 - (s // 2) % 2)

    OWN = lambda s: s * tiles
    A1 = lambda s: along(s) * tiles
    B1 = lambda s: against(s) * tiles
    A2 = lambda s: (s + 8 * flip(s)) * tiles
    B2 = lambda s: jnp.where(inner(s), s - 8 * flip(s), -owner_count) * tiles

    peers = moved(queries, across)
    block = pack(keys, values)
    a1, b1 = moved(block, along), moved(block, against)
    level = (queries, moved(queries, sibling), peers, moved(peers, sibling))
    bounds, far = meta(lambda s: [s, sibling(s), across(s), sibling(across(s))], image_tiles, rows)
    fold = functools.partial(attend, bounds, level)
    states = fold([block], [OWN], [], which=[0, 1]) + fold([block], [OWN], [], which=[2, 3])
    states = fold([b1], [B1], states)

    def merge(blocks, places, states, shifts=None):
        beside, diagonal = fold(blocks, places, states, which=[1, 3], shifts=shifts)
        beside, diagonal = moved(beside, sibling), moved(diagonal, sibling)
        mine, peer = fold(blocks, places, states, which=[0, 2], shifts=shifts)
        keep, over_x, over_y, over_both = messages([mine, beside], [peer, diagonal])
        pairs = [(2 * across(s) + 1 - x, 2 * s + x) for s in owners for x in range(2)]
        over_both = lax.ppermute(over_both, ("seq", "head"), pairs)
        over_y = moved(over_y, across)
        over_x = lax.ppermute(over_x, "head", [(0, 1), (1, 0)])
        return settle(over_both, over_x, over_y, keep)

    def near_only(block, a1, b1, states):
        return merge([a1], [A1], states)

    def both_ways(block, a1, b1, states):
        first = core(lax.axis_index("seq")) == 0
        a2 = moved(jnp.where(first, a1, b1), near_side)
        b2 = moved(corner_of(jnp.where(first, b1, a1), block), far_side, inner)
        states = fold([a1], [A1], states)
        return merge([a2, b2], [A2, B2], states, [None, lambda s: 2 * TILE * core(s)])

    return lax.cond(far > 0, both_ways, near_only, block, a1, b1, states)


def ring_shards(owner_count, queries, keys, values, image_tiles):
    rows, columns = queries.shape
    tiles = rows // TILE
    reach = min(owner_count - 1, -(-(MOST_TILES - 1) // tiles))
    block = pack(keys, values)
    bounds, _ = meta(lambda s: [s], image_tiles, rows)
    fold = functools.partial(attend, bounds, (queries,))
    up = [(i, i + 1) for i in range(owner_count - 1)]
    down = [(i + 1, i) for i in range(owner_count - 1)]
    below = above = block
    states = []
    held, places = [block], [lambda s: s * tiles]
    for k in range(1, reach + 1):
        below = lax.ppermute(below, "seq", up)
        above = lax.ppermute(above, "seq", down)
        states = fold(held, places, states)
        held, places = [below, above], [lambda s, k=k: (s - k) * tiles, lambda s, k=k: (s + k) * tiles]
    attended = finish(fold(held, places, states), rows, columns)
    return lax.all_to_all(attended, "head", split_axis=0, concat_axis=1, tiled=True)


def solution(mesh):
    owner_count = mesh.shape["seq"]
    plan = paired_shards if chip_pairs(mesh) else ring_shards
    placed = (P("seq", "head"), P("seq", "head"), P("seq", "head"), P())
    return jax.shard_map(
        functools.partial(plan, owner_count),
        mesh=mesh,
        in_specs=placed,
        out_specs=P(("seq", "head"), None),
        check_vma=False,
    )
```

```python
import functools
import math

import jax
import jax.numpy as jnp
from jax import lax
from jax.experimental import pallas as pl
from jax.experimental.pallas import tpu as pltpu
from jax.sharding import PartitionSpec as P

HEAD_DIM = 128
TILE = 128
MOST_TILES = 21

LOWEST = -1e30
SCALE2 = math.log2(math.e) / math.sqrt(HEAD_DIM)
COST = 2

VMEM = pl.BlockSpec(memory_space=pltpu.VMEM)
SMEM = pl.BlockSpec(memory_space=pltpu.SMEM)
HBM = pl.BlockSpec(memory_space=pl.ANY)


def params():
    return pltpu.CompilerParams(vmem_limit_bytes=16 * 1024 * 1024)


def head_columns(h):
    return slice(h * HEAD_DIM, (h + 1) * HEAD_DIM)


def tile_rows(t):
    return slice(t * TILE, (t + 1) * TILE)


def image_bounds(tiles_ref, tile):
    first = jnp.int32(0)
    start, end = jnp.int32(0), jnp.int32(0)
    for i in range(tiles_ref.shape[0]):
        after = first + tiles_ref[i]
        inside = (tile >= first) & (tile < after)
        start = jnp.where(inside, first, start)
        end = jnp.where(inside, after, end)
        first = after
    return start, end


def meta_kernel(halves, tiles_ref, bounds_ref, far_ref):
    tiles = bounds_ref.shape[1] // TILE
    me = lax.axis_index("seq")
    bounds_ref[...] = jnp.zeros(bounds_ref.shape, jnp.int32)
    for half, owner in enumerate(halves(me)):
        for t in range(tiles):
            start, end = image_bounds(tiles_ref, owner * tiles + t)
            bounds_ref[2 * half : 2 * half + 1, tile_rows(t)] = jnp.full((1, TILE), start, jnp.int32)
            bounds_ref[2 * half + 1 : 2 * half + 2, tile_rows(t)] = jnp.full((1, TILE), end, jnp.int32)
    first = jnp.int32(0)
    far = jnp.int32(0)
    for i in range(tiles_ref.shape[0]):
        after = first + tiles_ref[i]
        levels = (after - 1) // (4 * tiles) - first // (4 * tiles)
        far = jnp.where(levels >= 2, 1, far)
        first = after
    far_ref[0] = far


def meta(halves, image_tiles, rows):
    bounds, far = pl.pallas_call(
        functools.partial(meta_kernel, halves),
        out_shape=[jax.ShapeDtypeStruct((8, rows), jnp.int32), jax.ShapeDtypeStruct((1,), jnp.int32)],
        in_specs=[SMEM],
        out_specs=[VMEM, SMEM],
        compiler_params=params(),
        cost_estimate=pl.CostEstimate(flops=COST * 2**28, bytes_accessed=0, transcendentals=0),
        name="meta",
    )(image_tiles)
    return bounds, far[0]


def pack_kernel(k_ref, v_ref, out_ref, held, sems):
    rows, columns = k_ref.shape
    tiles = rows // TILE
    copies = []
    for t in range(tiles):
        copies.append(pltpu.make_async_copy(v_ref.at[tile_rows(t)], held.at[tile_rows(t)], sems.at[2 * t]))
        copies.append(pltpu.make_async_copy(k_ref.at[tile_rows(t)], out_ref.at[tile_rows(2 * t)], sems.at[2 * t + 1]))
    for copy in copies:
        copy.start()
    for t in range(tiles):
        copies[2 * t].wait()
        for h in range(columns // HEAD_DIM):
            out_ref[tile_rows(2 * t + 1), head_columns(h)] = held[tile_rows(t), head_columns(h)].T
    for copy in copies[1::2]:
        copy.wait()


def pack(keys, values):
    rows, columns = keys.shape
    return pl.pallas_call(
        pack_kernel,
        out_shape=jax.ShapeDtypeStruct((2 * rows, columns), keys.dtype),
        in_specs=[HBM, HBM],
        out_specs=VMEM,
        scratch_shapes=[pltpu.VMEM(values.shape, values.dtype), pltpu.SemaphoreType.DMA((2 * rows // TILE,))],
        name="pack",
    )(keys, values)


def corner_kernel(block_ref, own_ref, out_ref):
    skip = pl.multiple_of((lax.axis_index("seq") % 2) * 2 * TILE, 2 * TILE)
    out_ref[...] = block_ref[pl.ds(skip, out_ref.shape[0])]


def corner_of(block, own):
    return pl.pallas_call(
        corner_kernel,
        out_shape=jax.ShapeDtypeStruct((block.shape[0] - 2 * TILE, block.shape[1]), block.dtype),
        in_specs=[VMEM, HBM],
        out_specs=VMEM,
        compiler_params=params(),
        name="corner",
    )(block, own)


def attend_kernel(which, places, arrays, fresh, bounds_ref, *refs):
    halves = len(which)
    q_refs, refs = refs[:halves], refs[halves:]
    array_refs, refs = refs[: len(arrays)], refs[len(arrays) :]
    old_refs, refs = (None, refs) if fresh else (refs[:halves], refs[halves:])
    new_refs, (held_q, held, state) = refs[:halves], refs[halves:]
    rows, columns = q_refs[0].shape
    tiles = rows // TILE
    count = held.shape[1] // 2 // TILE
    heads = columns // HEAD_DIM
    me = lax.axis_index("seq")

    for half in range(halves):
        held_q[half] = q_refs[half][...]
        if fresh:
            state[half, :columns] = jnp.zeros((columns, rows), jnp.float32)
            state[half, columns : columns + heads] = jnp.full((heads, rows), LOWEST, jnp.float32)
            state[half, columns + heads :] = jnp.zeros((state.shape[1] - columns - heads, rows), jnp.float32)
        else:
            state[half] = old_refs[half][...]
    for slot, (array, shift) in enumerate(arrays):
        size = array_refs[array].shape[0]
        if size < held.shape[1]:
            held[slot] = jnp.zeros(held.shape[1:], held.dtype)
        at = 0 if shift is None else pl.multiple_of(shift(me), 2 * TILE)
        held[slot, pl.ds(at, size)] = array_refs[array][...]
    begins = [bounds_ref[2 * w, 0] for w in which]
    stops = [bounds_ref[2 * w + 1, rows - 1] for w in which]

    def chosen(at, options):
        return functools.reduce(lambda x, i: jnp.where(at == i, options[i], x), range(1, len(options)), options[0])

    def fold(half, slot, first):
        row = 2 * (which[0] + half * (which[-1] - which[0]) // max(len(which) - 1, 1))
        low = bounds_ref[pl.ds(row, 1), :]
        high = bounds_ref[pl.ds(row + 1, 1), :]
        off = [
            jnp.where((first + j >= low) & (first + j < high), 0.0, -LOWEST).astype(jnp.float32)
            for j in range(count)
        ]
        maxima = [[state[half, pl.ds(columns + h, 1), tile_rows(t)] for t in range(tiles)] for h in range(heads)]
        totals = [state[half, pl.ds(columns + heads + h, 1), :] for h in range(heads)]
        scores = [
            lax.dot_general(
                jnp.concatenate([held[slot, tile_rows(2 * j), head_columns(h)] for j in range(count)], axis=0),
                held_q[half, :, head_columns(h)],
                (((1,), (1,)), ((), ())),
                preferred_element_type=jnp.float32,
            )
            for h in range(heads)
        ]
        factors, sums, updates, largest = [], [], [], []
        for h in range(heads):
            factor, rounded, total, new = [], [], [], []
            for t in range(tiles):
                lanes = tile_rows(t)
                parts = [scores[h][tile_rows(j), lanes] for j in range(count)]
                new_max = maxima[h][t]
                for j in range(count):
                    new_max = jnp.maximum(new_max, jnp.max(parts[j], axis=0, keepdims=True) - off[j][:, lanes])
                scaled = new_max * SCALE2
                weights = [jnp.exp2(parts[j] * SCALE2 - (scaled + off[j][:, lanes])) for j in range(count)]
                factor.append(jnp.exp2((maxima[h][t] - new_max) * SCALE2))
                total.append(jnp.sum(functools.reduce(jnp.add, weights), axis=0, keepdims=True))
                new.append(new_max)
                rounded.append(jnp.concatenate([w.astype(jnp.bfloat16) for w in weights], axis=0))
            updates.append(
                jnp.dot(
                    jnp.concatenate([held[slot, tile_rows(2 * j + 1), head_columns(h)] for j in range(count)], axis=1),
                    jnp.concatenate(rounded, axis=1),
                    preferred_element_type=jnp.float32,
                )
            )
            factors.append(jnp.concatenate(factor, axis=1))
            sums.append(jnp.concatenate(total, axis=1))
            largest.append(jnp.concatenate(new, axis=1))
        for h in range(heads):
            own = head_columns(h)
            state[half, own] = state[half, own] * factors[h] + updates[h]
            state[half, pl.ds(columns + h, 1), :] = largest[h]
            state[half, pl.ds(columns + heads + h, 1), :] = totals[h] * factors[h] + sums[h]

    @pl.loop(0, halves * len(places))
    def _(unit):
        half, slot = unit // len(places), unit % len(places)
        first = chosen(slot, [place(me) for place in places])

        @pl.when((first < chosen(half, stops)) & (first + count > chosen(half, begins)))
        def _():
            fold(half, slot, first)

    for half in range(halves):
        new_refs[half][...] = state[half]


def attend(bounds, queries, blocks, places, states, which=None, shifts=None):
    which = list(range(len(queries))) if which is None else which
    queries, states = [queries[w] for w in which], [states[w] for w in which] if states else []
    halves = len(which)
    rows, columns = queries[0].shape
    depth = blocks[0].shape[0]
    heads = columns // HEAD_DIM
    shape = jax.ShapeDtypeStruct((columns + -(-2 * heads // 8) * 8, rows), jnp.float32)
    arrays = list(enumerate(shifts or [None] * len(blocks)))
    pairs = halves * (rows // TILE) * heads * len(blocks) * (depth // 2 // TILE)
    return pl.pallas_call(
        functools.partial(attend_kernel, which, places, arrays, not states),
        out_shape=[shape] * halves,
        in_specs=[VMEM] * (1 + halves + len(blocks) + len(states)),
        out_specs=[VMEM] * halves,
        scratch_shapes=[
            pltpu.VMEM((halves, rows, columns), queries[0].dtype),
            pltpu.VMEM((len(blocks), depth, columns), blocks[0].dtype),
            pltpu.VMEM((halves,) + shape.shape, jnp.float32),
        ],
        compiler_params=params(),
        cost_estimate=pl.CostEstimate(
            flops=COST * pairs * 4 * TILE * TILE * HEAD_DIM,
            bytes_accessed=2 * len(blocks) * depth * columns + 4 * halves * rows * columns,
            transcendentals=pairs * TILE * TILE,
        ),
        name="attend",
    )(bounds, *queries, *blocks, *states)


def merged(states, columns):
    heads = columns // HEAD_DIM
    for h in range(heads):
        maxima = [ref[columns + h : columns + h + 1] for ref in states]
        totals = [ref[columns + heads + h : columns + heads + h + 1] for ref in states]
        largest = functools.reduce(jnp.maximum, maxima)
        factors = [jnp.exp2((m - largest) * SCALE2) for m in maxima]
        total = functools.reduce(jnp.add, [f * t for f, t in zip(factors, totals)])
        parts = [ref[head_columns(h)] * (f / total) for ref, f in zip(states, factors)]
        yield head_columns(h), functools.reduce(jnp.add, parts).T


def finish_kernel(*refs):
    out_ref = refs[-1]
    for own, done in merged(refs[:-1], out_ref.shape[1]):
        out_ref[:, own] = done.astype(out_ref.dtype)


def finish(states, rows, columns):
    return pl.pallas_call(
        finish_kernel,
        out_shape=jax.ShapeDtypeStruct((rows, columns), jnp.bfloat16),
        in_specs=[VMEM] * len(states),
        out_specs=VMEM,
        compiler_params=params(),
        name="finish",
    )(*states)


def message_kernel(*refs):
    states, outs, held = refs[:4], refs[4:8], refs[8]
    rows = outs[0].shape[0] - 2 * 8
    columns = outs[0].shape[1]
    heads = columns // HEAD_DIM
    mine = lax.axis_index("head")
    for part in range(2):
        pair, (keep_ref, send_ref) = states[2 * part : 2 * part + 2], outs[2 * part : 2 * part + 2]
        logs = []
        for h in range(heads):
            maxima = [ref[columns + h : columns + h + 1] for ref in pair]
            totals = [ref[columns + heads + h : columns + heads + h + 1] for ref in pair]
            largest = jnp.maximum(*maxima)
            factors = [jnp.exp2((m - largest) * SCALE2) for m in maxima]
            total = factors[0] * totals[0] + factors[1] * totals[1]
            some = jnp.where(total > 0, total, 1.0)
            scale = [f / some for f in factors]
            own = head_columns(h)
            held[:, own] = (pair[0][own] * scale[0] + pair[1][own] * scale[1]).T.astype(held.dtype)
            left = jnp.where(total > 0, largest * SCALE2 + jnp.log2(some), LOWEST)
            for _ in range(3):
                summand = left.astype(held.dtype).astype(jnp.float32)
                logs.append(summand)
                left = left - summand
        logs = jnp.concatenate(logs + [jnp.zeros((2 * 8 - len(logs), held.shape[0]), jnp.float32)], axis=0)
        later = pltpu.roll(logs, rows, 1)
        for ref, which in ((send_ref, 1 - mine), (keep_ref, mine)):
            ref[:rows] = held[pl.ds(pl.multiple_of(which * rows, 2 * 8), rows), :]
            ref[rows:] = jnp.where(which == 0, logs, later).astype(ref.dtype)


def messages(mine, peers):
    rows, columns = mine[0].shape[1], mine[0].shape[0] // HEAD_DIM * HEAD_DIM
    shape = jax.ShapeDtypeStruct((rows // 2 + 2 * 8, columns), jnp.bfloat16)
    return pl.pallas_call(
        message_kernel,
        out_shape=[shape] * 4,
        in_specs=[VMEM] * 4,
        out_specs=[VMEM] * 4,
        scratch_shapes=[pltpu.VMEM((rows, columns), jnp.bfloat16)],
        compiler_params=params(),
        name="message",
    )(*mine, *peers)


def settle_kernel(*refs):
    parts, out_ref, logs = refs[:4], refs[4], refs[5]
    rows, columns = out_ref.shape[0], parts[0].shape[1]
    heads = columns // HEAD_DIM
    mine = lax.axis_index("head")
    logs[...] = jnp.zeros(logs.shape, jnp.float32)
    for i, ref in enumerate(parts):
        summands = ref[rows:].astype(jnp.float32)
        for h in range(heads):
            at = i * heads + h
            logs[at : at + 1] = functools.reduce(jnp.add, [summands[3 * h + n : 3 * h + n + 1] for n in range(3)])
    turned = logs[...].T[:rows]
    for side, base in ((0, 1 - mine), (1, mine)):
        for h in range(heads):
            both = [turned[:, at : at + 1] for at in (2 * side * heads + h, (2 * side + 1) * heads + h)]
            largest = jnp.maximum(*both)
            weights = [jnp.exp2(x - largest) for x in both]
            sums = [ref[:rows, head_columns(h)].astype(jnp.float32) for ref in parts[2 * side : 2 * side + 2]]
            total = weights[0] + weights[1]
            done = sums[0] * (weights[0] / total) + sums[1] * (weights[1] / total)
            at = pl.multiple_of(base * columns + h * HEAD_DIM, HEAD_DIM)
            out_ref[:, pl.ds(at, HEAD_DIM)] = done.astype(out_ref.dtype)


def settle(diagonal, beside, across, own):
    rows, columns = own.shape[0] - 2 * 8, own.shape[1]
    return pl.pallas_call(
        settle_kernel,
        out_shape=jax.ShapeDtypeStruct((rows, 2 * columns), own.dtype),
        in_specs=[VMEM] * 4,
        out_specs=VMEM,
        scratch_shapes=[pltpu.VMEM((TILE, columns), jnp.float32)],
        compiler_params=params(),
        name="settle",
    )(diagonal, beside, across, own)


def chip_pairs(mesh):
    places = [tuple(getattr(d, "coords", ())) for d in mesh.devices[:, 0]]
    count = len(places)
    if count % 4 or not places[0] or mesh.shape["head"] != 2:
        return False
    cores = all(places[i] == places[i + 1] for i in range(0, count, 2))
    level = all(places[i][2] == places[i + 3][2] for i in range(0, count, 4))
    climb = all(places[i][2] != places[i + 4][2] for i in range(0, count - 4))
    return cores and level and climb


def paired_shards(owner_count, queries, keys, values, image_tiles):
    rows, columns = queries.shape
    tiles = rows // TILE
    owners = range(owner_count)

    def flip(s):
        return 1 - 2 * ((s // 2) % 2)

    def core(s):
        return s % 2

    def moved(array, source, takes=lambda s: True):
        pairs = [(source(s), s) for s in owners if takes(s) and 0 <= source(s) < owner_count]
        return lax.ppermute(array, "seq", pairs)

    across = lambda s: s + 2 * flip(s)
    near_side = lambda s: s + 4 * flip(s)
    far_side = lambda s: s - 4 * flip(s)
    along = lambda s: s + 4 * flip(s) * (1 - 2 * core(s))
    against = lambda s: s - 4 * flip(s) * (1 - 2 * core(s))
    sibling = lambda s: s + 1 - 2 * core(s)
    inner = lambda s: core(s) == (1 - (s // 2) % 2)

    OWN = lambda s: s * tiles
    A1 = lambda s: along(s) * tiles
    B1 = lambda s: against(s) * tiles
    A2 = lambda s: (s + 8 * flip(s)) * tiles
    B2 = lambda s: jnp.where(inner(s), s - 8 * flip(s), -owner_count) * tiles

    peers = moved(queries, across)
    block = pack(keys, values)
    a1, b1 = moved(block, along), moved(block, against)
    level = (queries, moved(queries, sibling), peers, moved(peers, sibling))
    bounds, far = meta(lambda s: [s, sibling(s), across(s), sibling(across(s))], image_tiles, rows)
    fold = functools.partial(attend, bounds, level)
    states = fold([block], [OWN], [], which=[0, 1]) + fold([block], [OWN], [], which=[2, 3])
    states = fold([b1], [B1], states)

    def merge(blocks, places, states, shifts=None):
        beside, diagonal = fold(blocks, places, states, which=[1, 3], shifts=shifts)
        beside, diagonal = moved(beside, sibling), moved(diagonal, sibling)
        mine, peer = fold(blocks, places, states, which=[0, 2], shifts=shifts)
        keep, over_x, over_y, over_both = messages([mine, beside], [peer, diagonal])
        pairs = [(2 * across(s) + 1 - x, 2 * s + x) for s in owners for x in range(2)]
        over_both = lax.ppermute(over_both, ("seq", "head"), pairs)
        over_y = moved(over_y, across)
        over_x = lax.ppermute(over_x, "head", [(0, 1), (1, 0)])
        return settle(over_both, over_x, over_y, keep)

    def near_only(block, a1, b1, states):
        return merge([a1], [A1], states)

    def both_ways(block, a1, b1, states):
        first = core(lax.axis_index("seq")) == 0
        a2 = moved(jnp.where(first, a1, b1), near_side)
        b2 = moved(corner_of(jnp.where(first, b1, a1), block), far_side, inner)
        states = fold([a1], [A1], states)
        return merge([a2, b2], [A2, B2], states, [None, lambda s: 2 * TILE * core(s)])

    return lax.cond(far > 0, both_ways, near_only, block, a1, b1, states)


def ring_shards(owner_count, queries, keys, values, image_tiles):
    rows, columns = queries.shape
    tiles = rows // TILE
    reach = min(owner_count - 1, -(-(MOST_TILES - 1) // tiles))
    block = pack(keys, values)
    bounds, _ = meta(lambda s: [s], image_tiles, rows)
    fold = functools.partial(attend, bounds, (queries,))
    up = [(i, i + 1) for i in range(owner_count - 1)]
    down = [(i + 1, i) for i in range(owner_count - 1)]
    below = above = block
    states = []
    held, places = [block], [lambda s: s * tiles]
    for k in range(1, reach + 1):
        below = lax.ppermute(below, "seq", up)
        above = lax.ppermute(above, "seq", down)
        states = fold(held, places, states)
        held, places = [below, above], [lambda s, k=k: (s - k) * tiles, lambda s, k=k: (s + k) * tiles]
    attended = finish(fold(held, places, states), rows, columns)
    return lax.all_to_all(attended, "head", split_axis=0, concat_axis=1, tiled=True)


def solution(mesh):
    owner_count = mesh.shape["seq"]
    plan = paired_shards if chip_pairs(mesh) else ring_shards
    placed = (P("seq", "head"), P("seq", "head"), P("seq", "head"), P())
    return jax.shard_map(
        functools.partial(plan, owner_count),
        mesh=mesh,
        in_specs=placed,
        out_specs=P(("seq", "head"), None),
        check_vma=False,
    )
```

```python
import functools
import math

import jax
import jax.numpy as jnp
from jax import lax
from jax.experimental import pallas as pl
from jax.experimental.pallas import tpu as pltpu
from jax.sharding import PartitionSpec as P

HEAD_DIM = 128
TILE = 128
MOST_TILES = 21

LOWEST = -1e30
SCALE2 = math.log2(math.e) / math.sqrt(HEAD_DIM)
COST = 2

VMEM = pl.BlockSpec(memory_space=pltpu.VMEM)
SMEM = pl.BlockSpec(memory_space=pltpu.SMEM)
HBM = pl.BlockSpec(memory_space=pl.ANY)


def params():
    return pltpu.CompilerParams(vmem_limit_bytes=16 * 1024 * 1024)


def head_columns(h):
    return slice(h * HEAD_DIM, (h + 1) * HEAD_DIM)


def tile_rows(t):
    return slice(t * TILE, (t + 1) * TILE)


def image_bounds(tiles_ref, tile):
    first = jnp.int32(0)
    start, end = jnp.int32(0), jnp.int32(0)
    for i in range(tiles_ref.shape[0]):
        after = first + tiles_ref[i]
        inside = (tile >= first) & (tile < after)
        start = jnp.where(inside, first, start)
        end = jnp.where(inside, after, end)
        first = after
    return start, end


def meta_kernel(halves, tiles_ref, bounds_ref, far_ref):
    tiles = bounds_ref.shape[1] // TILE
    me = lax.axis_index("seq")
    bounds_ref[...] = jnp.zeros(bounds_ref.shape, jnp.int32)
    for half, owner in enumerate(halves(me)):
        for t in range(tiles):
            start, end = image_bounds(tiles_ref, owner * tiles + t)
            bounds_ref[2 * half : 2 * half + 1, tile_rows(t)] = jnp.full((1, TILE), start, jnp.int32)
            bounds_ref[2 * half + 1 : 2 * half + 2, tile_rows(t)] = jnp.full((1, TILE), end, jnp.int32)
    first = jnp.int32(0)
    far = jnp.int32(0)
    for i in range(tiles_ref.shape[0]):
        after = first + tiles_ref[i]
        levels = (after - 1) // (4 * tiles) - first // (4 * tiles)
        far = jnp.where(levels >= 2, 1, far)
        first = after
    far_ref[0] = far


def meta(halves, image_tiles, rows):
    bounds, far = pl.pallas_call(
        functools.partial(meta_kernel, halves),
        out_shape=[jax.ShapeDtypeStruct((8, rows), jnp.int32), jax.ShapeDtypeStruct((1,), jnp.int32)],
        in_specs=[SMEM],
        out_specs=[VMEM, SMEM],
        compiler_params=params(),
        cost_estimate=pl.CostEstimate(flops=COST * 2**28, bytes_accessed=0, transcendentals=0),
        name="meta",
    )(image_tiles)
    return bounds, far[0]


def pack_kernel(k_ref, v_ref, out_ref, held, sems):
    rows, columns = k_ref.shape
    tiles = rows // TILE
    copies = []
    for t in range(tiles):
        copies.append(pltpu.make_async_copy(v_ref.at[tile_rows(t)], held.at[tile_rows(t)], sems.at[2 * t]))
        copies.append(pltpu.make_async_copy(k_ref.at[tile_rows(t)], out_ref.at[tile_rows(2 * t)], sems.at[2 * t + 1]))
    for copy in copies:
        copy.start()
    for t in range(tiles):
        copies[2 * t].wait()
        for h in range(columns // HEAD_DIM):
            out_ref[tile_rows(2 * t + 1), head_columns(h)] = held[tile_rows(t), head_columns(h)].T
    for copy in copies[1::2]:
        copy.wait()


def pack(keys, values):
    rows, columns = keys.shape
    return pl.pallas_call(
        pack_kernel,
        out_shape=jax.ShapeDtypeStruct((2 * rows, columns), keys.dtype),
        in_specs=[HBM, HBM],
        out_specs=VMEM,
        scratch_shapes=[pltpu.VMEM(values.shape, values.dtype), pltpu.SemaphoreType.DMA((2 * rows // TILE,))],
        name="pack",
    )(keys, values)


def onward_kernel(a1_ref, b1_ref, own_ref, near_ref, corner_ref):
    upper = lax.axis_index("seq") % 2
    rows = corner_ref.shape[0]

    @pl.when(upper == 0)
    def _():
        near_ref[...] = a1_ref[...]
        corner_ref[...] = b1_ref[:rows]

    @pl.when(upper == 1)
    def _():
        near_ref[...] = b1_ref[...]
        corner_ref[...] = a1_ref[-rows:]


def onward(a1, b1, own):
    rows, columns = a1.shape
    return pl.pallas_call(
        onward_kernel,
        out_shape=[
            jax.ShapeDtypeStruct((rows, columns), a1.dtype),
            jax.ShapeDtypeStruct((rows - 2 * TILE, columns), a1.dtype),
        ],
        in_specs=[VMEM, VMEM, HBM],
        out_specs=[VMEM, VMEM],
        compiler_params=params(),
        name="onward",
    )(a1, b1, own)


def attend_kernel(which, places, arrays, fresh, bounds_ref, *refs):
    halves = len(which)
    q_refs, refs = refs[:halves], refs[halves:]
    array_refs, refs = refs[: len(arrays)], refs[len(arrays) :]
    old_refs, refs = (None, refs) if fresh else (refs[:halves], refs[halves:])
    new_refs, (held_q, held, state) = refs[:halves], refs[halves:]
    rows, columns = q_refs[0].shape
    tiles = rows // TILE
    count = held.shape[1] // 2 // TILE
    heads = columns // HEAD_DIM
    me = lax.axis_index("seq")

    for half in range(halves):
        held_q[half] = q_refs[half][...]
        if fresh:
            state[half, :columns] = jnp.zeros((columns, rows), jnp.float32)
            state[half, columns : columns + heads] = jnp.full((heads, rows), LOWEST, jnp.float32)
            state[half, columns + heads :] = jnp.zeros((state.shape[1] - columns - heads, rows), jnp.float32)
        else:
            state[half] = old_refs[half][...]
    for slot, (array, shift) in enumerate(arrays):
        size = array_refs[array].shape[0]
        if size < held.shape[1]:
            held[slot] = jnp.zeros(held.shape[1:], held.dtype)
        at = 0 if shift is None else pl.multiple_of(shift(me), 2 * TILE)
        held[slot, pl.ds(at, size)] = array_refs[array][...]
    begins = [bounds_ref[2 * w, 0] for w in which]
    stops = [bounds_ref[2 * w + 1, rows - 1] for w in which]

    def chosen(at, options):
        return functools.reduce(lambda x, i: jnp.where(at == i, options[i], x), range(1, len(options)), options[0])

    def fold(half, slot, first):
        row = 2 * (which[0] + half * (which[-1] - which[0]) // max(len(which) - 1, 1))
        low = bounds_ref[pl.ds(row, 1), :]
        high = bounds_ref[pl.ds(row + 1, 1), :]
        off = [
            jnp.where((first + j >= low) & (first + j < high), 0.0, -LOWEST).astype(jnp.float32)
            for j in range(count)
        ]
        maxima = [[state[half, pl.ds(columns + h, 1), tile_rows(t)] for t in range(tiles)] for h in range(heads)]
        totals = [state[half, pl.ds(columns + heads + h, 1), :] for h in range(heads)]
        scores = [
            lax.dot_general(
                jnp.concatenate([held[slot, tile_rows(2 * j), head_columns(h)] for j in range(count)], axis=0),
                held_q[half, :, head_columns(h)],
                (((1,), (1,)), ((), ())),
                preferred_element_type=jnp.float32,
            )
            for h in range(heads)
        ]
        factors, sums, updates, largest = [], [], [], []
        for h in range(heads):
            factor, rounded, total, new = [], [], [], []
            for t in range(tiles):
                lanes = tile_rows(t)
                parts = [scores[h][tile_rows(j), lanes] for j in range(count)]
                new_max = maxima[h][t]
                for j in range(count):
                    new_max = jnp.maximum(new_max, jnp.max(parts[j], axis=0, keepdims=True) - off[j][:, lanes])
                scaled = new_max * SCALE2
                weights = [jnp.exp2(parts[j] * SCALE2 - (scaled + off[j][:, lanes])) for j in range(count)]
                factor.append(jnp.exp2((maxima[h][t] - new_max) * SCALE2))
                total.append(jnp.sum(functools.reduce(jnp.add, weights), axis=0, keepdims=True))
                new.append(new_max)
                rounded.append(jnp.concatenate([w.astype(jnp.bfloat16) for w in weights], axis=0))
            updates.append(
                jnp.dot(
                    jnp.concatenate([held[slot, tile_rows(2 * j + 1), head_columns(h)] for j in range(count)], axis=1),
                    jnp.concatenate(rounded, axis=1),
                    preferred_element_type=jnp.float32,
                )
            )
            factors.append(jnp.concatenate(factor, axis=1))
            sums.append(jnp.concatenate(total, axis=1))
            largest.append(jnp.concatenate(new, axis=1))
        for h in range(heads):
            own = head_columns(h)
            state[half, own] = state[half, own] * factors[h] + updates[h]
            state[half, pl.ds(columns + h, 1), :] = largest[h]
            state[half, pl.ds(columns + heads + h, 1), :] = totals[h] * factors[h] + sums[h]

    @pl.loop(0, halves * len(places))
    def _(unit):
        half, slot = unit // len(places), unit % len(places)
        first = chosen(slot, [place(me) for place in places])

        @pl.when((first < chosen(half, stops)) & (first + count > chosen(half, begins)))
        def _():
            fold(half, slot, first)

    for half in range(halves):
        new_refs[half][...] = state[half]


def attend(bounds, queries, blocks, places, states, which=None, shifts=None):
    which = list(range(len(queries))) if which is None else which
    queries, states = [queries[w] for w in which], [states[w] for w in which] if states else []
    halves = len(which)
    rows, columns = queries[0].shape
    depth = blocks[0].shape[0]
    heads = columns // HEAD_DIM
    shape = jax.ShapeDtypeStruct((columns + -(-2 * heads // 8) * 8, rows), jnp.float32)
    arrays = list(enumerate(shifts or [None] * len(blocks)))
    pairs = halves * (rows // TILE) * heads * len(blocks) * (depth // 2 // TILE)
    return pl.pallas_call(
        functools.partial(attend_kernel, which, places, arrays, not states),
        out_shape=[shape] * halves,
        in_specs=[VMEM] * (1 + halves + len(blocks) + len(states)),
        out_specs=[VMEM] * halves,
        scratch_shapes=[
            pltpu.VMEM((halves, rows, columns), queries[0].dtype),
            pltpu.VMEM((len(blocks), depth, columns), blocks[0].dtype),
            pltpu.VMEM((halves,) + shape.shape, jnp.float32),
        ],
        compiler_params=params(),
        cost_estimate=pl.CostEstimate(
            flops=COST * pairs * 4 * TILE * TILE * HEAD_DIM,
            bytes_accessed=2 * len(blocks) * depth * columns + 4 * halves * rows * columns,
            transcendentals=pairs * TILE * TILE,
        ),
        name="attend",
    )(bounds, *queries, *blocks, *states)


def merged(states, columns):
    heads = columns // HEAD_DIM
    for h in range(heads):
        maxima = [ref[columns + h : columns + h + 1] for ref in states]
        totals = [ref[columns + heads + h : columns + heads + h + 1] for ref in states]
        largest = functools.reduce(jnp.maximum, maxima)
        factors = [jnp.exp2((m - largest) * SCALE2) for m in maxima]
        total = functools.reduce(jnp.add, [f * t for f, t in zip(factors, totals)])
        parts = [ref[head_columns(h)] * (f / total) for ref, f in zip(states, factors)]
        yield head_columns(h), functools.reduce(jnp.add, parts).T


def finish_kernel(*refs):
    out_ref = refs[-1]
    for own, done in merged(refs[:-1], out_ref.shape[1]):
        out_ref[:, own] = done.astype(out_ref.dtype)


def finish(states, rows, columns):
    return pl.pallas_call(
        finish_kernel,
        out_shape=jax.ShapeDtypeStruct((rows, columns), jnp.bfloat16),
        in_specs=[VMEM] * len(states),
        out_specs=VMEM,
        compiler_params=params(),
        name="finish",
    )(*states)


def message_kernel(*refs):
    states, outs, held = refs[:4], refs[4:8], refs[8]
    rows = outs[0].shape[0] - 2 * 8
    columns = outs[0].shape[1]
    heads = columns // HEAD_DIM
    mine = lax.axis_index("head")
    for part in range(2):
        pair, (keep_ref, send_ref) = states[2 * part : 2 * part + 2], outs[2 * part : 2 * part + 2]
        logs = []
        for h in range(heads):
            maxima = [ref[columns + h : columns + h + 1] for ref in pair]
            totals = [ref[columns + heads + h : columns + heads + h + 1] for ref in pair]
            largest = jnp.maximum(*maxima)
            factors = [jnp.exp2((m - largest) * SCALE2) for m in maxima]
            total = factors[0] * totals[0] + factors[1] * totals[1]
            some = jnp.where(total > 0, total, 1.0)
            scale = [f / some for f in factors]
            own = head_columns(h)
            held[:, own] = (pair[0][own] * scale[0] + pair[1][own] * scale[1]).T.astype(held.dtype)
            left = jnp.where(total > 0, largest * SCALE2 + jnp.log2(some), LOWEST)
            for _ in range(3):
                summand = left.astype(held.dtype).astype(jnp.float32)
                logs.append(summand)
                left = left - summand
        logs = jnp.concatenate(logs + [jnp.zeros((2 * 8 - len(logs), held.shape[0]), jnp.float32)], axis=0)
        later = pltpu.roll(logs, rows, 1)
        for ref, which in ((send_ref, 1 - mine), (keep_ref, mine)):
            ref[:rows] = held[pl.ds(pl.multiple_of(which * rows, 2 * 8), rows), :]
            ref[rows:] = jnp.where(which == 0, logs, later).astype(ref.dtype)


def messages(mine, peers):
    rows, columns = mine[0].shape[1], mine[0].shape[0] // HEAD_DIM * HEAD_DIM
    shape = jax.ShapeDtypeStruct((rows // 2 + 2 * 8, columns), jnp.bfloat16)
    return pl.pallas_call(
        message_kernel,
        out_shape=[shape] * 4,
        in_specs=[VMEM] * 4,
        out_specs=[VMEM] * 4,
        scratch_shapes=[pltpu.VMEM((rows, columns), jnp.bfloat16)],
        compiler_params=params(),
        name="message",
    )(*mine, *peers)


def settle_kernel(*refs):
    parts, out_ref, logs = refs[:4], refs[4], refs[5]
    rows, columns = out_ref.shape[0], parts[0].shape[1]
    heads = columns // HEAD_DIM
    mine = lax.axis_index("head")
    logs[...] = jnp.zeros(logs.shape, jnp.float32)
    for i, ref in enumerate(parts):
        summands = ref[rows:].astype(jnp.float32)
        for h in range(heads):
            at = i * heads + h
            logs[at : at + 1] = functools.reduce(jnp.add, [summands[3 * h + n : 3 * h + n + 1] for n in range(3)])
    turned = logs[...].T[:rows]
    for side, base in ((0, 1 - mine), (1, mine)):
        for h in range(heads):
            both = [turned[:, at : at + 1] for at in (2 * side * heads + h, (2 * side + 1) * heads + h)]
            largest = jnp.maximum(*both)
            weights = [jnp.exp2(x - largest) for x in both]
            sums = [ref[:rows, head_columns(h)].astype(jnp.float32) for ref in parts[2 * side : 2 * side + 2]]
            total = weights[0] + weights[1]
            done = sums[0] * (weights[0] / total) + sums[1] * (weights[1] / total)
            at = pl.multiple_of(base * columns + h * HEAD_DIM, HEAD_DIM)
            out_ref[:, pl.ds(at, HEAD_DIM)] = done.astype(out_ref.dtype)


def settle(diagonal, beside, across, own):
    rows, columns = own.shape[0] - 2 * 8, own.shape[1]
    return pl.pallas_call(
        settle_kernel,
        out_shape=jax.ShapeDtypeStruct((rows, 2 * columns), own.dtype),
        in_specs=[VMEM] * 4,
        out_specs=VMEM,
        scratch_shapes=[pltpu.VMEM((TILE, columns), jnp.float32)],
        compiler_params=params(),
        name="settle",
    )(diagonal, beside, across, own)


def chip_pairs(mesh):
    places = [tuple(getattr(d, "coords", ())) for d in mesh.devices[:, 0]]
    count = len(places)
    if count % 4 or not places[0] or mesh.shape["head"] != 2:
        return False
    cores = all(places[i] == places[i + 1] for i in range(0, count, 2))
    level = all(places[i][2] == places[i + 3][2] for i in range(0, count, 4))
    climb = all(places[i][2] != places[i + 4][2] for i in range(0, count - 4))
    return cores and level and climb


def paired_shards(owner_count, queries, keys, values, image_tiles):
    rows, columns = queries.shape
    tiles = rows // TILE
    owners = range(owner_count)

    def flip(s):
        return 1 - 2 * ((s // 2) % 2)

    def core(s):
        return s % 2

    def moved(array, source, takes=lambda s: True):
        pairs = [(source(s), s) for s in owners if takes(s) and 0 <= source(s) < owner_count]
        return lax.ppermute(array, "seq", pairs)

    across = lambda s: s + 2 * flip(s)
    near_side = lambda s: s + 4 * flip(s)
    far_side = lambda s: s - 4 * flip(s)
    along = lambda s: s + 4 * flip(s) * (1 - 2 * core(s))
    against = lambda s: s - 4 * flip(s) * (1 - 2 * core(s))
    sibling = lambda s: s + 1 - 2 * core(s)
    inner = lambda s: core(s) == (1 - (s // 2) % 2)

    OWN = lambda s: s * tiles
    A1 = lambda s: along(s) * tiles
    B1 = lambda s: against(s) * tiles
    A2 = lambda s: (s + 8 * flip(s)) * tiles
    B2 = lambda s: jnp.where(inner(s), s - 8 * flip(s), -owner_count) * tiles

    peers = moved(queries, across)
    block = pack(keys, values)
    a1, b1 = moved(block, along), moved(block, against)
    level = (queries, moved(queries, sibling), peers, moved(peers, sibling))
    bounds, far = meta(lambda s: [s, sibling(s), across(s), sibling(across(s))], image_tiles, rows)
    fold = functools.partial(attend, bounds, level)
    states = fold([block], [OWN], [], which=[0, 1]) + fold([block], [OWN], [], which=[2, 3])
    states = fold([b1], [B1], states)

    def merge(blocks, places, states, shifts=None):
        beside, diagonal = fold(blocks, places, states, which=[1, 3], shifts=shifts)
        beside, diagonal = moved(beside, sibling), moved(diagonal, sibling)
        mine, peer = fold(blocks, places, states, which=[0, 2], shifts=shifts)
        keep, over_x, over_y, over_both = messages([mine, beside], [peer, diagonal])
        pairs = [(2 * across(s) + 1 - x, 2 * s + x) for s in owners for x in range(2)]
        over_both = lax.ppermute(over_both, ("seq", "head"), pairs)
        over_y = moved(over_y, across)
        over_x = lax.ppermute(over_x, "head", [(0, 1), (1, 0)])
        return settle(over_both, over_x, over_y, keep)

    def near_only(block, a1, b1, states):
        return merge([a1], [A1], states)

    def both_ways(block, a1, b1, states):
        near, corner = onward(a1, b1, block)
        a2, b2 = moved(near, near_side), moved(corner, far_side, inner)
        states = fold([a1], [A1], states)
        return merge([a2, b2], [A2, B2], states, [None, lambda s: 2 * TILE * core(s)])

    return lax.cond(far > 0, both_ways, near_only, block, a1, b1, states)


def ring_shards(owner_count, queries, keys, values, image_tiles):
    rows, columns = queries.shape
    tiles = rows // TILE
    reach = min(owner_count - 1, -(-(MOST_TILES - 1) // tiles))
    block = pack(keys, values)
    bounds, _ = meta(lambda s: [s], image_tiles, rows)
    fold = functools.partial(attend, bounds, (queries,))
    up = [(i, i + 1) for i in range(owner_count - 1)]
    down = [(i + 1, i) for i in range(owner_count - 1)]
    below = above = block
    states = []
    held, places = [block], [lambda s: s * tiles]
    for k in range(1, reach + 1):
        below = lax.ppermute(below, "seq", up)
        above = lax.ppermute(above, "seq", down)
        states = fold(held, places, states)
        held, places = [below, above], [lambda s, k=k: (s - k) * tiles, lambda s, k=k: (s + k) * tiles]
    attended = finish(fold(held, places, states), rows, columns)
    return lax.all_to_all(attended, "head", split_axis=0, concat_axis=1, tiled=True)


def solution(mesh):
    owner_count = mesh.shape["seq"]
    plan = paired_shards if chip_pairs(mesh) else ring_shards
    placed = (P("seq", "head"), P("seq", "head"), P("seq", "head"), P())
    return jax.shard_map(
        functools.partial(plan, owner_count),
        mesh=mesh,
        in_specs=placed,
        out_specs=P(("seq", "head"), None),
        check_vma=False,
    )
```

```python
import functools
import math

import jax
import jax.numpy as jnp
from jax import lax
from jax.experimental import pallas as pl
from jax.experimental.pallas import tpu as pltpu
from jax.sharding import PartitionSpec as P

HEAD_DIM = 128
TILE = 128
MOST_TILES = 21

LOWEST = -1e30
SCALE2 = math.log2(math.e) / math.sqrt(HEAD_DIM)
COST = 2

VMEM = pl.BlockSpec(memory_space=pltpu.VMEM)
SMEM = pl.BlockSpec(memory_space=pltpu.SMEM)
HBM = pl.BlockSpec(memory_space=pl.ANY)


def params():
    return pltpu.CompilerParams(vmem_limit_bytes=16 * 1024 * 1024)


def head_columns(h):
    return slice(h * HEAD_DIM, (h + 1) * HEAD_DIM)


def tile_rows(t):
    return slice(t * TILE, (t + 1) * TILE)


def image_bounds(tiles_ref, tile):
    first = jnp.int32(0)
    start, end = jnp.int32(0), jnp.int32(0)
    for i in range(tiles_ref.shape[0]):
        after = first + tiles_ref[i]
        inside = (tile >= first) & (tile < after)
        start = jnp.where(inside, first, start)
        end = jnp.where(inside, after, end)
        first = after
    return start, end


def meta_kernel(halves, tiles_ref, bounds_ref, far_ref):
    tiles = bounds_ref.shape[1] // TILE
    me = lax.axis_index("seq")
    bounds_ref[...] = jnp.zeros(bounds_ref.shape, jnp.int32)
    for half, owner in enumerate(halves(me)):
        for t in range(tiles):
            start, end = image_bounds(tiles_ref, owner * tiles + t)
            bounds_ref[2 * half : 2 * half + 1, tile_rows(t)] = jnp.full((1, TILE), start, jnp.int32)
            bounds_ref[2 * half + 1 : 2 * half + 2, tile_rows(t)] = jnp.full((1, TILE), end, jnp.int32)
    first = jnp.int32(0)
    far = jnp.int32(0)
    for i in range(tiles_ref.shape[0]):
        after = first + tiles_ref[i]
        levels = (after - 1) // (4 * tiles) - first // (4 * tiles)
        far = jnp.where(levels >= 2, 1, far)
        first = after
    far_ref[0] = far
    bounds_ref[8:9] = jnp.full((1, bounds_ref.shape[1]), far, jnp.int32)


def meta(halves, image_tiles, rows):
    bounds, far = pl.pallas_call(
        functools.partial(meta_kernel, halves),
        out_shape=[jax.ShapeDtypeStruct((16, rows), jnp.int32), jax.ShapeDtypeStruct((1,), jnp.int32)],
        in_specs=[SMEM],
        out_specs=[VMEM, SMEM],
        compiler_params=params(),
        cost_estimate=pl.CostEstimate(flops=COST * 2**28, bytes_accessed=0, transcendentals=0),
        name="meta",
    )(image_tiles)
    return bounds, far[0]


def pack_kernel(k_ref, v_ref, out_ref, held, sems):
    rows, columns = k_ref.shape
    tiles = rows // TILE
    copies = []
    for t in range(tiles):
        copies.append(pltpu.make_async_copy(v_ref.at[tile_rows(t)], held.at[tile_rows(t)], sems.at[2 * t]))
        copies.append(pltpu.make_async_copy(k_ref.at[tile_rows(t)], out_ref.at[tile_rows(2 * t)], sems.at[2 * t + 1]))
    for copy in copies:
        copy.start()
    for t in range(tiles):
        copies[2 * t].wait()
        for h in range(columns // HEAD_DIM):
            out_ref[tile_rows(2 * t + 1), head_columns(h)] = held[tile_rows(t), head_columns(h)].T
    for copy in copies[1::2]:
        copy.wait()


def pack(keys, values):
    rows, columns = keys.shape
    return pl.pallas_call(
        pack_kernel,
        out_shape=jax.ShapeDtypeStruct((2 * rows, columns), keys.dtype),
        in_specs=[HBM, HBM],
        out_specs=VMEM,
        scratch_shapes=[pltpu.VMEM(values.shape, values.dtype), pltpu.SemaphoreType.DMA((2 * rows // TILE,))],
        name="pack",
    )(keys, values)


def onward_kernel(a1_ref, b1_ref, own_ref, near_ref, corner_ref):
    upper = lax.axis_index("seq") % 2
    rows = corner_ref.shape[0]

    @pl.when(upper == 0)
    def _():
        near_ref[...] = a1_ref[...]
        corner_ref[...] = b1_ref[:rows]

    @pl.when(upper == 1)
    def _():
        near_ref[...] = b1_ref[...]
        corner_ref[...] = a1_ref[-rows:]


def onward(a1, b1, own):
    rows, columns = a1.shape
    return pl.pallas_call(
        onward_kernel,
        out_shape=[
            jax.ShapeDtypeStruct((rows, columns), a1.dtype),
            jax.ShapeDtypeStruct((rows - 2 * TILE, columns), a1.dtype),
        ],
        in_specs=[VMEM, VMEM, HBM],
        out_specs=[VMEM, VMEM],
        compiler_params=params(),
        name="onward",
    )(a1, b1, own)


def attend_kernel(which, places, arrays, fresh, unless_far, bounds_ref, *refs):
    halves = len(which)
    q_refs, refs = refs[:halves], refs[halves:]
    array_refs, refs = refs[: len(arrays)], refs[len(arrays) :]
    old_refs, refs = (None, refs) if fresh else (refs[:halves], refs[halves:])
    new_refs, (held_q, held, state) = refs[:halves], refs[halves:]
    rows, columns = q_refs[0].shape
    tiles = rows // TILE
    count = held.shape[1] // 2 // TILE
    heads = columns // HEAD_DIM
    me = lax.axis_index("seq")

    for half in range(halves):
        held_q[half] = q_refs[half][...]
        if fresh:
            state[half, :columns] = jnp.zeros((columns, rows), jnp.float32)
            state[half, columns : columns + heads] = jnp.full((heads, rows), LOWEST, jnp.float32)
            state[half, columns + heads :] = jnp.zeros((state.shape[1] - columns - heads, rows), jnp.float32)
        else:
            state[half] = old_refs[half][...]
    for slot, (array, shift) in enumerate(arrays):
        size = array_refs[array].shape[0]
        if size < held.shape[1]:
            held[slot] = jnp.zeros(held.shape[1:], held.dtype)
        at = 0 if shift is None else pl.multiple_of(shift(me), 2 * TILE)
        held[slot, pl.ds(at, size)] = array_refs[array][...]
    begins = [bounds_ref[2 * w, 0] for w in which]
    stops = [bounds_ref[2 * w + 1, rows - 1] for w in which]

    far = bounds_ref[8, 0] if unless_far else None

    def chosen(at, options):
        return functools.reduce(lambda x, i: jnp.where(at == i, options[i], x), range(1, len(options)), options[0])

    def fold(half, slot, first):
        row = 2 * (which[0] + half * (which[-1] - which[0]) // max(len(which) - 1, 1))
        low = bounds_ref[pl.ds(row, 1), :]
        high = bounds_ref[pl.ds(row + 1, 1), :]
        off = [
            jnp.where((first + j >= low) & (first + j < high), 0.0, -LOWEST).astype(jnp.float32)
            for j in range(count)
        ]
        maxima = [[state[half, pl.ds(columns + h, 1), tile_rows(t)] for t in range(tiles)] for h in range(heads)]
        totals = [state[half, pl.ds(columns + heads + h, 1), :] for h in range(heads)]
        scores = [
            lax.dot_general(
                jnp.concatenate([held[slot, tile_rows(2 * j), head_columns(h)] for j in range(count)], axis=0),
                held_q[half, :, head_columns(h)],
                (((1,), (1,)), ((), ())),
                preferred_element_type=jnp.float32,
            )
            for h in range(heads)
        ]
        factors, sums, updates, largest = [], [], [], []
        for h in range(heads):
            factor, rounded, total, new = [], [], [], []
            for t in range(tiles):
                lanes = tile_rows(t)
                parts = [scores[h][tile_rows(j), lanes] for j in range(count)]
                new_max = maxima[h][t]
                for j in range(count):
                    new_max = jnp.maximum(new_max, jnp.max(parts[j], axis=0, keepdims=True) - off[j][:, lanes])
                scaled = new_max * SCALE2
                weights = [jnp.exp2(parts[j] * SCALE2 - (scaled + off[j][:, lanes])) for j in range(count)]
                factor.append(jnp.exp2((maxima[h][t] - new_max) * SCALE2))
                total.append(jnp.sum(functools.reduce(jnp.add, weights), axis=0, keepdims=True))
                new.append(new_max)
                rounded.append(jnp.concatenate([w.astype(jnp.bfloat16) for w in weights], axis=0))
            updates.append(
                jnp.dot(
                    jnp.concatenate([held[slot, tile_rows(2 * j + 1), head_columns(h)] for j in range(count)], axis=1),
                    jnp.concatenate(rounded, axis=1),
                    preferred_element_type=jnp.float32,
                )
            )
            factors.append(jnp.concatenate(factor, axis=1))
            sums.append(jnp.concatenate(total, axis=1))
            largest.append(jnp.concatenate(new, axis=1))
        for h in range(heads):
            own = head_columns(h)
            state[half, own] = state[half, own] * factors[h] + updates[h]
            state[half, pl.ds(columns + h, 1), :] = largest[h]
            state[half, pl.ds(columns + heads + h, 1), :] = totals[h] * factors[h] + sums[h]

    @pl.loop(0, halves * len(places))
    def _(unit):
        half, slot = unit // len(places), unit % len(places)
        first = chosen(slot, [place(me) for place in places])

        if unless_far:
            first = jnp.where(far > 0, -count, first)

        @pl.when((first < chosen(half, stops)) & (first + count > chosen(half, begins)))
        def _():
            fold(half, slot, first)

    for half in range(halves):
        new_refs[half][...] = state[half]


def attend(bounds, queries, blocks, places, states, which=None, shifts=None, unless_far=False):
    which = list(range(len(queries))) if which is None else which
    queries, states = [queries[w] for w in which], [states[w] for w in which] if states else []
    halves = len(which)
    rows, columns = queries[0].shape
    depth = blocks[0].shape[0]
    heads = columns // HEAD_DIM
    shape = jax.ShapeDtypeStruct((columns + -(-2 * heads // 8) * 8, rows), jnp.float32)
    arrays = list(enumerate(shifts or [None] * len(blocks)))
    pairs = halves * (rows // TILE) * heads * len(blocks) * (depth // 2 // TILE)
    return pl.pallas_call(
        functools.partial(attend_kernel, which, places, arrays, not states, unless_far),
        out_shape=[shape] * halves,
        in_specs=[VMEM] * (1 + halves + len(blocks) + len(states)),
        out_specs=[VMEM] * halves,
        scratch_shapes=[
            pltpu.VMEM((halves, rows, columns), queries[0].dtype),
            pltpu.VMEM((len(blocks), depth, columns), blocks[0].dtype),
            pltpu.VMEM((halves,) + shape.shape, jnp.float32),
        ],
        compiler_params=params(),
        cost_estimate=pl.CostEstimate(
            flops=COST * pairs * 4 * TILE * TILE * HEAD_DIM,
            bytes_accessed=2 * len(blocks) * depth * columns + 4 * halves * rows * columns,
            transcendentals=pairs * TILE * TILE,
        ),
        name="attend",
    )(bounds, *queries, *blocks, *states)


def merged(states, columns):
    heads = columns // HEAD_DIM
    for h in range(heads):
        maxima = [ref[columns + h : columns + h + 1] for ref in states]
        totals = [ref[columns + heads + h : columns + heads + h + 1] for ref in states]
        largest = functools.reduce(jnp.maximum, maxima)
        factors = [jnp.exp2((m - largest) * SCALE2) for m in maxima]
        total = functools.reduce(jnp.add, [f * t for f, t in zip(factors, totals)])
        parts = [ref[head_columns(h)] * (f / total) for ref, f in zip(states, factors)]
        yield head_columns(h), functools.reduce(jnp.add, parts).T


def finish_kernel(*refs):
    out_ref = refs[-1]
    for own, done in merged(refs[:-1], out_ref.shape[1]):
        out_ref[:, own] = done.astype(out_ref.dtype)


def finish(states, rows, columns):
    return pl.pallas_call(
        finish_kernel,
        out_shape=jax.ShapeDtypeStruct((rows, columns), jnp.bfloat16),
        in_specs=[VMEM] * len(states),
        out_specs=VMEM,
        compiler_params=params(),
        name="finish",
    )(*states)


def message_kernel(*refs):
    states, outs, held = refs[:4], refs[4:8], refs[8]
    rows = outs[0].shape[0] - 2 * 8
    columns = outs[0].shape[1]
    heads = columns // HEAD_DIM
    mine = lax.axis_index("head")
    for part in range(2):
        pair, (keep_ref, send_ref) = states[2 * part : 2 * part + 2], outs[2 * part : 2 * part + 2]
        logs = []
        for h in range(heads):
            maxima = [ref[columns + h : columns + h + 1] for ref in pair]
            totals = [ref[columns + heads + h : columns + heads + h + 1] for ref in pair]
            largest = jnp.maximum(*maxima)
            factors = [jnp.exp2((m - largest) * SCALE2) for m in maxima]
            total = factors[0] * totals[0] + factors[1] * totals[1]
            some = jnp.where(total > 0, total, 1.0)
            scale = [f / some for f in factors]
            own = head_columns(h)
            held[:, own] = (pair[0][own] * scale[0] + pair[1][own] * scale[1]).T.astype(held.dtype)
            left = jnp.where(total > 0, largest * SCALE2 + jnp.log2(some), LOWEST)
            for _ in range(3):
                summand = left.astype(held.dtype).astype(jnp.float32)
                logs.append(summand)
                left = left - summand
        logs = jnp.concatenate(logs + [jnp.zeros((2 * 8 - len(logs), held.shape[0]), jnp.float32)], axis=0)
        later = pltpu.roll(logs, rows, 1)
        for ref, which in ((send_ref, 1 - mine), (keep_ref, mine)):
            ref[:rows] = held[pl.ds(pl.multiple_of(which * rows, 2 * 8), rows), :]
            ref[rows:] = jnp.where(which == 0, logs, later).astype(ref.dtype)


def messages(mine, peers):
    rows, columns = mine[0].shape[1], mine[0].shape[0] // HEAD_DIM * HEAD_DIM
    shape = jax.ShapeDtypeStruct((rows // 2 + 2 * 8, columns), jnp.bfloat16)
    return pl.pallas_call(
        message_kernel,
        out_shape=[shape] * 4,
        in_specs=[VMEM] * 4,
        out_specs=[VMEM] * 4,
        scratch_shapes=[pltpu.VMEM((rows, columns), jnp.bfloat16)],
        compiler_params=params(),
        name="message",
    )(*mine, *peers)


def settle_kernel(*refs):
    parts, out_ref, logs = refs[:4], refs[4], refs[5]
    rows, columns = out_ref.shape[0], parts[0].shape[1]
    heads = columns // HEAD_DIM
    mine = lax.axis_index("head")
    logs[...] = jnp.zeros(logs.shape, jnp.float32)
    for i, ref in enumerate(parts):
        summands = ref[rows:].astype(jnp.float32)
        for h in range(heads):
            at = i * heads + h
            logs[at : at + 1] = functools.reduce(jnp.add, [summands[3 * h + n : 3 * h + n + 1] for n in range(3)])
    turned = logs[...].T[:rows]
    for side, base in ((0, 1 - mine), (1, mine)):
        for h in range(heads):
            both = [turned[:, at : at + 1] for at in (2 * side * heads + h, (2 * side + 1) * heads + h)]
            largest = jnp.maximum(*both)
            weights = [jnp.exp2(x - largest) for x in both]
            sums = [ref[:rows, head_columns(h)].astype(jnp.float32) for ref in parts[2 * side : 2 * side + 2]]
            total = weights[0] + weights[1]
            done = sums[0] * (weights[0] / total) + sums[1] * (weights[1] / total)
            at = pl.multiple_of(base * columns + h * HEAD_DIM, HEAD_DIM)
            out_ref[:, pl.ds(at, HEAD_DIM)] = done.astype(out_ref.dtype)


def settle(diagonal, beside, across, own):
    rows, columns = own.shape[0] - 2 * 8, own.shape[1]
    return pl.pallas_call(
        settle_kernel,
        out_shape=jax.ShapeDtypeStruct((rows, 2 * columns), own.dtype),
        in_specs=[VMEM] * 4,
        out_specs=VMEM,
        scratch_shapes=[pltpu.VMEM((TILE, columns), jnp.float32)],
        compiler_params=params(),
        name="settle",
    )(diagonal, beside, across, own)


def chip_pairs(mesh):
    places = [tuple(getattr(d, "coords", ())) for d in mesh.devices[:, 0]]
    count = len(places)
    if count % 4 or not places[0] or mesh.shape["head"] != 2:
        return False
    cores = all(places[i] == places[i + 1] for i in range(0, count, 2))
    level = all(places[i][2] == places[i + 3][2] for i in range(0, count, 4))
    climb = all(places[i][2] != places[i + 4][2] for i in range(0, count - 4))
    return cores and level and climb


def paired_shards(owner_count, queries, keys, values, image_tiles):
    rows, columns = queries.shape
    tiles = rows // TILE
    owners = range(owner_count)

    def flip(s):
        return 1 - 2 * ((s // 2) % 2)

    def core(s):
        return s % 2

    def moved(array, source, takes=lambda s: True):
        pairs = [(source(s), s) for s in owners if takes(s) and 0 <= source(s) < owner_count]
        return lax.ppermute(array, "seq", pairs)

    across = lambda s: s + 2 * flip(s)
    near_side = lambda s: s + 4 * flip(s)
    far_side = lambda s: s - 4 * flip(s)
    along = lambda s: s + 4 * flip(s) * (1 - 2 * core(s))
    against = lambda s: s - 4 * flip(s) * (1 - 2 * core(s))
    sibling = lambda s: s + 1 - 2 * core(s)
    inner = lambda s: core(s) == (1 - (s // 2) % 2)

    OWN = lambda s: s * tiles
    A1 = lambda s: along(s) * tiles
    B1 = lambda s: against(s) * tiles
    A2 = lambda s: (s + 8 * flip(s)) * tiles
    B2 = lambda s: jnp.where(inner(s), s - 8 * flip(s), -owner_count) * tiles

    peers = moved(queries, across)
    block = pack(keys, values)
    a1, b1 = moved(block, along), moved(block, against)
    level = (queries, moved(queries, sibling), peers, moved(peers, sibling))
    bounds, far = meta(lambda s: [s, sibling(s), across(s), sibling(across(s))], image_tiles, rows)
    fold = functools.partial(attend, bounds, level)
    states = fold([block], [OWN], [], which=[0, 1]) + fold([block], [OWN], [], which=[2, 3])
    states = fold([b1], [B1], states, unless_far=True)

    def merge(blocks, places, states, shifts=None):
        beside, diagonal = fold(blocks, places, states, which=[1, 3], shifts=shifts)
        beside, diagonal = moved(beside, sibling), moved(diagonal, sibling)
        mine, peer = fold(blocks, places, states, which=[0, 2], shifts=shifts)
        keep, over_x, over_y, over_both = messages([mine, beside], [peer, diagonal])
        pairs = [(2 * across(s) + 1 - x, 2 * s + x) for s in owners for x in range(2)]
        over_both = lax.ppermute(over_both, ("seq", "head"), pairs)
        over_y = moved(over_y, across)
        over_x = lax.ppermute(over_x, "head", [(0, 1), (1, 0)])
        return settle(over_both, over_x, over_y, keep)

    def near_only(block, a1, b1, states):
        return merge([a1], [A1], states)

    def both_ways(block, a1, b1, states):
        near, corner = onward(a1, b1, block)
        a2, b2 = moved(near, near_side), moved(corner, far_side, inner)
        states = fold([a1, b1], [A1, B1], states)
        return merge([a2, b2], [A2, B2], states, [None, lambda s: 2 * TILE * core(s)])

    return lax.cond(far > 0, both_ways, near_only, block, a1, b1, states)


def ring_shards(owner_count, queries, keys, values, image_tiles):
    rows, columns = queries.shape
    tiles = rows // TILE
    reach = min(owner_count - 1, -(-(MOST_TILES - 1) // tiles))
    block = pack(keys, values)
    bounds, _ = meta(lambda s: [s], image_tiles, rows)
    fold = functools.partial(attend, bounds, (queries,))
    up = [(i, i + 1) for i in range(owner_count - 1)]
    down = [(i + 1, i) for i in range(owner_count - 1)]
    below = above = block
    states = []
    held, places = [block], [lambda s: s * tiles]
    for k in range(1, reach + 1):
        below = lax.ppermute(below, "seq", up)
        above = lax.ppermute(above, "seq", down)
        states = fold(held, places, states)
        held, places = [below, above], [lambda s, k=k: (s - k) * tiles, lambda s, k=k: (s + k) * tiles]
    attended = finish(fold(held, places, states), rows, columns)
    return lax.all_to_all(attended, "head", split_axis=0, concat_axis=1, tiled=True)


def solution(mesh):
    owner_count = mesh.shape["seq"]
    plan = paired_shards if chip_pairs(mesh) else ring_shards
    placed = (P("seq", "head"), P("seq", "head"), P("seq", "head"), P())
    return jax.shard_map(
        functools.partial(plan, owner_count),
        mesh=mesh,
        in_specs=placed,
        out_specs=P(("seq", "head"), None),
        check_vma=False,
    )
```

```python
import functools
import math

import jax
import jax.numpy as jnp
from jax import lax
from jax.experimental import pallas as pl
from jax.experimental.pallas import tpu as pltpu
from jax.sharding import PartitionSpec as P

HEAD_DIM = 128
TILE = 128
MOST_TILES = 21

LOWEST = -1e30
SCALE2 = math.log2(math.e) / math.sqrt(HEAD_DIM)
COST = 1

VMEM = pl.BlockSpec(memory_space=pltpu.VMEM)
SMEM = pl.BlockSpec(memory_space=pltpu.SMEM)
HBM = pl.BlockSpec(memory_space=pl.ANY)


def params():
    return pltpu.CompilerParams(vmem_limit_bytes=16 * 1024 * 1024)


def head_columns(h):
    return slice(h * HEAD_DIM, (h + 1) * HEAD_DIM)


def tile_rows(t):
    return slice(t * TILE, (t + 1) * TILE)


def image_bounds(tiles_ref, tile):
    first = jnp.int32(0)
    start, end = jnp.int32(0), jnp.int32(0)
    for i in range(tiles_ref.shape[0]):
        after = first + tiles_ref[i]
        inside = (tile >= first) & (tile < after)
        start = jnp.where(inside, first, start)
        end = jnp.where(inside, after, end)
        first = after
    return start, end


def meta_kernel(halves, tiles_ref, bounds_ref, far_ref):
    tiles = bounds_ref.shape[1] // TILE
    me = lax.axis_index("seq")
    bounds_ref[...] = jnp.zeros(bounds_ref.shape, jnp.int32)
    for half, owner in enumerate(halves(me)):
        for t in range(tiles):
            start, end = image_bounds(tiles_ref, owner * tiles + t)
            bounds_ref[2 * half : 2 * half + 1, tile_rows(t)] = jnp.full((1, TILE), start, jnp.int32)
            bounds_ref[2 * half + 1 : 2 * half + 2, tile_rows(t)] = jnp.full((1, TILE), end, jnp.int32)
    first = jnp.int32(0)
    far = jnp.int32(0)
    for i in range(tiles_ref.shape[0]):
        after = first + tiles_ref[i]
        levels = (after - 1) // (4 * tiles) - first // (4 * tiles)
        far = jnp.where(levels >= 2, 1, far)
        first = after
    far_ref[0] = far
    bounds_ref[8:9] = jnp.full((1, bounds_ref.shape[1]), far, jnp.int32)


def meta(halves, image_tiles, rows):
    bounds, far = pl.pallas_call(
        functools.partial(meta_kernel, halves),
        out_shape=[jax.ShapeDtypeStruct((16, rows), jnp.int32), jax.ShapeDtypeStruct((1,), jnp.int32)],
        in_specs=[SMEM],
        out_specs=[VMEM, SMEM],
        compiler_params=params(),
        cost_estimate=pl.CostEstimate(flops=COST * 2**28, bytes_accessed=0, transcendentals=0),
        name="meta",
    )(image_tiles)
    return bounds, far[0]


def pack_kernel(k_ref, v_ref, out_ref, held, sems):
    rows, columns = k_ref.shape
    tiles = rows // TILE
    copies = []
    for t in range(tiles):
        copies.append(pltpu.make_async_copy(v_ref.at[tile_rows(t)], held.at[tile_rows(t)], sems.at[2 * t]))
        copies.append(pltpu.make_async_copy(k_ref.at[tile_rows(t)], out_ref.at[tile_rows(2 * t)], sems.at[2 * t + 1]))
    for copy in copies:
        copy.start()
    for t in range(tiles):
        copies[2 * t].wait()
        for h in range(columns // HEAD_DIM):
            out_ref[tile_rows(2 * t + 1), head_columns(h)] = held[tile_rows(t), head_columns(h)].T
    for copy in copies[1::2]:
        copy.wait()


def pack(keys, values):
    rows, columns = keys.shape
    return pl.pallas_call(
        pack_kernel,
        out_shape=jax.ShapeDtypeStruct((2 * rows, columns), keys.dtype),
        in_specs=[HBM, HBM],
        out_specs=VMEM,
        scratch_shapes=[pltpu.VMEM(values.shape, values.dtype), pltpu.SemaphoreType.DMA((2 * rows // TILE,))],
        name="pack",
    )(keys, values)


def onward_kernel(a1_ref, b1_ref, own_ref, near_ref, corner_ref):
    upper = lax.axis_index("seq") % 2
    rows = corner_ref.shape[0]

    @pl.when(upper == 0)
    def _():
        near_ref[...] = a1_ref[...]
        corner_ref[...] = b1_ref[:rows]

    @pl.when(upper == 1)
    def _():
        near_ref[...] = b1_ref[...]
        corner_ref[...] = a1_ref[-rows:]


def onward(a1, b1, own):
    rows, columns = a1.shape
    return pl.pallas_call(
        onward_kernel,
        out_shape=[
            jax.ShapeDtypeStruct((rows, columns), a1.dtype),
            jax.ShapeDtypeStruct((rows - 2 * TILE, columns), a1.dtype),
        ],
        in_specs=[VMEM, VMEM, HBM],
        out_specs=[VMEM, VMEM],
        compiler_params=params(),
        name="onward",
    )(a1, b1, own)


def attend_kernel(which, places, arrays, fresh, unless_far, bounds_ref, *refs):
    halves = len(which)
    q_refs, refs = refs[:halves], refs[halves:]
    array_refs, refs = refs[: len(arrays)], refs[len(arrays) :]
    old_refs, refs = (None, refs) if fresh else (refs[:halves], refs[halves:])
    new_refs, (held_q, held, state) = refs[:halves], refs[halves:]
    rows, columns = q_refs[0].shape
    tiles = rows // TILE
    count = held.shape[1] // 2 // TILE
    heads = columns // HEAD_DIM
    me = lax.axis_index("seq")

    for half in range(halves):
        held_q[half] = q_refs[half][...]
        if fresh:
            state[half, :columns] = jnp.zeros((columns, rows), jnp.float32)
            state[half, columns : columns + heads] = jnp.full((heads, rows), LOWEST, jnp.float32)
            state[half, columns + heads :] = jnp.zeros((state.shape[1] - columns - heads, rows), jnp.float32)
        else:
            state[half] = old_refs[half][...]
    for slot, (array, shift) in enumerate(arrays):
        size = array_refs[array].shape[0]
        if size < held.shape[1]:
            held[slot] = jnp.zeros(held.shape[1:], held.dtype)
        at = 0 if shift is None else pl.multiple_of(shift(me), 2 * TILE)
        held[slot, pl.ds(at, size)] = array_refs[array][...]
    begins = [bounds_ref[2 * w, 0] for w in which]
    stops = [bounds_ref[2 * w + 1, rows - 1] for w in which]

    far = bounds_ref[8, 0] if unless_far else None

    def chosen(at, options):
        return functools.reduce(lambda x, i: jnp.where(at == i, options[i], x), range(1, len(options)), options[0])

    def fold(half, slot, first):
        row = 2 * (which[0] + half * (which[-1] - which[0]) // max(len(which) - 1, 1))
        low = bounds_ref[pl.ds(row, 1), :]
        high = bounds_ref[pl.ds(row + 1, 1), :]
        off = [
            jnp.where((first + j >= low) & (first + j < high), 0.0, -LOWEST).astype(jnp.float32)
            for j in range(count)
        ]
        maxima = [[state[half, pl.ds(columns + h, 1), tile_rows(t)] for t in range(tiles)] for h in range(heads)]
        totals = [state[half, pl.ds(columns + heads + h, 1), :] for h in range(heads)]
        scores = [
            lax.dot_general(
                jnp.concatenate([held[slot, tile_rows(2 * j), head_columns(h)] for j in range(count)], axis=0),
                held_q[half, :, head_columns(h)],
                (((1,), (1,)), ((), ())),
                preferred_element_type=jnp.float32,
            )
            for h in range(heads)
        ]
        factors, sums, updates, largest = [], [], [], []
        for h in range(heads):
            factor, rounded, total, new = [], [], [], []
            for t in range(tiles):
                lanes = tile_rows(t)
                parts = [scores[h][tile_rows(j), lanes] for j in range(count)]
                new_max = maxima[h][t]
                for j in range(count):
                    new_max = jnp.maximum(new_max, jnp.max(parts[j], axis=0, keepdims=True) - off[j][:, lanes])
                scaled = new_max * SCALE2
                weights = [jnp.exp2(parts[j] * SCALE2 - (scaled + off[j][:, lanes])) for j in range(count)]
                factor.append(jnp.exp2((maxima[h][t] - new_max) * SCALE2))
                total.append(jnp.sum(functools.reduce(jnp.add, weights), axis=0, keepdims=True))
                new.append(new_max)
                rounded.append(jnp.concatenate([w.astype(jnp.bfloat16) for w in weights], axis=0))
            updates.append(
                jnp.dot(
                    jnp.concatenate([held[slot, tile_rows(2 * j + 1), head_columns(h)] for j in range(count)], axis=1),
                    jnp.concatenate(rounded, axis=1),
                    preferred_element_type=jnp.float32,
                )
            )
            factors.append(jnp.concatenate(factor, axis=1))
            sums.append(jnp.concatenate(total, axis=1))
            largest.append(jnp.concatenate(new, axis=1))
        for h in range(heads):
            own = head_columns(h)
            state[half, own] = state[half, own] * factors[h] + updates[h]
            state[half, pl.ds(columns + h, 1), :] = largest[h]
            state[half, pl.ds(columns + heads + h, 1), :] = totals[h] * factors[h] + sums[h]

    @pl.loop(0, halves * len(places))
    def _(unit):
        half, slot = unit // len(places), unit % len(places)
        first = chosen(slot, [place(me) for place in places])

        if unless_far:
            first = jnp.where(far > 0, -count, first)

        @pl.when((first < chosen(half, stops)) & (first + count > chosen(half, begins)))
        def _():
            fold(half, slot, first)

    for half in range(halves):
        new_refs[half][...] = state[half]


def attend(bounds, queries, blocks, places, states, which=None, shifts=None, unless_far=False):
    which = list(range(len(queries))) if which is None else which
    queries, states = [queries[w] for w in which], [states[w] for w in which] if states else []
    halves = len(which)
    rows, columns = queries[0].shape
    depth = blocks[0].shape[0]
    heads = columns // HEAD_DIM
    shape = jax.ShapeDtypeStruct((columns + -(-2 * heads // 8) * 8, rows), jnp.float32)
    arrays = list(enumerate(shifts or [None] * len(blocks)))
    pairs = halves * (rows // TILE) * heads * len(blocks) * (depth // 2 // TILE)
    return pl.pallas_call(
        functools.partial(attend_kernel, which, places, arrays, not states, unless_far),
        out_shape=[shape] * halves,
        in_specs=[VMEM] * (1 + halves + len(blocks) + len(states)),
        out_specs=[VMEM] * halves,
        scratch_shapes=[
            pltpu.VMEM((halves, rows, columns), queries[0].dtype),
            pltpu.VMEM((len(blocks), depth, columns), blocks[0].dtype),
            pltpu.VMEM((halves,) + shape.shape, jnp.float32),
        ],
        compiler_params=params(),
        cost_estimate=pl.CostEstimate(
            flops=COST * pairs * 4 * TILE * TILE * HEAD_DIM,
            bytes_accessed=2 * len(blocks) * depth * columns + 4 * halves * rows * columns,
            transcendentals=pairs * TILE * TILE,
        ),
        name="attend",
    )(bounds, *queries, *blocks, *states)


def merged(states, columns):
    heads = columns // HEAD_DIM
    for h in range(heads):
        maxima = [ref[columns + h : columns + h + 1] for ref in states]
        totals = [ref[columns + heads + h : columns + heads + h + 1] for ref in states]
        largest = functools.reduce(jnp.maximum, maxima)
        factors = [jnp.exp2((m - largest) * SCALE2) for m in maxima]
        total = functools.reduce(jnp.add, [f * t for f, t in zip(factors, totals)])
        parts = [ref[head_columns(h)] * (f / total) for ref, f in zip(states, factors)]
        yield head_columns(h), functools.reduce(jnp.add, parts).T


def finish_kernel(*refs):
    out_ref = refs[-1]
    for own, done in merged(refs[:-1], out_ref.shape[1]):
        out_ref[:, own] = done.astype(out_ref.dtype)


def finish(states, rows, columns):
    return pl.pallas_call(
        finish_kernel,
        out_shape=jax.ShapeDtypeStruct((rows, columns), jnp.bfloat16),
        in_specs=[VMEM] * len(states),
        out_specs=VMEM,
        compiler_params=params(),
        name="finish",
    )(*states)


def message_kernel(*refs):
    states, outs, held = refs[:4], refs[4:8], refs[8]
    rows = outs[0].shape[0] - 2 * 8
    columns = outs[0].shape[1]
    heads = columns // HEAD_DIM
    mine = lax.axis_index("head")
    for part in range(2):
        pair, (keep_ref, send_ref) = states[2 * part : 2 * part + 2], outs[2 * part : 2 * part + 2]
        logs = []
        for h in range(heads):
            maxima = [ref[columns + h : columns + h + 1] for ref in pair]
            totals = [ref[columns + heads + h : columns + heads + h + 1] for ref in pair]
            largest = jnp.maximum(*maxima)
            factors = [jnp.exp2((m - largest) * SCALE2) for m in maxima]
            total = factors[0] * totals[0] + factors[1] * totals[1]
            some = jnp.where(total > 0, total, 1.0)
            scale = [f / some for f in factors]
            own = head_columns(h)
            held[:, own] = (pair[0][own] * scale[0] + pair[1][own] * scale[1]).T.astype(held.dtype)
            left = jnp.where(total > 0, largest * SCALE2 + jnp.log2(some), LOWEST)
            for _ in range(3):
                summand = left.astype(held.dtype).astype(jnp.float32)
                logs.append(summand)
                left = left - summand
        logs = jnp.concatenate(logs + [jnp.zeros((2 * 8 - len(logs), held.shape[0]), jnp.float32)], axis=0)
        later = pltpu.roll(logs, rows, 1)
        for ref, which in ((send_ref, 1 - mine), (keep_ref, mine)):
            ref[:rows] = held[pl.ds(pl.multiple_of(which * rows, 2 * 8), rows), :]
            ref[rows:] = jnp.where(which == 0, logs, later).astype(ref.dtype)


def messages(mine, peers):
    rows, columns = mine[0].shape[1], mine[0].shape[0] // HEAD_DIM * HEAD_DIM
    shape = jax.ShapeDtypeStruct((rows // 2 + 2 * 8, columns), jnp.bfloat16)
    return pl.pallas_call(
        message_kernel,
        out_shape=[shape] * 4,
        in_specs=[VMEM] * 4,
        out_specs=[VMEM] * 4,
        scratch_shapes=[pltpu.VMEM((rows, columns), jnp.bfloat16)],
        compiler_params=params(),
        name="message",
    )(*mine, *peers)


def settle_kernel(*refs):
    parts, out_ref, logs = refs[:4], refs[4], refs[5]
    rows, columns = out_ref.shape[0], parts[0].shape[1]
    heads = columns // HEAD_DIM
    mine = lax.axis_index("head")
    logs[...] = jnp.zeros(logs.shape, jnp.float32)
    for i, ref in enumerate(parts):
        summands = ref[rows:].astype(jnp.float32)
        for h in range(heads):
            at = i * heads + h
            logs[at : at + 1] = functools.reduce(jnp.add, [summands[3 * h + n : 3 * h + n + 1] for n in range(3)])
    turned = logs[...].T[:rows]
    for side, base in ((0, 1 - mine), (1, mine)):
        for h in range(heads):
            both = [turned[:, at : at + 1] for at in (2 * side * heads + h, (2 * side + 1) * heads + h)]
            largest = jnp.maximum(*both)
            weights = [jnp.exp2(x - largest) for x in both]
            sums = [ref[:rows, head_columns(h)].astype(jnp.float32) for ref in parts[2 * side : 2 * side + 2]]
            total = weights[0] + weights[1]
            done = sums[0] * (weights[0] / total) + sums[1] * (weights[1] / total)
            at = pl.multiple_of(base * columns + h * HEAD_DIM, HEAD_DIM)
            out_ref[:, pl.ds(at, HEAD_DIM)] = done.astype(out_ref.dtype)


def settle(diagonal, beside, across, own):
    rows, columns = own.shape[0] - 2 * 8, own.shape[1]
    return pl.pallas_call(
        settle_kernel,
        out_shape=jax.ShapeDtypeStruct((rows, 2 * columns), own.dtype),
        in_specs=[VMEM] * 4,
        out_specs=VMEM,
        scratch_shapes=[pltpu.VMEM((TILE, columns), jnp.float32)],
        compiler_params=params(),
        name="settle",
    )(diagonal, beside, across, own)


def chip_pairs(mesh):
    places = [tuple(getattr(d, "coords", ())) for d in mesh.devices[:, 0]]
    count = len(places)
    if count % 4 or not places[0] or mesh.shape["head"] != 2:
        return False
    cores = all(places[i] == places[i + 1] for i in range(0, count, 2))
    level = all(places[i][2] == places[i + 3][2] for i in range(0, count, 4))
    climb = all(places[i][2] != places[i + 4][2] for i in range(0, count - 4))
    return cores and level and climb


def paired_shards(owner_count, queries, keys, values, image_tiles):
    rows, columns = queries.shape
    tiles = rows // TILE
    owners = range(owner_count)

    def flip(s):
        return 1 - 2 * ((s // 2) % 2)

    def core(s):
        return s % 2

    def moved(array, source, takes=lambda s: True):
        pairs = [(source(s), s) for s in owners if takes(s) and 0 <= source(s) < owner_count]
        return lax.ppermute(array, "seq", pairs)

    across = lambda s: s + 2 * flip(s)
    near_side = lambda s: s + 4 * flip(s)
    far_side = lambda s: s - 4 * flip(s)
    along = lambda s: s + 4 * flip(s) * (1 - 2 * core(s))
    against = lambda s: s - 4 * flip(s) * (1 - 2 * core(s))
    sibling = lambda s: s + 1 - 2 * core(s)
    inner = lambda s: core(s) == (1 - (s // 2) % 2)

    OWN = lambda s: s * tiles
    A1 = lambda s: along(s) * tiles
    B1 = lambda s: against(s) * tiles
    A2 = lambda s: (s + 8 * flip(s)) * tiles
    B2 = lambda s: jnp.where(inner(s), s - 8 * flip(s), -owner_count) * tiles

    peers = moved(queries, across)
    block = pack(keys, values)
    a1, b1 = moved(block, along), moved(block, against)
    level = (queries, moved(queries, sibling), peers, moved(peers, sibling))
    bounds, far = meta(lambda s: [s, sibling(s), across(s), sibling(across(s))], image_tiles, rows)
    fold = functools.partial(attend, bounds, level)
    states = fold([block], [OWN], [], which=[0, 1]) + fold([block], [OWN], [], which=[2, 3])
    states = fold([b1], [B1], states, unless_far=True)

    def merge(blocks, places, states, shifts=None):
        beside, diagonal = fold(blocks, places, states, which=[1, 3], shifts=shifts)
        beside, diagonal = moved(beside, sibling), moved(diagonal, sibling)
        mine, peer = fold(blocks, places, states, which=[0, 2], shifts=shifts)
        keep, over_x, over_y, over_both = messages([mine, beside], [peer, diagonal])
        pairs = [(2 * across(s) + 1 - x, 2 * s + x) for s in owners for x in range(2)]
        over_both = lax.ppermute(over_both, ("seq", "head"), pairs)
        over_y = moved(over_y, across)
        over_x = lax.ppermute(over_x, "head", [(0, 1), (1, 0)])
        return settle(over_both, over_x, over_y, keep)

    def near_only(block, a1, b1, states):
        return merge([a1], [A1], states)

    def both_ways(block, a1, b1, states):
        near, corner = onward(a1, b1, block)
        a2, b2 = moved(near, near_side), moved(corner, far_side, inner)
        states = fold([a1, b1], [A1, B1], states)
        return merge([a2, b2], [A2, B2], states, [None, lambda s: 2 * TILE * core(s)])

    return lax.cond(far > 0, both_ways, near_only, block, a1, b1, states)


def ring_shards(owner_count, queries, keys, values, image_tiles):
    rows, columns = queries.shape
    tiles = rows // TILE
    reach = min(owner_count - 1, -(-(MOST_TILES - 1) // tiles))
    block = pack(keys, values)
    bounds, _ = meta(lambda s: [s], image_tiles, rows)
    fold = functools.partial(attend, bounds, (queries,))
    up = [(i, i + 1) for i in range(owner_count - 1)]
    down = [(i + 1, i) for i in range(owner_count - 1)]
    below = above = block
    states = []
    held, places = [block], [lambda s: s * tiles]
    for k in range(1, reach + 1):
        below = lax.ppermute(below, "seq", up)
        above = lax.ppermute(above, "seq", down)
        states = fold(held, places, states)
        held, places = [below, above], [lambda s, k=k: (s - k) * tiles, lambda s, k=k: (s + k) * tiles]
    attended = finish(fold(held, places, states), rows, columns)
    return lax.all_to_all(attended, "head", split_axis=0, concat_axis=1, tiled=True)


def solution(mesh):
    owner_count = mesh.shape["seq"]
    plan = paired_shards if chip_pairs(mesh) else ring_shards
    placed = (P("seq", "head"), P("seq", "head"), P("seq", "head"), P())
    return jax.shard_map(
        functools.partial(plan, owner_count),
        mesh=mesh,
        in_specs=placed,
        out_specs=P(("seq", "head"), None),
        check_vma=False,
    )
```

```python
import functools
import math

import jax
import jax.numpy as jnp
from jax import lax
from jax.experimental import pallas as pl
from jax.experimental.pallas import tpu as pltpu
from jax.sharding import PartitionSpec as P

HEAD_DIM = 128
TILE = 128
MOST_TILES = 21

LOWEST = -1e30
SCALE2 = math.log2(math.e) / math.sqrt(HEAD_DIM)
COST = 1

VMEM = pl.BlockSpec(memory_space=pltpu.VMEM)
SMEM = pl.BlockSpec(memory_space=pltpu.SMEM)
HBM = pl.BlockSpec(memory_space=pl.ANY)


def params():
    return pltpu.CompilerParams(vmem_limit_bytes=16 * 1024 * 1024)


def head_columns(h):
    return slice(h * HEAD_DIM, (h + 1) * HEAD_DIM)


def tile_rows(t):
    return slice(t * TILE, (t + 1) * TILE)


def image_bounds(tiles_ref, tile):
    first = jnp.int32(0)
    start, end = jnp.int32(0), jnp.int32(0)
    for i in range(tiles_ref.shape[0]):
        after = first + tiles_ref[i]
        inside = (tile >= first) & (tile < after)
        start = jnp.where(inside, first, start)
        end = jnp.where(inside, after, end)
        first = after
    return start, end


def meta_kernel(halves, tiles_ref, bounds_ref, far_ref):
    tiles = bounds_ref.shape[1] // TILE
    me = lax.axis_index("seq")
    bounds_ref[...] = jnp.zeros(bounds_ref.shape, jnp.int32)
    for half, owner in enumerate(halves(me)):
        for t in range(tiles):
            start, end = image_bounds(tiles_ref, owner * tiles + t)
            bounds_ref[2 * half : 2 * half + 1, tile_rows(t)] = jnp.full((1, TILE), start, jnp.int32)
            bounds_ref[2 * half + 1 : 2 * half + 2, tile_rows(t)] = jnp.full((1, TILE), end, jnp.int32)
    first = jnp.int32(0)
    far = jnp.int32(0)
    for i in range(tiles_ref.shape[0]):
        after = first + tiles_ref[i]
        levels = (after - 1) // (4 * tiles) - first // (4 * tiles)
        far = jnp.where(levels >= 2, 1, far)
        first = after
    far_ref[0] = far
    bounds_ref[8:9] = jnp.full((1, bounds_ref.shape[1]), far, jnp.int32)


def meta(halves, image_tiles, rows):
    bounds, far = pl.pallas_call(
        functools.partial(meta_kernel, halves),
        out_shape=[jax.ShapeDtypeStruct((16, rows), jnp.int32), jax.ShapeDtypeStruct((1,), jnp.int32)],
        in_specs=[SMEM],
        out_specs=[VMEM, SMEM],
        compiler_params=params(),
        cost_estimate=pl.CostEstimate(flops=COST * 2**28, bytes_accessed=0, transcendentals=0),
        name="meta",
    )(image_tiles)
    return bounds, far[0]


def pack_kernel(k_ref, v_ref, out_ref, held, sems):
    rows, columns = k_ref.shape
    tiles = rows // TILE
    copies = []
    for t in range(tiles):
        copies.append(pltpu.make_async_copy(v_ref.at[tile_rows(t)], held.at[tile_rows(t)], sems.at[2 * t]))
        copies.append(pltpu.make_async_copy(k_ref.at[tile_rows(t)], out_ref.at[tile_rows(2 * t)], sems.at[2 * t + 1]))
    for copy in copies:
        copy.start()
    for t in range(tiles):
        copies[2 * t].wait()
        for h in range(columns // HEAD_DIM):
            out_ref[tile_rows(2 * t + 1), head_columns(h)] = held[tile_rows(t), head_columns(h)].T
    for copy in copies[1::2]:
        copy.wait()


def pack(keys, values):
    rows, columns = keys.shape
    return pl.pallas_call(
        pack_kernel,
        out_shape=jax.ShapeDtypeStruct((2 * rows, columns), keys.dtype),
        in_specs=[HBM, HBM],
        out_specs=VMEM,
        scratch_shapes=[pltpu.VMEM(values.shape, values.dtype), pltpu.SemaphoreType.DMA((2 * rows // TILE,))],
        name="pack",
    )(keys, values)


def onward_kernel(a1_ref, b1_ref, own_ref, near_ref, corner_ref):
    upper = lax.axis_index("seq") % 2
    rows = corner_ref.shape[0]

    @pl.when(upper == 0)
    def _():
        near_ref[...] = a1_ref[...]
        corner_ref[...] = b1_ref[:rows]

    @pl.when(upper == 1)
    def _():
        near_ref[...] = b1_ref[...]
        corner_ref[...] = a1_ref[-rows:]


def onward(a1, b1, own):
    rows, columns = a1.shape
    return pl.pallas_call(
        onward_kernel,
        out_shape=[
            jax.ShapeDtypeStruct((rows, columns), a1.dtype),
            jax.ShapeDtypeStruct((rows - 2 * TILE, columns), a1.dtype),
        ],
        in_specs=[VMEM, VMEM, HBM],
        out_specs=[VMEM, VMEM],
        compiler_params=params(),
        name="onward",
    )(a1, b1, own)


def summands(rows):
    parts = []
    for _ in range(3):
        parts.append(rows.astype(jnp.bfloat16))
        rows = rows - parts[-1].astype(jnp.float32)
    return parts


def attend_kernel(which, places, arrays, fresh, unless_far, brief, bounds_ref, *refs):
    halves = len(which)
    q_refs, refs = refs[:halves], refs[halves:]
    array_refs, refs = refs[: len(arrays)], refs[len(arrays) :]
    old_refs, refs = (None, refs) if fresh else (refs[:halves], refs[halves:])
    new_refs, (held_q, held, state) = refs[:halves], refs[halves:]
    rows, columns = q_refs[0].shape
    tiles = rows // TILE
    count = held.shape[1] // 2 // TILE
    heads = columns // HEAD_DIM
    me = lax.axis_index("seq")

    for half in range(halves):
        held_q[half] = q_refs[half][...]
        if fresh:
            state[half, :columns] = jnp.zeros((columns, rows), jnp.float32)
            state[half, columns : columns + heads] = jnp.full((heads, rows), LOWEST, jnp.float32)
            state[half, columns + heads :] = jnp.zeros((state.shape[1] - columns - heads, rows), jnp.float32)
        else:
            state[half] = old_refs[half][...]
    for slot, (array, shift) in enumerate(arrays):
        size = array_refs[array].shape[0]
        if size < held.shape[1]:
            held[slot] = jnp.zeros(held.shape[1:], held.dtype)
        at = 0 if shift is None else pl.multiple_of(shift(me), 2 * TILE)
        held[slot, pl.ds(at, size)] = array_refs[array][...]
    begins = [bounds_ref[2 * w, 0] for w in which]
    stops = [bounds_ref[2 * w + 1, rows - 1] for w in which]

    far = bounds_ref[8, 0] if unless_far else None

    def chosen(at, options):
        return functools.reduce(lambda x, i: jnp.where(at == i, options[i], x), range(1, len(options)), options[0])

    def fold(half, slot, first):
        row = 2 * (which[0] + half * (which[-1] - which[0]) // max(len(which) - 1, 1))
        low = bounds_ref[pl.ds(row, 1), :]
        high = bounds_ref[pl.ds(row + 1, 1), :]
        off = [
            jnp.where((first + j >= low) & (first + j < high), 0.0, -LOWEST).astype(jnp.float32)
            for j in range(count)
        ]
        maxima = [[state[half, pl.ds(columns + h, 1), tile_rows(t)] for t in range(tiles)] for h in range(heads)]
        totals = [state[half, pl.ds(columns + heads + h, 1), :] for h in range(heads)]
        scores = [
            lax.dot_general(
                jnp.concatenate([held[slot, tile_rows(2 * j), head_columns(h)] for j in range(count)], axis=0),
                held_q[half, :, head_columns(h)],
                (((1,), (1,)), ((), ())),
                preferred_element_type=jnp.float32,
            )
            for h in range(heads)
        ]
        factors, sums, updates, largest = [], [], [], []
        for h in range(heads):
            factor, rounded, total, new = [], [], [], []
            for t in range(tiles):
                lanes = tile_rows(t)
                parts = [scores[h][tile_rows(j), lanes] for j in range(count)]
                new_max = maxima[h][t]
                for j in range(count):
                    new_max = jnp.maximum(new_max, jnp.max(parts[j], axis=0, keepdims=True) - off[j][:, lanes])
                scaled = new_max * SCALE2
                weights = [jnp.exp2(parts[j] * SCALE2 - (scaled + off[j][:, lanes])) for j in range(count)]
                factor.append(jnp.exp2((maxima[h][t] - new_max) * SCALE2))
                total.append(jnp.sum(functools.reduce(jnp.add, weights), axis=0, keepdims=True))
                new.append(new_max)
                rounded.append(jnp.concatenate([w.astype(jnp.bfloat16) for w in weights], axis=0))
            updates.append(
                jnp.dot(
                    jnp.concatenate([held[slot, tile_rows(2 * j + 1), head_columns(h)] for j in range(count)], axis=1),
                    jnp.concatenate(rounded, axis=1),
                    preferred_element_type=jnp.float32,
                )
            )
            factors.append(jnp.concatenate(factor, axis=1))
            sums.append(jnp.concatenate(total, axis=1))
            largest.append(jnp.concatenate(new, axis=1))
        for h in range(heads):
            own = head_columns(h)
            state[half, own] = state[half, own] * factors[h] + updates[h]
            state[half, pl.ds(columns + h, 1), :] = largest[h]
            state[half, pl.ds(columns + heads + h, 1), :] = totals[h] * factors[h] + sums[h]

    @pl.loop(0, halves * len(places))
    def _(unit):
        half, slot = unit // len(places), unit % len(places)
        first = chosen(slot, [place(me) for place in places])

        if unless_far:
            first = jnp.where(far > 0, -count, first)

        @pl.when((first < chosen(half, stops)) & (first + count > chosen(half, begins)))
        def _():
            fold(half, slot, first)

    for half in range(halves):
        if brief:
            new_refs[half][:columns] = state[half, :columns].astype(jnp.bfloat16)
            statistics = state[half, columns:]
            for n, part in enumerate(summands(statistics)):
                at = columns + n * 2 * 8
                new_refs[half][at : at + 2 * 8] = jnp.concatenate([part, part], axis=0)
        else:
            new_refs[half][...] = state[half]


def attend(bounds, queries, blocks, places, states, which=None, shifts=None, unless_far=False, brief=False):
    which = list(range(len(queries))) if which is None else which
    queries, states = [queries[w] for w in which], [states[w] for w in which] if states else []
    halves = len(which)
    rows, columns = queries[0].shape
    depth = blocks[0].shape[0]
    heads = columns // HEAD_DIM
    shape = jax.ShapeDtypeStruct((columns + -(-2 * heads // 8) * 8, rows), jnp.float32)
    arrays = list(enumerate(shifts or [None] * len(blocks)))
    pairs = halves * (rows // TILE) * heads * len(blocks) * (depth // 2 // TILE)
    sent = jax.ShapeDtypeStruct((columns + 3 * 2 * 8, rows), jnp.bfloat16)
    return pl.pallas_call(
        functools.partial(attend_kernel, which, places, arrays, not states, unless_far, brief),
        out_shape=[sent if brief else shape] * halves,
        in_specs=[VMEM] * (1 + halves + len(blocks) + len(states)),
        out_specs=[VMEM] * halves,
        scratch_shapes=[
            pltpu.VMEM((halves, rows, columns), queries[0].dtype),
            pltpu.VMEM((len(blocks), depth, columns), blocks[0].dtype),
            pltpu.VMEM((halves,) + shape.shape, jnp.float32),
        ],
        compiler_params=params(),
        cost_estimate=pl.CostEstimate(
            flops=COST * pairs * 4 * TILE * TILE * HEAD_DIM,
            bytes_accessed=2 * len(blocks) * depth * columns + 4 * halves * rows * columns,
            transcendentals=pairs * TILE * TILE,
        ),
        name="attend",
    )(bounds, *queries, *blocks, *states)


def merged(states, columns):
    heads = columns // HEAD_DIM
    for h in range(heads):
        maxima = [ref[columns + h : columns + h + 1] for ref in states]
        totals = [ref[columns + heads + h : columns + heads + h + 1] for ref in states]
        largest = functools.reduce(jnp.maximum, maxima)
        factors = [jnp.exp2((m - largest) * SCALE2) for m in maxima]
        total = functools.reduce(jnp.add, [f * t for f, t in zip(factors, totals)])
        parts = [ref[head_columns(h)] * (f / total) for ref, f in zip(states, factors)]
        yield head_columns(h), functools.reduce(jnp.add, parts).T


def finish_kernel(*refs):
    out_ref = refs[-1]
    for own, done in merged(refs[:-1], out_ref.shape[1]):
        out_ref[:, own] = done.astype(out_ref.dtype)


def finish(states, rows, columns):
    return pl.pallas_call(
        finish_kernel,
        out_shape=jax.ShapeDtypeStruct((rows, columns), jnp.bfloat16),
        in_specs=[VMEM] * len(states),
        out_specs=VMEM,
        compiler_params=params(),
        name="finish",
    )(*states)


def message_kernel(*refs):
    states, outs, held = refs[:4], refs[4:8], refs[8]
    rows = outs[0].shape[0] - 2 * 8
    columns = outs[0].shape[1]
    heads = columns // HEAD_DIM
    mine = lax.axis_index("head")
    for part in range(2):
        pair, (keep_ref, send_ref) = states[2 * part : 2 * part + 2], outs[2 * part : 2 * part + 2]
        logs = []
        rest = pair[1][columns:].astype(jnp.float32)
        statistics = functools.reduce(jnp.add, [rest[n * 2 * 8 : n * 2 * 8 + 8] for n in range(3)])
        for h in range(heads):
            maxima = [pair[0][columns + h : columns + h + 1], statistics[h : h + 1]]
            totals = [pair[0][columns + heads + h : columns + heads + h + 1], statistics[heads + h : heads + h + 1]]
            largest = jnp.maximum(*maxima)
            factors = [jnp.exp2((m - largest) * SCALE2) for m in maxima]
            total = factors[0] * totals[0] + factors[1] * totals[1]
            some = jnp.where(total > 0, total, 1.0)
            scale = [f / some for f in factors]
            own = head_columns(h)
            sums = pair[0][own] * scale[0] + pair[1][own].astype(jnp.float32) * scale[1]
            held[:, own] = sums.T.astype(held.dtype)
            log = jnp.where(total > 0, largest * SCALE2 + jnp.log2(some), LOWEST)
            logs += [part.astype(jnp.float32) for part in summands(log)]
        logs = jnp.concatenate(logs + [jnp.zeros((2 * 8 - len(logs), held.shape[0]), jnp.float32)], axis=0)
        later = pltpu.roll(logs, rows, 1)
        for ref, which in ((send_ref, 1 - mine), (keep_ref, mine)):
            ref[:rows] = held[pl.ds(pl.multiple_of(which * rows, 2 * 8), rows), :]
            ref[rows:] = jnp.where(which == 0, logs, later).astype(ref.dtype)


def messages(mine, peers):
    rows, columns = mine[0].shape[1], mine[0].shape[0] // HEAD_DIM * HEAD_DIM
    shape = jax.ShapeDtypeStruct((rows // 2 + 2 * 8, columns), jnp.bfloat16)
    return pl.pallas_call(
        message_kernel,
        out_shape=[shape] * 4,
        in_specs=[VMEM] * 4,
        out_specs=[VMEM] * 4,
        scratch_shapes=[pltpu.VMEM((rows, columns), jnp.bfloat16)],
        compiler_params=params(),
        name="message",
    )(*mine, *peers)


def settle_kernel(*refs):
    parts, out_ref, logs = refs[:4], refs[4], refs[5]
    rows, columns = out_ref.shape[0], parts[0].shape[1]
    heads = columns // HEAD_DIM
    mine = lax.axis_index("head")
    logs[...] = jnp.zeros(logs.shape, jnp.float32)
    for i, ref in enumerate(parts):
        summands = ref[rows:].astype(jnp.float32)
        for h in range(heads):
            at = i * heads + h
            logs[at : at + 1] = functools.reduce(jnp.add, [summands[3 * h + n : 3 * h + n + 1] for n in range(3)])
    turned = logs[...].T[:rows]
    for side, base in ((0, 1 - mine), (1, mine)):
        for h in range(heads):
            both = [turned[:, at : at + 1] for at in (2 * side * heads + h, (2 * side + 1) * heads + h)]
            largest = jnp.maximum(*both)
            weights = [jnp.exp2(x - largest) for x in both]
            sums = [ref[:rows, head_columns(h)].astype(jnp.float32) for ref in parts[2 * side : 2 * side + 2]]
            total = weights[0] + weights[1]
            done = sums[0] * (weights[0] / total) + sums[1] * (weights[1] / total)
            at = pl.multiple_of(base * columns + h * HEAD_DIM, HEAD_DIM)
            out_ref[:, pl.ds(at, HEAD_DIM)] = done.astype(out_ref.dtype)


def settle(diagonal, beside, across, own):
    rows, columns = own.shape[0] - 2 * 8, own.shape[1]
    return pl.pallas_call(
        settle_kernel,
        out_shape=jax.ShapeDtypeStruct((rows, 2 * columns), own.dtype),
        in_specs=[VMEM] * 4,
        out_specs=VMEM,
        scratch_shapes=[pltpu.VMEM((TILE, columns), jnp.float32)],
        compiler_params=params(),
        name="settle",
    )(diagonal, beside, across, own)


def chip_pairs(mesh):
    places = [tuple(getattr(d, "coords", ())) for d in mesh.devices[:, 0]]
    count = len(places)
    if count % 4 or not places[0] or mesh.shape["head"] != 2:
        return False
    cores = all(places[i] == places[i + 1] for i in range(0, count, 2))
    level = all(places[i][2] == places[i + 3][2] for i in range(0, count, 4))
    climb = all(places[i][2] != places[i + 4][2] for i in range(0, count - 4))
    return cores and level and climb


def paired_shards(owner_count, queries, keys, values, image_tiles):
    rows, columns = queries.shape
    tiles = rows // TILE
    owners = range(owner_count)

    def flip(s):
        return 1 - 2 * ((s // 2) % 2)

    def core(s):
        return s % 2

    def moved(array, source, takes=lambda s: True):
        pairs = [(source(s), s) for s in owners if takes(s) and 0 <= source(s) < owner_count]
        return lax.ppermute(array, "seq", pairs)

    across = lambda s: s + 2 * flip(s)
    near_side = lambda s: s + 4 * flip(s)
    far_side = lambda s: s - 4 * flip(s)
    along = lambda s: s + 4 * flip(s) * (1 - 2 * core(s))
    against = lambda s: s - 4 * flip(s) * (1 - 2 * core(s))
    sibling = lambda s: s + 1 - 2 * core(s)
    inner = lambda s: core(s) == (1 - (s // 2) % 2)

    OWN = lambda s: s * tiles
    A1 = lambda s: along(s) * tiles
    B1 = lambda s: against(s) * tiles
    A2 = lambda s: (s + 8 * flip(s)) * tiles
    B2 = lambda s: jnp.where(inner(s), s - 8 * flip(s), -owner_count) * tiles

    peers = moved(queries, across)
    block = pack(keys, values)
    a1, b1 = moved(block, along), moved(block, against)
    level = (queries, moved(queries, sibling), peers, moved(peers, sibling))
    bounds, far = meta(lambda s: [s, sibling(s), across(s), sibling(across(s))], image_tiles, rows)
    fold = functools.partial(attend, bounds, level)
    states = fold([block], [OWN], [], which=[0, 1]) + fold([block], [OWN], [], which=[2, 3])
    states = fold([b1], [B1], states, unless_far=True)

    def merge(blocks, places, states, shifts=None):
        beside, diagonal = fold(blocks, places, states, which=[1, 3], shifts=shifts, brief=True)
        beside, diagonal = moved(beside, sibling), moved(diagonal, sibling)
        mine, peer = fold(blocks, places, states, which=[0, 2], shifts=shifts)
        keep, over_x, over_y, over_both = messages([mine, beside], [peer, diagonal])
        pairs = [(2 * across(s) + 1 - x, 2 * s + x) for s in owners for x in range(2)]
        over_both = lax.ppermute(over_both, ("seq", "head"), pairs)
        over_y = moved(over_y, across)
        over_x = lax.ppermute(over_x, "head", [(0, 1), (1, 0)])
        return settle(over_both, over_x, over_y, keep)

    def near_only(block, a1, b1, states):
        return merge([a1], [A1], states)

    def both_ways(block, a1, b1, states):
        near, corner = onward(a1, b1, block)
        a2, b2 = moved(near, near_side), moved(corner, far_side, inner)
        states = fold([a1, b1], [A1, B1], states)
        return merge([a2, b2], [A2, B2], states, [None, lambda s: 2 * TILE * core(s)])

    return lax.cond(far > 0, both_ways, near_only, block, a1, b1, states)


def ring_shards(owner_count, queries, keys, values, image_tiles):
    rows, columns = queries.shape
    tiles = rows // TILE
    reach = min(owner_count - 1, -(-(MOST_TILES - 1) // tiles))
    block = pack(keys, values)
    bounds, _ = meta(lambda s: [s], image_tiles, rows)
    fold = functools.partial(attend, bounds, (queries,))
    up = [(i, i + 1) for i in range(owner_count - 1)]
    down = [(i + 1, i) for i in range(owner_count - 1)]
    below = above = block
    states = []
    held, places = [block], [lambda s: s * tiles]
    for k in range(1, reach + 1):
        below = lax.ppermute(below, "seq", up)
        above = lax.ppermute(above, "seq", down)
        states = fold(held, places, states)
        held, places = [below, above], [lambda s, k=k: (s - k) * tiles, lambda s, k=k: (s + k) * tiles]
    attended = finish(fold(held, places, states), rows, columns)
    return lax.all_to_all(attended, "head", split_axis=0, concat_axis=1, tiled=True)


def solution(mesh):
    owner_count = mesh.shape["seq"]
    plan = paired_shards if chip_pairs(mesh) else ring_shards
    placed = (P("seq", "head"), P("seq", "head"), P("seq", "head"), P())
    return jax.shard_map(
        functools.partial(plan, owner_count),
        mesh=mesh,
        in_specs=placed,
        out_specs=P(("seq", "head"), None),
        check_vma=False,
    )
```

```python
import functools
import math

import jax
import jax.numpy as jnp
from jax import lax
from jax.experimental import pallas as pl
from jax.experimental.pallas import tpu as pltpu
from jax.sharding import PartitionSpec as P

HEAD_DIM = 128
TILE = 128
MOST_TILES = 21

LOWEST = -1e30
SCALE2 = math.log2(math.e) / math.sqrt(HEAD_DIM)
COST = 1

VMEM = pl.BlockSpec(memory_space=pltpu.VMEM)
SMEM = pl.BlockSpec(memory_space=pltpu.SMEM)
HBM = pl.BlockSpec(memory_space=pl.ANY)


def params():
    return pltpu.CompilerParams(vmem_limit_bytes=16 * 1024 * 1024)


def head_columns(h):
    return slice(h * HEAD_DIM, (h + 1) * HEAD_DIM)


def tile_rows(t):
    return slice(t * TILE, (t + 1) * TILE)


def image_bounds(tiles_ref, tile):
    first = jnp.int32(0)
    start, end = jnp.int32(0), jnp.int32(0)
    for i in range(tiles_ref.shape[0]):
        after = first + tiles_ref[i]
        inside = (tile >= first) & (tile < after)
        start = jnp.where(inside, first, start)
        end = jnp.where(inside, after, end)
        first = after
    return start, end


def meta_kernel(halves, tiles_ref, bounds_ref, far_ref):
    tiles = bounds_ref.shape[1] // TILE
    me = lax.axis_index("seq")
    bounds_ref[...] = jnp.zeros(bounds_ref.shape, jnp.int32)
    for half, owner in enumerate(halves(me)):
        for t in range(tiles):
            start, end = image_bounds(tiles_ref, owner * tiles + t)
            bounds_ref[2 * half : 2 * half + 1, tile_rows(t)] = jnp.full((1, TILE), start, jnp.int32)
            bounds_ref[2 * half + 1 : 2 * half + 2, tile_rows(t)] = jnp.full((1, TILE), end, jnp.int32)
    first = jnp.int32(0)
    far = jnp.int32(0)
    for i in range(tiles_ref.shape[0]):
        after = first + tiles_ref[i]
        levels = (after - 1) // (4 * tiles) - first // (4 * tiles)
        far = jnp.where(levels >= 2, 1, far)
        first = after
    far_ref[0] = far
    bounds_ref[8:9] = jnp.full((1, bounds_ref.shape[1]), far, jnp.int32)


def meta(halves, image_tiles, rows):
    bounds, far = pl.pallas_call(
        functools.partial(meta_kernel, halves),
        out_shape=[jax.ShapeDtypeStruct((16, rows), jnp.int32), jax.ShapeDtypeStruct((1,), jnp.int32)],
        in_specs=[SMEM],
        out_specs=[VMEM, SMEM],
        compiler_params=params(),
        cost_estimate=pl.CostEstimate(flops=COST * 2**28, bytes_accessed=0, transcendentals=0),
        name="meta",
    )(image_tiles)
    return bounds, far[0]


def pack_kernel(k_ref, v_ref, out_ref, held, sems):
    rows, columns = k_ref.shape
    tiles = rows // TILE
    copies = []
    for t in range(tiles):
        copies.append(pltpu.make_async_copy(v_ref.at[tile_rows(t)], held.at[tile_rows(t)], sems.at[2 * t]))
        copies.append(pltpu.make_async_copy(k_ref.at[tile_rows(t)], out_ref.at[tile_rows(2 * t)], sems.at[2 * t + 1]))
    for copy in copies:
        copy.start()
    for t in range(tiles):
        copies[2 * t].wait()
        for h in range(columns // HEAD_DIM):
            out_ref[tile_rows(2 * t + 1), head_columns(h)] = held[tile_rows(t), head_columns(h)].T
    for copy in copies[1::2]:
        copy.wait()


def pack(keys, values):
    rows, columns = keys.shape
    return pl.pallas_call(
        pack_kernel,
        out_shape=jax.ShapeDtypeStruct((2 * rows, columns), keys.dtype),
        in_specs=[HBM, HBM],
        out_specs=VMEM,
        scratch_shapes=[pltpu.VMEM(values.shape, values.dtype), pltpu.SemaphoreType.DMA((2 * rows // TILE,))],
        name="pack",
    )(keys, values)


def onward_kernel(a1_ref, b1_ref, own_ref, near_ref, corner_ref):
    upper = lax.axis_index("seq") % 2
    rows = corner_ref.shape[0]

    @pl.when(upper == 0)
    def _():
        near_ref[...] = a1_ref[...]
        corner_ref[...] = b1_ref[:rows]

    @pl.when(upper == 1)
    def _():
        near_ref[...] = b1_ref[...]
        corner_ref[...] = a1_ref[-rows:]


def onward(a1, b1, own):
    rows, columns = a1.shape
    return pl.pallas_call(
        onward_kernel,
        out_shape=[
            jax.ShapeDtypeStruct((rows, columns), a1.dtype),
            jax.ShapeDtypeStruct((rows - 2 * TILE, columns), a1.dtype),
        ],
        in_specs=[VMEM, VMEM, HBM],
        out_specs=[VMEM, VMEM],
        compiler_params=params(),
        name="onward",
    )(a1, b1, own)


def summands(rows):
    parts = []
    for _ in range(3):
        parts.append(rows.astype(jnp.bfloat16))
        rows = rows - parts[-1].astype(jnp.float32)
    return parts


def attend_kernel(which, places, arrays, fresh, unless_far, brief, bounds_ref, *refs):
    halves = len(which)
    q_refs, refs = refs[:halves], refs[halves:]
    array_refs, refs = refs[: len(arrays)], refs[len(arrays) :]
    old_refs, refs = (None, refs) if fresh else (refs[:halves], refs[halves:])
    new_refs, (held_q, held, state) = refs[:-3], refs[-3:]
    rows, columns = q_refs[0].shape
    tiles = rows // TILE
    count = held.shape[1] // 2 // TILE
    heads = columns // HEAD_DIM
    me = lax.axis_index("seq")

    for half in range(halves):
        held_q[half] = q_refs[half][...]
        if fresh:
            state[half, :columns] = jnp.zeros((columns, rows), jnp.float32)
            state[half, columns : columns + heads] = jnp.full((heads, rows), LOWEST, jnp.float32)
            state[half, columns + heads :] = jnp.zeros((state.shape[1] - columns - heads, rows), jnp.float32)
        else:
            state[half] = old_refs[half][...]
    for slot, (array, shift) in enumerate(arrays):
        size = array_refs[array].shape[0]
        if size < held.shape[1]:
            held[slot] = jnp.zeros(held.shape[1:], held.dtype)
        at = 0 if shift is None else pl.multiple_of(shift(me), 2 * TILE)
        held[slot, pl.ds(at, size)] = array_refs[array][...]
    begins = [bounds_ref[2 * w, 0] for w in which]
    stops = [bounds_ref[2 * w + 1, rows - 1] for w in which]

    far = bounds_ref[8, 0] if unless_far else None

    def chosen(at, options):
        return functools.reduce(lambda x, i: jnp.where(at == i, options[i], x), range(1, len(options)), options[0])

    def fold(half, slot, first):
        row = 2 * (which[0] + half * (which[-1] - which[0]) // max(len(which) - 1, 1))
        low = bounds_ref[pl.ds(row, 1), :]
        high = bounds_ref[pl.ds(row + 1, 1), :]
        off = [
            jnp.where((first + j >= low) & (first + j < high), 0.0, -LOWEST).astype(jnp.float32)
            for j in range(count)
        ]
        maxima = [[state[half, pl.ds(columns + h, 1), tile_rows(t)] for t in range(tiles)] for h in range(heads)]
        totals = [state[half, pl.ds(columns + heads + h, 1), :] for h in range(heads)]
        scores = [
            lax.dot_general(
                jnp.concatenate([held[slot, tile_rows(2 * j), head_columns(h)] for j in range(count)], axis=0),
                held_q[half, :, head_columns(h)],
                (((1,), (1,)), ((), ())),
                preferred_element_type=jnp.float32,
            )
            for h in range(heads)
        ]
        factors, sums, updates, largest = [], [], [], []
        for h in range(heads):
            factor, rounded, total, new = [], [], [], []
            for t in range(tiles):
                lanes = tile_rows(t)
                parts = [scores[h][tile_rows(j), lanes] for j in range(count)]
                new_max = maxima[h][t]
                for j in range(count):
                    new_max = jnp.maximum(new_max, jnp.max(parts[j], axis=0, keepdims=True) - off[j][:, lanes])
                scaled = new_max * SCALE2
                weights = [jnp.exp2(parts[j] * SCALE2 - (scaled + off[j][:, lanes])) for j in range(count)]
                factor.append(jnp.exp2((maxima[h][t] - new_max) * SCALE2))
                total.append(jnp.sum(functools.reduce(jnp.add, weights), axis=0, keepdims=True))
                new.append(new_max)
                rounded.append(jnp.concatenate([w.astype(jnp.bfloat16) for w in weights], axis=0))
            updates.append(
                jnp.dot(
                    jnp.concatenate([held[slot, tile_rows(2 * j + 1), head_columns(h)] for j in range(count)], axis=1),
                    jnp.concatenate(rounded, axis=1),
                    preferred_element_type=jnp.float32,
                )
            )
            factors.append(jnp.concatenate(factor, axis=1))
            sums.append(jnp.concatenate(total, axis=1))
            largest.append(jnp.concatenate(new, axis=1))
        for h in range(heads):
            own = head_columns(h)
            state[half, own] = state[half, own] * factors[h] + updates[h]
            state[half, pl.ds(columns + h, 1), :] = largest[h]
            state[half, pl.ds(columns + heads + h, 1), :] = totals[h] * factors[h] + sums[h]

    @pl.loop(0, halves * len(places))
    def _(unit):
        half, slot = unit // len(places), unit % len(places)
        first = chosen(slot, [place(me) for place in places])

        if unless_far:
            first = jnp.where(far > 0, -count, first)

        @pl.when((first < chosen(half, stops)) & (first + count > chosen(half, begins)))
        def _():
            fold(half, slot, first)

    for half in range(halves):
        if brief:
            at = half * new_refs[0].shape[0] // halves
            new_refs[0][at : at + columns] = state[half, :columns].astype(jnp.bfloat16)
            for n, part in enumerate(summands(state[half, columns:])):
                row = at + columns + n * 2 * 8
                new_refs[0][row : row + 2 * 8] = jnp.concatenate([part, part], axis=0)
        else:
            new_refs[half][...] = state[half]


def attend(bounds, queries, blocks, places, states, which=None, shifts=None, unless_far=False, brief=False):
    which = list(range(len(queries))) if which is None else which
    queries, states = [queries[w] for w in which], [states[w] for w in which] if states else []
    halves = len(which)
    rows, columns = queries[0].shape
    depth = blocks[0].shape[0]
    heads = columns // HEAD_DIM
    shape = jax.ShapeDtypeStruct((columns + -(-2 * heads // 8) * 8, rows), jnp.float32)
    arrays = list(enumerate(shifts or [None] * len(blocks)))
    pairs = halves * (rows // TILE) * heads * len(blocks) * (depth // 2 // TILE)
    sent = jax.ShapeDtypeStruct((halves * (columns + 3 * 2 * 8), rows), jnp.bfloat16)
    return pl.pallas_call(
        functools.partial(attend_kernel, which, places, arrays, not states, unless_far, brief),
        out_shape=[sent] if brief else [shape] * halves,
        in_specs=[VMEM] * (1 + halves + len(blocks) + len(states)),
        out_specs=[VMEM] * (1 if brief else halves),
        scratch_shapes=[
            pltpu.VMEM((halves, rows, columns), queries[0].dtype),
            pltpu.VMEM((len(blocks), depth, columns), blocks[0].dtype),
            pltpu.VMEM((halves,) + shape.shape, jnp.float32),
        ],
        compiler_params=params(),
        cost_estimate=pl.CostEstimate(
            flops=COST * pairs * 4 * TILE * TILE * HEAD_DIM,
            bytes_accessed=2 * len(blocks) * depth * columns + 4 * halves * rows * columns,
            transcendentals=pairs * TILE * TILE,
        ),
        name="attend",
    )(bounds, *queries, *blocks, *states)


def merged(states, columns):
    heads = columns // HEAD_DIM
    for h in range(heads):
        maxima = [ref[columns + h : columns + h + 1] for ref in states]
        totals = [ref[columns + heads + h : columns + heads + h + 1] for ref in states]
        largest = functools.reduce(jnp.maximum, maxima)
        factors = [jnp.exp2((m - largest) * SCALE2) for m in maxima]
        total = functools.reduce(jnp.add, [f * t for f, t in zip(factors, totals)])
        parts = [ref[head_columns(h)] * (f / total) for ref, f in zip(states, factors)]
        yield head_columns(h), functools.reduce(jnp.add, parts).T


def finish_kernel(*refs):
    out_ref = refs[-1]
    for own, done in merged(refs[:-1], out_ref.shape[1]):
        out_ref[:, own] = done.astype(out_ref.dtype)


def finish(states, rows, columns):
    return pl.pallas_call(
        finish_kernel,
        out_shape=jax.ShapeDtypeStruct((rows, columns), jnp.bfloat16),
        in_specs=[VMEM] * len(states),
        out_specs=VMEM,
        compiler_params=params(),
        name="finish",
    )(*states)


def message_kernel(*refs):
    states, got_ref, outs, held = refs[:2], refs[2], refs[3:7], refs[7]
    rows = outs[0].shape[0] - 2 * 8
    columns = outs[0].shape[1]
    heads = columns // HEAD_DIM
    mine = lax.axis_index("head")
    for part in range(2):
        ref, (keep_ref, send_ref) = states[part], outs[2 * part : 2 * part + 2]
        at = part * got_ref.shape[0] // 2
        logs = []
        rest = got_ref[at + columns : at + got_ref.shape[0] // 2].astype(jnp.float32)
        statistics = functools.reduce(jnp.add, [rest[n * 2 * 8 : n * 2 * 8 + 8] for n in range(3)])
        for h in range(heads):
            maxima = [ref[columns + h : columns + h + 1], statistics[h : h + 1]]
            totals = [ref[columns + heads + h : columns + heads + h + 1], statistics[heads + h : heads + h + 1]]
            largest = jnp.maximum(*maxima)
            factors = [jnp.exp2((m - largest) * SCALE2) for m in maxima]
            total = factors[0] * totals[0] + factors[1] * totals[1]
            some = jnp.where(total > 0, total, 1.0)
            scale = [f / some for f in factors]
            own = head_columns(h)
            got = got_ref[at + h * HEAD_DIM : at + (h + 1) * HEAD_DIM].astype(jnp.float32)
            sums = ref[own] * scale[0] + got * scale[1]
            held[:, own] = sums.T.astype(held.dtype)
            log = jnp.where(total > 0, largest * SCALE2 + jnp.log2(some), LOWEST)
            logs += [part.astype(jnp.float32) for part in summands(log)]
        logs = jnp.concatenate(logs + [jnp.zeros((2 * 8 - len(logs), held.shape[0]), jnp.float32)], axis=0)
        later = pltpu.roll(logs, rows, 1)
        for out_ref, which in ((send_ref, 1 - mine), (keep_ref, mine)):
            out_ref[:rows] = held[pl.ds(pl.multiple_of(which * rows, 2 * 8), rows), :]
            out_ref[rows:] = jnp.where(which == 0, logs, later).astype(out_ref.dtype)


def messages(mine, peer, got):
    rows, columns = mine.shape[1], mine.shape[0] // HEAD_DIM * HEAD_DIM
    shape = jax.ShapeDtypeStruct((rows // 2 + 2 * 8, columns), jnp.bfloat16)
    return pl.pallas_call(
        message_kernel,
        out_shape=[shape] * 4,
        in_specs=[VMEM] * 3,
        out_specs=[VMEM] * 4,
        scratch_shapes=[pltpu.VMEM((rows, columns), jnp.bfloat16)],
        compiler_params=params(),
        name="message",
    )(mine, peer, got)


def settle_kernel(*refs):
    parts, out_ref, logs = refs[:4], refs[4], refs[5]
    rows, columns = out_ref.shape[0], parts[0].shape[1]
    heads = columns // HEAD_DIM
    mine = lax.axis_index("head")
    logs[...] = jnp.zeros(logs.shape, jnp.float32)
    for i, ref in enumerate(parts):
        summands = ref[rows:].astype(jnp.float32)
        for h in range(heads):
            at = i * heads + h
            logs[at : at + 1] = functools.reduce(jnp.add, [summands[3 * h + n : 3 * h + n + 1] for n in range(3)])
    turned = logs[...].T[:rows]
    for side, base in ((0, 1 - mine), (1, mine)):
        for h in range(heads):
            both = [turned[:, at : at + 1] for at in (2 * side * heads + h, (2 * side + 1) * heads + h)]
            largest = jnp.maximum(*both)
            weights = [jnp.exp2(x - largest) for x in both]
            sums = [ref[:rows, head_columns(h)].astype(jnp.float32) for ref in parts[2 * side : 2 * side + 2]]
            total = weights[0] + weights[1]
            done = sums[0] * (weights[0] / total) + sums[1] * (weights[1] / total)
            at = pl.multiple_of(base * columns + h * HEAD_DIM, HEAD_DIM)
            out_ref[:, pl.ds(at, HEAD_DIM)] = done.astype(out_ref.dtype)


def settle(diagonal, beside, across, own):
    rows, columns = own.shape[0] - 2 * 8, own.shape[1]
    return pl.pallas_call(
        settle_kernel,
        out_shape=jax.ShapeDtypeStruct((rows, 2 * columns), own.dtype),
        in_specs=[VMEM] * 4,
        out_specs=VMEM,
        scratch_shapes=[pltpu.VMEM((TILE, columns), jnp.float32)],
        compiler_params=params(),
        name="settle",
    )(diagonal, beside, across, own)


def chip_pairs(mesh):
    places = [tuple(getattr(d, "coords", ())) for d in mesh.devices[:, 0]]
    count = len(places)
    if count % 4 or not places[0] or mesh.shape["head"] != 2:
        return False
    cores = all(places[i] == places[i + 1] for i in range(0, count, 2))
    level = all(places[i][2] == places[i + 3][2] for i in range(0, count, 4))
    climb = all(places[i][2] != places[i + 4][2] for i in range(0, count - 4))
    return cores and level and climb


def paired_shards(owner_count, queries, keys, values, image_tiles):
    rows, columns = queries.shape
    tiles = rows // TILE
    owners = range(owner_count)

    def flip(s):
        return 1 - 2 * ((s // 2) % 2)

    def core(s):
        return s % 2

    def moved(array, source, takes=lambda s: True):
        pairs = [(source(s), s) for s in owners if takes(s) and 0 <= source(s) < owner_count]
        return lax.ppermute(array, "seq", pairs)

    across = lambda s: s + 2 * flip(s)
    near_side = lambda s: s + 4 * flip(s)
    far_side = lambda s: s - 4 * flip(s)
    along = lambda s: s + 4 * flip(s) * (1 - 2 * core(s))
    against = lambda s: s - 4 * flip(s) * (1 - 2 * core(s))
    sibling = lambda s: s + 1 - 2 * core(s)
    inner = lambda s: core(s) == (1 - (s // 2) % 2)

    OWN = lambda s: s * tiles
    A1 = lambda s: along(s) * tiles
    B1 = lambda s: against(s) * tiles
    A2 = lambda s: (s + 8 * flip(s)) * tiles
    B2 = lambda s: jnp.where(inner(s), s - 8 * flip(s), -owner_count) * tiles

    peers = moved(queries, across)
    block = pack(keys, values)
    a1, b1 = moved(block, along), moved(block, against)
    level = (queries, moved(queries, sibling), peers, moved(peers, sibling))
    bounds, far = meta(lambda s: [s, sibling(s), across(s), sibling(across(s))], image_tiles, rows)
    fold = functools.partial(attend, bounds, level)
    states = fold([block], [OWN], [], which=[0, 1]) + fold([block], [OWN], [], which=[2, 3])
    states = fold([b1], [B1], states, unless_far=True)

    def merge(blocks, places, states, shifts=None):
        (others,) = fold(blocks, places, states, which=[1, 3], shifts=shifts, brief=True)
        got = moved(others, sibling)
        mine, peer = fold(blocks, places, states, which=[0, 2], shifts=shifts)
        keep, over_x, over_y, over_both = messages(mine, peer, got)
        pairs = [(2 * across(s) + 1 - x, 2 * s + x) for s in owners for x in range(2)]
        over_both = lax.ppermute(over_both, ("seq", "head"), pairs)
        over_y = moved(over_y, across)
        over_x = lax.ppermute(over_x, "head", [(0, 1), (1, 0)])
        return settle(over_both, over_x, over_y, keep)

    def near_only(block, a1, b1, states):
        return merge([a1], [A1], states)

    def both_ways(block, a1, b1, states):
        near, corner = onward(a1, b1, block)
        a2, b2 = moved(near, near_side), moved(corner, far_side, inner)
        states = fold([a1, b1], [A1, B1], states)
        return merge([a2, b2], [A2, B2], states, [None, lambda s: 2 * TILE * core(s)])

    return lax.cond(far > 0, both_ways, near_only, block, a1, b1, states)


def ring_shards(owner_count, queries, keys, values, image_tiles):
    rows, columns = queries.shape
    tiles = rows // TILE
    reach = min(owner_count - 1, -(-(MOST_TILES - 1) // tiles))
    block = pack(keys, values)
    bounds, _ = meta(lambda s: [s], image_tiles, rows)
    fold = functools.partial(attend, bounds, (queries,))
    up = [(i, i + 1) for i in range(owner_count - 1)]
    down = [(i + 1, i) for i in range(owner_count - 1)]
    below = above = block
    states = []
    held, places = [block], [lambda s: s * tiles]
    for k in range(1, reach + 1):
        below = lax.ppermute(below, "seq", up)
        above = lax.ppermute(above, "seq", down)
        states = fold(held, places, states)
        held, places = [below, above], [lambda s, k=k: (s - k) * tiles, lambda s, k=k: (s + k) * tiles]
    attended = finish(fold(held, places, states), rows, columns)
    return lax.all_to_all(attended, "head", split_axis=0, concat_axis=1, tiled=True)


def solution(mesh):
    owner_count = mesh.shape["seq"]
    plan = paired_shards if chip_pairs(mesh) else ring_shards
    placed = (P("seq", "head"), P("seq", "head"), P("seq", "head"), P())
    return jax.shard_map(
        functools.partial(plan, owner_count),
        mesh=mesh,
        in_specs=placed,
        out_specs=P(("seq", "head"), None),
        check_vma=False,
    )
```

```python
import functools
import math

import jax
import jax.numpy as jnp
from jax import lax
from jax.experimental import pallas as pl
from jax.experimental.pallas import tpu as pltpu
from jax.sharding import PartitionSpec as P

HEAD_DIM = 128
TILE = 128
MOST_TILES = 21

LOWEST = -1e30
SCALE2 = math.log2(math.e) / math.sqrt(HEAD_DIM)
COST = 2

VMEM = pl.BlockSpec(memory_space=pltpu.VMEM)
SMEM = pl.BlockSpec(memory_space=pltpu.SMEM)
HBM = pl.BlockSpec(memory_space=pl.ANY)


def params():
    return pltpu.CompilerParams(vmem_limit_bytes=16 * 1024 * 1024)


def head_columns(h):
    return slice(h * HEAD_DIM, (h + 1) * HEAD_DIM)


def tile_rows(t):
    return slice(t * TILE, (t + 1) * TILE)


def image_bounds(tiles_ref, tile):
    first = jnp.int32(0)
    start, end = jnp.int32(0), jnp.int32(0)
    for i in range(tiles_ref.shape[0]):
        after = first + tiles_ref[i]
        inside = (tile >= first) & (tile < after)
        start = jnp.where(inside, first, start)
        end = jnp.where(inside, after, end)
        first = after
    return start, end


def meta_kernel(halves, tiles_ref, bounds_ref, far_ref):
    tiles = bounds_ref.shape[1] // TILE
    me = lax.axis_index("seq")
    bounds_ref[...] = jnp.zeros(bounds_ref.shape, jnp.int32)
    for half, owner in enumerate(halves(me)):
        for t in range(tiles):
            start, end = image_bounds(tiles_ref, owner * tiles + t)
            bounds_ref[2 * half : 2 * half + 1, tile_rows(t)] = jnp.full((1, TILE), start, jnp.int32)
            bounds_ref[2 * half + 1 : 2 * half + 2, tile_rows(t)] = jnp.full((1, TILE), end, jnp.int32)
    first = jnp.int32(0)
    far = jnp.int32(0)
    for i in range(tiles_ref.shape[0]):
        after = first + tiles_ref[i]
        levels = (after - 1) // (4 * tiles) - first // (4 * tiles)
        far = jnp.where(levels >= 2, 1, far)
        first = after
    far_ref[0] = far
    bounds_ref[8:9] = jnp.full((1, bounds_ref.shape[1]), far, jnp.int32)


def meta(halves, image_tiles, rows):
    bounds, far = pl.pallas_call(
        functools.partial(meta_kernel, halves),
        out_shape=[jax.ShapeDtypeStruct((16, rows), jnp.int32), jax.ShapeDtypeStruct((1,), jnp.int32)],
        in_specs=[SMEM],
        out_specs=[VMEM, SMEM],
        compiler_params=params(),
        cost_estimate=pl.CostEstimate(flops=COST * 2**28, bytes_accessed=0, transcendentals=0),
        name="meta",
    )(image_tiles)
    return bounds, far[0]


def pack_kernel(k_ref, v_ref, out_ref, held, sems):
    rows, columns = k_ref.shape
    tiles = rows // TILE
    copies = []
    for t in range(tiles):
        copies.append(pltpu.make_async_copy(v_ref.at[tile_rows(t)], held.at[tile_rows(t)], sems.at[2 * t]))
        copies.append(pltpu.make_async_copy(k_ref.at[tile_rows(t)], out_ref.at[tile_rows(2 * t)], sems.at[2 * t + 1]))
    for copy in copies:
        copy.start()
    for t in range(tiles):
        copies[2 * t].wait()
        for h in range(columns // HEAD_DIM):
            out_ref[tile_rows(2 * t + 1), head_columns(h)] = held[tile_rows(t), head_columns(h)].T
    for copy in copies[1::2]:
        copy.wait()


def pack(keys, values):
    rows, columns = keys.shape
    return pl.pallas_call(
        pack_kernel,
        out_shape=jax.ShapeDtypeStruct((2 * rows, columns), keys.dtype),
        in_specs=[HBM, HBM],
        out_specs=VMEM,
        scratch_shapes=[pltpu.VMEM(values.shape, values.dtype), pltpu.SemaphoreType.DMA((2 * rows // TILE,))],
        name="pack",
    )(keys, values)


def onward_kernel(a1_ref, b1_ref, own_ref, near_ref, corner_ref):
    upper = lax.axis_index("seq") % 2
    rows = corner_ref.shape[0]

    @pl.when(upper == 0)
    def _():
        near_ref[...] = a1_ref[...]
        corner_ref[...] = b1_ref[:rows]

    @pl.when(upper == 1)
    def _():
        near_ref[...] = b1_ref[...]
        corner_ref[...] = a1_ref[-rows:]


def onward(a1, b1, own):
    rows, columns = a1.shape
    return pl.pallas_call(
        onward_kernel,
        out_shape=[
            jax.ShapeDtypeStruct((rows, columns), a1.dtype),
            jax.ShapeDtypeStruct((rows - 2 * TILE, columns), a1.dtype),
        ],
        in_specs=[VMEM, VMEM, HBM],
        out_specs=[VMEM, VMEM],
        compiler_params=params(),
        name="onward",
    )(a1, b1, own)


def summands(rows):
    parts = []
    for _ in range(3):
        parts.append(rows.astype(jnp.bfloat16))
        rows = rows - parts[-1].astype(jnp.float32)
    return parts


def attend_kernel(which, places, arrays, fresh, unless_far, brief, bounds_ref, *refs):
    halves = len(which)
    q_refs, refs = refs[:halves], refs[halves:]
    array_refs, refs = refs[: len(arrays)], refs[len(arrays) :]
    old_refs, refs = (None, refs) if fresh else (refs[:halves], refs[halves:])
    new_refs, (held_q, held, state) = refs[:-3], refs[-3:]
    rows, columns = q_refs[0].shape
    tiles = rows // TILE
    count = held.shape[1] // 2 // TILE
    heads = columns // HEAD_DIM
    me = lax.axis_index("seq")

    for half in range(halves):
        held_q[half] = q_refs[half][...]
        if fresh:
            state[half, :columns] = jnp.zeros((columns, rows), jnp.float32)
            state[half, columns : columns + heads] = jnp.full((heads, rows), LOWEST, jnp.float32)
            state[half, columns + heads :] = jnp.zeros((state.shape[1] - columns - heads, rows), jnp.float32)
        else:
            state[half] = old_refs[half][...]
    for slot, (array, shift) in enumerate(arrays):
        size = array_refs[array].shape[0]
        if size < held.shape[1]:
            held[slot] = jnp.zeros(held.shape[1:], held.dtype)
        at = 0 if shift is None else pl.multiple_of(shift(me), 2 * TILE)
        held[slot, pl.ds(at, size)] = array_refs[array][...]
    begins = [bounds_ref[2 * w, 0] for w in which]
    stops = [bounds_ref[2 * w + 1, rows - 1] for w in which]

    far = bounds_ref[8, 0] if unless_far else None

    def chosen(at, options):
        return functools.reduce(lambda x, i: jnp.where(at == i, options[i], x), range(1, len(options)), options[0])

    def fold(half, slot, first):
        row = 2 * (which[0] + half * (which[-1] - which[0]) // max(len(which) - 1, 1))
        low = bounds_ref[pl.ds(row, 1), :]
        high = bounds_ref[pl.ds(row + 1, 1), :]
        off = [
            jnp.where((first + j >= low) & (first + j < high), 0.0, -LOWEST).astype(jnp.float32)
            for j in range(count)
        ]
        maxima = [[state[half, pl.ds(columns + h, 1), tile_rows(t)] for t in range(tiles)] for h in range(heads)]
        totals = [state[half, pl.ds(columns + heads + h, 1), :] for h in range(heads)]
        scores = [
            lax.dot_general(
                jnp.concatenate([held[slot, tile_rows(2 * j), head_columns(h)] for j in range(count)], axis=0),
                held_q[half, :, head_columns(h)],
                (((1,), (1,)), ((), ())),
                preferred_element_type=jnp.float32,
            )
            for h in range(heads)
        ]
        factors, sums, updates, largest = [], [], [], []
        for h in range(heads):
            factor, rounded, total, new = [], [], [], []
            for t in range(tiles):
                lanes = tile_rows(t)
                parts = [scores[h][tile_rows(j), lanes] for j in range(count)]
                new_max = maxima[h][t]
                for j in range(count):
                    new_max = jnp.maximum(new_max, jnp.max(parts[j], axis=0, keepdims=True) - off[j][:, lanes])
                scaled = new_max * SCALE2
                weights = [jnp.exp2(parts[j] * SCALE2 - (scaled + off[j][:, lanes])) for j in range(count)]
                factor.append(jnp.exp2((maxima[h][t] - new_max) * SCALE2))
                total.append(jnp.sum(functools.reduce(jnp.add, weights), axis=0, keepdims=True))
                new.append(new_max)
                rounded.append(jnp.concatenate([w.astype(jnp.bfloat16) for w in weights], axis=0))
            updates.append(
                jnp.dot(
                    jnp.concatenate([held[slot, tile_rows(2 * j + 1), head_columns(h)] for j in range(count)], axis=1),
                    jnp.concatenate(rounded, axis=1),
                    preferred_element_type=jnp.float32,
                )
            )
            factors.append(jnp.concatenate(factor, axis=1))
            sums.append(jnp.concatenate(total, axis=1))
            largest.append(jnp.concatenate(new, axis=1))
        for h in range(heads):
            own = head_columns(h)
            state[half, own] = state[half, own] * factors[h] + updates[h]
            state[half, pl.ds(columns + h, 1), :] = largest[h]
            state[half, pl.ds(columns + heads + h, 1), :] = totals[h] * factors[h] + sums[h]

    @pl.loop(0, halves * len(places))
    def _(unit):
        half, slot = unit // len(places), unit % len(places)
        first = chosen(slot, [place(me) for place in places])

        if unless_far:
            first = jnp.where(far > 0, -count, first)

        @pl.when((first < chosen(half, stops)) & (first + count > chosen(half, begins)))
        def _():
            fold(half, slot, first)

    for half in range(halves):
        if brief:
            at = half * new_refs[0].shape[0] // halves
            new_refs[0][at : at + columns] = state[half, :columns].astype(jnp.bfloat16)
            for n, part in enumerate(summands(state[half, columns:])):
                row = at + columns + n * 2 * 8
                new_refs[0][row : row + 2 * 8] = jnp.concatenate([part, part], axis=0)
        else:
            new_refs[half][...] = state[half]


def attend(bounds, queries, blocks, places, states, which=None, shifts=None, unless_far=False, brief=False):
    which = list(range(len(queries))) if which is None else which
    queries, states = [queries[w] for w in which], [states[w] for w in which] if states else []
    halves = len(which)
    rows, columns = queries[0].shape
    depth = blocks[0].shape[0]
    heads = columns // HEAD_DIM
    shape = jax.ShapeDtypeStruct((columns + -(-2 * heads // 8) * 8, rows), jnp.float32)
    arrays = list(enumerate(shifts or [None] * len(blocks)))
    pairs = halves * (rows // TILE) * heads * len(blocks) * (depth // 2 // TILE)
    sent = jax.ShapeDtypeStruct((halves * (columns + 3 * 2 * 8), rows), jnp.bfloat16)
    return pl.pallas_call(
        functools.partial(attend_kernel, which, places, arrays, not states, unless_far, brief),
        out_shape=[sent] if brief else [shape] * halves,
        in_specs=[VMEM] * (1 + halves + len(blocks) + len(states)),
        out_specs=[VMEM] * (1 if brief else halves),
        scratch_shapes=[
            pltpu.VMEM((halves, rows, columns), queries[0].dtype),
            pltpu.VMEM((len(blocks), depth, columns), blocks[0].dtype),
            pltpu.VMEM((halves,) + shape.shape, jnp.float32),
        ],
        compiler_params=params(),
        cost_estimate=pl.CostEstimate(
            flops=COST * pairs * 4 * TILE * TILE * HEAD_DIM,
            bytes_accessed=2 * len(blocks) * depth * columns + 4 * halves * rows * columns,
            transcendentals=pairs * TILE * TILE,
        ),
        name="attend",
    )(bounds, *queries, *blocks, *states)


def merged(states, columns):
    heads = columns // HEAD_DIM
    for h in range(heads):
        maxima = [ref[columns + h : columns + h + 1] for ref in states]
        totals = [ref[columns + heads + h : columns + heads + h + 1] for ref in states]
        largest = functools.reduce(jnp.maximum, maxima)
        factors = [jnp.exp2((m - largest) * SCALE2) for m in maxima]
        total = functools.reduce(jnp.add, [f * t for f, t in zip(factors, totals)])
        parts = [ref[head_columns(h)] * (f / total) for ref, f in zip(states, factors)]
        yield head_columns(h), functools.reduce(jnp.add, parts).T


def finish_kernel(*refs):
    out_ref = refs[-1]
    for own, done in merged(refs[:-1], out_ref.shape[1]):
        out_ref[:, own] = done.astype(out_ref.dtype)


def finish(states, rows, columns):
    return pl.pallas_call(
        finish_kernel,
        out_shape=jax.ShapeDtypeStruct((rows, columns), jnp.bfloat16),
        in_specs=[VMEM] * len(states),
        out_specs=VMEM,
        compiler_params=params(),
        name="finish",
    )(*states)


def message_kernel(*refs):
    states, got_ref, outs, held = refs[:2], refs[2], refs[3:7], refs[7]
    rows = outs[0].shape[0] - 2 * 8
    columns = outs[0].shape[1]
    heads = columns // HEAD_DIM
    mine = lax.axis_index("head")
    for part in range(2):
        ref, (keep_ref, send_ref) = states[part], outs[2 * part : 2 * part + 2]
        at = part * got_ref.shape[0] // 2
        logs = []
        rest = got_ref[at + columns : at + got_ref.shape[0] // 2].astype(jnp.float32)
        statistics = functools.reduce(jnp.add, [rest[n * 2 * 8 : n * 2 * 8 + 8] for n in range(3)])
        for h in range(heads):
            maxima = [ref[columns + h : columns + h + 1], statistics[h : h + 1]]
            totals = [ref[columns + heads + h : columns + heads + h + 1], statistics[heads + h : heads + h + 1]]
            largest = jnp.maximum(*maxima)
            factors = [jnp.exp2((m - largest) * SCALE2) for m in maxima]
            total = factors[0] * totals[0] + factors[1] * totals[1]
            some = jnp.where(total > 0, total, 1.0)
            scale = [f / some for f in factors]
            own = head_columns(h)
            got = got_ref[at + h * HEAD_DIM : at + (h + 1) * HEAD_DIM].astype(jnp.float32)
            sums = ref[own] * scale[0] + got * scale[1]
            held[:, own] = sums.T.astype(held.dtype)
            log = jnp.where(total > 0, largest * SCALE2 + jnp.log2(some), LOWEST)
            logs += [part.astype(jnp.float32) for part in summands(log)]
        logs = jnp.concatenate(logs + [jnp.zeros((2 * 8 - len(logs), held.shape[0]), jnp.float32)], axis=0)
        later = pltpu.roll(logs, rows, 1)
        for out_ref, which in ((send_ref, 1 - mine), (keep_ref, mine)):
            out_ref[:rows] = held[pl.ds(pl.multiple_of(which * rows, 2 * 8), rows), :]
            out_ref[rows:] = jnp.where(which == 0, logs, later).astype(out_ref.dtype)


def messages(mine, peer, got):
    rows, columns = mine.shape[1], mine.shape[0] // HEAD_DIM * HEAD_DIM
    shape = jax.ShapeDtypeStruct((rows // 2 + 2 * 8, columns), jnp.bfloat16)
    return pl.pallas_call(
        message_kernel,
        out_shape=[shape] * 4,
        in_specs=[VMEM] * 3,
        out_specs=[VMEM] * 4,
        scratch_shapes=[pltpu.VMEM((rows, columns), jnp.bfloat16)],
        compiler_params=params(),
        name="message",
    )(mine, peer, got)


def settle_kernel(*refs):
    parts, out_ref, logs = refs[:4], refs[4], refs[5]
    rows, columns = out_ref.shape[0], parts[0].shape[1]
    heads = columns // HEAD_DIM
    mine = lax.axis_index("head")
    logs[...] = jnp.zeros(logs.shape, jnp.float32)
    for i, ref in enumerate(parts):
        summands = ref[rows:].astype(jnp.float32)
        for h in range(heads):
            at = i * heads + h
            logs[at : at + 1] = functools.reduce(jnp.add, [summands[3 * h + n : 3 * h + n + 1] for n in range(3)])
    turned = logs[...].T[:rows]
    for side, base in ((0, 1 - mine), (1, mine)):
        for h in range(heads):
            both = [turned[:, at : at + 1] for at in (2 * side * heads + h, (2 * side + 1) * heads + h)]
            largest = jnp.maximum(*both)
            weights = [jnp.exp2(x - largest) for x in both]
            sums = [ref[:rows, head_columns(h)].astype(jnp.float32) for ref in parts[2 * side : 2 * side + 2]]
            total = weights[0] + weights[1]
            done = sums[0] * (weights[0] / total) + sums[1] * (weights[1] / total)
            at = pl.multiple_of(base * columns + h * HEAD_DIM, HEAD_DIM)
            out_ref[:, pl.ds(at, HEAD_DIM)] = done.astype(out_ref.dtype)


def settle(diagonal, beside, across, own):
    rows, columns = own.shape[0] - 2 * 8, own.shape[1]
    return pl.pallas_call(
        settle_kernel,
        out_shape=jax.ShapeDtypeStruct((rows, 2 * columns), own.dtype),
        in_specs=[VMEM] * 4,
        out_specs=VMEM,
        scratch_shapes=[pltpu.VMEM((TILE, columns), jnp.float32)],
        compiler_params=params(),
        name="settle",
    )(diagonal, beside, across, own)


def chip_pairs(mesh):
    places = [tuple(getattr(d, "coords", ())) for d in mesh.devices[:, 0]]
    count = len(places)
    if count % 4 or not places[0] or mesh.shape["head"] != 2:
        return False
    cores = all(places[i] == places[i + 1] for i in range(0, count, 2))
    level = all(places[i][2] == places[i + 3][2] for i in range(0, count, 4))
    climb = all(places[i][2] != places[i + 4][2] for i in range(0, count - 4))
    return cores and level and climb


def paired_shards(owner_count, queries, keys, values, image_tiles):
    rows, columns = queries.shape
    tiles = rows // TILE
    owners = range(owner_count)

    def flip(s):
        return 1 - 2 * ((s // 2) % 2)

    def core(s):
        return s % 2

    def moved(array, source, takes=lambda s: True):
        pairs = [(source(s), s) for s in owners if takes(s) and 0 <= source(s) < owner_count]
        return lax.ppermute(array, "seq", pairs)

    across = lambda s: s + 2 * flip(s)
    near_side = lambda s: s + 4 * flip(s)
    far_side = lambda s: s - 4 * flip(s)
    along = lambda s: s + 4 * flip(s) * (1 - 2 * core(s))
    against = lambda s: s - 4 * flip(s) * (1 - 2 * core(s))
    sibling = lambda s: s + 1 - 2 * core(s)
    inner = lambda s: core(s) == (1 - (s // 2) % 2)

    OWN = lambda s: s * tiles
    A1 = lambda s: along(s) * tiles
    B1 = lambda s: against(s) * tiles
    A2 = lambda s: (s + 8 * flip(s)) * tiles
    B2 = lambda s: jnp.where(inner(s), s - 8 * flip(s), -owner_count) * tiles

    peers = moved(queries, across)
    block = pack(keys, values)
    a1, b1 = moved(block, along), moved(block, against)
    level = (queries, moved(queries, sibling), peers, moved(peers, sibling))
    bounds, far = meta(lambda s: [s, sibling(s), across(s), sibling(across(s))], image_tiles, rows)
    fold = functools.partial(attend, bounds, level)
    states = fold([block], [OWN], [], which=[0, 1]) + fold([block], [OWN], [], which=[2, 3])
    states = fold([b1], [B1], states, unless_far=True)

    def merge(blocks, places, states, shifts=None):
        (others,) = fold(blocks, places, states, which=[1, 3], shifts=shifts, brief=True)
        got = moved(others, sibling)
        mine, peer = fold(blocks, places, states, which=[0, 2], shifts=shifts)
        keep, over_x, over_y, over_both = messages(mine, peer, got)
        pairs = [(2 * across(s) + 1 - x, 2 * s + x) for s in owners for x in range(2)]
        over_both = lax.ppermute(over_both, ("seq", "head"), pairs)
        over_y = moved(over_y, across)
        over_x = lax.ppermute(over_x, "head", [(0, 1), (1, 0)])
        return settle(over_both, over_x, over_y, keep)

    def near_only(block, a1, b1, states):
        return merge([a1], [A1], states)

    def both_ways(block, a1, b1, states):
        near, corner = onward(a1, b1, block)
        a2, b2 = moved(near, near_side), moved(corner, far_side, inner)
        states = fold([a1, b1], [A1, B1], states)
        return merge([a2, b2], [A2, B2], states, [None, lambda s: 2 * TILE * core(s)])

    return lax.cond(far > 0, both_ways, near_only, block, a1, b1, states)


def ring_shards(owner_count, queries, keys, values, image_tiles):
    rows, columns = queries.shape
    tiles = rows // TILE
    reach = min(owner_count - 1, -(-(MOST_TILES - 1) // tiles))
    block = pack(keys, values)
    bounds, _ = meta(lambda s: [s], image_tiles, rows)
    fold = functools.partial(attend, bounds, (queries,))
    up = [(i, i + 1) for i in range(owner_count - 1)]
    down = [(i + 1, i) for i in range(owner_count - 1)]
    below = above = block
    states = []
    held, places = [block], [lambda s: s * tiles]
    for k in range(1, reach + 1):
        below = lax.ppermute(below, "seq", up)
        above = lax.ppermute(above, "seq", down)
        states = fold(held, places, states)
        held, places = [below, above], [lambda s, k=k: (s - k) * tiles, lambda s, k=k: (s + k) * tiles]
    attended = finish(fold(held, places, states), rows, columns)
    return lax.all_to_all(attended, "head", split_axis=0, concat_axis=1, tiled=True)


def solution(mesh):
    owner_count = mesh.shape["seq"]
    plan = paired_shards if chip_pairs(mesh) else ring_shards
    placed = (P("seq", "head"), P("seq", "head"), P("seq", "head"), P())
    return jax.shard_map(
        functools.partial(plan, owner_count),
        mesh=mesh,
        in_specs=placed,
        out_specs=P(("seq", "head"), None),
        check_vma=False,
    )
```

```python
import functools
import math

import jax
import jax.numpy as jnp
from jax import lax
from jax.experimental import pallas as pl
from jax.experimental.pallas import tpu as pltpu
from jax.sharding import PartitionSpec as P

HEAD_DIM = 128
TILE = 128
MOST_TILES = 21

LOWEST = -1e30
SCALE2 = math.log2(math.e) / math.sqrt(HEAD_DIM)
COST = 2

VMEM = pl.BlockSpec(memory_space=pltpu.VMEM)
SMEM = pl.BlockSpec(memory_space=pltpu.SMEM)
HBM = pl.BlockSpec(memory_space=pl.ANY)


def params():
    return pltpu.CompilerParams(vmem_limit_bytes=16 * 1024 * 1024)


def head_columns(h):
    return slice(h * HEAD_DIM, (h + 1) * HEAD_DIM)


def tile_rows(t):
    return slice(t * TILE, (t + 1) * TILE)


def image_bounds(tiles_ref, tile):
    first = jnp.int32(0)
    start, end = jnp.int32(0), jnp.int32(0)
    for i in range(tiles_ref.shape[0]):
        after = first + tiles_ref[i]
        inside = (tile >= first) & (tile < after)
        start = jnp.where(inside, first, start)
        end = jnp.where(inside, after, end)
        first = after
    return start, end


def meta_kernel(halves, tiles_ref, bounds_ref, far_ref):
    tiles = bounds_ref.shape[1] // TILE
    me = lax.axis_index("seq")
    bounds_ref[...] = jnp.zeros(bounds_ref.shape, jnp.int32)
    for half, owner in enumerate(halves(me)):
        for t in range(tiles):
            start, end = image_bounds(tiles_ref, owner * tiles + t)
            bounds_ref[2 * half : 2 * half + 1, tile_rows(t)] = jnp.full((1, TILE), start, jnp.int32)
            bounds_ref[2 * half + 1 : 2 * half + 2, tile_rows(t)] = jnp.full((1, TILE), end, jnp.int32)
    first = jnp.int32(0)
    far = jnp.int32(0)
    for i in range(tiles_ref.shape[0]):
        after = first + tiles_ref[i]
        levels = (after - 1) // (4 * tiles) - first // (4 * tiles)
        far = jnp.where(levels >= 2, 1, far)
        first = after
    far_ref[0] = far
    bounds_ref[8:9] = jnp.full((1, bounds_ref.shape[1]), far, jnp.int32)


def meta(halves, image_tiles, rows):
    bounds, far = pl.pallas_call(
        functools.partial(meta_kernel, halves),
        out_shape=[jax.ShapeDtypeStruct((16, rows), jnp.int32), jax.ShapeDtypeStruct((1,), jnp.int32)],
        in_specs=[SMEM],
        out_specs=[VMEM, SMEM],
        compiler_params=params(),
        cost_estimate=pl.CostEstimate(flops=COST * 2**28, bytes_accessed=0, transcendentals=0),
        name="meta",
    )(image_tiles)
    return bounds, far[0]


def pack_kernel(k_ref, v_ref, out_ref, held, sems):
    rows, columns = k_ref.shape
    tiles = rows // TILE
    copies = []
    for t in range(tiles):
        copies.append(pltpu.make_async_copy(v_ref.at[tile_rows(t)], held.at[tile_rows(t)], sems.at[2 * t]))
        copies.append(pltpu.make_async_copy(k_ref.at[tile_rows(t)], out_ref.at[tile_rows(2 * t)], sems.at[2 * t + 1]))
    for copy in copies:
        copy.start()
    for t in range(tiles):
        copies[2 * t].wait()
        for h in range(columns // HEAD_DIM):
            out_ref[tile_rows(2 * t + 1), head_columns(h)] = held[tile_rows(t), head_columns(h)].T
    for copy in copies[1::2]:
        copy.wait()


def pack(keys, values):
    rows, columns = keys.shape
    return pl.pallas_call(
        pack_kernel,
        out_shape=jax.ShapeDtypeStruct((2 * rows, columns), keys.dtype),
        in_specs=[HBM, HBM],
        out_specs=VMEM,
        scratch_shapes=[pltpu.VMEM(values.shape, values.dtype), pltpu.SemaphoreType.DMA((2 * rows // TILE,))],
        name="pack",
    )(keys, values)


def onward_kernel(a1_ref, b1_ref, own_ref, near_ref, corner_ref):
    upper = lax.axis_index("seq") % 2
    rows = corner_ref.shape[0]

    @pl.when(upper == 0)
    def _():
        near_ref[...] = a1_ref[...]
        corner_ref[...] = b1_ref[:rows]

    @pl.when(upper == 1)
    def _():
        near_ref[...] = b1_ref[...]
        corner_ref[...] = a1_ref[-rows:]


def onward(a1, b1, own):
    rows, columns = a1.shape
    return pl.pallas_call(
        onward_kernel,
        out_shape=[
            jax.ShapeDtypeStruct((rows, columns), a1.dtype),
            jax.ShapeDtypeStruct((rows - 2 * TILE, columns), a1.dtype),
        ],
        in_specs=[VMEM, VMEM, HBM],
        out_specs=[VMEM, VMEM],
        compiler_params=params(),
        name="onward",
    )(a1, b1, own)


def summands(rows):
    parts = []
    for _ in range(3):
        parts.append(rows.astype(jnp.bfloat16))
        rows = rows - parts[-1].astype(jnp.float32)
    return parts


def attend_kernel(which, places, arrays, fresh, unless_far, brief, bounds_ref, *refs):
    halves = len(which)
    q_refs, refs = refs[:halves], refs[halves:]
    array_refs, refs = refs[: len(arrays)], refs[len(arrays) :]
    old_refs, refs = (None, refs) if fresh else (refs[:halves], refs[halves:])
    new_refs, (held_q, held, state) = refs[:-3], refs[-3:]
    rows, columns = q_refs[0].shape
    tiles = rows // TILE
    count = held.shape[1] // 2 // TILE
    heads = columns // HEAD_DIM
    me = lax.axis_index("seq")

    for half in range(halves):
        held_q[half] = q_refs[half][...]
        if fresh:
            state[half, :columns] = jnp.zeros((columns, rows), jnp.float32)
            state[half, columns : columns + heads] = jnp.full((heads, rows), LOWEST, jnp.float32)
            state[half, columns + heads :] = jnp.zeros((state.shape[1] - columns - heads, rows), jnp.float32)
        else:
            state[half] = old_refs[half][...]
    alone = len(arrays) == 1
    for slot, (array, shift) in enumerate([] if alone else arrays):
        size = array_refs[array].shape[0]
        if size < held.shape[1]:
            held[slot] = jnp.zeros(held.shape[1:], held.dtype)
        at = 0 if shift is None else pl.multiple_of(shift(me), 2 * TILE)
        held[slot, pl.ds(at, size)] = array_refs[array][...]
    begins = [bounds_ref[2 * w, 0] for w in which]
    stops = [bounds_ref[2 * w + 1, rows - 1] for w in which]

    far = bounds_ref[8, 0] if unless_far else None

    def chosen(at, options):
        return functools.reduce(lambda x, i: jnp.where(at == i, options[i], x), range(1, len(options)), options[0])

    def piece(slot, at, h):
        if alone:
            return array_refs[0][tile_rows(at), head_columns(h)]
        return held[slot, tile_rows(at), head_columns(h)]

    def fold(half, slot, first):
        row = 2 * (which[0] + half * (which[-1] - which[0]) // max(len(which) - 1, 1))
        low = bounds_ref[pl.ds(row, 1), :]
        high = bounds_ref[pl.ds(row + 1, 1), :]
        off = [
            jnp.where((first + j >= low) & (first + j < high), 0.0, -LOWEST).astype(jnp.float32)
            for j in range(count)
        ]
        maxima = [[state[half, pl.ds(columns + h, 1), tile_rows(t)] for t in range(tiles)] for h in range(heads)]
        totals = [state[half, pl.ds(columns + heads + h, 1), :] for h in range(heads)]
        scores = [
            lax.dot_general(
                jnp.concatenate([piece(slot, 2 * j, h) for j in range(count)], axis=0),
                held_q[half, :, head_columns(h)],
                (((1,), (1,)), ((), ())),
                preferred_element_type=jnp.float32,
            )
            for h in range(heads)
        ]
        factors, sums, updates, largest = [], [], [], []
        for h in range(heads):
            factor, rounded, total, new = [], [], [], []
            for t in range(tiles):
                lanes = tile_rows(t)
                parts = [scores[h][tile_rows(j), lanes] for j in range(count)]
                new_max = maxima[h][t]
                for j in range(count):
                    new_max = jnp.maximum(new_max, jnp.max(parts[j], axis=0, keepdims=True) - off[j][:, lanes])
                scaled = new_max * SCALE2
                weights = [jnp.exp2(parts[j] * SCALE2 - (scaled + off[j][:, lanes])) for j in range(count)]
                factor.append(jnp.exp2((maxima[h][t] - new_max) * SCALE2))
                total.append(jnp.sum(functools.reduce(jnp.add, weights), axis=0, keepdims=True))
                new.append(new_max)
                rounded.append(jnp.concatenate([w.astype(jnp.bfloat16) for w in weights], axis=0))
            updates.append(
                jnp.dot(
                    jnp.concatenate([piece(slot, 2 * j + 1, h) for j in range(count)], axis=1),
                    jnp.concatenate(rounded, axis=1),
                    preferred_element_type=jnp.float32,
                )
            )
            factors.append(jnp.concatenate(factor, axis=1))
            sums.append(jnp.concatenate(total, axis=1))
            largest.append(jnp.concatenate(new, axis=1))
        for h in range(heads):
            own = head_columns(h)
            state[half, own] = state[half, own] * factors[h] + updates[h]
            state[half, pl.ds(columns + h, 1), :] = largest[h]
            state[half, pl.ds(columns + heads + h, 1), :] = totals[h] * factors[h] + sums[h]

    @pl.loop(0, halves * len(places))
    def _(unit):
        half, slot = unit // len(places), unit % len(places)
        first = chosen(slot, [place(me) for place in places])

        if unless_far:
            first = jnp.where(far > 0, -count, first)

        @pl.when((first < chosen(half, stops)) & (first + count > chosen(half, begins)))
        def _():
            fold(half, slot, first)

    for half in range(halves):
        if brief:
            at = half * new_refs[0].shape[0] // halves
            new_refs[0][at : at + columns] = state[half, :columns].astype(jnp.bfloat16)
            for n, part in enumerate(summands(state[half, columns:])):
                row = at + columns + n * 2 * 8
                new_refs[0][row : row + 2 * 8] = jnp.concatenate([part, part], axis=0)
        else:
            new_refs[half][...] = state[half]


def attend(bounds, queries, blocks, places, states, which=None, shifts=None, unless_far=False, brief=False):
    which = list(range(len(queries))) if which is None else which
    queries, states = [queries[w] for w in which], [states[w] for w in which] if states else []
    halves = len(which)
    rows, columns = queries[0].shape
    depth = blocks[0].shape[0]
    heads = columns // HEAD_DIM
    shape = jax.ShapeDtypeStruct((columns + -(-2 * heads // 8) * 8, rows), jnp.float32)
    arrays = list(enumerate(shifts or [None] * len(blocks)))
    pairs = halves * (rows // TILE) * heads * len(blocks) * (depth // 2 // TILE)
    sent = jax.ShapeDtypeStruct((halves * (columns + 3 * 2 * 8), rows), jnp.bfloat16)
    return pl.pallas_call(
        functools.partial(attend_kernel, which, places, arrays, not states, unless_far, brief),
        out_shape=[sent] if brief else [shape] * halves,
        in_specs=[VMEM] * (1 + halves + len(blocks) + len(states)),
        out_specs=[VMEM] * (1 if brief else halves),
        scratch_shapes=[
            pltpu.VMEM((halves, rows, columns), queries[0].dtype),
            pltpu.VMEM((len(blocks), depth, columns), blocks[0].dtype),
            pltpu.VMEM((halves,) + shape.shape, jnp.float32),
        ],
        compiler_params=params(),
        cost_estimate=pl.CostEstimate(
            flops=COST * pairs * 4 * TILE * TILE * HEAD_DIM,
            bytes_accessed=2 * len(blocks) * depth * columns + 4 * halves * rows * columns,
            transcendentals=pairs * TILE * TILE,
        ),
        name="attend",
    )(bounds, *queries, *blocks, *states)


def merged(states, columns):
    heads = columns // HEAD_DIM
    for h in range(heads):
        maxima = [ref[columns + h : columns + h + 1] for ref in states]
        totals = [ref[columns + heads + h : columns + heads + h + 1] for ref in states]
        largest = functools.reduce(jnp.maximum, maxima)
        factors = [jnp.exp2((m - largest) * SCALE2) for m in maxima]
        total = functools.reduce(jnp.add, [f * t for f, t in zip(factors, totals)])
        parts = [ref[head_columns(h)] * (f / total) for ref, f in zip(states, factors)]
        yield head_columns(h), functools.reduce(jnp.add, parts).T


def finish_kernel(*refs):
    out_ref = refs[-1]
    for own, done in merged(refs[:-1], out_ref.shape[1]):
        out_ref[:, own] = done.astype(out_ref.dtype)


def finish(states, rows, columns):
    return pl.pallas_call(
        finish_kernel,
        out_shape=jax.ShapeDtypeStruct((rows, columns), jnp.bfloat16),
        in_specs=[VMEM] * len(states),
        out_specs=VMEM,
        compiler_params=params(),
        name="finish",
    )(*states)


def message_kernel(part, ref, got_ref, *refs):
    keep_ref, send_ref, held = refs[-3:]
    rows = keep_ref.shape[0] - 2 * 8
    columns = keep_ref.shape[1]
    heads = columns // HEAD_DIM
    mine = lax.axis_index("head")
    at = part * got_ref.shape[0] // 2
    logs = []
    rest = got_ref[at + columns : at + got_ref.shape[0] // 2].astype(jnp.float32)
    statistics = functools.reduce(jnp.add, [rest[n * 2 * 8 : n * 2 * 8 + 8] for n in range(3)])
    for h in range(heads):
        maxima = [ref[columns + h : columns + h + 1], statistics[h : h + 1]]
        totals = [ref[columns + heads + h : columns + heads + h + 1], statistics[heads + h : heads + h + 1]]
        largest = jnp.maximum(*maxima)
        factors = [jnp.exp2((m - largest) * SCALE2) for m in maxima]
        total = factors[0] * totals[0] + factors[1] * totals[1]
        some = jnp.where(total > 0, total, 1.0)
        scale = [f / some for f in factors]
        own = head_columns(h)
        got = got_ref[at + h * HEAD_DIM : at + (h + 1) * HEAD_DIM].astype(jnp.float32)
        sums = ref[own] * scale[0] + got * scale[1]
        held[:, own] = sums.T.astype(held.dtype)
        log = jnp.where(total > 0, largest * SCALE2 + jnp.log2(some), LOWEST)
        logs += [part.astype(jnp.float32) for part in summands(log)]
    logs = jnp.concatenate(logs + [jnp.zeros((2 * 8 - len(logs), held.shape[0]), jnp.float32)], axis=0)
    later = pltpu.roll(logs, rows, 1)
    for out_ref, which in ((send_ref, 1 - mine), (keep_ref, mine)):
        out_ref[:rows] = held[pl.ds(pl.multiple_of(which * rows, 2 * 8), rows), :]
        out_ref[rows:] = jnp.where(which == 0, logs, later).astype(out_ref.dtype)


def messages(part, state, got, *after):
    rows, columns = state.shape[1], state.shape[0] // HEAD_DIM * HEAD_DIM
    shape = jax.ShapeDtypeStruct((rows // 2 + 2 * 8, columns), jnp.bfloat16)
    return pl.pallas_call(
        functools.partial(message_kernel, part),
        out_shape=[shape] * 2,
        in_specs=[VMEM] * 2 + [HBM] * len(after),
        out_specs=[VMEM] * 2,
        scratch_shapes=[pltpu.VMEM((rows, columns), jnp.bfloat16)],
        compiler_params=params(),
        name="message",
    )(state, got, *after)


def settle_kernel(*refs):
    parts, out_ref, logs = refs[:4], refs[4], refs[5]
    rows, columns = out_ref.shape[0], parts[0].shape[1]
    heads = columns // HEAD_DIM
    mine = lax.axis_index("head")
    logs[...] = jnp.zeros(logs.shape, jnp.float32)
    for i, ref in enumerate(parts):
        summands = ref[rows:].astype(jnp.float32)
        for h in range(heads):
            at = i * heads + h
            logs[at : at + 1] = functools.reduce(jnp.add, [summands[3 * h + n : 3 * h + n + 1] for n in range(3)])
    turned = logs[...].T[:rows]
    for side, base in ((0, 1 - mine), (1, mine)):
        for h in range(heads):
            both = [turned[:, at : at + 1] for at in (2 * side * heads + h, (2 * side + 1) * heads + h)]
            largest = jnp.maximum(*both)
            weights = [jnp.exp2(x - largest) for x in both]
            sums = [ref[:rows, head_columns(h)].astype(jnp.float32) for ref in parts[2 * side : 2 * side + 2]]
            total = weights[0] + weights[1]
            done = sums[0] * (weights[0] / total) + sums[1] * (weights[1] / total)
            at = pl.multiple_of(base * columns + h * HEAD_DIM, HEAD_DIM)
            out_ref[:, pl.ds(at, HEAD_DIM)] = done.astype(out_ref.dtype)


def settle(diagonal, beside, across, own):
    rows, columns = own.shape[0] - 2 * 8, own.shape[1]
    return pl.pallas_call(
        settle_kernel,
        out_shape=jax.ShapeDtypeStruct((rows, 2 * columns), own.dtype),
        in_specs=[VMEM] * 4,
        out_specs=VMEM,
        scratch_shapes=[pltpu.VMEM((TILE, columns), jnp.float32)],
        compiler_params=params(),
        name="settle",
    )(diagonal, beside, across, own)


def chip_pairs(mesh):
    places = [tuple(getattr(d, "coords", ())) for d in mesh.devices[:, 0]]
    count = len(places)
    if count % 4 or not places[0] or mesh.shape["head"] != 2:
        return False
    cores = all(places[i] == places[i + 1] for i in range(0, count, 2))
    level = all(places[i][2] == places[i + 3][2] for i in range(0, count, 4))
    climb = all(places[i][2] != places[i + 4][2] for i in range(0, count - 4))
    return cores and level and climb


def paired_shards(owner_count, queries, keys, values, image_tiles):
    rows, columns = queries.shape
    tiles = rows // TILE
    owners = range(owner_count)

    def flip(s):
        return 1 - 2 * ((s // 2) % 2)

    def core(s):
        return s % 2

    def moved(array, source, takes=lambda s: True):
        pairs = [(source(s), s) for s in owners if takes(s) and 0 <= source(s) < owner_count]
        return lax.ppermute(array, "seq", pairs)

    across = lambda s: s + 2 * flip(s)
    near_side = lambda s: s + 4 * flip(s)
    far_side = lambda s: s - 4 * flip(s)
    along = lambda s: s + 4 * flip(s) * (1 - 2 * core(s))
    against = lambda s: s - 4 * flip(s) * (1 - 2 * core(s))
    sibling = lambda s: s + 1 - 2 * core(s)
    inner = lambda s: core(s) == (1 - (s // 2) % 2)

    OWN = lambda s: s * tiles
    A1 = lambda s: along(s) * tiles
    B1 = lambda s: against(s) * tiles
    A2 = lambda s: (s + 8 * flip(s)) * tiles
    B2 = lambda s: jnp.where(inner(s), s - 8 * flip(s), -owner_count) * tiles

    peers = moved(queries, across)
    block = pack(keys, values)
    a1, b1 = moved(block, along), moved(block, against)
    level = (queries, moved(queries, sibling), peers, moved(peers, sibling))
    bounds, far = meta(lambda s: [s, sibling(s), across(s), sibling(across(s))], image_tiles, rows)
    fold = functools.partial(attend, bounds, level)
    states = fold([block], [OWN], [], which=[0, 1]) + fold([block], [OWN], [], which=[2, 3])
    states = fold([b1], [B1], states, unless_far=True)

    def merge(blocks, places, states, shifts=None):
        (others,) = fold(blocks, places, states, which=[1, 3], shifts=shifts, brief=True)
        got = moved(others, sibling)
        mine, peer = fold(blocks, places, states, which=[0, 2], shifts=shifts)
        over_y, over_both = messages(1, peer, got)
        keep, over_x = messages(0, mine, got, over_y)
        pairs = [(2 * across(s) + 1 - x, 2 * s + x) for s in owners for x in range(2)]
        over_both = lax.ppermute(over_both, ("seq", "head"), pairs)
        over_y = moved(over_y, across)
        over_x = lax.ppermute(over_x, "head", [(0, 1), (1, 0)])
        return settle(over_both, over_x, over_y, keep)

    def near_only(block, a1, b1, states):
        return merge([a1], [A1], states)

    def both_ways(block, a1, b1, states):
        near, corner = onward(a1, b1, block)
        a2, b2 = moved(near, near_side), moved(corner, far_side, inner)
        states = fold([a1, b1], [A1, B1], states)
        return merge([a2, b2], [A2, B2], states, [None, lambda s: 2 * TILE * core(s)])

    return lax.cond(far > 0, both_ways, near_only, block, a1, b1, states)


def ring_shards(owner_count, queries, keys, values, image_tiles):
    rows, columns = queries.shape
    tiles = rows // TILE
    reach = min(owner_count - 1, -(-(MOST_TILES - 1) // tiles))
    block = pack(keys, values)
    bounds, _ = meta(lambda s: [s], image_tiles, rows)
    fold = functools.partial(attend, bounds, (queries,))
    up = [(i, i + 1) for i in range(owner_count - 1)]
    down = [(i + 1, i) for i in range(owner_count - 1)]
    below = above = block
    states = []
    held, places = [block], [lambda s: s * tiles]
    for k in range(1, reach + 1):
        below = lax.ppermute(below, "seq", up)
        above = lax.ppermute(above, "seq", down)
        states = fold(held, places, states)
        held, places = [below, above], [lambda s, k=k: (s - k) * tiles, lambda s, k=k: (s + k) * tiles]
    attended = finish(fold(held, places, states), rows, columns)
    return lax.all_to_all(attended, "head", split_axis=0, concat_axis=1, tiled=True)


def solution(mesh):
    owner_count = mesh.shape["seq"]
    plan = paired_shards if chip_pairs(mesh) else ring_shards
    placed = (P("seq", "head"), P("seq", "head"), P("seq", "head"), P())
    return jax.shard_map(
        functools.partial(plan, owner_count),
        mesh=mesh,
        in_specs=placed,
        out_specs=P(("seq", "head"), None),
        check_vma=False,
    )
```

```python
import functools
import math

import jax
import jax.numpy as jnp
from jax import lax
from jax.experimental import pallas as pl
from jax.experimental.pallas import tpu as pltpu
from jax.sharding import PartitionSpec as P

HEAD_DIM = 128
TILE = 128
MOST_TILES = 21

LOWEST = -1e30
SCALE2 = math.log2(math.e) / math.sqrt(HEAD_DIM)
COST = 2

VMEM = pl.BlockSpec(memory_space=pltpu.VMEM)
SMEM = pl.BlockSpec(memory_space=pltpu.SMEM)
HBM = pl.BlockSpec(memory_space=pl.ANY)


def params():
    return pltpu.CompilerParams(vmem_limit_bytes=16 * 1024 * 1024)


def head_columns(h):
    return slice(h * HEAD_DIM, (h + 1) * HEAD_DIM)


def tile_rows(t):
    return slice(t * TILE, (t + 1) * TILE)


def image_bounds(tiles_ref, tile):
    first = jnp.int32(0)
    start, end = jnp.int32(0), jnp.int32(0)
    for i in range(tiles_ref.shape[0]):
        after = first + tiles_ref[i]
        inside = (tile >= first) & (tile < after)
        start = jnp.where(inside, first, start)
        end = jnp.where(inside, after, end)
        first = after
    return start, end


def meta_kernel(halves, tiles_ref, bounds_ref, far_ref):
    tiles = bounds_ref.shape[1] // TILE
    me = lax.axis_index("seq")
    bounds_ref[...] = jnp.zeros(bounds_ref.shape, jnp.int32)
    for half, owner in enumerate(halves(me)):
        for t in range(tiles):
            start, end = image_bounds(tiles_ref, owner * tiles + t)
            bounds_ref[2 * half : 2 * half + 1, tile_rows(t)] = jnp.full((1, TILE), start, jnp.int32)
            bounds_ref[2 * half + 1 : 2 * half + 2, tile_rows(t)] = jnp.full((1, TILE), end, jnp.int32)
    first = jnp.int32(0)
    far = jnp.int32(0)
    for i in range(tiles_ref.shape[0]):
        after = first + tiles_ref[i]
        levels = (after - 1) // (4 * tiles) - first // (4 * tiles)
        far = jnp.where(levels >= 2, 1, far)
        first = after
    far_ref[0] = far
    bounds_ref[8:9] = jnp.full((1, bounds_ref.shape[1]), far, jnp.int32)


def meta(halves, image_tiles, rows):
    bounds, far = pl.pallas_call(
        functools.partial(meta_kernel, halves),
        out_shape=[jax.ShapeDtypeStruct((16, rows), jnp.int32), jax.ShapeDtypeStruct((1,), jnp.int32)],
        in_specs=[SMEM],
        out_specs=[VMEM, SMEM],
        compiler_params=params(),
        cost_estimate=pl.CostEstimate(flops=COST * 2**28, bytes_accessed=0, transcendentals=0),
        name="meta",
    )(image_tiles)
    return bounds, far[0]


def pack_kernel(k_ref, v_ref, out_ref, held, sems):
    rows, columns = k_ref.shape
    tiles = rows // TILE
    copies = []
    for t in range(tiles):
        copies.append(pltpu.make_async_copy(v_ref.at[tile_rows(t)], held.at[tile_rows(t)], sems.at[2 * t]))
        copies.append(pltpu.make_async_copy(k_ref.at[tile_rows(t)], out_ref.at[tile_rows(2 * t)], sems.at[2 * t + 1]))
    for copy in copies:
        copy.start()
    for t in range(tiles):
        copies[2 * t].wait()
        for h in range(columns // HEAD_DIM):
            out_ref[tile_rows(2 * t + 1), head_columns(h)] = held[tile_rows(t), head_columns(h)].T
    for copy in copies[1::2]:
        copy.wait()


def pack(keys, values):
    rows, columns = keys.shape
    return pl.pallas_call(
        pack_kernel,
        out_shape=jax.ShapeDtypeStruct((2 * rows, columns), keys.dtype),
        in_specs=[HBM, HBM],
        out_specs=VMEM,
        scratch_shapes=[pltpu.VMEM(values.shape, values.dtype), pltpu.SemaphoreType.DMA((2 * rows // TILE,))],
        name="pack",
    )(keys, values)


def onward_kernel(a1_ref, b1_ref, own_ref, near_ref, corner_ref):
    upper = lax.axis_index("seq") % 2
    rows = corner_ref.shape[0]

    @pl.when(upper == 0)
    def _():
        near_ref[...] = a1_ref[...]
        corner_ref[...] = b1_ref[:rows]

    @pl.when(upper == 1)
    def _():
        near_ref[...] = b1_ref[...]
        corner_ref[...] = a1_ref[-rows:]


def onward(a1, b1, own):
    rows, columns = a1.shape
    return pl.pallas_call(
        onward_kernel,
        out_shape=[
            jax.ShapeDtypeStruct((rows, columns), a1.dtype),
            jax.ShapeDtypeStruct((rows - 2 * TILE, columns), a1.dtype),
        ],
        in_specs=[VMEM, VMEM, HBM],
        out_specs=[VMEM, VMEM],
        compiler_params=params(),
        name="onward",
    )(a1, b1, own)


def summands(rows):
    parts = []
    for _ in range(3):
        parts.append(rows.astype(jnp.bfloat16))
        rows = rows - parts[-1].astype(jnp.float32)
    return parts


def attend_kernel(which, places, arrays, fresh, unless_far, brief, bounds_ref, *refs):
    halves = len(which)
    q_refs, refs = refs[:halves], refs[halves:]
    array_refs, refs = refs[: len(arrays)], refs[len(arrays) :]
    old_refs, refs = (None, refs) if fresh else (refs[:halves], refs[halves:])
    new_refs, (held_q, held, state) = refs[:-3], refs[-3:]
    rows, columns = q_refs[0].shape
    tiles = rows // TILE
    count = held.shape[1] // 2 // TILE
    heads = columns // HEAD_DIM
    me = lax.axis_index("seq")

    for half in range(halves):
        held_q[half] = q_refs[half][...]
        if fresh:
            state[half, :columns] = jnp.zeros((columns, rows), jnp.float32)
            state[half, columns : columns + heads] = jnp.full((heads, rows), LOWEST, jnp.float32)
            state[half, columns + heads :] = jnp.zeros((state.shape[1] - columns - heads, rows), jnp.float32)
        else:
            state[half] = old_refs[half][...]
    alone = len(arrays) == 1
    for slot, (array, shift) in enumerate([] if alone else arrays):
        size = array_refs[array].shape[0]
        if size < held.shape[1]:
            held[slot] = jnp.zeros(held.shape[1:], held.dtype)
        at = 0 if shift is None else pl.multiple_of(shift(me), 2 * TILE)
        held[slot, pl.ds(at, size)] = array_refs[array][...]
    begins = [bounds_ref[2 * w, 0] for w in which]
    stops = [bounds_ref[2 * w + 1, rows - 1] for w in which]

    far = bounds_ref[8, 0] if unless_far else None

    def chosen(at, options):
        return functools.reduce(lambda x, i: jnp.where(at == i, options[i], x), range(1, len(options)), options[0])

    def piece(slot, at, h):
        if alone:
            return array_refs[0][tile_rows(at), head_columns(h)]
        return held[slot, tile_rows(at), head_columns(h)]

    def fold(half, slot, first):
        row = 2 * (which[0] + half * (which[-1] - which[0]) // max(len(which) - 1, 1))
        low = bounds_ref[pl.ds(row, 1), :]
        high = bounds_ref[pl.ds(row + 1, 1), :]
        off = [
            jnp.where((first + j >= low) & (first + j < high), 0.0, -LOWEST).astype(jnp.float32)
            for j in range(count)
        ]
        maxima = [[state[half, pl.ds(columns + h, 1), tile_rows(t)] for t in range(tiles)] for h in range(heads)]
        totals = [state[half, pl.ds(columns + heads + h, 1), :] for h in range(heads)]
        scores = [
            lax.dot_general(
                jnp.concatenate([piece(slot, 2 * j, h) for j in range(count)], axis=0),
                held_q[half, :, head_columns(h)],
                (((1,), (1,)), ((), ())),
                preferred_element_type=jnp.float32,
            )
            for h in range(heads)
        ]
        factors, sums, updates, largest = [], [], [], []
        for h in range(heads):
            factor, rounded, total, new = [], [], [], []
            for t in range(tiles):
                lanes = tile_rows(t)
                parts = [scores[h][tile_rows(j), lanes] for j in range(count)]
                new_max = maxima[h][t]
                for j in range(count):
                    new_max = jnp.maximum(new_max, jnp.max(parts[j], axis=0, keepdims=True) - off[j][:, lanes])
                scaled = new_max * SCALE2
                weights = [jnp.exp2(parts[j] * SCALE2 - (scaled + off[j][:, lanes])) for j in range(count)]
                factor.append(jnp.exp2((maxima[h][t] - new_max) * SCALE2))
                total.append(jnp.sum(functools.reduce(jnp.add, weights), axis=0, keepdims=True))
                new.append(new_max)
                rounded.append(jnp.concatenate([w.astype(jnp.bfloat16) for w in weights], axis=0))
            updates.append(
                jnp.dot(
                    jnp.concatenate([piece(slot, 2 * j + 1, h) for j in range(count)], axis=1),
                    jnp.concatenate(rounded, axis=1),
                    preferred_element_type=jnp.float32,
                )
            )
            factors.append(jnp.concatenate(factor, axis=1))
            sums.append(jnp.concatenate(total, axis=1))
            largest.append(jnp.concatenate(new, axis=1))
        for h in range(heads):
            own = head_columns(h)
            state[half, own] = state[half, own] * factors[h] + updates[h]
            state[half, pl.ds(columns + h, 1), :] = largest[h]
            state[half, pl.ds(columns + heads + h, 1), :] = totals[h] * factors[h] + sums[h]

    @pl.loop(0, halves * len(places))
    def _(unit):
        half, slot = unit // len(places), unit % len(places)
        first = chosen(slot, [place(me) for place in places])

        if unless_far:
            first = jnp.where(far > 0, -count, first)

        @pl.when((first < chosen(half, stops)) & (first + count > chosen(half, begins)))
        def _():
            fold(half, slot, first)

    for half in range(halves):
        if brief:
            at = half * new_refs[0].shape[0] // halves
            new_refs[0][at : at + columns] = state[half, :columns].astype(jnp.bfloat16)
            for n, part in enumerate(summands(state[half, columns:])):
                row = at + columns + n * 2 * 8
                new_refs[0][row : row + 2 * 8] = jnp.concatenate([part, part], axis=0)
        else:
            new_refs[half][...] = state[half]


def attend(bounds, queries, blocks, places, states, which=None, shifts=None, unless_far=False, brief=False):
    which = list(range(len(queries))) if which is None else which
    queries, states = [queries[w] for w in which], [states[w] for w in which] if states else []
    halves = len(which)
    rows, columns = queries[0].shape
    depth = blocks[0].shape[0]
    heads = columns // HEAD_DIM
    shape = jax.ShapeDtypeStruct((columns + -(-2 * heads // 8) * 8, rows), jnp.float32)
    arrays = list(enumerate(shifts or [None] * len(blocks)))
    pairs = halves * (rows // TILE) * heads * len(blocks) * (depth // 2 // TILE)
    sent = jax.ShapeDtypeStruct((halves * (columns + 3 * 2 * 8), rows), jnp.bfloat16)
    return pl.pallas_call(
        functools.partial(attend_kernel, which, places, arrays, not states, unless_far, brief),
        out_shape=[sent] if brief else [shape] * halves,
        in_specs=[VMEM] * (1 + halves + len(blocks) + len(states)),
        out_specs=[VMEM] * (1 if brief else halves),
        scratch_shapes=[
            pltpu.VMEM((halves, rows, columns), queries[0].dtype),
            pltpu.VMEM((len(blocks), depth, columns), blocks[0].dtype),
            pltpu.VMEM((halves,) + shape.shape, jnp.float32),
        ],
        compiler_params=params(),
        cost_estimate=pl.CostEstimate(
            flops=COST * pairs * 4 * TILE * TILE * HEAD_DIM,
            bytes_accessed=2 * len(blocks) * depth * columns + 4 * halves * rows * columns,
            transcendentals=pairs * TILE * TILE,
        ),
        name="attend",
    )(bounds, *queries, *blocks, *states)


def merged(states, columns):
    heads = columns // HEAD_DIM
    for h in range(heads):
        maxima = [ref[columns + h : columns + h + 1] for ref in states]
        totals = [ref[columns + heads + h : columns + heads + h + 1] for ref in states]
        largest = functools.reduce(jnp.maximum, maxima)
        factors = [jnp.exp2((m - largest) * SCALE2) for m in maxima]
        total = functools.reduce(jnp.add, [f * t for f, t in zip(factors, totals)])
        parts = [ref[head_columns(h)] * (f / total) for ref, f in zip(states, factors)]
        yield head_columns(h), functools.reduce(jnp.add, parts).T


def finish_kernel(*refs):
    out_ref = refs[-1]
    for own, done in merged(refs[:-1], out_ref.shape[1]):
        out_ref[:, own] = done.astype(out_ref.dtype)


def finish(states, rows, columns):
    return pl.pallas_call(
        finish_kernel,
        out_shape=jax.ShapeDtypeStruct((rows, columns), jnp.bfloat16),
        in_specs=[VMEM] * len(states),
        out_specs=VMEM,
        compiler_params=params(),
        name="finish",
    )(*states)


def message_kernel(part, ref, got_ref, *refs):
    keep_ref, send_ref, held = refs[-3:]
    rows = keep_ref.shape[0] - 2 * 8
    columns = keep_ref.shape[1]
    heads = columns // HEAD_DIM
    mine = lax.axis_index("head")
    at = part * got_ref.shape[0] // 2
    logs = []
    rest = got_ref[at + columns : at + got_ref.shape[0] // 2].astype(jnp.float32)
    statistics = functools.reduce(jnp.add, [rest[n * 2 * 8 : n * 2 * 8 + 8] for n in range(3)])
    for h in range(heads):
        maxima = [ref[columns + h : columns + h + 1], statistics[h : h + 1]]
        totals = [ref[columns + heads + h : columns + heads + h + 1], statistics[heads + h : heads + h + 1]]
        largest = jnp.maximum(*maxima)
        factors = [jnp.exp2((m - largest) * SCALE2) for m in maxima]
        total = factors[0] * totals[0] + factors[1] * totals[1]
        some = jnp.where(total > 0, total, 1.0)
        scale = [f / some for f in factors]
        own = head_columns(h)
        got = got_ref[at + h * HEAD_DIM : at + (h + 1) * HEAD_DIM].astype(jnp.float32)
        sums = ref[own] * scale[0] + got * scale[1]
        held[:, own] = sums.T.astype(held.dtype)
        log = jnp.where(total > 0, largest * SCALE2 + jnp.log2(some), LOWEST)
        logs += [part.astype(jnp.float32) for part in summands(log)]
    logs = jnp.concatenate(logs + [jnp.zeros((2 * 8 - len(logs), held.shape[0]), jnp.float32)], axis=0)
    later = pltpu.roll(logs, rows, 1)
    for out_ref, which in ((send_ref, 1 - mine), (keep_ref, mine)):
        out_ref[:rows] = held[pl.ds(pl.multiple_of(which * rows, 2 * 8), rows), :]
        out_ref[rows:] = jnp.where(which == 0, logs, later).astype(out_ref.dtype)


def messages(part, state, got, *after):
    rows, columns = state.shape[1], state.shape[0] // HEAD_DIM * HEAD_DIM
    shape = jax.ShapeDtypeStruct((rows // 2 + 2 * 8, columns), jnp.bfloat16)
    return pl.pallas_call(
        functools.partial(message_kernel, part),
        out_shape=[shape] * 2,
        in_specs=[VMEM] * 2 + [HBM] * len(after),
        out_specs=[VMEM] * 2,
        scratch_shapes=[pltpu.VMEM((rows, columns), jnp.bfloat16)],
        compiler_params=params(),
        name="message",
    )(state, got, *after)


def settle_kernel(*refs):
    parts, out_ref, logs = [refs[0], refs[2], refs[1], refs[3]], refs[4], refs[5]
    rows, columns = out_ref.shape[0], parts[0].shape[1]
    heads = columns // HEAD_DIM
    mine = lax.axis_index("head")
    logs[...] = jnp.zeros(logs.shape, jnp.float32)
    for i, ref in enumerate(parts):
        summands = ref[rows:].astype(jnp.float32)
        for h in range(heads):
            at = i * heads + h
            logs[at : at + 1] = functools.reduce(jnp.add, [summands[3 * h + n : 3 * h + n + 1] for n in range(3)])
    turned = logs[...].T[:rows]
    for side, base in ((0, 1 - mine), (1, mine)):
        for h in range(heads):
            both = [turned[:, at : at + 1] for at in (2 * side * heads + h, (2 * side + 1) * heads + h)]
            largest = jnp.maximum(*both)
            weights = [jnp.exp2(x - largest) for x in both]
            sums = [ref[:rows, head_columns(h)].astype(jnp.float32) for ref in parts[2 * side : 2 * side + 2]]
            total = weights[0] + weights[1]
            done = sums[0] * (weights[0] / total) + sums[1] * (weights[1] / total)
            at = pl.multiple_of(base * columns + h * HEAD_DIM, HEAD_DIM)
            out_ref[:, pl.ds(at, HEAD_DIM)] = done.astype(out_ref.dtype)


def settle(diagonal, across, beside, own):
    rows, columns = own.shape[0] - 2 * 8, own.shape[1]
    return pl.pallas_call(
        settle_kernel,
        out_shape=jax.ShapeDtypeStruct((rows, 2 * columns), own.dtype),
        in_specs=[VMEM] * 4,
        out_specs=VMEM,
        scratch_shapes=[pltpu.VMEM((TILE, columns), jnp.float32)],
        compiler_params=params(),
        name="settle",
    )(diagonal, across, beside, own)


def chip_pairs(mesh):
    places = [tuple(getattr(d, "coords", ())) for d in mesh.devices[:, 0]]
    count = len(places)
    if count % 4 or not places[0] or mesh.shape["head"] != 2:
        return False
    cores = all(places[i] == places[i + 1] for i in range(0, count, 2))
    level = all(places[i][2] == places[i + 3][2] for i in range(0, count, 4))
    climb = all(places[i][2] != places[i + 4][2] for i in range(0, count - 4))
    return cores and level and climb


def paired_shards(owner_count, queries, keys, values, image_tiles):
    rows, columns = queries.shape
    tiles = rows // TILE
    owners = range(owner_count)

    def flip(s):
        return 1 - 2 * ((s // 2) % 2)

    def core(s):
        return s % 2

    def moved(array, source, takes=lambda s: True):
        pairs = [(source(s), s) for s in owners if takes(s) and 0 <= source(s) < owner_count]
        return lax.ppermute(array, "seq", pairs)

    across = lambda s: s + 2 * flip(s)
    near_side = lambda s: s + 4 * flip(s)
    far_side = lambda s: s - 4 * flip(s)
    along = lambda s: s + 4 * flip(s) * (1 - 2 * core(s))
    against = lambda s: s - 4 * flip(s) * (1 - 2 * core(s))
    sibling = lambda s: s + 1 - 2 * core(s)
    inner = lambda s: core(s) == (1 - (s // 2) % 2)

    OWN = lambda s: s * tiles
    A1 = lambda s: along(s) * tiles
    B1 = lambda s: against(s) * tiles
    A2 = lambda s: (s + 8 * flip(s)) * tiles
    B2 = lambda s: jnp.where(inner(s), s - 8 * flip(s), -owner_count) * tiles

    peers = moved(queries, across)
    block = pack(keys, values)
    a1, b1 = moved(block, along), moved(block, against)
    level = (queries, moved(queries, sibling), peers, moved(peers, sibling))
    bounds, far = meta(lambda s: [s, sibling(s), across(s), sibling(across(s))], image_tiles, rows)
    fold = functools.partial(attend, bounds, level)
    states = fold([block], [OWN], [], which=[0, 1]) + fold([block], [OWN], [], which=[2, 3])
    states = fold([b1], [B1], states, unless_far=True)

    def merge(blocks, places, states, shifts=None):
        (others,) = fold(blocks, places, states, which=[1, 3], shifts=shifts, brief=True)
        got = moved(others, sibling)
        mine, peer = fold(blocks, places, states, which=[0, 2], shifts=shifts)
        over_y, over_both = messages(1, peer, got)
        keep, over_x = messages(0, mine, got, over_y)
        pairs = [(2 * across(s) + 1 - x, 2 * s + x) for s in owners for x in range(2)]
        over_both = lax.ppermute(over_both, ("seq", "head"), pairs)
        over_y = moved(over_y, across)
        over_x = lax.ppermute(over_x, "head", [(0, 1), (1, 0)])
        return settle(over_both, over_y, over_x, keep)

    def near_only(block, a1, b1, states):
        return merge([a1], [A1], states)

    def both_ways(block, a1, b1, states):
        near, corner = onward(a1, b1, block)
        a2, b2 = moved(near, near_side), moved(corner, far_side, inner)
        states = fold([a1, b1], [A1, B1], states)
        return merge([a2, b2], [A2, B2], states, [None, lambda s: 2 * TILE * core(s)])

    return lax.cond(far > 0, both_ways, near_only, block, a1, b1, states)


def ring_shards(owner_count, queries, keys, values, image_tiles):
    rows, columns = queries.shape
    tiles = rows // TILE
    reach = min(owner_count - 1, -(-(MOST_TILES - 1) // tiles))
    block = pack(keys, values)
    bounds, _ = meta(lambda s: [s], image_tiles, rows)
    fold = functools.partial(attend, bounds, (queries,))
    up = [(i, i + 1) for i in range(owner_count - 1)]
    down = [(i + 1, i) for i in range(owner_count - 1)]
    below = above = block
    states = []
    held, places = [block], [lambda s: s * tiles]
    for k in range(1, reach + 1):
        below = lax.ppermute(below, "seq", up)
        above = lax.ppermute(above, "seq", down)
        states = fold(held, places, states)
        held, places = [below, above], [lambda s, k=k: (s - k) * tiles, lambda s, k=k: (s + k) * tiles]
    attended = finish(fold(held, places, states), rows, columns)
    return lax.all_to_all(attended, "head", split_axis=0, concat_axis=1, tiled=True)


def solution(mesh):
    owner_count = mesh.shape["seq"]
    plan = paired_shards if chip_pairs(mesh) else ring_shards
    placed = (P("seq", "head"), P("seq", "head"), P("seq", "head"), P())
    return jax.shard_map(
        functools.partial(plan, owner_count),
        mesh=mesh,
        in_specs=placed,
        out_specs=P(("seq", "head"), None),
        check_vma=False,
    )
```
